32 devices in a mesh: req: 4 (over y, core), tp: 8 (over z, x).
Axes of the slice: x: 2, y: 2, z: 4, core: 2. Of those that a mesh axis runs over, the one named last changes fastest.
Arguments:
- queries: bfloat16 [512, 1536], P(('req', 'tp')), may hold values from -8 to 8
- new_kv: bfloat16 [512, 1024], P(('req', 'tp')), may hold values from -6 to 6
- residual: bfloat16 [512, 1536], P(('req', 'tp')), may hold values from -6 to 6
- placement: int32 [8], P('req'), may hold values from 0 to 7, as said below
- lengths: int32 [8], P('req'), may hold values from 2 to 1024
- page_table: int32 [8, 1, 8], P('req', None, 'tp'), may hold values from 0 to 1, as said below
- cache_keys: bfloat16 [64, 128, 512], P(('req', 'tp')), may hold values from -6 to 6
- cache_values: bfloat16 [64, 128, 512], P(('req', 'tp')), may hold values from -6 to 6
- parents: int32 [8, 64], P('req'), may hold values from 0 to 62, as said below
- accept_leaf: int32 [8], P('req'), may hold values from 0 to 63
- out_weight: bfloat16 [1536, 1536], replicated, may hold values from -0.15625 to 0.15625
- norm_gain: float32 [1536], replicated, may hold values from 0.1 to 1.9
- router_weight: bfloat16 [1536, 40], replicated, may hold values from -0.15625 to 0.15625
- expert_ids: int32 [512, 8], P('req'), may hold values from 0 to 39, all different within a row
- gate_up: bfloat16 [160, 1536, 256], P('tp'), may hold values from -0.15625 to 0.15625
- down_weight: bfloat16 [160, 128, 1536], P('tp'), may hold values from -0.25 to 0.25
Outputs:
- attn_out: bfloat16 [512, 1536], P(('req', 'tp'))
- layer_out: bfloat16 [512, 1536], P(('req', 'tp'))
- accepted_kv: bfloat16 [512, 1024], P(('req', 'tp'))
The draws below stay inside these ranges and needn't reach their ends.
Inputs may be any that keep to these rules, and one draw needn't show every extreme that they name: `placement`: slot s of each group of 2 slots holds a request whose index is s modulo 2; every request is held once. `page_table`: within each group of 2 slots and each last index, the 2 entries are distinct. parents[s, n] < n for n > 0; parents[s, 0] = 0.
All inputs are finite; a program needn't handle non-finite values.
Results may differ from the reference program's by a relative error of at most 0.01.
Values may be sent and summed in bfloat16 or wider, within the bound.
No kernel may reach another device: no remote copies, remote signals or barrier semaphores. Data moves between devices by JAX's collectives and lax.ppermute only.
A program may use at most 128 MiB of HBM per device.

```python
import math
import jax
import jax.numpy as jnp
from jax import lax

D = 1536
HEADS = 24
KV_HEADS = 8
HEAD = 64
EXPERTS = 40
FF_E = 512
TOPK = 8
UNIT = 128
DRAFT = 64
PAGE = 128
LOCAL_PAGES = 1
REQ_DEV = 2
REQS = 8
TOKENS = 512
UNITS = 160
MAXPAGES = 8
MAXLEN = 1024
PAGES = 64
N_TP = 8


def draw_queries(key, part):
    fresh_key = jax.random.fold_in(key, 11)
    base_draw = jnp.clip(2.0 * jax.random.normal(fresh_key, (TOKENS, HEADS, HEAD), jnp.float32), -8.0, 8.0)
    return base_draw.reshape(TOKENS, HEADS * HEAD).astype(jnp.bfloat16)


def draw_cache_keys(key, part):
    fresh_key = jax.random.fold_in(key, 23)
    base_draw = jnp.clip(jax.random.normal(fresh_key, (PAGES, PAGE, KV_HEADS, HEAD), jnp.float32), -6.0, 6.0)
    return base_draw.reshape(PAGES, PAGE, KV_HEADS * HEAD).astype(jnp.bfloat16)


def permute_groups(one_key):
    return jax.random.permutation(one_key, REQS // REQ_DEV)


def draw_placement(key, part):
    slot_keys = jax.random.split(jax.random.fold_in(key, 31), REQ_DEV)
    orders = jax.vmap(permute_groups)(slot_keys)
    slot_ids = jnp.arange(REQ_DEV, dtype=jnp.int32)
    placed = jnp.transpose(orders).astype(jnp.int32) * REQ_DEV + slot_ids[None, :]
    return placed.reshape(REQS).astype(jnp.int32)


def draw_lengths(key, part):
    base_draw = jax.random.randint(jax.random.fold_in(key, 41), (REQS,), 2, MAXLEN + 1)
    shifts = jax.random.randint(jax.random.fold_in(key, 43), (REQS,), 0, 6)
    drawn = jnp.maximum(jnp.right_shift(base_draw, shifts), 2)
    top_index = jax.random.randint(jax.random.fold_in(key, 45), (), 0, REQS // 2)
    low_index = REQS // 2 + jax.random.randint(jax.random.fold_in(key, 47), (), 0, REQS - REQS // 2)
    drawn = drawn.at[top_index].set(MAXLEN)
    drawn = drawn.at[low_index].set(2)
    return drawn.astype(jnp.int32)


def permute_pool(one_key):
    return jax.random.permutation(one_key, REQ_DEV * LOCAL_PAGES)


def draw_page_table(key, part):
    columns = PAGES // (REQS * LOCAL_PAGES)
    group_count = REQS // REQ_DEV
    pool_keys = jax.random.split(jax.random.fold_in(key, 53), group_count * columns)
    orders = jax.vmap(permute_pool)(pool_keys)
    table = orders.reshape(group_count, columns, REQ_DEV, LOCAL_PAGES)
    return jnp.transpose(table, (0, 2, 3, 1)).reshape(REQS, LOCAL_PAGES, columns).astype(jnp.int32)


def draw_parents(key, part):
    node_ids = jnp.arange(DRAFT, dtype=jnp.int32)
    raw_draw = jax.random.randint(jax.random.fold_in(key, 61), (REQS, DRAFT), 0, 1 << 20)
    drawn = raw_draw % jnp.maximum(node_ids, 1)[None, :]
    drawn = drawn.at[:, DRAFT - 1].set(DRAFT - 2)
    return drawn.astype(jnp.int32)


def draw_accept_leaf(key, part):
    drawn = jax.random.randint(jax.random.fold_in(key, 71), (REQS,), 0, DRAFT)
    top_index = jax.random.randint(jax.random.fold_in(key, 73), (), 0, REQS // 2)
    low_index = REQS // 2 + jax.random.randint(jax.random.fold_in(key, 75), (), 0, REQS - REQS // 2)
    drawn = drawn.at[top_index].set(DRAFT - 1)
    drawn = drawn.at[low_index].set(0)
    return drawn.astype(jnp.int32)


def shard_levels(own_key, dims, pieces, low, top_value):
    factor_of = 1.0
    for position, shards_of in pieces:
        draws = jax.random.uniform(jax.random.fold_in(jax.random.fold_in(own_key, 6), position), (shards_of,), jnp.float32, low / len(pieces), top_value / len(pieces))
        factor_of = factor_of * jnp.repeat(jnp.exp(draws), dims[position] // shards_of).reshape((-1,) + (1,) * (len(dims) - 1 - position))
    return factor_of


def distinct(rng, rows, count, top, lift):
    order = jax.random.permutation(jax.random.fold_in(rng, 1), count)
    pull = order
    for power in range(3):
        pull = pull * pull // count
    pull = pull * lift // count
    tickets = jax.random.randint(jax.random.fold_in(rng, 2), (rows, count), 0, 4096) + pull
    fixed_rows = jax.random.permutation(jax.random.fold_in(rng, 3), rows)[jnp.arange(count) % rows]
    tickets = jnp.where(jnp.arange(rows)[:, None] == fixed_rows[None, :], 1 << 14, tickets)
    score = tickets * count + jnp.arange(count)
    return lax.top_k(score.astype(jnp.int32), top)[1].astype(jnp.int32)


def bell_draw(own_key, shape, deviation, bound, pieces=(), kind=jnp.bfloat16):
    array = deviation * jax.random.normal(own_key, shape, jnp.float32)
    if pieces:
        array = array * shard_levels(own_key, shape, pieces, -0.22, 0.18)
    return jnp.clip(array, -bound, bound).astype(kind)


def setup_inputs(seed: int = 0) -> dict:
    key_list = jax.random.split(jax.random.key(seed), 17)
    return {
        "queries": draw_queries(jax.random.fold_in(key_list[16], 71), 0),
        "new_kv": bell_draw(key_list[1], (TOKENS, 2 * KV_HEADS * HEAD), 1.0, 6.0, ((0, 32),)),
        "residual": bell_draw(key_list[2], (TOKENS, D), 1.0, 6.0, ((0, 32),)),
        "placement": draw_placement(jax.random.fold_in(key_list[16], 71), 0),
        "lengths": draw_lengths(jax.random.fold_in(key_list[16], 71), 0),
        "page_table": draw_page_table(jax.random.fold_in(key_list[16], 71), 0),
        "cache_keys": draw_cache_keys(jax.random.fold_in(key_list[16], 71), 0),
        "cache_values": bell_draw(key_list[7], (PAGES, PAGE, KV_HEADS * HEAD), 1.0, 6.0, ((0, 32),)),
        "parents": draw_parents(jax.random.fold_in(key_list[16], 71), 0),
        "accept_leaf": draw_accept_leaf(jax.random.fold_in(key_list[16], 71), 0),
        "out_weight": bell_draw(key_list[10], (HEADS * HEAD, D), (HEADS * HEAD) ** -0.5, 0.15625),
        "norm_gain": jnp.clip(1.0 + 0.18 * jax.random.normal(key_list[11], (D,), jnp.float32), 0.1, 1.9),
        "router_weight": bell_draw(key_list[12], (D, EXPERTS), D ** -0.5, 0.15625),
        "expert_ids": distinct(key_list[13], TOKENS, EXPERTS, TOPK, 3276),
        "gate_up": bell_draw(key_list[14], (UNITS, D, 2 * UNIT), D ** -0.5, 0.15625, ((0, 8),)),
        "down_weight": bell_draw(key_list[15], (UNITS, UNIT, D), FF_E ** -0.5, 0.25, ((0, 8),)),
    }


neg_big = -1e+30
norm_eps = 1e-06

def ancestry(parents):
    node_count = parents.shape[-1]
    node_ids = jnp.arange(node_count, dtype=jnp.int32)
    linked = (parents[:, :, None] == node_ids[None, None, :]) & (node_ids[None, :, None] > 0)
    reached = jnp.maximum(linked.astype(jnp.float32), jnp.eye(node_count, dtype=jnp.float32)[None])
    for _ in range(node_count.bit_length()):
        reached = jnp.minimum(jnp.einsum('rnm,rmk->rnk', reached, reached, precision=lax.Precision.HIGHEST), 1.0)
    return reached

def reference(queries, new_kv, residual, placement, lengths, page_table, cache_keys, cache_values, parents, accept_leaf, out_weight, norm_gain, router_weight, expert_ids, gate_up, down_weight):
    group_size = HEADS // KV_HEADS
    kv_width = KV_HEADS * HEAD
    score_scale = 1.0 / math.sqrt(HEAD)
    pool_size = REQ_DEV * LOCAL_PAGES
    placed_q = jnp.take(queries.reshape(REQS, DRAFT, HEADS * HEAD), placement, axis=0)
    placed_kv = jnp.take(new_kv.reshape(REQS, DRAFT, 2 * kv_width), placement, axis=0)
    placed_res = jnp.take(residual.reshape(REQS, DRAFT, D), placement, axis=0).reshape(TOKENS, D)
    reached = ancestry(parents)
    page_index = jnp.arange(MAXPAGES, dtype=jnp.int32)
    page_col = page_index % N_TP
    page_loc = page_index // N_TP
    slot_index = jnp.arange(REQS, dtype=jnp.int32)
    node_ids = jnp.arange(DRAFT, dtype=jnp.int32)

    def one_slot(slot_items):
        slot_id, q_rows, kv_rows, slot_len, table_row, reach_slot, leaf_node = slot_items
        page_ids = (slot_id // REQ_DEV * N_TP + page_col) * pool_size + table_row[page_loc, page_col]
        keys_slot = jnp.take(cache_keys, page_ids, axis=0).reshape(MAXPAGES, PAGE, KV_HEADS, HEAD).astype(jnp.float32)
        values_slot = jnp.take(cache_values, page_ids, axis=0).reshape(MAXPAGES, PAGE, KV_HEADS, HEAD).astype(jnp.float32)
        query_blocks = q_rows.astype(jnp.float32).reshape(DRAFT, KV_HEADS, group_size, HEAD)
        scores = jnp.einsum('sgrd,ptgd->sgrpt', query_blocks, keys_slot) * score_scale
        positions = page_index[:, None] * PAGE + jnp.arange(PAGE, dtype=jnp.int32)[None, :]
        is_valid = (positions < slot_len)[None, None, None]
        scores = jnp.where(is_valid, scores, neg_big)
        block_max = lax.optimization_barrier(jnp.max(scores, axis=-1))
        weights = jnp.where(is_valid, jnp.exp(scores - block_max[..., None]), 0.0).astype(jnp.bfloat16).astype(jnp.float32)
        block_sum = lax.optimization_barrier(jnp.sum(weights, axis=-1))
        block_out = jnp.einsum('sgrpt,ptgd->sgrpd', weights, values_slot)
        tree_keys = kv_rows[:, :kv_width].astype(jnp.float32).reshape(DRAFT, KV_HEADS, HEAD)
        tree_values = kv_rows[:, kv_width:].astype(jnp.float32).reshape(DRAFT, KV_HEADS, HEAD)
        tree_scores = jnp.einsum('sgrd,tgd->sgrt', query_blocks, tree_keys) * score_scale
        tree_mask = (reach_slot > 0.5)[:, None, None, :]
        tree_scores = jnp.where(tree_mask, tree_scores, neg_big)
        tree_max = lax.optimization_barrier(jnp.max(tree_scores, axis=-1))
        tree_weights = jnp.where(tree_mask, jnp.exp(tree_scores - tree_max[..., None]), 0.0).astype(jnp.bfloat16).astype(jnp.float32)
        tree_sum = lax.optimization_barrier(jnp.sum(tree_weights, axis=-1))
        tree_out = jnp.einsum('sgrt,tgd->sgrd', tree_weights, tree_values)
        top_score = jnp.maximum(lax.optimization_barrier(jnp.max(block_max, axis=-1)), tree_max)
        block_scale = jnp.exp(block_max - top_score[..., None])
        tree_scale = jnp.exp(tree_max - top_score)
        running = lax.optimization_barrier(jnp.sum(block_sum * block_scale, axis=-1)) + tree_sum * tree_scale
        summed = jnp.einsum('sgrp,sgrpd->sgrd', block_scale, block_out) + tree_out * tree_scale[..., None]
        attn_rows = (summed / running[..., None]).reshape(DRAFT, HEADS * HEAD).astype(jnp.bfloat16)
        path_flags = (jnp.take(reach_slot, leaf_node, axis=0) > 0.5).astype(jnp.int32)
        path_rank = jnp.cumsum(path_flags) - 1
        select = ((path_flags[None, :] > 0) & (path_rank[None, :] == node_ids[:, None])).astype(jnp.float32)
        accepted_rows = jnp.dot(select, kv_rows.astype(jnp.float32), precision=lax.Precision.HIGHEST).astype(jnp.bfloat16)
        return (attn_rows, accepted_rows)
    attn_all, accepted_all = lax.map(one_slot, (slot_index, placed_q, placed_kv, lengths, page_table, reached, accept_leaf))
    attn_out = attn_all.reshape(TOKENS, HEADS * HEAD)
    hidden = placed_res.astype(jnp.float32) + jnp.dot(attn_out, out_weight, preferred_element_type=jnp.float32)
    normed = (hidden * lax.rsqrt(lax.optimization_barrier(jnp.mean(hidden * hidden, axis=-1, keepdims=True)) + norm_eps) * norm_gain.astype(jnp.float32)).astype(jnp.bfloat16)
    logits = jnp.dot(normed, router_weight, preferred_element_type=jnp.float32)
    onehot = (expert_ids[:, :, None] == jnp.arange(EXPERTS, dtype=jnp.int32)[None, None, :]).astype(jnp.float32)
    chosen = lax.optimization_barrier(jnp.sum(logits[:, None, :] * onehot, axis=-1))
    expo_chosen = jnp.exp(chosen)
    expert_probs = expo_chosen / lax.optimization_barrier(jnp.sum(expo_chosen, axis=-1, keepdims=True))
    routing = lax.optimization_barrier(jnp.sum(expert_probs[:, :, None] * onehot, axis=1))
    unit_span = FF_E // UNIT

    def add_unit(running, unit_items):
        unit_id, weights_gu, weights_down = unit_items
        gate_both = jnp.dot(normed, weights_gu, preferred_element_type=jnp.float32)
        share = lax.dynamic_slice_in_dim(routing, (unit_id // unit_span).astype(jnp.int32), 1, 1)
        activated = (jax.nn.silu(gate_both[:, :UNIT]) * gate_both[:, UNIT:] * share).astype(jnp.bfloat16)
        return (running + jnp.dot(activated, weights_down, preferred_element_type=jnp.float32), None)
    moe, _ = lax.scan(add_unit, jnp.zeros((TOKENS, D), jnp.float32), (jnp.arange(UNITS, dtype=jnp.int32), gate_up, down_weight))
    layer_out = (hidden + moe).astype(jnp.bfloat16)
    return (attn_out, layer_out, accepted_all.reshape(TOKENS, 2 * kv_width))
```

```python
import functools
import math

import jax
import jax.numpy as jnp
from jax import lax
from jax.experimental import pallas as pl
from jax.experimental.pallas import tpu as pltpu
from jax.sharding import PartitionSpec as P

HEADS = 24
KV_HEADS = 8
HEAD = 64
FF_E = 512
UNIT = 128
DRAFT = 64
WIDE = 128


neg_big = -1e30
norm_eps = 1e-06


def joined_2(part, axis, combine):
    gathered = jax.tree.map(lambda a: lax.all_gather(a, axis), part)

    def take(source):
        return jax.tree.map(lambda a: lax.dynamic_index_in_dim(a, source, 0, False), gathered)

    return lax.fori_loop(
        1, lax.axis_size(axis), lambda source, state: combine(state, take(source)), take(0)
    )


def ancestry(parents):
    node_count = parents.shape[-1]
    node_ids = jnp.arange(node_count, dtype=jnp.int32)
    linked = (parents[:, :, None] == node_ids[None, None, :]) & (node_ids[None, :, None] > 0)
    reached = jnp.maximum(linked.astype(jnp.float32), jnp.eye(node_count, dtype=jnp.float32)[None])
    for _ in range(node_count.bit_length()):
        reached = jnp.minimum(
            jnp.einsum("rnm,rmk->rnk", reached, reached, precision=lax.Precision.HIGHEST), 1.0
        )
    return reached


def combine_stats(left_stats, right_stats):
    left_max, left_sum, left_out = left_stats
    right_max, right_sum, right_out = right_stats
    top_score = jnp.maximum(left_max, right_max)
    left_scale = jnp.exp(left_max - top_score)
    right_scale = jnp.exp(right_max - top_score)
    row_count, head_count = left_max.shape
    out_sum = (
        left_out.reshape(row_count, head_count, -1) * left_scale[..., None]
        + right_out.reshape(row_count, head_count, -1) * right_scale[..., None]
    )
    return (
        top_score,
        left_sum * left_scale + right_sum * right_scale,
        out_sum.reshape(row_count, -1),
    )


def finish_rows(stat_sum, stat_out):
    row_count, head_count = stat_sum.shape
    return (
        (stat_out.reshape(row_count, head_count, -1) / stat_sum[..., None])
        .reshape(row_count, -1)
        .astype(jnp.bfloat16)
    )


def project_rows(attn_rows, res_rows, out_weight):
    return res_rows.astype(jnp.float32) + jnp.dot(
        attn_rows, out_weight, preferred_element_type=jnp.float32
    )


def rms_normed(hidden, norm_gain):
    scale_rows = lax.rsqrt(jnp.mean(hidden * hidden, axis=-1, keepdims=True) + norm_eps)
    return (hidden * scale_rows * norm_gain).astype(jnp.bfloat16)


def unit_shares(normed_all, router_weight, expert_ids, tp_rank, units_dev):
    logits = jnp.dot(normed_all, router_weight, preferred_element_type=jnp.float32)
    expert_range = jnp.arange(router_weight.shape[1], dtype=jnp.int32)
    onehot = (expert_ids[:, :, None] == expert_range[None, None, :]).astype(jnp.float32)
    chosen = jnp.sum(logits[:, None, :] * onehot, axis=-1)
    expo_chosen = jnp.exp(chosen)
    expert_probs = expo_chosen / jnp.sum(expo_chosen, axis=-1, keepdims=True)
    routing = jnp.sum(expert_probs[:, :, None] * onehot, axis=1)
    unit_ids = tp_rank * units_dev + jnp.arange(units_dev, dtype=jnp.int32)
    expert_of_unit = unit_ids // (FF_E // UNIT)
    pick = (expert_range[:, None] == expert_of_unit[None, :]).astype(jnp.float32)
    return jnp.dot(routing, pick, precision=lax.Precision.HIGHEST)


def per_device_plain(
    queries,
    new_kv,
    residual,
    placement,
    lengths,
    page_table,
    cache_keys,
    cache_values,
    parents,
    accept_leaf,
    out_weight,
    norm_gain,
    router_weight,
    expert_ids,
    gate_up,
    down_weight,
):
    tok_dev = queries.shape[0]
    tp_count = lax.axis_size("tp")
    tp_rank = lax.axis_index("tp")
    group_rows = tok_dev * tp_count
    slot_count = placement.shape[0]
    kv_width = cache_keys.shape[2]
    page_len = cache_keys.shape[1]
    group_size = HEADS // KV_HEADS
    score_scale = 1.0 / math.sqrt(HEAD)
    row_start = tp_rank * tok_dev
    pulled_q, pulled_kv, pulled_res = (
        lax.all_gather(queries, "req", axis=0, tiled=True),
        lax.all_gather(new_kv, "req", axis=0, tiled=True),
        lax.all_gather(residual, "req", axis=0, tiled=True),
    )
    row_offsets = jnp.arange(tok_dev, dtype=jnp.int32)
    row_pos = row_start + row_offsets
    row_slot = row_pos // DRAFT
    slot_match = row_slot[:, None] == jnp.arange(slot_count, dtype=jnp.int32)[None, :]
    source_group = jnp.sum(jnp.where(slot_match, placement[None, :] // slot_count, 0), axis=1)
    source_rows = source_group * tok_dev + row_offsets
    own_q = jnp.take(pulled_q, source_rows, axis=0)
    own_kv = jnp.take(pulled_kv, source_rows, axis=0)
    own_res = jnp.take(pulled_res, source_rows, axis=0)
    all_q, all_kv = (
        lax.all_gather(own_q, "tp", axis=0, tiled=True),
        lax.all_gather(own_kv, "tp", axis=0, tiled=True),
    )
    local_pages = page_table.shape[1]
    page_ids = page_table[:, :, 0].reshape(-1)
    keys_local = jnp.take(cache_keys, page_ids, axis=0).reshape(
        slot_count, local_pages, page_len, KV_HEADS, HEAD
    )
    values_local = jnp.take(cache_values, page_ids, axis=0).reshape(
        slot_count, local_pages, page_len, KV_HEADS, HEAD
    )
    query_blocks = all_q.reshape(slot_count, DRAFT, KV_HEADS, group_size, HEAD)
    scores = (
        jnp.einsum(
            "sqgrd,sltgd->sqgrlt", query_blocks, keys_local, preferred_element_type=jnp.float32
        )
        * score_scale
    )
    positions = (
        jnp.arange(local_pages, dtype=jnp.int32)[:, None] * tp_count + tp_rank
    ) * page_len + jnp.arange(page_len, dtype=jnp.int32)[None, :]
    is_valid = (positions[None] < lengths[:, None, None])[:, None, None, None]
    scores = jnp.where(is_valid, scores, neg_big)
    block_max = jnp.max(scores, axis=-1)
    weights = jnp.where(is_valid, jnp.exp(scores - block_max[..., None]), 0.0).astype(jnp.bfloat16)
    block_sum = jnp.sum(weights.astype(jnp.float32), axis=-1)
    block_out = jnp.einsum(
        "sqgrlt,sltgd->sqgrld", weights, values_local, preferred_element_type=jnp.float32
    )
    page_top = jnp.max(block_max, axis=-1)
    page_scale = jnp.exp(block_max - page_top[..., None])
    stat_max = page_top.reshape(group_rows, HEADS)
    stat_sum = jnp.sum(block_sum * page_scale, axis=-1).reshape(group_rows, HEADS)
    stat_out = jnp.sum(block_out * page_scale[..., None], axis=-2).reshape(group_rows, HEADS * HEAD)
    reached = ancestry(parents)
    reach_rows = jnp.take(reached.reshape(slot_count * DRAFT, DRAFT), row_pos, axis=0)
    key_slot = jnp.arange(group_rows, dtype=jnp.int32) // DRAFT
    same_slot = key_slot[None, :] == row_slot[:, None]
    allowed = same_slot & (jnp.tile(reach_rows, (1, slot_count)) > 0.5)
    tree_keys = all_kv[:, :kv_width].reshape(group_rows, KV_HEADS, HEAD)
    tree_values = all_kv[:, kv_width:].reshape(group_rows, KV_HEADS, HEAD)
    own_blocks = own_q.reshape(tok_dev, KV_HEADS, group_size, HEAD)
    tree_scores = (
        jnp.einsum("igrd,kgd->igrk", own_blocks, tree_keys, preferred_element_type=jnp.float32)
        * score_scale
    )
    tree_mask = allowed[:, None, None, :]
    tree_scores = jnp.where(tree_mask, tree_scores, neg_big)
    tree_max = jnp.max(tree_scores, axis=-1)
    tree_weights = jnp.where(tree_mask, jnp.exp(tree_scores - tree_max[..., None]), 0.0).astype(
        jnp.bfloat16
    )
    tree_sum = jnp.sum(tree_weights.astype(jnp.float32), axis=-1)
    tree_out = jnp.einsum(
        "igrk,kgd->igrd", tree_weights, tree_values, preferred_element_type=jnp.float32
    )
    own_stats = (
        lax.dynamic_slice_in_dim(stat_max, row_start, tok_dev, 0),
        lax.dynamic_slice_in_dim(stat_sum, row_start, tok_dev, 0),
        lax.dynamic_slice_in_dim(stat_out, row_start, tok_dev, 0),
    )
    tree_stats = (
        tree_max.reshape(tok_dev, HEADS),
        tree_sum.reshape(tok_dev, HEADS),
        tree_out.reshape(tok_dev, HEADS * HEAD),
    )
    joined = combine_stats(own_stats, tree_stats)
    stat_max = lax.dynamic_update_slice_in_dim(stat_max, joined[0], row_start, 0)
    stat_sum = lax.dynamic_update_slice_in_dim(stat_sum, joined[1], row_start, 0)
    stat_out = lax.dynamic_update_slice_in_dim(stat_out, joined[2], row_start, 0)
    normed_all = None
    merged = joined_2((stat_max, stat_sum, stat_out), "tp", combine_stats)
    attn_own = finish_rows(
        lax.dynamic_slice_in_dim(merged[1], row_start, tok_dev, 0),
        lax.dynamic_slice_in_dim(merged[2], row_start, tok_dev, 0),
    )
    hidden_own = project_rows(attn_own, own_res, out_weight)
    normed_own = rms_normed(hidden_own, norm_gain)
    units_dev = gate_up.shape[0]
    unit_width = gate_up.shape[2] // 2
    normed_all = lax.all_gather(normed_own, "tp", axis=0, tiled=True)
    shares = unit_shares(normed_all, router_weight, expert_ids, tp_rank, units_dev)
    gate_both = jnp.einsum("td,udh->tuh", normed_all, gate_up, preferred_element_type=jnp.float32)
    activated = (
        jax.nn.silu(gate_both[..., :unit_width]) * gate_both[..., unit_width:] * shares[:, :, None]
    ).astype(jnp.bfloat16)
    moe_own = lax.psum_scatter(
        jnp.einsum("tuh,uhd->td", activated, down_weight, preferred_element_type=jnp.float32),
        "tp",
        scatter_dimension=0,
        tiled=True,
    )
    layer_out = (hidden_own + moe_own).astype(jnp.bfloat16)
    node_ids = jnp.arange(DRAFT, dtype=jnp.int32)
    leaf_pick = (accept_leaf[:, None] == node_ids[None, :]).astype(jnp.float32)
    path_weight = jnp.einsum("sn,snk->sk", leaf_pick, reached, precision=lax.Precision.HIGHEST)
    path_flags = (path_weight > 0.5).astype(jnp.int32)
    path_rank = jnp.cumsum(path_flags, axis=1) - 1
    chosen_node = (path_flags[:, None, :] > 0) & (path_rank[:, None, :] == node_ids[None, :, None])
    own_choice = jnp.take(chosen_node.reshape(slot_count * DRAFT, DRAFT), row_pos, axis=0)
    spread = same_slot & jnp.tile(own_choice, (1, slot_count))
    accepted = jnp.dot(
        spread.astype(jnp.bfloat16), all_kv, preferred_element_type=jnp.float32
    ).astype(jnp.bfloat16)
    return (attn_own, layer_out, accepted)


def pack_kernel(
    row_slot, placement_ref, pages_ref, pulled_ref, keys_ref, values_ref, sent_ref, res_ref
):
    slot_count = placement_ref.shape[0]
    group_size = HEADS // KV_HEADS
    page_len = keys_ref.shape[1]
    kv_width = keys_ref.shape[2]
    q_width = HEADS * HEAD
    tok_dev = pulled_ref.shape[1]
    slot = row_slot(lax.axis_index("tp"))
    source = placement_ref[slot] // slot_count
    rows = pulled_ref[source]
    res_ref[...] = rows[:, q_width + 2 * kv_width :]
    head_rows = group_size * HEAD
    tail = jnp.zeros((tok_dev, 2 * WIDE - head_rows), rows.dtype)
    cache_rows = slot_count * page_len
    for head in range(KV_HEADS):
        low = head * HEAD
        for s in range(slot_count):
            page = pages_ref[s, 0, 0]
            sent_ref[head, s * page_len : (s + 1) * page_len, :] = jnp.concatenate(
                [keys_ref[page, :, low : low + HEAD], values_ref[page, :, low : low + HEAD]], axis=1
            )
        q_low = head * head_rows
        pair = jnp.concatenate([rows[:, q_low : q_low + head_rows], tail], axis=1)
        sent_ref[head, cache_rows : cache_rows + tok_dev, :] = pair[:, :WIDE]
        sent_ref[head, cache_rows + tok_dev : cache_rows + 2 * tok_dev, :] = pair[:, WIDE:]
        k_low = q_width + low
        sent_ref[head, cache_rows + 2 * tok_dev :, :] = jnp.concatenate(
            [rows[:, k_low : k_low + HEAD], rows[:, k_low + kv_width : k_low + kv_width + HEAD]],
            axis=1,
        )


def ancestor_rows(parents_ref):
    slot_count = parents_ref.shape[0]
    total = slot_count * DRAFT
    row = jnp.concatenate(
        [parents_ref[s : s + 1, :] + s * DRAFT for s in range(slot_count)], axis=1
    )
    from_ids = lax.broadcasted_iota(jnp.int32, (total, total), 0)
    to_ids = lax.broadcasted_iota(jnp.int32, (total, total), 1)
    linked = (from_ids == jnp.broadcast_to(row, (total, total))) & (lax.rem(to_ids, DRAFT) > 0)
    reached = jnp.where(linked | (from_ids == to_ids), 1.0, 0.0)
    for _ in range((DRAFT - 1).bit_length()):
        half = reached.astype(jnp.bfloat16)
        reached = jnp.minimum(jnp.dot(half, half, preferred_element_type=jnp.float32), 1.0)
    return reached.T


def attend_kernel(
    lengths_ref, leaf_ref, parents_ref, got_ref, res_ref, sent_ref, reach_ref
):
    slot_count = lengths_ref.shape[0]
    sources = got_ref.shape[0]
    tok_dev = res_ref.shape[0]
    page_len = (got_ref.shape[1] - 3 * tok_dev) // slot_count
    cache_rows = slot_count * page_len
    per_slot = DRAFT // tok_dev
    group_size = HEADS // KV_HEADS
    f32, bf16 = jnp.float32, jnp.bfloat16
    reach_ref[...] = ancestor_rows(parents_ref)
    lane_low = lax.broadcasted_iota(jnp.int32, (DRAFT, WIDE), 1) < HEAD
    positions = lax.broadcasted_iota(jnp.int32, (1, sources * page_len), 1)
    outs, picked = [], []
    for s in range(slot_count):
        first = s * per_slot
        part = lambda k: jnp.concatenate(
            [
                got_ref[first + i, cache_rows + k * tok_dev : cache_rows + (k + 1) * tok_dev, :]
                for i in range(per_slot)
            ],
            axis=0,
        )
        q_pair = part(0).astype(f32) * (1.0 / math.sqrt(HEAD))
        q_last = part(1).astype(f32) * (1.0 / math.sqrt(HEAD))
        tree_kv = part(2)
        q_rows = jnp.concatenate(
            [
                jnp.where(lane_low, q_pair, 0.0),
                jnp.where(lane_low, pltpu.roll(q_pair, HEAD, 1), 0.0),
                jnp.where(lane_low, q_last, 0.0),
            ],
            axis=0,
        ).astype(bf16)
        cache_kv = got_ref[:, s * page_len : (s + 1) * page_len, :].reshape(
            sources * page_len, WIDE
        )
        dims = (((1,), (1,)), ((), ()))
        scores = lax.dot_general(q_rows, cache_kv, dims, preferred_element_type=f32)
        is_valid = positions < lengths_ref[s]
        scores = jnp.where(is_valid, scores, neg_big)
        reach = reach_ref[s * DRAFT : (s + 1) * DRAFT, s * DRAFT : (s + 1) * DRAFT]
        allowed = jnp.concatenate([reach] * group_size, axis=0) > 0.5
        tree_scores = lax.dot_general(q_rows, tree_kv, dims, preferred_element_type=f32)
        tree_scores = jnp.where(allowed, tree_scores, neg_big)
        top = jnp.maximum(
            jnp.max(scores, axis=1, keepdims=True), jnp.max(tree_scores, axis=1, keepdims=True)
        )
        weights = jnp.where(is_valid, jnp.exp(scores - top), 0.0).astype(bf16)
        tree_weights = jnp.where(allowed, jnp.exp(tree_scores - top), 0.0).astype(bf16)
        total = jnp.sum(weights.astype(f32), axis=1, keepdims=True) + jnp.sum(
            tree_weights.astype(f32), axis=1, keepdims=True
        )
        mixed = jnp.dot(weights, cache_kv, preferred_element_type=f32) + jnp.dot(
            tree_weights, tree_kv, preferred_element_type=f32
        )
        outs.append(mixed / total)
        path = reach_ref[pl.ds(s * DRAFT + leaf_ref[s], 1), s * DRAFT : (s + 1) * DRAFT]
        path = jnp.broadcast_to(path, (DRAFT, DRAFT))
        node_from = lax.broadcasted_iota(jnp.int32, (DRAFT, DRAFT), 0)
        node_to = lax.broadcasted_iota(jnp.int32, (DRAFT, DRAFT), 1)
        upto = jnp.where(node_from <= node_to, 1.0, 0.0).astype(bf16)
        rank = jnp.dot(path.astype(bf16), upto, preferred_element_type=f32)
        chosen = (path > 0.5) & (rank == (node_from + 1).astype(f32))
        picked.append(
            jnp.dot(
                jnp.where(chosen, 1.0, 0.0).astype(bf16), tree_kv, preferred_element_type=f32
            ).astype(bf16)
        )
    pair_rows, last_rows = [], []
    for s in range(slot_count):
        out = outs[s]
        head_out = [out[r * DRAFT : (r + 1) * DRAFT] for r in range(group_size)]
        pair_rows.append(
            jnp.where(lane_low, pltpu.roll(head_out[0], HEAD, 1), head_out[1]).astype(bf16)
        )
        last_rows.append(head_out[2])
    last = jnp.where(lane_low, pltpu.roll(last_rows[0], HEAD, 1), last_rows[1]).astype(bf16)
    res_tiles = [res_ref[:, c * WIDE : (c + 1) * WIDE] for c in range(res_ref.shape[1] // WIDE)]
    shared = jnp.concatenate(pair_rows + [last] + res_tiles, axis=0)
    shared_rows = shared.shape[0]
    for target in range(sources):
        sent_ref[target, :shared_rows, :] = shared
        row = (target % per_slot) * tok_dev
        sent_ref[target, shared_rows:, :] = picked[target // per_slot][row : row + tok_dev]


def expert_kernel(
    got_ref, ids_ref, gain_ref, out_weight_ref, router_ref, gate_up_ref, down_ref,
    moe_ref, hidden_ref, attn_ref, accepted_ref, x_ref, hid_ref, normed_ref, share_ref,
):
    f32, bf16 = jnp.float32, jnp.bfloat16
    sources = got_ref.shape[0]
    tok_dev = hidden_ref.shape[0]
    group_rows = sources * tok_dev
    half = group_rows // 2
    width = out_weight_ref.shape[0]
    model = out_weight_ref.shape[1]
    rank = lax.axis_index("tp")
    lane_low = lax.broadcasted_iota(jnp.int32, (half, WIDE), 1) < HEAD
    head_rows = width // sources
    res_start = group_rows + half
    res_rows = (model // WIDE) * tok_dev
    for p in range(sources // 2):
        even, odd = got_ref.at[2 * p], got_ref.at[2 * p + 1]
        last_even = even[group_rows:res_start, :].astype(f32)
        last_odd = odd[group_rows:res_start, :].astype(f32)
        pair_odd = odd[:group_rows, :].astype(f32)
        odd_swapped = pltpu.roll(pair_odd, HEAD, 1)
        base = 2 * p * head_rows
        x_ref[:, base : base + WIDE] = even[:group_rows, :]
        x_ref[:half, base + WIDE : base + 2 * WIDE] = jnp.where(
            lane_low, last_even, odd_swapped[:half]
        ).astype(bf16)
        x_ref[half:, base + WIDE : base + 2 * WIDE] = jnp.where(
            lane_low, pltpu.roll(last_even, HEAD, 1), odd_swapped[half:]
        ).astype(bf16)
        x_ref[:half, base + 2 * WIDE : base + 3 * WIDE] = jnp.where(
            lane_low, odd_swapped[:half], pltpu.roll(last_odd, HEAD, 1)
        ).astype(bf16)
        x_ref[half:, base + 2 * WIDE : base + 3 * WIDE] = jnp.where(
            lane_low, odd_swapped[half:], last_odd
        ).astype(bf16)
        kv_even = even[res_start + res_rows :, :].astype(f32)
        kv_odd = odd[res_start + res_rows :, :].astype(f32)
        low = lane_low[:tok_dev]
        kv_width = accepted_ref.shape[1] // 2
        accepted_ref[:, p * WIDE : (p + 1) * WIDE] = jnp.where(
            low, kv_even, pltpu.roll(kv_odd, HEAD, 1)
        ).astype(bf16)
        accepted_ref[:, kv_width + p * WIDE : kv_width + (p + 1) * WIDE] = jnp.where(
            low, pltpu.roll(kv_even, HEAD, 1), kv_odd
        ).astype(bf16)
    own = pl.multiple_of(rank * tok_dev, tok_dev)
    attn_ref[...] = x_ref[pl.ds(own, tok_dev), :]
    projected = jnp.dot(x_ref[...], out_weight_ref[...], preferred_element_type=f32)
    residual = jnp.concatenate(
        [
            jnp.concatenate(
                [
                    got_ref[j, res_start + c * tok_dev : res_start + (c + 1) * tok_dev, :]
                    for c in range(model // WIDE)
                ],
                axis=1,
            )
            for j in range(sources)
        ],
        axis=0,
    )
    hidden = residual.astype(f32) + projected
    hid_ref[...] = hidden
    scale = lax.rsqrt(jnp.mean(hidden * hidden, axis=1, keepdims=True) + norm_eps)
    normed_ref[...] = (hidden * scale * gain_ref[...]).astype(bf16)
    hidden_ref[...] = hid_ref[pl.ds(own, tok_dev), :]
    logits = jnp.dot(normed_ref[...], router_ref[...], preferred_element_type=f32)
    experts = router_ref.shape[1]
    expert_range = lax.broadcasted_iota(jnp.int32, (group_rows, experts), 1)
    count = jnp.zeros((group_rows, experts), f32)
    for k in range(ids_ref.shape[1]):
        count = count + jnp.where(ids_ref[:, k : k + 1] == expert_range, 1.0, 0.0)
    expo = jnp.where(count > 0.0, jnp.exp(logits), 0.0) * count
    routing = expo / jnp.sum(expo, axis=1, keepdims=True)
    units = gate_up_ref.shape[0]
    unit_width = gate_up_ref.shape[2] // 2
    span = FF_E // unit_width
    for u in range(units):
        expert = (rank * units + u) // span
        share_ref[u] = jnp.broadcast_to(
            jnp.sum(jnp.where(expert_range == expert, routing, 0.0), axis=1, keepdims=True),
            (group_rows, unit_width),
        )

    def one_unit(u):
        both = jnp.dot(normed_ref[...], gate_up_ref[u], preferred_element_type=f32)
        gate, up = both[:, :unit_width], both[:, unit_width:]
        return (gate / (1.0 + jnp.exp(-gate)) * up * share_ref[u]).astype(bf16)

    step = 2

    def body(i, total):
        act = jnp.concatenate([one_unit(i * step + k) for k in range(step)], axis=1)
        down = down_ref[pl.ds(i * step, step)].reshape(step * unit_width, model)
        hid_ref[...] += jnp.dot(act, down, preferred_element_type=f32)
        return total

    hid_ref[...] = jnp.zeros_like(hid_ref)
    lax.fori_loop(0, units // step, body, 0)
    moe_ref[...] = hid_ref[...].astype(bf16)


def in_vmem(*arrays):
    return tuple(pltpu.with_memory_space_constraint(a, pltpu.VMEM) for a in arrays)


def spaces(text):
    kinds = {"s": pltpu.SMEM, "v": pltpu.VMEM}
    return [pl.BlockSpec(memory_space=kinds[c]) for c in text]


def params():
    return pltpu.CompilerParams(vmem_limit_bytes=20 << 20)


def per_device_packed(
    queries,
    new_kv,
    residual,
    placement,
    lengths,
    page_table,
    cache_keys,
    cache_values,
    parents,
    accept_leaf,
    out_weight,
    norm_gain,
    router_weight,
    expert_ids,
    gate_up,
    down_weight,
):
    f32, bf16 = jnp.float32, jnp.bfloat16
    tok_dev, model = residual.shape
    tp_count = lax.axis_size("tp")
    slot_count = placement.shape[0]
    page_len, kv_width = cache_keys.shape[1:]
    group_rows = tok_dev * tp_count
    sent = lambda rows: jax.ShapeDtypeStruct((tp_count, rows, WIDE), bf16)
    row_slot = lambda rank: rank * tok_dev // DRAFT
    pulled = lax.all_gather(
        jnp.concatenate([queries, new_kv, residual], axis=1), "req", axis=0
    )
    pack_rows = slot_count * page_len + 3 * tok_dev
    packed, own_res = pl.pallas_call(
        functools.partial(pack_kernel, row_slot),
        out_shape=(sent(pack_rows), jax.ShapeDtypeStruct(residual.shape, bf16)),
        in_specs=spaces("ssvvv"),
        out_specs=tuple(spaces("vv")),
        compiler_params=params(),
        name="pack",
    )(placement, page_table, pulled, cache_keys, cache_values)
    packed = lax.all_to_all(packed, "tp", 0, 0, tiled=True)
    out_rows = group_rows + group_rows // 2 + (model // WIDE) * tok_dev + tok_dev
    outs = pl.pallas_call(
        attend_kernel,
        out_shape=sent(out_rows),
        in_specs=spaces("ssvvv"),
        out_specs=spaces("v")[0],
        scratch_shapes=[pltpu.VMEM((slot_count * DRAFT, slot_count * DRAFT), f32)],
        compiler_params=params(),
        name="attend",
    )(lengths, accept_leaf, parents, packed, own_res)
    outs = lax.all_to_all(outs, "tp", 0, 0, tiled=True)
    weights = in_vmem(out_weight, router_weight, gate_up, down_weight)
    moe, hidden, attn_own, accepted = pl.pallas_call(
        expert_kernel,
        out_shape=(
            jax.ShapeDtypeStruct((group_rows, model), bf16),
            jax.ShapeDtypeStruct((tok_dev, model), f32),
            jax.ShapeDtypeStruct(queries.shape, bf16),
            jax.ShapeDtypeStruct(new_kv.shape, bf16),
        ),
        in_specs=spaces("vvvvvvv"),
        out_specs=tuple(spaces("vvvv")),
        scratch_shapes=[
            pltpu.VMEM((group_rows, HEADS * HEAD), bf16),
            pltpu.VMEM((group_rows, model), f32),
            pltpu.VMEM((group_rows, model), bf16),
            pltpu.VMEM((gate_up.shape[0], group_rows, gate_up.shape[2] // 2), f32),
        ],
        compiler_params=params(),
        name="experts",
    )(outs, expert_ids, norm_gain[None, :], *weights)
    parts = lax.all_to_all(moe, "tp", 0, 0, tiled=True).reshape(tp_count, tok_dev, model)
    layer_out = (hidden + jnp.sum(parts.astype(f32), axis=0)).astype(bf16)
    return attn_own, layer_out, accepted


def per_device(queries, new_kv, residual, placement, *rest):
    tok_dev = queries.shape[0]
    one_head_each = lax.axis_size("tp") == KV_HEADS
    whole_tiles = tok_dev % 16 == 0 and tok_dev * KV_HEADS == 2 * DRAFT
    if one_head_each and whole_tiles and rest[1].shape[1] == 1:
        return per_device_packed(queries, new_kv, residual, placement, *rest)
    return per_device_plain(queries, new_kv, residual, placement, *rest)


def solution(mesh):
    in_specs = (
        P(("req", "tp"), None),
        P(("req", "tp"), None),
        P(("req", "tp"), None),
        P("req"),
        P("req"),
        P("req", None, "tp"),
        P(("req", "tp"), None, None),
        P(("req", "tp"), None, None),
        P("req", None),
        P("req"),
        P(),
        P(),
        P(),
        P("req", None),
        P("tp", None, None),
        P("tp", None, None),
    )
    out_specs = (P(("req", "tp"), None), P(("req", "tp"), None), P(("req", "tp"), None))
    return jax.shard_map(
        per_device, mesh=mesh, in_specs=in_specs, out_specs=out_specs, check_vma=False
    )
```

```python
import functools
import math

import jax
import jax.numpy as jnp
from jax import lax
from jax.experimental import pallas as pl
from jax.experimental.pallas import tpu as pltpu
from jax.sharding import PartitionSpec as P

HEADS = 24
KV_HEADS = 8
HEAD = 64
FF_E = 512
UNIT = 128
DRAFT = 64
WIDE = 128
STEP = 2
AHEAD = 4


neg_big = -1e30
norm_eps = 1e-06


def joined_2(part, axis, combine):
    gathered = jax.tree.map(lambda a: lax.all_gather(a, axis), part)

    def take(source):
        return jax.tree.map(lambda a: lax.dynamic_index_in_dim(a, source, 0, False), gathered)

    return lax.fori_loop(
        1, lax.axis_size(axis), lambda source, state: combine(state, take(source)), take(0)
    )


def ancestry(parents):
    node_count = parents.shape[-1]
    node_ids = jnp.arange(node_count, dtype=jnp.int32)
    linked = (parents[:, :, None] == node_ids[None, None, :]) & (node_ids[None, :, None] > 0)
    reached = jnp.maximum(linked.astype(jnp.float32), jnp.eye(node_count, dtype=jnp.float32)[None])
    for _ in range(node_count.bit_length()):
        reached = jnp.minimum(
            jnp.einsum("rnm,rmk->rnk", reached, reached, precision=lax.Precision.HIGHEST), 1.0
        )
    return reached


def combine_stats(left_stats, right_stats):
    left_max, left_sum, left_out = left_stats
    right_max, right_sum, right_out = right_stats
    top_score = jnp.maximum(left_max, right_max)
    left_scale = jnp.exp(left_max - top_score)
    right_scale = jnp.exp(right_max - top_score)
    row_count, head_count = left_max.shape
    out_sum = (
        left_out.reshape(row_count, head_count, -1) * left_scale[..., None]
        + right_out.reshape(row_count, head_count, -1) * right_scale[..., None]
    )
    return (
        top_score,
        left_sum * left_scale + right_sum * right_scale,
        out_sum.reshape(row_count, -1),
    )


def finish_rows(stat_sum, stat_out):
    row_count, head_count = stat_sum.shape
    return (
        (stat_out.reshape(row_count, head_count, -1) / stat_sum[..., None])
        .reshape(row_count, -1)
        .astype(jnp.bfloat16)
    )


def project_rows(attn_rows, res_rows, out_weight):
    return res_rows.astype(jnp.float32) + jnp.dot(
        attn_rows, out_weight, preferred_element_type=jnp.float32
    )


def rms_normed(hidden, norm_gain):
    scale_rows = lax.rsqrt(jnp.mean(hidden * hidden, axis=-1, keepdims=True) + norm_eps)
    return (hidden * scale_rows * norm_gain).astype(jnp.bfloat16)


def unit_shares(normed_all, router_weight, expert_ids, tp_rank, units_dev):
    logits = jnp.dot(normed_all, router_weight, preferred_element_type=jnp.float32)
    expert_range = jnp.arange(router_weight.shape[1], dtype=jnp.int32)
    onehot = (expert_ids[:, :, None] == expert_range[None, None, :]).astype(jnp.float32)
    chosen = jnp.sum(logits[:, None, :] * onehot, axis=-1)
    expo_chosen = jnp.exp(chosen)
    expert_probs = expo_chosen / jnp.sum(expo_chosen, axis=-1, keepdims=True)
    routing = jnp.sum(expert_probs[:, :, None] * onehot, axis=1)
    unit_ids = tp_rank * units_dev + jnp.arange(units_dev, dtype=jnp.int32)
    expert_of_unit = unit_ids // (FF_E // UNIT)
    pick = (expert_range[:, None] == expert_of_unit[None, :]).astype(jnp.float32)
    return jnp.dot(routing, pick, precision=lax.Precision.HIGHEST)


def per_device_plain(
    queries,
    new_kv,
    residual,
    placement,
    lengths,
    page_table,
    cache_keys,
    cache_values,
    parents,
    accept_leaf,
    out_weight,
    norm_gain,
    router_weight,
    expert_ids,
    gate_up,
    down_weight,
):
    tok_dev = queries.shape[0]
    tp_count = lax.axis_size("tp")
    tp_rank = lax.axis_index("tp")
    group_rows = tok_dev * tp_count
    slot_count = placement.shape[0]
    kv_width = cache_keys.shape[2]
    page_len = cache_keys.shape[1]
    group_size = HEADS // KV_HEADS
    score_scale = 1.0 / math.sqrt(HEAD)
    row_start = tp_rank * tok_dev
    pulled_q, pulled_kv, pulled_res = (
        lax.all_gather(queries, "req", axis=0, tiled=True),
        lax.all_gather(new_kv, "req", axis=0, tiled=True),
        lax.all_gather(residual, "req", axis=0, tiled=True),
    )
    row_offsets = jnp.arange(tok_dev, dtype=jnp.int32)
    row_pos = row_start + row_offsets
    row_slot = row_pos // DRAFT
    slot_match = row_slot[:, None] == jnp.arange(slot_count, dtype=jnp.int32)[None, :]
    source_group = jnp.sum(jnp.where(slot_match, placement[None, :] // slot_count, 0), axis=1)
    source_rows = source_group * tok_dev + row_offsets
    own_q = jnp.take(pulled_q, source_rows, axis=0)
    own_kv = jnp.take(pulled_kv, source_rows, axis=0)
    own_res = jnp.take(pulled_res, source_rows, axis=0)
    all_q, all_kv = (
        lax.all_gather(own_q, "tp", axis=0, tiled=True),
        lax.all_gather(own_kv, "tp", axis=0, tiled=True),
    )
    local_pages = page_table.shape[1]
    page_ids = page_table[:, :, 0].reshape(-1)
    keys_local = jnp.take(cache_keys, page_ids, axis=0).reshape(
        slot_count, local_pages, page_len, KV_HEADS, HEAD
    )
    values_local = jnp.take(cache_values, page_ids, axis=0).reshape(
        slot_count, local_pages, page_len, KV_HEADS, HEAD
    )
    query_blocks = all_q.reshape(slot_count, DRAFT, KV_HEADS, group_size, HEAD)
    scores = (
        jnp.einsum(
            "sqgrd,sltgd->sqgrlt", query_blocks, keys_local, preferred_element_type=jnp.float32
        )
        * score_scale
    )
    positions = (
        jnp.arange(local_pages, dtype=jnp.int32)[:, None] * tp_count + tp_rank
    ) * page_len + jnp.arange(page_len, dtype=jnp.int32)[None, :]
    is_valid = (positions[None] < lengths[:, None, None])[:, None, None, None]
    scores = jnp.where(is_valid, scores, neg_big)
    block_max = jnp.max(scores, axis=-1)
    weights = jnp.where(is_valid, jnp.exp(scores - block_max[..., None]), 0.0).astype(jnp.bfloat16)
    block_sum = jnp.sum(weights.astype(jnp.float32), axis=-1)
    block_out = jnp.einsum(
        "sqgrlt,sltgd->sqgrld", weights, values_local, preferred_element_type=jnp.float32
    )
    page_top = jnp.max(block_max, axis=-1)
    page_scale = jnp.exp(block_max - page_top[..., None])
    stat_max = page_top.reshape(group_rows, HEADS)
    stat_sum = jnp.sum(block_sum * page_scale, axis=-1).reshape(group_rows, HEADS)
    stat_out = jnp.sum(block_out * page_scale[..., None], axis=-2).reshape(group_rows, HEADS * HEAD)
    reached = ancestry(parents)
    reach_rows = jnp.take(reached.reshape(slot_count * DRAFT, DRAFT), row_pos, axis=0)
    key_slot = jnp.arange(group_rows, dtype=jnp.int32) // DRAFT
    same_slot = key_slot[None, :] == row_slot[:, None]
    allowed = same_slot & (jnp.tile(reach_rows, (1, slot_count)) > 0.5)
    tree_keys = all_kv[:, :kv_width].reshape(group_rows, KV_HEADS, HEAD)
    tree_values = all_kv[:, kv_width:].reshape(group_rows, KV_HEADS, HEAD)
    own_blocks = own_q.reshape(tok_dev, KV_HEADS, group_size, HEAD)
    tree_scores = (
        jnp.einsum("igrd,kgd->igrk", own_blocks, tree_keys, preferred_element_type=jnp.float32)
        * score_scale
    )
    tree_mask = allowed[:, None, None, :]
    tree_scores = jnp.where(tree_mask, tree_scores, neg_big)
    tree_max = jnp.max(tree_scores, axis=-1)
    tree_weights = jnp.where(tree_mask, jnp.exp(tree_scores - tree_max[..., None]), 0.0).astype(
        jnp.bfloat16
    )
    tree_sum = jnp.sum(tree_weights.astype(jnp.float32), axis=-1)
    tree_out = jnp.einsum(
        "igrk,kgd->igrd", tree_weights, tree_values, preferred_element_type=jnp.float32
    )
    own_stats = (
        lax.dynamic_slice_in_dim(stat_max, row_start, tok_dev, 0),
        lax.dynamic_slice_in_dim(stat_sum, row_start, tok_dev, 0),
        lax.dynamic_slice_in_dim(stat_out, row_start, tok_dev, 0),
    )
    tree_stats = (
        tree_max.reshape(tok_dev, HEADS),
        tree_sum.reshape(tok_dev, HEADS),
        tree_out.reshape(tok_dev, HEADS * HEAD),
    )
    joined = combine_stats(own_stats, tree_stats)
    stat_max = lax.dynamic_update_slice_in_dim(stat_max, joined[0], row_start, 0)
    stat_sum = lax.dynamic_update_slice_in_dim(stat_sum, joined[1], row_start, 0)
    stat_out = lax.dynamic_update_slice_in_dim(stat_out, joined[2], row_start, 0)
    normed_all = None
    merged = joined_2((stat_max, stat_sum, stat_out), "tp", combine_stats)
    attn_own = finish_rows(
        lax.dynamic_slice_in_dim(merged[1], row_start, tok_dev, 0),
        lax.dynamic_slice_in_dim(merged[2], row_start, tok_dev, 0),
    )
    hidden_own = project_rows(attn_own, own_res, out_weight)
    normed_own = rms_normed(hidden_own, norm_gain)
    units_dev = gate_up.shape[0]
    unit_width = gate_up.shape[2] // 2
    normed_all = lax.all_gather(normed_own, "tp", axis=0, tiled=True)
    shares = unit_shares(normed_all, router_weight, expert_ids, tp_rank, units_dev)
    gate_both = jnp.einsum("td,udh->tuh", normed_all, gate_up, preferred_element_type=jnp.float32)
    activated = (
        jax.nn.silu(gate_both[..., :unit_width]) * gate_both[..., unit_width:] * shares[:, :, None]
    ).astype(jnp.bfloat16)
    moe_own = lax.psum_scatter(
        jnp.einsum("tuh,uhd->td", activated, down_weight, preferred_element_type=jnp.float32),
        "tp",
        scatter_dimension=0,
        tiled=True,
    )
    layer_out = (hidden_own + moe_own).astype(jnp.bfloat16)
    node_ids = jnp.arange(DRAFT, dtype=jnp.int32)
    leaf_pick = (accept_leaf[:, None] == node_ids[None, :]).astype(jnp.float32)
    path_weight = jnp.einsum("sn,snk->sk", leaf_pick, reached, precision=lax.Precision.HIGHEST)
    path_flags = (path_weight > 0.5).astype(jnp.int32)
    path_rank = jnp.cumsum(path_flags, axis=1) - 1
    chosen_node = (path_flags[:, None, :] > 0) & (path_rank[:, None, :] == node_ids[None, :, None])
    own_choice = jnp.take(chosen_node.reshape(slot_count * DRAFT, DRAFT), row_pos, axis=0)
    spread = same_slot & jnp.tile(own_choice, (1, slot_count))
    accepted = jnp.dot(
        spread.astype(jnp.bfloat16), all_kv, preferred_element_type=jnp.float32
    ).astype(jnp.bfloat16)
    return (attn_own, layer_out, accepted)


def start_all(copies):
    for copy in copies:
        copy.start()
    for copy in copies:
        copy.wait()


def pack_kernel(
    slot_of, placement_hbm, pages_hbm, keys_hbm, values_hbm, pulled_ref, sent_ref, res_ref,
    placement_ref, pages_ref, keys_ref, values_ref, sems,
):
    slot_count = placement_ref.shape[0]
    page_len, kv_width = keys_ref.shape[1:]
    start_all(
        [
            pltpu.make_async_copy(source, target, sems.at[k])
            for k, (source, target) in enumerate(
                [
                    (placement_hbm, placement_ref),
                    (pages_hbm, pages_ref),
                    (keys_hbm, keys_ref),
                    (values_hbm, values_ref),
                ]
            )
        ]
    )
    q_width = HEADS * HEAD
    tok_dev = pulled_ref.shape[1]
    slot = slot_of(lax.axis_index("tp"))
    source = lax.div(placement_ref[slot], slot_count)
    rows = pulled_ref[source]
    res_ref[...] = rows[:, q_width + 2 * kv_width :]
    head_rows = (HEADS // KV_HEADS) * HEAD
    tail = jnp.zeros((tok_dev, 2 * WIDE - head_rows), rows.dtype)
    base = slot_count * page_len
    for head in range(KV_HEADS):
        low = head * HEAD
        for s in range(slot_count):
            page = pages_ref[s]
            sent_ref[head, s * page_len : (s + 1) * page_len, :] = jnp.concatenate(
                [keys_ref[page, :, low : low + HEAD], values_ref[page, :, low : low + HEAD]], axis=1
            )
        q_low = head * head_rows
        pair = jnp.concatenate([rows[:, q_low : q_low + head_rows], tail], axis=1)
        sent_ref[head, base : base + tok_dev, :] = pair[:, :WIDE]
        sent_ref[head, base + tok_dev : base + 2 * tok_dev, :] = pair[:, WIDE:]
        k_low = q_width + low
        sent_ref[head, base + 2 * tok_dev :, :] = jnp.concatenate(
            [rows[:, k_low : k_low + HEAD], rows[:, k_low + kv_width : k_low + kv_width + HEAD]],
            axis=1,
        )


def ancestor_rows(parents_ref):
    slot_count = parents_ref.shape[0]
    total = slot_count * DRAFT
    row = jnp.concatenate(
        [parents_ref[s : s + 1, :] + s * DRAFT for s in range(slot_count)], axis=1
    )
    from_ids = lax.broadcasted_iota(jnp.int32, (total, total), 0)
    to_ids = lax.broadcasted_iota(jnp.int32, (total, total), 1)
    linked = (from_ids == jnp.broadcast_to(row, (total, total))) & (lax.rem(to_ids, DRAFT) > 0)
    reached = jnp.where(linked | (from_ids == to_ids), 1.0, 0.0)
    for _ in range((DRAFT - 1).bit_length()):
        half = reached.astype(jnp.bfloat16)
        reached = jnp.minimum(jnp.dot(half, half, preferred_element_type=jnp.float32), 1.0)
    return reached.T


def attend_kernel(
    lengths_hbm, leaf_hbm, parents_hbm, weight_hbm, got_ref, res_ref, sent_ref, picked_ref,
    weight_ref,
    lengths_ref, leaf_ref, parents_ref, reach_ref, sems,
):
    start_all(
        [
            pltpu.make_async_copy(lengths_hbm, lengths_ref, sems.at[0]),
            pltpu.make_async_copy(leaf_hbm, leaf_ref, sems.at[1]),
            pltpu.make_async_copy(parents_hbm, parents_ref, sems.at[2]),
        ]
    )
    weight_copy = pltpu.make_async_copy(weight_hbm, weight_ref, sems.at[3])
    weight_copy.start()
    reach_ref[...] = ancestor_rows(parents_ref)
    slot_count = lengths_ref.shape[0]
    sources = got_ref.shape[0]
    tok_dev = res_ref.shape[0]
    base = got_ref.shape[1] - 3 * tok_dev
    page_len = base // slot_count
    per_slot = DRAFT // tok_dev
    group_size = HEADS // KV_HEADS
    f32, bf16 = jnp.float32, jnp.bfloat16
    lane_low = lax.broadcasted_iota(jnp.int32, (DRAFT, WIDE), 1) < HEAD
    positions = lax.broadcasted_iota(jnp.int32, (1, sources * page_len), 1)
    dims = (((1,), (1,)), ((), ()))
    scale = 1.0 / math.sqrt(HEAD)
    node_from = lax.broadcasted_iota(jnp.int32, (DRAFT, DRAFT), 0)
    node_to = lax.broadcasted_iota(jnp.int32, (DRAFT, DRAFT), 1)
    upto = jnp.where(node_from <= node_to, 1.0, 0.0).astype(bf16)
    outs, picked = [], []
    for s in range(slot_count):
        first = s * per_slot

        def part(k):
            low = base + k * tok_dev
            return jnp.concatenate(
                [got_ref[first + i, low : low + tok_dev, :] for i in range(per_slot)], axis=0
            )

        q_pair, q_last, tree_kv = part(0).astype(f32) * scale, part(1).astype(f32) * scale, part(2)
        q_rows = jnp.concatenate(
            [
                jnp.where(lane_low, q_pair, 0.0),
                jnp.where(lane_low, pltpu.roll(q_pair, HEAD, 1), 0.0),
                jnp.where(lane_low, q_last, 0.0),
            ],
            axis=0,
        ).astype(bf16)
        cache_kv = got_ref[:, s * page_len : (s + 1) * page_len, :].reshape(
            sources * page_len, WIDE
        )
        scores = lax.dot_general(q_rows, cache_kv, dims, preferred_element_type=f32)
        is_valid = positions < lengths_ref[s]
        scores = jnp.where(is_valid, scores, neg_big)
        reach = reach_ref[s * DRAFT : (s + 1) * DRAFT, s * DRAFT : (s + 1) * DRAFT]
        allowed = jnp.concatenate([reach] * group_size, axis=0) > 0.5
        tree_scores = lax.dot_general(q_rows, tree_kv, dims, preferred_element_type=f32)
        tree_scores = jnp.where(allowed, tree_scores, neg_big)
        top = jnp.maximum(
            jnp.max(scores, axis=1, keepdims=True), jnp.max(tree_scores, axis=1, keepdims=True)
        )
        weights = jnp.where(is_valid, jnp.exp(scores - top), 0.0).astype(bf16)
        tree_weights = jnp.where(allowed, jnp.exp(tree_scores - top), 0.0).astype(bf16)
        total = jnp.sum(weights.astype(f32), axis=1, keepdims=True) + jnp.sum(
            tree_weights.astype(f32), axis=1, keepdims=True
        )
        mixed = jnp.dot(weights, cache_kv, preferred_element_type=f32) + jnp.dot(
            tree_weights, tree_kv, preferred_element_type=f32
        )
        outs.append(mixed / total)
        path = reach_ref[pl.ds(s * DRAFT + leaf_ref[s], 1), s * DRAFT : (s + 1) * DRAFT]
        path = jnp.broadcast_to(path, (DRAFT, DRAFT))
        rank = jnp.dot(path.astype(bf16), upto, preferred_element_type=f32)
        chosen = (path > 0.5) & (rank == (node_from + 1).astype(f32))
        chosen = jnp.where(chosen, 1.0, 0.0).astype(bf16)
        picked.append(jnp.dot(chosen, tree_kv, preferred_element_type=f32).astype(bf16))
    pair_rows, last_rows = [], []
    for out in outs:
        head_out = [out[r * DRAFT : (r + 1) * DRAFT] for r in range(group_size)]
        pair_rows.append(
            jnp.where(lane_low, pltpu.roll(head_out[0], HEAD, 1), head_out[1]).astype(bf16)
        )
        last_rows.append(head_out[2])
    last = jnp.where(lane_low, pltpu.roll(last_rows[0], HEAD, 1), last_rows[1]).astype(bf16)
    res_tiles = [res_ref[:, c * WIDE : (c + 1) * WIDE] for c in range(res_ref.shape[1] // WIDE)]
    sent_ref[...] = jnp.concatenate(pair_rows + [last] + res_tiles, axis=0)
    for target in range(sources):
        row = (target % per_slot) * tok_dev
        picked_ref[target] = picked[target // per_slot][row : row + tok_dev]
    weight_copy.wait()


def expert_kernel(
    router_hbm, ids_hbm, gain_hbm, gate_up_hbm, down_hbm, out_weight_ref, picked_ref, *refs
):
    blocks, refs = refs[:KV_HEADS], refs[KV_HEADS:]
    moe_ref, hidden_ref, attn_ref, x_ref, hid_ref, normed_ref, share_ref = refs[:7]
    router_ref, ids_ref, gain_ref, gate_up_ref, down_ref, sems, unit_sems, down_sems = refs[7:]
    f32, bf16 = jnp.float32, jnp.bfloat16
    units = gate_up_ref.shape[0]
    small = [
        pltpu.make_async_copy(router_hbm, router_ref, sems.at[0]),
        pltpu.make_async_copy(ids_hbm, ids_ref, sems.at[1]),
        pltpu.make_async_copy(gain_hbm, gain_ref, sems.at[2]),
    ]
    for copy in small:
        copy.start()

    def unit_copy(u):
        return pltpu.make_async_copy(gate_up_hbm.at[u], gate_up_ref.at[u], unit_sems.at[u])

    def down_copy(i):
        at = pl.ds(i * STEP, STEP)
        return pltpu.make_async_copy(down_hbm.at[at], down_ref.at[at], down_sems.at[i])

    def start_step(i):
        for k in range(STEP):
            unit_copy(i * STEP + k).start()
        down_copy(i).start()

    steps = units // STEP
    for i in range(min(AHEAD, steps)):
        start_step(i)
    tok_dev = hidden_ref.shape[0]
    sources = len(blocks)
    group_rows = sources * tok_dev
    half = group_rows // 2
    width, model = out_weight_ref.shape
    rank = lax.axis_index("tp")
    lane_low = lax.broadcasted_iota(jnp.int32, (half, WIDE), 1) < HEAD
    head_rows = width // sources
    res_start = group_rows + half
    is_even = lax.rem(rank, 2) == 0
    for k in range(sources // 2):
        pair = lax.bitwise_xor(lax.div(rank, 2), k)
        mine, other = blocks[2 * k][...], blocks[2 * k + 1][...]
        even, odd = jnp.where(is_even, mine, other), jnp.where(is_even, other, mine)
        last_even = even[group_rows:res_start].astype(f32)
        last_odd = odd[group_rows:res_start].astype(f32)
        odd_swapped = pltpu.roll(odd[:group_rows].astype(f32), HEAD, 1)
        middle = jnp.concatenate(
            [
                jnp.where(lane_low, last_even, odd_swapped[:half]),
                jnp.where(lane_low, pltpu.roll(last_even, HEAD, 1), odd_swapped[half:]),
            ],
            axis=0,
        ).astype(bf16)
        end = jnp.concatenate(
            [
                jnp.where(lane_low, odd_swapped[:half], pltpu.roll(last_odd, HEAD, 1)),
                jnp.where(lane_low, odd_swapped[half:], last_odd),
            ],
            axis=0,
        ).astype(bf16)
        base = pl.multiple_of(pair * 2 * head_rows, WIDE)
        x_ref[:, pl.ds(base, 2 * head_rows)] = jnp.concatenate(
            [even[:group_rows], middle, end], axis=1
        )
        for q, block in enumerate((even, odd)):
            row = pl.multiple_of((2 * pair + q) * tok_dev, tok_dev)
            hid_ref[pl.ds(row, tok_dev), :] = jnp.concatenate(
                [
                    block[res_start + c * tok_dev : res_start + (c + 1) * tok_dev]
                    for c in range(model // WIDE)
                ],
                axis=1,
            ).astype(f32)
    own = pl.multiple_of(rank * tok_dev, tok_dev)
    attn_ref[...] = x_ref[pl.ds(own, tok_dev), :]
    projected = jnp.dot(x_ref[...], out_weight_ref[...], preferred_element_type=f32)
    hidden = hid_ref[...] + projected
    hid_ref[...] = hidden
    for copy in small:
        copy.wait()
    gain = jnp.concatenate([gain_ref[c : c + 1, :] for c in range(model // WIDE)], axis=1)
    scale = lax.rsqrt(jnp.mean(hidden * hidden, axis=1, keepdims=True) + norm_eps)
    normed_ref[...] = (hidden * scale * gain).astype(bf16)
    hidden_ref[...] = hid_ref[pl.ds(own, tok_dev), :]
    logits = lax.dot_general(
        normed_ref[...], router_ref[...], (((1,), (1,)), ((), ())), preferred_element_type=f32
    )
    experts = router_ref.shape[0]
    ids = ids_ref[...].astype(f32).T
    expert_range = lax.broadcasted_iota(jnp.int32, (group_rows, experts), 1)
    expert_names = expert_range.astype(f32)
    count = jnp.zeros((group_rows, experts), f32)
    for k in range(ids_ref.shape[0]):
        count = count + jnp.where(ids[:, k : k + 1] == expert_names, 1.0, 0.0)
    expo = jnp.where(count > 0.0, jnp.exp(logits), 0.0) * count
    routing = expo / jnp.sum(expo, axis=1, keepdims=True)
    unit_width = gate_up_ref.shape[2] // 2
    span = FF_E // unit_width
    for u in range(units):
        expert = (rank * units + u) // span
        share_ref[u] = jnp.broadcast_to(
            jnp.sum(jnp.where(expert_range == expert, routing, 0.0), axis=1, keepdims=True),
            (group_rows, unit_width),
        )

    def one_unit(u):
        both = jnp.dot(normed_ref[...], gate_up_ref[u], preferred_element_type=f32)
        gate, up = both[:, :unit_width], both[:, unit_width:]
        return (gate / (1.0 + jnp.exp(-gate)) * up * share_ref[u]).astype(bf16)

    def body(i, carry):
        @pl.when(i + AHEAD < steps)
        def _():
            start_step(i + AHEAD)

        for k in range(STEP):
            unit_copy(i * STEP + k).wait()
        act = jnp.concatenate([one_unit(i * STEP + k) for k in range(STEP)], axis=1)
        down_copy(i).wait()
        down = down_ref[pl.ds(i * STEP, STEP)].reshape(STEP * unit_width, model)
        hid_ref[...] += jnp.dot(act, down, preferred_element_type=f32)
        return carry

    hid_ref[...] = jnp.zeros_like(hid_ref)
    lax.fori_loop(0, steps, body, 0)
    for j in range(sources):
        moe_ref[j, :, :model] = hid_ref[j * tok_dev : (j + 1) * tok_dev, :].astype(bf16)
    moe_ref[:, :, model:] = picked_ref[...]


def finish_kernel(parts_ref, hidden_ref, layer_ref, accepted_ref):
    f32, bf16 = jnp.float32, jnp.bfloat16
    model = hidden_ref.shape[1]
    kv_width = accepted_ref.shape[1] // 2
    total = hidden_ref[...]
    for j in range(parts_ref.shape[0]):
        total = total + parts_ref[j, :, :model].astype(f32)
    layer_ref[...] = total.astype(bf16)
    low = lax.broadcasted_iota(jnp.int32, (hidden_ref.shape[0], WIDE), 1) < HEAD
    for p in range(parts_ref.shape[0] // 2):
        even = parts_ref[2 * p, :, model:].astype(f32)
        odd = parts_ref[2 * p + 1, :, model:].astype(f32)
        at = p * WIDE
        accepted_ref[:, at : at + WIDE] = jnp.where(low, even, pltpu.roll(odd, HEAD, 1)).astype(bf16)
        at = kv_width + p * WIDE
        accepted_ref[:, at : at + WIDE] = jnp.where(low, pltpu.roll(even, HEAD, 1), odd).astype(bf16)


def in_hbm(*arrays):
    return tuple(pltpu.with_memory_space_constraint(a, pltpu.HBM) for a in arrays)


def spaces(text):
    kinds = {"a": pl.ANY, "v": pltpu.VMEM}
    return [pl.BlockSpec(memory_space=kinds[c]) for c in text]


def params(mebibytes=12):
    return pltpu.CompilerParams(vmem_limit_bytes=mebibytes << 20)


def swap(rows, mask):
    count = lax.axis_size("tp")
    return lax.ppermute(rows, "tp", [(i, i ^ mask) for i in range(count)])


def gather_blocks(block):
    pairs = [block] + [swap(block, 2 * k) for k in range(1, lax.axis_size("tp") // 2)]
    return [a for rows in pairs for a in (rows, swap(rows, 1))]


def per_device_packed(
    queries,
    new_kv,
    residual,
    placement,
    lengths,
    page_table,
    cache_keys,
    cache_values,
    parents,
    accept_leaf,
    out_weight,
    norm_gain,
    router_weight,
    expert_ids,
    gate_up,
    down_weight,
):
    f32, bf16 = jnp.float32, jnp.bfloat16
    tok_dev, model = residual.shape
    tp_count = lax.axis_size("tp")
    slot_count = placement.shape[0]
    page_len, kv_width = cache_keys.shape[1:]
    group_rows = tok_dev * tp_count
    sent = lambda rows: jax.ShapeDtypeStruct((tp_count, rows, WIDE), bf16)
    dma = pltpu.SemaphoreType.DMA
    slots_smem = pltpu.SMEM((slot_count,), jnp.int32)
    pulled = lax.all_gather(
        jnp.concatenate([queries, new_kv, residual], axis=1), "req", axis=0
    )
    packed, own_res = pl.pallas_call(
        functools.partial(pack_kernel, lambda rank: lax.div(rank * tok_dev, DRAFT)),
        out_shape=(
            sent(slot_count * page_len + 3 * tok_dev),
            jax.ShapeDtypeStruct(residual.shape, bf16),
        ),
        in_specs=spaces("aaaav"),
        out_specs=tuple(spaces("vv")),
        scratch_shapes=[
            slots_smem,
            slots_smem,
            pltpu.VMEM(cache_keys.shape, bf16),
            pltpu.VMEM(cache_values.shape, bf16),
            dma((4,)),
        ],
        compiler_params=params(),
        name="pack",
    )(*in_hbm(placement, page_table.reshape(slot_count), cache_keys, cache_values), pulled)
    packed = lax.all_to_all(packed, "tp", 0, 0, tiled=True)
    block, picked, out_weight = pl.pallas_call(
        attend_kernel,
        out_shape=(
            jax.ShapeDtypeStruct(
                (group_rows + group_rows // 2 + (model // WIDE) * tok_dev, WIDE), bf16
            ),
            sent(tok_dev),
            pltpu.VMEM(out_weight.shape, bf16),
        ),
        in_specs=spaces("aaaavv"),
        out_specs=tuple(spaces("vvv")),
        scratch_shapes=[
            slots_smem,
            slots_smem,
            pltpu.VMEM((slot_count, DRAFT), jnp.int32),
            pltpu.VMEM((slot_count * DRAFT, slot_count * DRAFT), f32),
            dma((4,)),
        ],
        compiler_params=params(),
        name="attend",
    )(*in_hbm(lengths, accept_leaf, parents, out_weight), packed, own_res)
    blocks = gather_blocks(block)
    streamed = (
        router_weight.T,
        expert_ids.T,
        norm_gain.reshape(model // WIDE, WIDE),
        gate_up,
        down_weight,
    )
    units = gate_up.shape[0]
    moe, hidden, attn_own = pl.pallas_call(
        expert_kernel,
        out_shape=(
            jax.ShapeDtypeStruct((tp_count, tok_dev, model + WIDE), bf16),
            jax.ShapeDtypeStruct((tok_dev, model), f32),
            jax.ShapeDtypeStruct(queries.shape, bf16),
        ),
        in_specs=spaces("aaaaav" + "v" * (1 + tp_count)),
        out_specs=tuple(spaces("vvv")),
        scratch_shapes=[
            pltpu.VMEM((group_rows, HEADS * HEAD), bf16),
            pltpu.VMEM((group_rows, model), f32),
            pltpu.VMEM((group_rows, model), bf16),
            pltpu.VMEM((units, group_rows, gate_up.shape[2] // 2), f32),
            *[pltpu.VMEM(a.shape, a.dtype) for a in streamed],
            dma((3,)),
            dma((units,)),
            dma((units // STEP,)),
        ],
        compiler_params=params(36),
        name="experts",
    )(
        *in_hbm(*streamed),
        out_weight,
        picked,
        *blocks,
    )
    parts = lax.all_to_all(moe, "tp", 0, 0, tiled=True)
    layer_out, accepted = pl.pallas_call(
        finish_kernel,
        out_shape=(
            jax.ShapeDtypeStruct(residual.shape, bf16),
            jax.ShapeDtypeStruct(new_kv.shape, bf16),
        ),
        in_specs=spaces("vv"),
        out_specs=tuple(spaces("vv")),
        compiler_params=params(),
        name="finish",
    )(parts, hidden)
    return attn_own, layer_out, accepted


def per_device(queries, new_kv, residual, placement, *rest):
    tok_dev = queries.shape[0]
    one_head_each = lax.axis_size("tp") == KV_HEADS
    whole_tiles = tok_dev % 16 == 0 and tok_dev * KV_HEADS == 2 * DRAFT
    if one_head_each and whole_tiles and rest[1].shape[1] == 1:
        return per_device_packed(queries, new_kv, residual, placement, *rest)
    return per_device_plain(queries, new_kv, residual, placement, *rest)


def solution(mesh):
    in_specs = (
        P(("req", "tp"), None),
        P(("req", "tp"), None),
        P(("req", "tp"), None),
        P("req"),
        P("req"),
        P("req", None, "tp"),
        P(("req", "tp"), None, None),
        P(("req", "tp"), None, None),
        P("req", None),
        P("req"),
        P(),
        P(),
        P(),
        P("req", None),
        P("tp", None, None),
        P("tp", None, None),
    )
    out_specs = (P(("req", "tp"), None), P(("req", "tp"), None), P(("req", "tp"), None))
    return jax.shard_map(
        per_device, mesh=mesh, in_specs=in_specs, out_specs=out_specs, check_vma=False
    )
```

```python
import functools
import math

import jax
import jax.numpy as jnp
from jax import lax
from jax.experimental import pallas as pl
from jax.experimental.pallas import tpu as pltpu
from jax.sharding import PartitionSpec as P

HEADS = 24
KV_HEADS = 8
HEAD = 64
FF_E = 512
UNIT = 128
DRAFT = 64
WIDE = 128
STEP = 2


neg_big = -1e30
norm_eps = 1e-06


def joined_2(part, axis, combine):
    gathered = jax.tree.map(lambda a: lax.all_gather(a, axis), part)

    def take(source):
        return jax.tree.map(lambda a: lax.dynamic_index_in_dim(a, source, 0, False), gathered)

    return lax.fori_loop(
        1, lax.axis_size(axis), lambda source, state: combine(state, take(source)), take(0)
    )


def ancestry(parents):
    node_count = parents.shape[-1]
    node_ids = jnp.arange(node_count, dtype=jnp.int32)
    linked = (parents[:, :, None] == node_ids[None, None, :]) & (node_ids[None, :, None] > 0)
    reached = jnp.maximum(linked.astype(jnp.float32), jnp.eye(node_count, dtype=jnp.float32)[None])
    for _ in range(node_count.bit_length()):
        reached = jnp.minimum(
            jnp.einsum("rnm,rmk->rnk", reached, reached, precision=lax.Precision.HIGHEST), 1.0
        )
    return reached


def combine_stats(left_stats, right_stats):
    left_max, left_sum, left_out = left_stats
    right_max, right_sum, right_out = right_stats
    top_score = jnp.maximum(left_max, right_max)
    left_scale = jnp.exp(left_max - top_score)
    right_scale = jnp.exp(right_max - top_score)
    row_count, head_count = left_max.shape
    out_sum = (
        left_out.reshape(row_count, head_count, -1) * left_scale[..., None]
        + right_out.reshape(row_count, head_count, -1) * right_scale[..., None]
    )
    return (
        top_score,
        left_sum * left_scale + right_sum * right_scale,
        out_sum.reshape(row_count, -1),
    )


def finish_rows(stat_sum, stat_out):
    row_count, head_count = stat_sum.shape
    return (
        (stat_out.reshape(row_count, head_count, -1) / stat_sum[..., None])
        .reshape(row_count, -1)
        .astype(jnp.bfloat16)
    )


def project_rows(attn_rows, res_rows, out_weight):
    return res_rows.astype(jnp.float32) + jnp.dot(
        attn_rows, out_weight, preferred_element_type=jnp.float32
    )


def rms_normed(hidden, norm_gain):
    scale_rows = lax.rsqrt(jnp.mean(hidden * hidden, axis=-1, keepdims=True) + norm_eps)
    return (hidden * scale_rows * norm_gain).astype(jnp.bfloat16)


def unit_shares(normed_all, router_weight, expert_ids, tp_rank, units_dev):
    logits = jnp.dot(normed_all, router_weight, preferred_element_type=jnp.float32)
    expert_range = jnp.arange(router_weight.shape[1], dtype=jnp.int32)
    onehot = (expert_ids[:, :, None] == expert_range[None, None, :]).astype(jnp.float32)
    chosen = jnp.sum(logits[:, None, :] * onehot, axis=-1)
    expo_chosen = jnp.exp(chosen)
    expert_probs = expo_chosen / jnp.sum(expo_chosen, axis=-1, keepdims=True)
    routing = jnp.sum(expert_probs[:, :, None] * onehot, axis=1)
    unit_ids = tp_rank * units_dev + jnp.arange(units_dev, dtype=jnp.int32)
    expert_of_unit = unit_ids // (FF_E // UNIT)
    pick = (expert_range[:, None] == expert_of_unit[None, :]).astype(jnp.float32)
    return jnp.dot(routing, pick, precision=lax.Precision.HIGHEST)


def per_device_plain(
    queries,
    new_kv,
    residual,
    placement,
    lengths,
    page_table,
    cache_keys,
    cache_values,
    parents,
    accept_leaf,
    out_weight,
    norm_gain,
    router_weight,
    expert_ids,
    gate_up,
    down_weight,
):
    tok_dev = queries.shape[0]
    tp_count = lax.axis_size("tp")
    tp_rank = lax.axis_index("tp")
    group_rows = tok_dev * tp_count
    slot_count = placement.shape[0]
    kv_width = cache_keys.shape[2]
    page_len = cache_keys.shape[1]
    group_size = HEADS // KV_HEADS
    score_scale = 1.0 / math.sqrt(HEAD)
    row_start = tp_rank * tok_dev
    pulled_q, pulled_kv, pulled_res = (
        lax.all_gather(queries, "req", axis=0, tiled=True),
        lax.all_gather(new_kv, "req", axis=0, tiled=True),
        lax.all_gather(residual, "req", axis=0, tiled=True),
    )
    row_offsets = jnp.arange(tok_dev, dtype=jnp.int32)
    row_pos = row_start + row_offsets
    row_slot = row_pos // DRAFT
    slot_match = row_slot[:, None] == jnp.arange(slot_count, dtype=jnp.int32)[None, :]
    source_group = jnp.sum(jnp.where(slot_match, placement[None, :] // slot_count, 0), axis=1)
    source_rows = source_group * tok_dev + row_offsets
    own_q = jnp.take(pulled_q, source_rows, axis=0)
    own_kv = jnp.take(pulled_kv, source_rows, axis=0)
    own_res = jnp.take(pulled_res, source_rows, axis=0)
    all_q, all_kv = (
        lax.all_gather(own_q, "tp", axis=0, tiled=True),
        lax.all_gather(own_kv, "tp", axis=0, tiled=True),
    )
    local_pages = page_table.shape[1]
    page_ids = page_table[:, :, 0].reshape(-1)
    keys_local = jnp.take(cache_keys, page_ids, axis=0).reshape(
        slot_count, local_pages, page_len, KV_HEADS, HEAD
    )
    values_local = jnp.take(cache_values, page_ids, axis=0).reshape(
        slot_count, local_pages, page_len, KV_HEADS, HEAD
    )
    query_blocks = all_q.reshape(slot_count, DRAFT, KV_HEADS, group_size, HEAD)
    scores = (
        jnp.einsum(
            "sqgrd,sltgd->sqgrlt", query_blocks, keys_local, preferred_element_type=jnp.float32
        )
        * score_scale
    )
    positions = (
        jnp.arange(local_pages, dtype=jnp.int32)[:, None] * tp_count + tp_rank
    ) * page_len + jnp.arange(page_len, dtype=jnp.int32)[None, :]
    is_valid = (positions[None] < lengths[:, None, None])[:, None, None, None]
    scores = jnp.where(is_valid, scores, neg_big)
    block_max = jnp.max(scores, axis=-1)
    weights = jnp.where(is_valid, jnp.exp(scores - block_max[..., None]), 0.0).astype(jnp.bfloat16)
    block_sum = jnp.sum(weights.astype(jnp.float32), axis=-1)
    block_out = jnp.einsum(
        "sqgrlt,sltgd->sqgrld", weights, values_local, preferred_element_type=jnp.float32
    )
    page_top = jnp.max(block_max, axis=-1)
    page_scale = jnp.exp(block_max - page_top[..., None])
    stat_max = page_top.reshape(group_rows, HEADS)
    stat_sum = jnp.sum(block_sum * page_scale, axis=-1).reshape(group_rows, HEADS)
    stat_out = jnp.sum(block_out * page_scale[..., None], axis=-2).reshape(group_rows, HEADS * HEAD)
    reached = ancestry(parents)
    reach_rows = jnp.take(reached.reshape(slot_count * DRAFT, DRAFT), row_pos, axis=0)
    key_slot = jnp.arange(group_rows, dtype=jnp.int32) // DRAFT
    same_slot = key_slot[None, :] == row_slot[:, None]
    allowed = same_slot & (jnp.tile(reach_rows, (1, slot_count)) > 0.5)
    tree_keys = all_kv[:, :kv_width].reshape(group_rows, KV_HEADS, HEAD)
    tree_values = all_kv[:, kv_width:].reshape(group_rows, KV_HEADS, HEAD)
    own_blocks = own_q.reshape(tok_dev, KV_HEADS, group_size, HEAD)
    tree_scores = (
        jnp.einsum("igrd,kgd->igrk", own_blocks, tree_keys, preferred_element_type=jnp.float32)
        * score_scale
    )
    tree_mask = allowed[:, None, None, :]
    tree_scores = jnp.where(tree_mask, tree_scores, neg_big)
    tree_max = jnp.max(tree_scores, axis=-1)
    tree_weights = jnp.where(tree_mask, jnp.exp(tree_scores - tree_max[..., None]), 0.0).astype(
        jnp.bfloat16
    )
    tree_sum = jnp.sum(tree_weights.astype(jnp.float32), axis=-1)
    tree_out = jnp.einsum(
        "igrk,kgd->igrd", tree_weights, tree_values, preferred_element_type=jnp.float32
    )
    own_stats = (
        lax.dynamic_slice_in_dim(stat_max, row_start, tok_dev, 0),
        lax.dynamic_slice_in_dim(stat_sum, row_start, tok_dev, 0),
        lax.dynamic_slice_in_dim(stat_out, row_start, tok_dev, 0),
    )
    tree_stats = (
        tree_max.reshape(tok_dev, HEADS),
        tree_sum.reshape(tok_dev, HEADS),
        tree_out.reshape(tok_dev, HEADS * HEAD),
    )
    joined = combine_stats(own_stats, tree_stats)
    stat_max = lax.dynamic_update_slice_in_dim(stat_max, joined[0], row_start, 0)
    stat_sum = lax.dynamic_update_slice_in_dim(stat_sum, joined[1], row_start, 0)
    stat_out = lax.dynamic_update_slice_in_dim(stat_out, joined[2], row_start, 0)
    normed_all = None
    merged = joined_2((stat_max, stat_sum, stat_out), "tp", combine_stats)
    attn_own = finish_rows(
        lax.dynamic_slice_in_dim(merged[1], row_start, tok_dev, 0),
        lax.dynamic_slice_in_dim(merged[2], row_start, tok_dev, 0),
    )
    hidden_own = project_rows(attn_own, own_res, out_weight)
    normed_own = rms_normed(hidden_own, norm_gain)
    units_dev = gate_up.shape[0]
    unit_width = gate_up.shape[2] // 2
    normed_all = lax.all_gather(normed_own, "tp", axis=0, tiled=True)
    shares = unit_shares(normed_all, router_weight, expert_ids, tp_rank, units_dev)
    gate_both = jnp.einsum("td,udh->tuh", normed_all, gate_up, preferred_element_type=jnp.float32)
    activated = (
        jax.nn.silu(gate_both[..., :unit_width]) * gate_both[..., unit_width:] * shares[:, :, None]
    ).astype(jnp.bfloat16)
    moe_own = lax.psum_scatter(
        jnp.einsum("tuh,uhd->td", activated, down_weight, preferred_element_type=jnp.float32),
        "tp",
        scatter_dimension=0,
        tiled=True,
    )
    layer_out = (hidden_own + moe_own).astype(jnp.bfloat16)
    node_ids = jnp.arange(DRAFT, dtype=jnp.int32)
    leaf_pick = (accept_leaf[:, None] == node_ids[None, :]).astype(jnp.float32)
    path_weight = jnp.einsum("sn,snk->sk", leaf_pick, reached, precision=lax.Precision.HIGHEST)
    path_flags = (path_weight > 0.5).astype(jnp.int32)
    path_rank = jnp.cumsum(path_flags, axis=1) - 1
    chosen_node = (path_flags[:, None, :] > 0) & (path_rank[:, None, :] == node_ids[None, :, None])
    own_choice = jnp.take(chosen_node.reshape(slot_count * DRAFT, DRAFT), row_pos, axis=0)
    spread = same_slot & jnp.tile(own_choice, (1, slot_count))
    accepted = jnp.dot(
        spread.astype(jnp.bfloat16), all_kv, preferred_element_type=jnp.float32
    ).astype(jnp.bfloat16)
    return (attn_own, layer_out, accepted)


def start_all(copies):
    for copy in copies:
        copy.start()
    for copy in copies:
        copy.wait()


def split_kernel(pairs, *refs):
    (
        pages_hbm, placement_hbm, lengths_hbm, leaf_hbm, keys_hbm, values_hbm, queries_hbm,
        new_kv_hbm, residual_hbm, parents_hbm, router_hbm, ids_hbm, gain_hbm,
    ) = refs[:13]
    parts, refs = refs[13 : 13 + pairs], refs[13 + pairs :]
    joined_ref, table_ref, parents_ref, router_ref, ids_ref, gain_ref = refs[:6]
    pages_ref, placement_ref, lengths_ref, leaf_ref, keys_ref, values_ref, split_ref, sems = refs[6:]
    slot_count = pages_ref.shape[0]
    page_len = keys_ref.shape[1]
    tok_dev = joined_ref.shape[0]
    moves = [
        (pages_hbm, pages_ref),
        (keys_hbm, keys_ref),
        (values_hbm, values_ref),
        (placement_hbm, placement_ref),
        (lengths_hbm, lengths_ref),
        (leaf_hbm, leaf_ref),
        (parents_hbm, parents_ref),
        (router_hbm, router_ref),
        (ids_hbm, ids_ref),
        (gain_hbm, gain_ref),
    ]
    column = 0
    for source in (queries_hbm, new_kv_hbm, residual_hbm):
        moves.append((source, joined_ref.at[:, column : column + source.shape[1]]))
        column += source.shape[1]
    start_all(
        [pltpu.make_async_copy(a, b, sems.at[k]) for k, (a, b) in enumerate(moves)]
    )
    slot = lax.div(lax.axis_index("tp") * tok_dev, DRAFT)
    numbers = [lax.div(placement_ref[slot], slot_count)]
    numbers += [lengths_ref[s] for s in range(slot_count)]
    numbers += [leaf_ref[s] for s in range(slot_count)]
    for row, number in enumerate(numbers):
        table_ref[row : row + 1, :] = jnp.full((1, WIDE), number, jnp.int32).astype(jnp.float32)
    for head in range(KV_HEADS):
        low = head * HEAD
        for s in range(slot_count):
            page = pages_ref[s]
            split_ref[head // 2, head % 2, s * page_len : (s + 1) * page_len, :] = jnp.concatenate(
                [keys_ref[page, :, low : low + HEAD], values_ref[page, :, low : low + HEAD]], axis=1
            )
    pair = lax.div(lax.axis_index("tp"), 2)
    for k, part in enumerate(parts):
        part[...] = split_ref[lax.bitwise_xor(pair, k)]


def number(table_ref, row):
    return jnp.max(table_ref[row : row + 1, :]).astype(jnp.int32)


def route_kernel(kv_width, after_ref, table_ref, pulled_ref, *refs):
    del after_ref
    parts, (sent_ref, res_ref, turned_ref) = refs[:-3], refs[-3:]
    rank = lax.axis_index("tp")
    other = 1 - lax.rem(rank, 2)
    for k, part in enumerate(parts):
        turned_ref[k] = part[other]
    q_width = HEADS * HEAD
    tok_dev = pulled_ref.shape[1]
    rows = pulled_ref[number(table_ref, 0)]
    res_ref[...] = rows[:, q_width + 2 * kv_width :]
    head_rows = (HEADS // KV_HEADS) * HEAD
    tail = jnp.zeros((tok_dev, 2 * WIDE - head_rows), rows.dtype)
    for head in range(KV_HEADS):
        q_low = head * head_rows
        pair = jnp.concatenate([rows[:, q_low : q_low + head_rows], tail], axis=1)
        sent_ref[head, :tok_dev, :] = pair[:, :WIDE]
        sent_ref[head, tok_dev : 2 * tok_dev, :] = pair[:, WIDE:]
        k_low = q_width + head * HEAD
        sent_ref[head, 2 * tok_dev :, :] = jnp.concatenate(
            [rows[:, k_low : k_low + HEAD], rows[:, k_low + kv_width : k_low + kv_width + HEAD]],
            axis=1,
        )


def ancestor_rows(parents_ref):
    slot_count = parents_ref.shape[0]
    total = slot_count * DRAFT
    row = jnp.concatenate(
        [parents_ref[s : s + 1, :] + s * DRAFT for s in range(slot_count)], axis=1
    )
    from_ids = lax.broadcasted_iota(jnp.int32, (total, total), 0)
    to_ids = lax.broadcasted_iota(jnp.int32, (total, total), 1)
    linked = (from_ids == jnp.broadcast_to(row, (total, total))) & (lax.rem(to_ids, DRAFT) > 0)
    reached = jnp.where(linked | (from_ids == to_ids), 1.0, 0.0)
    for _ in range((DRAFT - 1).bit_length()):
        half = reached.astype(jnp.bfloat16)
        reached = jnp.minimum(jnp.dot(half, half, preferred_element_type=jnp.float32), 1.0)
    return reached.T


def tree_kernel(
    after_ref, down_hbm, table_ref, parents_ref, down_ref, reach_ref, chosen_ref, sem
):
    del after_ref
    copy = pltpu.make_async_copy(down_hbm, down_ref, sem)
    copy.start()
    slot_count = parents_ref.shape[0]
    reach_ref[...] = ancestor_rows(parents_ref)
    node_from = lax.broadcasted_iota(jnp.int32, (DRAFT, DRAFT), 0)
    node_to = lax.broadcasted_iota(jnp.int32, (DRAFT, DRAFT), 1)
    upto = jnp.where(node_from <= node_to, 1.0, 0.0).astype(jnp.bfloat16)
    for s in range(slot_count):
        leaf = number(table_ref, 1 + slot_count + s)
        path = reach_ref[pl.ds(s * DRAFT + leaf, 1), s * DRAFT : (s + 1) * DRAFT]
        path = jnp.broadcast_to(path, (DRAFT, DRAFT))
        rank = jnp.dot(path.astype(jnp.bfloat16), upto, preferred_element_type=jnp.float32)
        chosen = (path > 0.5) & (rank == (node_from + 1).astype(jnp.float32))
        chosen_ref[s] = jnp.where(chosen, 1.0, 0.0).astype(jnp.bfloat16)
    copy.wait()


def attend_kernel(table_ref, reach_ref, chosen_ref, got_ref, res_ref, turned_ref, *refs):
    parts, (sent_ref, picked_ref) = refs[:-2], refs[-2:]
    slot_count = chosen_ref.shape[0]
    sources = got_ref.shape[0]
    tok_dev = res_ref.shape[0]
    page_len = turned_ref.shape[1] // slot_count
    per_slot = DRAFT // tok_dev
    group_size = HEADS // KV_HEADS
    f32, bf16 = jnp.float32, jnp.bfloat16
    lane_low = lax.broadcasted_iota(jnp.int32, (DRAFT, WIDE), 1) < HEAD
    rank = lax.axis_index("tp")
    side = lax.rem(rank, 2)
    within = lax.broadcasted_iota(jnp.int32, (1, page_len), 1)
    positions = []
    for k in range(len(parts)):
        pair = lax.bitwise_xor(lax.div(rank, 2), k)
        for page in (2 * pair + side, 2 * pair + 1 - side):
            positions.append(within + page * page_len)
    positions = jnp.concatenate(positions, axis=1)
    dims = (((1,), (1,)), ((), ()))
    scale = 1.0 / math.sqrt(HEAD)
    outs, picked = [], []
    for s in range(slot_count):
        first = s * per_slot

        def part(k):
            low = k * tok_dev
            return jnp.concatenate(
                [got_ref[first + i, low : low + tok_dev, :] for i in range(per_slot)], axis=0
            )

        q_pair, q_last, tree_kv = part(0).astype(f32) * scale, part(1).astype(f32) * scale, part(2)
        q_rows = jnp.concatenate(
            [
                jnp.where(lane_low, q_pair, 0.0),
                jnp.where(lane_low, pltpu.roll(q_pair, HEAD, 1), 0.0),
                jnp.where(lane_low, q_last, 0.0),
            ],
            axis=0,
        ).astype(bf16)
        at = slice(s * page_len, (s + 1) * page_len)
        cache_kv = jnp.concatenate(
            [a for k, part in enumerate(parts) for a in (part[side, at, :], turned_ref[k, at, :])],
            axis=0,
        )
        scores = lax.dot_general(q_rows, cache_kv, dims, preferred_element_type=f32)
        is_valid = positions < number(table_ref, 1 + s)
        scores = jnp.where(is_valid, scores, neg_big)
        reach = reach_ref[s * DRAFT : (s + 1) * DRAFT, s * DRAFT : (s + 1) * DRAFT]
        allowed = jnp.concatenate([reach] * group_size, axis=0) > 0.5
        tree_scores = lax.dot_general(q_rows, tree_kv, dims, preferred_element_type=f32)
        tree_scores = jnp.where(allowed, tree_scores, neg_big)
        top = jnp.maximum(
            jnp.max(scores, axis=1, keepdims=True), jnp.max(tree_scores, axis=1, keepdims=True)
        )
        weights = jnp.where(is_valid, jnp.exp(scores - top), 0.0).astype(bf16)
        tree_weights = jnp.where(allowed, jnp.exp(tree_scores - top), 0.0).astype(bf16)
        total = jnp.sum(weights.astype(f32), axis=1, keepdims=True) + jnp.sum(
            tree_weights.astype(f32), axis=1, keepdims=True
        )
        mixed = jnp.dot(weights, cache_kv, preferred_element_type=f32) + jnp.dot(
            tree_weights, tree_kv, preferred_element_type=f32
        )
        outs.append(mixed / total)
        picked.append(
            jnp.dot(chosen_ref[s], tree_kv, preferred_element_type=f32).astype(bf16)
        )
    pair_rows, last_rows = [], []
    for out in outs:
        head_out = [out[r * DRAFT : (r + 1) * DRAFT] for r in range(group_size)]
        pair_rows.append(
            jnp.where(lane_low, pltpu.roll(head_out[0], HEAD, 1), head_out[1]).astype(bf16)
        )
        last_rows.append(head_out[2])
    last = jnp.where(lane_low, pltpu.roll(last_rows[0], HEAD, 1), last_rows[1]).astype(bf16)
    res_tiles = [res_ref[:, c * WIDE : (c + 1) * WIDE] for c in range(res_ref.shape[1] // WIDE)]
    sent_ref[...] = jnp.concatenate(pair_rows + [last] + res_tiles, axis=0)
    for target in range(sources):
        row = (target % per_slot) * tok_dev
        picked_ref[target] = picked[target // per_slot][row : row + tok_dev]


def fetch_kernel(spans, after_ref, *refs):
    del after_ref
    count = len(spans)
    sems = refs[-1]
    start_all(
        [
            pltpu.make_async_copy(refs[k].at[pl.ds(*spans[k])], refs[count + k], sems.at[k])
            for k in range(count)
        ]
    )


def expert_kernel(
    router_ref, ids_ref, gain_ref, out_weight_ref, down_ref, early_ref, late_ref, picked_ref, *refs
):
    blocks, refs = refs[:KV_HEADS], refs[KV_HEADS:]
    mine_ref, sent_ref, hidden_ref, attn_ref, x_ref, hid_ref, normed_ref, share_ref = refs
    f32, bf16 = jnp.float32, jnp.bfloat16
    early = early_ref.shape[0]
    units = early + late_ref.shape[0]
    tok_dev = hidden_ref.shape[0]
    sources = len(blocks)
    group_rows = sources * tok_dev
    half = group_rows // 2
    width, model = out_weight_ref.shape
    rank = lax.axis_index("tp")
    lane_low = lax.broadcasted_iota(jnp.int32, (half, WIDE), 1) < HEAD
    head_rows = width // sources
    res_start = group_rows + half
    is_even = lax.rem(rank, 2) == 0
    for k in range(sources // 2):
        pair = lax.bitwise_xor(lax.div(rank, 2), k)
        mine, other = blocks[2 * k][...], blocks[2 * k + 1][...]
        even, odd = jnp.where(is_even, mine, other), jnp.where(is_even, other, mine)
        last_even = even[group_rows:res_start].astype(f32)
        last_odd = odd[group_rows:res_start].astype(f32)
        odd_swapped = pltpu.roll(odd[:group_rows].astype(f32), HEAD, 1)
        middle = jnp.concatenate(
            [
                jnp.where(lane_low, last_even, odd_swapped[:half]),
                jnp.where(lane_low, pltpu.roll(last_even, HEAD, 1), odd_swapped[half:]),
            ],
            axis=0,
        ).astype(bf16)
        end = jnp.concatenate(
            [
                jnp.where(lane_low, odd_swapped[:half], pltpu.roll(last_odd, HEAD, 1)),
                jnp.where(lane_low, odd_swapped[half:], last_odd),
            ],
            axis=0,
        ).astype(bf16)
        base = pl.multiple_of(pair * 2 * head_rows, WIDE)
        x_ref[:, pl.ds(base, 2 * head_rows)] = jnp.concatenate(
            [even[:group_rows], middle, end], axis=1
        )
        for q, block in enumerate((even, odd)):
            row = pl.multiple_of((2 * pair + q) * tok_dev, tok_dev)
            hid_ref[pl.ds(row, tok_dev), :] = jnp.concatenate(
                [
                    block[res_start + c * tok_dev : res_start + (c + 1) * tok_dev]
                    for c in range(model // WIDE)
                ],
                axis=1,
            ).astype(f32)
    own = pl.multiple_of(rank * tok_dev, tok_dev)
    attn_ref[...] = x_ref[pl.ds(own, tok_dev), :]
    projected = jnp.dot(x_ref[...], out_weight_ref[...], preferred_element_type=f32)
    hidden = hid_ref[...] + projected
    hid_ref[...] = hidden
    gain = jnp.concatenate([gain_ref[c : c + 1, :] for c in range(model // WIDE)], axis=1)
    scale = lax.rsqrt(jnp.mean(hidden * hidden, axis=1, keepdims=True) + norm_eps)
    normed_ref[...] = (hidden * scale * gain).astype(bf16)
    hidden_ref[...] = hid_ref[pl.ds(own, tok_dev), :]
    logits = lax.dot_general(
        normed_ref[...], router_ref[...], (((1,), (1,)), ((), ())), preferred_element_type=f32
    )
    experts = router_ref.shape[0]
    ids = ids_ref[...].astype(f32).T
    expert_range = lax.broadcasted_iota(jnp.int32, (group_rows, experts), 1)
    expert_names = expert_range.astype(f32)
    count = jnp.zeros((group_rows, experts), f32)
    for k in range(ids_ref.shape[0]):
        count = count + jnp.where(ids[:, k : k + 1] == expert_names, 1.0, 0.0)
    expo = jnp.where(count > 0.0, jnp.exp(logits), 0.0) * count
    routing = expo / jnp.sum(expo, axis=1, keepdims=True)
    unit_width = early_ref.shape[2] // 2
    span = FF_E // unit_width
    each = span if units % span == 0 else 1
    for u in range(0, units, each):
        expert = (rank * units + u) // span
        share = jnp.sum(jnp.where(expert_range == expert, routing, 0.0), axis=1, keepdims=True)
        share_ref[u : u + each] = jnp.broadcast_to(share[None], (each, group_rows, unit_width))

    def one_unit(u):
        weight = early_ref[u] if u < early else late_ref[u - early]
        both = jnp.dot(normed_ref[...], weight, preferred_element_type=f32)
        gate, up = both[:, :unit_width], both[:, unit_width:]
        return (gate / (1.0 + jnp.exp(-gate)) * up * share_ref[u]).astype(bf16)

    for i in range(units // STEP):
        act = jnp.concatenate([one_unit(i * STEP + k) for k in range(STEP)], axis=1)
        down = down_ref[i * STEP : (i + 1) * STEP].reshape(STEP * unit_width, model)
        part = jnp.dot(act, down, preferred_element_type=f32)
        hid_ref[...] = part if i == 0 else hid_ref[...] + part
    side = lax.rem(rank, 2)
    for k in range(sources // 2):
        pair = lax.bitwise_xor(lax.div(rank, 2), k)
        for target, ref in ((2 * pair + side, mine_ref), (2 * pair + 1 - side, sent_ref)):
            row = pl.multiple_of(target * tok_dev, tok_dev)
            ref[k, :, :model] = hid_ref[pl.ds(row, tok_dev), :].astype(ref.dtype)
            ref[k, :, model:] = picked_ref[target].astype(ref.dtype)


def fold_kernel(mine_ref, got_ref, hidden_ref, kept_ref, *sent_refs):
    model = hidden_ref.shape[1]
    is_even = lax.rem(lax.axis_index("tp"), 2) == 0
    for k, ref in enumerate((kept_ref,) + sent_refs):
        mine, got = mine_ref[k], got_ref[k].astype(jnp.float32)
        total = mine[:, :model] + got[:, :model]
        if k == 0:
            total = total + hidden_ref[...]
        ref[:, :model] = total.astype(ref.dtype)
        low, high = mine[:, model:], got[:, model:]
        even, odd = jnp.where(is_even, low, high), jnp.where(is_even, high, low)
        ref[:, model:] = jnp.concatenate([even, odd], axis=1).astype(ref.dtype)


def finish_kernel(attn_in_ref, *refs):
    parts, (attn_ref, layer_ref, accepted_ref) = refs[:-3], refs[-3:]
    attn_ref[...] = attn_in_ref[...]
    f32, bf16 = jnp.float32, jnp.bfloat16
    tok_dev, model = layer_ref.shape
    kv_width = accepted_ref.shape[1] // 2
    total = parts[0][:, :model]
    for part in parts[1:]:
        total = total + part[:, :model].astype(f32)
    layer_ref[...] = total.astype(bf16)
    low = lax.broadcasted_iota(jnp.int32, (tok_dev, WIDE), 1) < HEAD
    for k, part in enumerate(parts):
        pair = lax.bitwise_xor(lax.div(lax.axis_index("tp"), 2), k)
        even = part[:, model : model + WIDE].astype(f32)
        odd = part[:, model + WIDE :].astype(f32)
        at = pl.multiple_of(pair * WIDE, WIDE)
        accepted_ref[:, pl.ds(at, WIDE)] = jnp.where(low, even, pltpu.roll(odd, HEAD, 1)).astype(bf16)
        accepted_ref[:, pl.ds(kv_width + at, WIDE)] = jnp.where(
            low, pltpu.roll(even, HEAD, 1), odd
        ).astype(bf16)


def in_hbm(*arrays):
    return tuple(pltpu.with_memory_space_constraint(a, pltpu.HBM) for a in arrays)


def spaces(text):
    kinds = {"a": pl.ANY, "v": pltpu.VMEM}
    return [pl.BlockSpec(memory_space=kinds[c]) for c in text]


def params(mebibytes=12):
    return pltpu.CompilerParams(vmem_limit_bytes=mebibytes << 20)


def cost(mebibytes):
    return pl.CostEstimate(flops=0, transcendentals=0, bytes_accessed=mebibytes << 20)


def swap(rows, mask):
    count = lax.axis_size("tp")
    return lax.ppermute(rows, "tp", [(i, i ^ mask) for i in range(count)])


def gather_blocks(block, early):
    pairs = [swap(block, 2 * k) for k in range(1, lax.axis_size("tp") // 2)]
    pairs, early = lax.optimization_barrier((pairs, early))
    return [a for rows in [block] + pairs for a in (rows, swap(rows, 1))], early


def fetch(name, after, *spans):
    shapes = [(rows,) + array.shape[1:] for array, _, rows in spans]
    return pl.pallas_call(
        functools.partial(fetch_kernel, tuple((first, rows) for _, first, rows in spans)),
        out_shape=tuple(pltpu.VMEM(shape, jnp.bfloat16) for shape in shapes),
        in_specs=spaces("a" * (1 + len(spans))),
        out_specs=tuple(spaces("v" * len(spans))),
        scratch_shapes=[pltpu.SemaphoreType.DMA((len(spans),))],
        compiler_params=params(),
        cost_estimate=cost(sum(2 * math.prod(shape) for shape in shapes) >> 20),
        name="fetch_" + name,
    )(after, *in_hbm(*[array for array, _, _ in spans]))


def per_device_packed(
    queries,
    new_kv,
    residual,
    placement,
    lengths,
    page_table,
    cache_keys,
    cache_values,
    parents,
    accept_leaf,
    out_weight,
    norm_gain,
    router_weight,
    expert_ids,
    gate_up,
    down_weight,
):
    f32, bf16 = jnp.float32, jnp.bfloat16
    tok_dev, model = residual.shape
    tp_count = lax.axis_size("tp")
    slot_count = placement.shape[0]
    page_len, kv_width = cache_keys.shape[1:]
    group_rows = tok_dev * tp_count
    sent = lambda rows: jax.ShapeDtypeStruct((tp_count, rows, WIDE), bf16)
    dma = pltpu.SemaphoreType.DMA
    slots_smem = pltpu.SMEM((slot_count,), jnp.int32)
    pairs = tp_count // 2
    part = jax.ShapeDtypeStruct((2, slot_count * page_len, WIDE), bf16)
    loaded = (
        page_table.reshape(slot_count),
        placement,
        lengths,
        accept_leaf,
        cache_keys,
        cache_values,
        queries,
        new_kv,
        residual,
        parents,
        router_weight.T,
        expert_ids.T,
        norm_gain.reshape(model // WIDE, WIDE),
    )
    *parts, joined, table, parents, router, ids, gain = pl.pallas_call(
        functools.partial(split_kernel, pairs),
        out_shape=(part,) * pairs
        + (
            jax.ShapeDtypeStruct((tok_dev, 2 * (model + kv_width)), bf16),
            pltpu.VMEM((8, WIDE), f32),
        )
        + tuple(pltpu.VMEM(a.shape, a.dtype) for a in loaded[9:]),
        in_specs=spaces("a" * len(loaded)),
        out_specs=tuple(spaces("v" * (pairs + 6))),
        scratch_shapes=[
            slots_smem,
            slots_smem,
            slots_smem,
            slots_smem,
            pltpu.VMEM(cache_keys.shape, bf16),
            pltpu.VMEM(cache_values.shape, bf16),
            pltpu.VMEM((pairs,) + part.shape, bf16),
            dma((len(loaded),)),
        ],
        compiler_params=params(),
        cost_estimate=cost(4),
        name="split",
    )(*in_hbm(*loaded))
    parts = [parts[0]] + [swap(parts[k], 2 * k) for k in range(1, pairs)]
    pulled = lax.all_gather(joined, "req", axis=0)
    nodes = slot_count * DRAFT
    down_weight, reach, chosen = pl.pallas_call(
        tree_kernel,
        out_shape=(
            pltpu.VMEM(down_weight.shape, bf16),
            jax.ShapeDtypeStruct((nodes, nodes), f32),
            jax.ShapeDtypeStruct((slot_count, DRAFT, DRAFT), bf16),
        ),
        in_specs=spaces("aavv"),
        out_specs=tuple(spaces("vvv")),
        scratch_shapes=[dma],
        compiler_params=params(),
        cost_estimate=cost(8),
        name="tree",
    )(pulled, *in_hbm(down_weight), table, parents)
    packed, own_res, turned = pl.pallas_call(
        functools.partial(route_kernel, kv_width),
        out_shape=(
            sent(3 * tok_dev),
            jax.ShapeDtypeStruct(residual.shape, bf16),
            jax.ShapeDtypeStruct((pairs,) + part.shape[1:], bf16),
        ),
        in_specs=spaces("avv" + "v" * pairs),
        out_specs=tuple(spaces("vvv")),
        compiler_params=params(),
        cost_estimate=cost(4),
        name="route",
    )(down_weight, table, pulled, *parts)
    turned = swap(turned, 1)
    packed = lax.all_to_all(packed, "tp", 0, 0, tiled=True)
    block, picked = pl.pallas_call(
        attend_kernel,
        out_shape=(
            jax.ShapeDtypeStruct(
                (group_rows + group_rows // 2 + (model // WIDE) * tok_dev, WIDE), bf16
            ),
            sent(tok_dev),
        ),
        in_specs=spaces("v" * (6 + pairs)),
        out_specs=tuple(spaces("vv")),
        compiler_params=params(),
        cost_estimate=cost(8),
        name="attend",
    )(table, reach, chosen, packed, own_res, turned, *parts)
    units = gate_up.shape[0]
    early = units // (2 * STEP) * STEP
    ready = fetch("early", block, (gate_up, 0, early), (out_weight, 0, out_weight.shape[0]))
    blocks, (early_units, out_weight) = gather_blocks(block, ready)
    (late_units,) = fetch("late", block, (gate_up, early, units - early))
    mine, sent_sums, hidden, attn_own = pl.pallas_call(
        expert_kernel,
        out_shape=(
            jax.ShapeDtypeStruct((pairs, tok_dev, model + WIDE), f32),
            jax.ShapeDtypeStruct((pairs, tok_dev, model + WIDE), bf16),
            jax.ShapeDtypeStruct((tok_dev, model), f32),
            pltpu.VMEM(queries.shape, bf16),
        ),
        in_specs=spaces("v" * (8 + tp_count)),
        out_specs=tuple(spaces("vvvv")),
        scratch_shapes=[
            pltpu.VMEM((group_rows, HEADS * HEAD), bf16),
            pltpu.VMEM((group_rows, model), f32),
            pltpu.VMEM((group_rows, model), bf16),
            pltpu.VMEM((units, group_rows, gate_up.shape[2] // 2), f32),
        ],
        compiler_params=params(),
        name="experts",
    )(
        router,
        ids,
        gain,
        out_weight,
        down_weight,
        early_units,
        late_units,
        picked,
        *blocks,
    )
    sums = pl.pallas_call(
        fold_kernel,
        out_shape=tuple(
            jax.ShapeDtypeStruct((tok_dev, model + 2 * WIDE), f32 if k == 0 else bf16)
            for k in range(pairs)
        ),
        in_specs=spaces("vvv"),
        out_specs=tuple(spaces("v" * pairs)),
        compiler_params=params(),
        name="fold",
    )(mine, swap(sent_sums, 1), hidden)
    sums = [sums[0]] + [swap(sums[k], 2 * k) for k in range(1, pairs)]
    return pl.pallas_call(
        finish_kernel,
        out_shape=(
            jax.ShapeDtypeStruct(queries.shape, bf16),
            jax.ShapeDtypeStruct(residual.shape, bf16),
            jax.ShapeDtypeStruct(new_kv.shape, bf16),
        ),
        in_specs=spaces("v" * (1 + pairs)),
        out_specs=tuple(spaces("vvv")),
        compiler_params=params(),
        name="finish",
    )(attn_own, *sums)


def per_device(queries, new_kv, residual, placement, *rest):
    tok_dev = queries.shape[0]
    one_head_each = lax.axis_size("tp") == KV_HEADS
    whole_tiles = tok_dev % 16 == 0 and placement.shape[0] == 2 and tok_dev * KV_HEADS == 2 * DRAFT
    if one_head_each and whole_tiles and rest[1].shape[1] == 1:
        return per_device_packed(queries, new_kv, residual, placement, *rest)
    return per_device_plain(queries, new_kv, residual, placement, *rest)


def solution(mesh):
    in_specs = (
        P(("req", "tp"), None),
        P(("req", "tp"), None),
        P(("req", "tp"), None),
        P("req"),
        P("req"),
        P("req", None, "tp"),
        P(("req", "tp"), None, None),
        P(("req", "tp"), None, None),
        P("req", None),
        P("req"),
        P(),
        P(),
        P(),
        P("req", None),
        P("tp", None, None),
        P("tp", None, None),
    )
    out_specs = (P(("req", "tp"), None), P(("req", "tp"), None), P(("req", "tp"), None))
    return jax.shard_map(
        per_device, mesh=mesh, in_specs=in_specs, out_specs=out_specs, check_vma=False
    )
```

```python
import functools
import math

import jax
import jax.numpy as jnp
from jax import lax
from jax.experimental import pallas as pl
from jax.experimental.pallas import tpu as pltpu
from jax.sharding import PartitionSpec as P

HEADS = 24
KV_HEADS = 8
HEAD = 64
FF_E = 512
UNIT = 128
DRAFT = 64
WIDE = 128
STEP = 2
ORDER = (1, 3, 2)


neg_big = -1e30
norm_eps = 1e-06


def joined_2(part, axis, combine):
    gathered = jax.tree.map(lambda a: lax.all_gather(a, axis), part)

    def take(source):
        return jax.tree.map(lambda a: lax.dynamic_index_in_dim(a, source, 0, False), gathered)

    return lax.fori_loop(
        1, lax.axis_size(axis), lambda source, state: combine(state, take(source)), take(0)
    )


def ancestry(parents):
    node_count = parents.shape[-1]
    node_ids = jnp.arange(node_count, dtype=jnp.int32)
    linked = (parents[:, :, None] == node_ids[None, None, :]) & (node_ids[None, :, None] > 0)
    reached = jnp.maximum(linked.astype(jnp.float32), jnp.eye(node_count, dtype=jnp.float32)[None])
    for _ in range(node_count.bit_length()):
        reached = jnp.minimum(
            jnp.einsum("rnm,rmk->rnk", reached, reached, precision=lax.Precision.HIGHEST), 1.0
        )
    return reached


def combine_stats(left_stats, right_stats):
    left_max, left_sum, left_out = left_stats
    right_max, right_sum, right_out = right_stats
    top_score = jnp.maximum(left_max, right_max)
    left_scale = jnp.exp(left_max - top_score)
    right_scale = jnp.exp(right_max - top_score)
    row_count, head_count = left_max.shape
    out_sum = (
        left_out.reshape(row_count, head_count, -1) * left_scale[..., None]
        + right_out.reshape(row_count, head_count, -1) * right_scale[..., None]
    )
    return (
        top_score,
        left_sum * left_scale + right_sum * right_scale,
        out_sum.reshape(row_count, -1),
    )


def finish_rows(stat_sum, stat_out):
    row_count, head_count = stat_sum.shape
    return (
        (stat_out.reshape(row_count, head_count, -1) / stat_sum[..., None])
        .reshape(row_count, -1)
        .astype(jnp.bfloat16)
    )


def project_rows(attn_rows, res_rows, out_weight):
    return res_rows.astype(jnp.float32) + jnp.dot(
        attn_rows, out_weight, preferred_element_type=jnp.float32
    )


def rms_normed(hidden, norm_gain):
    scale_rows = lax.rsqrt(jnp.mean(hidden * hidden, axis=-1, keepdims=True) + norm_eps)
    return (hidden * scale_rows * norm_gain).astype(jnp.bfloat16)


def unit_shares(normed_all, router_weight, expert_ids, tp_rank, units_dev):
    logits = jnp.dot(normed_all, router_weight, preferred_element_type=jnp.float32)
    expert_range = jnp.arange(router_weight.shape[1], dtype=jnp.int32)
    onehot = (expert_ids[:, :, None] == expert_range[None, None, :]).astype(jnp.float32)
    chosen = jnp.sum(logits[:, None, :] * onehot, axis=-1)
    expo_chosen = jnp.exp(chosen)
    expert_probs = expo_chosen / jnp.sum(expo_chosen, axis=-1, keepdims=True)
    routing = jnp.sum(expert_probs[:, :, None] * onehot, axis=1)
    unit_ids = tp_rank * units_dev + jnp.arange(units_dev, dtype=jnp.int32)
    expert_of_unit = unit_ids // (FF_E // UNIT)
    pick = (expert_range[:, None] == expert_of_unit[None, :]).astype(jnp.float32)
    return jnp.dot(routing, pick, precision=lax.Precision.HIGHEST)


def per_device_plain(
    queries,
    new_kv,
    residual,
    placement,
    lengths,
    page_table,
    cache_keys,
    cache_values,
    parents,
    accept_leaf,
    out_weight,
    norm_gain,
    router_weight,
    expert_ids,
    gate_up,
    down_weight,
):
    tok_dev = queries.shape[0]
    tp_count = lax.axis_size("tp")
    tp_rank = lax.axis_index("tp")
    group_rows = tok_dev * tp_count
    slot_count = placement.shape[0]
    kv_width = cache_keys.shape[2]
    page_len = cache_keys.shape[1]
    group_size = HEADS // KV_HEADS
    score_scale = 1.0 / math.sqrt(HEAD)
    row_start = tp_rank * tok_dev
    pulled_q, pulled_kv, pulled_res = (
        lax.all_gather(queries, "req", axis=0, tiled=True),
        lax.all_gather(new_kv, "req", axis=0, tiled=True),
        lax.all_gather(residual, "req", axis=0, tiled=True),
    )
    row_offsets = jnp.arange(tok_dev, dtype=jnp.int32)
    row_pos = row_start + row_offsets
    row_slot = row_pos // DRAFT
    slot_match = row_slot[:, None] == jnp.arange(slot_count, dtype=jnp.int32)[None, :]
    source_group = jnp.sum(jnp.where(slot_match, placement[None, :] // slot_count, 0), axis=1)
    source_rows = source_group * tok_dev + row_offsets
    own_q = jnp.take(pulled_q, source_rows, axis=0)
    own_kv = jnp.take(pulled_kv, source_rows, axis=0)
    own_res = jnp.take(pulled_res, source_rows, axis=0)
    all_q, all_kv = (
        lax.all_gather(own_q, "tp", axis=0, tiled=True),
        lax.all_gather(own_kv, "tp", axis=0, tiled=True),
    )
    local_pages = page_table.shape[1]
    page_ids = page_table[:, :, 0].reshape(-1)
    keys_local = jnp.take(cache_keys, page_ids, axis=0).reshape(
        slot_count, local_pages, page_len, KV_HEADS, HEAD
    )
    values_local = jnp.take(cache_values, page_ids, axis=0).reshape(
        slot_count, local_pages, page_len, KV_HEADS, HEAD
    )
    query_blocks = all_q.reshape(slot_count, DRAFT, KV_HEADS, group_size, HEAD)
    scores = (
        jnp.einsum(
            "sqgrd,sltgd->sqgrlt", query_blocks, keys_local, preferred_element_type=jnp.float32
        )
        * score_scale
    )
    positions = (
        jnp.arange(local_pages, dtype=jnp.int32)[:, None] * tp_count + tp_rank
    ) * page_len + jnp.arange(page_len, dtype=jnp.int32)[None, :]
    is_valid = (positions[None] < lengths[:, None, None])[:, None, None, None]
    scores = jnp.where(is_valid, scores, neg_big)
    block_max = jnp.max(scores, axis=-1)
    weights = jnp.where(is_valid, jnp.exp(scores - block_max[..., None]), 0.0).astype(jnp.bfloat16)
    block_sum = jnp.sum(weights.astype(jnp.float32), axis=-1)
    block_out = jnp.einsum(
        "sqgrlt,sltgd->sqgrld", weights, values_local, preferred_element_type=jnp.float32
    )
    page_top = jnp.max(block_max, axis=-1)
    page_scale = jnp.exp(block_max - page_top[..., None])
    stat_max = page_top.reshape(group_rows, HEADS)
    stat_sum = jnp.sum(block_sum * page_scale, axis=-1).reshape(group_rows, HEADS)
    stat_out = jnp.sum(block_out * page_scale[..., None], axis=-2).reshape(group_rows, HEADS * HEAD)
    reached = ancestry(parents)
    reach_rows = jnp.take(reached.reshape(slot_count * DRAFT, DRAFT), row_pos, axis=0)
    key_slot = jnp.arange(group_rows, dtype=jnp.int32) // DRAFT
    same_slot = key_slot[None, :] == row_slot[:, None]
    allowed = same_slot & (jnp.tile(reach_rows, (1, slot_count)) > 0.5)
    tree_keys = all_kv[:, :kv_width].reshape(group_rows, KV_HEADS, HEAD)
    tree_values = all_kv[:, kv_width:].reshape(group_rows, KV_HEADS, HEAD)
    own_blocks = own_q.reshape(tok_dev, KV_HEADS, group_size, HEAD)
    tree_scores = (
        jnp.einsum("igrd,kgd->igrk", own_blocks, tree_keys, preferred_element_type=jnp.float32)
        * score_scale
    )
    tree_mask = allowed[:, None, None, :]
    tree_scores = jnp.where(tree_mask, tree_scores, neg_big)
    tree_max = jnp.max(tree_scores, axis=-1)
    tree_weights = jnp.where(tree_mask, jnp.exp(tree_scores - tree_max[..., None]), 0.0).astype(
        jnp.bfloat16
    )
    tree_sum = jnp.sum(tree_weights.astype(jnp.float32), axis=-1)
    tree_out = jnp.einsum(
        "igrk,kgd->igrd", tree_weights, tree_values, preferred_element_type=jnp.float32
    )
    own_stats = (
        lax.dynamic_slice_in_dim(stat_max, row_start, tok_dev, 0),
        lax.dynamic_slice_in_dim(stat_sum, row_start, tok_dev, 0),
        lax.dynamic_slice_in_dim(stat_out, row_start, tok_dev, 0),
    )
    tree_stats = (
        tree_max.reshape(tok_dev, HEADS),
        tree_sum.reshape(tok_dev, HEADS),
        tree_out.reshape(tok_dev, HEADS * HEAD),
    )
    joined = combine_stats(own_stats, tree_stats)
    stat_max = lax.dynamic_update_slice_in_dim(stat_max, joined[0], row_start, 0)
    stat_sum = lax.dynamic_update_slice_in_dim(stat_sum, joined[1], row_start, 0)
    stat_out = lax.dynamic_update_slice_in_dim(stat_out, joined[2], row_start, 0)
    normed_all = None
    merged = joined_2((stat_max, stat_sum, stat_out), "tp", combine_stats)
    attn_own = finish_rows(
        lax.dynamic_slice_in_dim(merged[1], row_start, tok_dev, 0),
        lax.dynamic_slice_in_dim(merged[2], row_start, tok_dev, 0),
    )
    hidden_own = project_rows(attn_own, own_res, out_weight)
    normed_own = rms_normed(hidden_own, norm_gain)
    units_dev = gate_up.shape[0]
    unit_width = gate_up.shape[2] // 2
    normed_all = lax.all_gather(normed_own, "tp", axis=0, tiled=True)
    shares = unit_shares(normed_all, router_weight, expert_ids, tp_rank, units_dev)
    gate_both = jnp.einsum("td,udh->tuh", normed_all, gate_up, preferred_element_type=jnp.float32)
    activated = (
        jax.nn.silu(gate_both[..., :unit_width]) * gate_both[..., unit_width:] * shares[:, :, None]
    ).astype(jnp.bfloat16)
    moe_own = lax.psum_scatter(
        jnp.einsum("tuh,uhd->td", activated, down_weight, preferred_element_type=jnp.float32),
        "tp",
        scatter_dimension=0,
        tiled=True,
    )
    layer_out = (hidden_own + moe_own).astype(jnp.bfloat16)
    node_ids = jnp.arange(DRAFT, dtype=jnp.int32)
    leaf_pick = (accept_leaf[:, None] == node_ids[None, :]).astype(jnp.float32)
    path_weight = jnp.einsum("sn,snk->sk", leaf_pick, reached, precision=lax.Precision.HIGHEST)
    path_flags = (path_weight > 0.5).astype(jnp.int32)
    path_rank = jnp.cumsum(path_flags, axis=1) - 1
    chosen_node = (path_flags[:, None, :] > 0) & (path_rank[:, None, :] == node_ids[None, :, None])
    own_choice = jnp.take(chosen_node.reshape(slot_count * DRAFT, DRAFT), row_pos, axis=0)
    spread = same_slot & jnp.tile(own_choice, (1, slot_count))
    accepted = jnp.dot(
        spread.astype(jnp.bfloat16), all_kv, preferred_element_type=jnp.float32
    ).astype(jnp.bfloat16)
    return (attn_own, layer_out, accepted)


def start_all(copies):
    for copy in copies:
        copy.start()
    for copy in copies:
        copy.wait()


def split_kernel(pairs, *refs):
    (
        pages_hbm, placement_hbm, lengths_hbm, leaf_hbm, keys_hbm, values_hbm, queries_hbm,
        new_kv_hbm, residual_hbm, parents_hbm, router_hbm, ids_hbm, gain_hbm,
    ) = refs[:13]
    parts, refs = refs[13 : 13 + pairs], refs[13 + pairs :]
    joined_ref, table_ref, parents_ref, router_ref, ids_ref, gain_ref = refs[:6]
    pages_ref, placement_ref, lengths_ref, leaf_ref, keys_ref, values_ref, split_ref, sems = refs[6:]
    slot_count = pages_ref.shape[0]
    page_len = keys_ref.shape[1]
    tok_dev = joined_ref.shape[0]
    moves = [
        (pages_hbm, pages_ref),
        (keys_hbm, keys_ref),
        (values_hbm, values_ref),
        (placement_hbm, placement_ref),
        (lengths_hbm, lengths_ref),
        (leaf_hbm, leaf_ref),
        (parents_hbm, parents_ref),
        (router_hbm, router_ref),
        (ids_hbm, ids_ref),
        (gain_hbm, gain_ref),
    ]
    column = 0
    for source in (queries_hbm, new_kv_hbm, residual_hbm):
        moves.append((source, joined_ref.at[:, column : column + source.shape[1]]))
        column += source.shape[1]
    start_all(
        [pltpu.make_async_copy(a, b, sems.at[k]) for k, (a, b) in enumerate(moves)]
    )
    slot = lax.div(lax.axis_index("tp") * tok_dev, DRAFT)
    numbers = [lax.div(placement_ref[slot], slot_count)]
    numbers += [lengths_ref[s] for s in range(slot_count)]
    numbers += [leaf_ref[s] for s in range(slot_count)]
    for row, number in enumerate(numbers):
        table_ref[row : row + 1, :] = jnp.full((1, WIDE), number, jnp.int32).astype(jnp.float32)
    for head in range(KV_HEADS):
        low = head * HEAD
        for s in range(slot_count):
            page = pages_ref[s]
            split_ref[head // 2, head % 2, s * page_len : (s + 1) * page_len, :] = jnp.concatenate(
                [keys_ref[page, :, low : low + HEAD], values_ref[page, :, low : low + HEAD]], axis=1
            )
    pair = lax.div(lax.axis_index("tp"), 2)
    for k, part in enumerate(parts):
        part[...] = split_ref[lax.bitwise_xor(pair, pairs - 1 - k)]


def number(table_ref, row):
    return jnp.max(table_ref[row : row + 1, :]).astype(jnp.int32)


def route_kernel(kv_width, after_ref, table_ref, pulled_ref, *refs):
    del after_ref
    parts, (sent_ref, res_ref, turned_ref) = refs[:-3], refs[-3:]
    rank = lax.axis_index("tp")
    other = 1 - lax.rem(rank, 2)
    for k, part in enumerate(parts):
        turned_ref[k] = part[other]
    q_width = HEADS * HEAD
    tok_dev = pulled_ref.shape[1]
    rows = pulled_ref[number(table_ref, 0)]
    res_ref[...] = rows[:, q_width + 2 * kv_width :]
    head_rows = (HEADS // KV_HEADS) * HEAD
    tail = jnp.zeros((tok_dev, 2 * WIDE - head_rows), rows.dtype)
    for head in range(KV_HEADS):
        q_low = head * head_rows
        pair = jnp.concatenate([rows[:, q_low : q_low + head_rows], tail], axis=1)
        sent_ref[head, :tok_dev, :] = pair[:, :WIDE]
        sent_ref[head, tok_dev : 2 * tok_dev, :] = pair[:, WIDE:]
        k_low = q_width + head * HEAD
        sent_ref[head, 2 * tok_dev :, :] = jnp.concatenate(
            [rows[:, k_low : k_low + HEAD], rows[:, k_low + kv_width : k_low + kv_width + HEAD]],
            axis=1,
        )


def ancestor_rows(parents_ref):
    slot_count = parents_ref.shape[0]
    total = slot_count * DRAFT
    row = jnp.concatenate(
        [parents_ref[s : s + 1, :] + s * DRAFT for s in range(slot_count)], axis=1
    )
    from_ids = lax.broadcasted_iota(jnp.int32, (total, total), 0)
    to_ids = lax.broadcasted_iota(jnp.int32, (total, total), 1)
    linked = (from_ids == jnp.broadcast_to(row, (total, total))) & (lax.rem(to_ids, DRAFT) > 0)
    reached = jnp.where(linked | (from_ids == to_ids), 1.0, 0.0)
    for _ in range((DRAFT - 1).bit_length()):
        half = reached.astype(jnp.bfloat16)
        reached = jnp.minimum(jnp.dot(half, half, preferred_element_type=jnp.float32), 1.0)
    return reached.T


def tree_kernel(
    after_ref, down_hbm, table_ref, parents_ref, down_ref, reach_ref, chosen_ref, sem
):
    del after_ref
    copy = pltpu.make_async_copy(down_hbm, down_ref, sem)
    copy.start()
    slot_count = parents_ref.shape[0]
    reach_ref[...] = ancestor_rows(parents_ref)
    node_from = lax.broadcasted_iota(jnp.int32, (DRAFT, DRAFT), 0)
    node_to = lax.broadcasted_iota(jnp.int32, (DRAFT, DRAFT), 1)
    upto = jnp.where(node_from <= node_to, 1.0, 0.0).astype(jnp.bfloat16)
    for s in range(slot_count):
        leaf = number(table_ref, 1 + slot_count + s)
        path = reach_ref[pl.ds(s * DRAFT + leaf, 1), s * DRAFT : (s + 1) * DRAFT]
        path = jnp.broadcast_to(path, (DRAFT, DRAFT))
        rank = jnp.dot(path.astype(jnp.bfloat16), upto, preferred_element_type=jnp.float32)
        chosen = (path > 0.5) & (rank == (node_from + 1).astype(jnp.float32))
        chosen_ref[s] = jnp.where(chosen, 1.0, 0.0).astype(jnp.bfloat16)
    copy.wait()


def attend_kernel(units_ref, table_ref, reach_ref, chosen_ref, got_ref, res_ref, turned_ref, *refs):
    del units_ref
    parts, (sent_ref, picked_ref) = refs[:-2], refs[-2:]
    slot_count = chosen_ref.shape[0]
    sources = got_ref.shape[0]
    tok_dev = res_ref.shape[0]
    page_len = turned_ref.shape[1] // slot_count
    per_slot = DRAFT // tok_dev
    group_size = HEADS // KV_HEADS
    f32, bf16 = jnp.float32, jnp.bfloat16
    lane_low = lax.broadcasted_iota(jnp.int32, (DRAFT, WIDE), 1) < HEAD
    rank = lax.axis_index("tp")
    side = lax.rem(rank, 2)
    within = lax.broadcasted_iota(jnp.int32, (1, page_len), 1)
    positions = []
    for k in range(len(parts)):
        pair = lax.bitwise_xor(lax.div(rank, 2), k)
        for page in (2 * pair + side, 2 * pair + 1 - side):
            positions.append(within + page * page_len)
    positions = jnp.concatenate(positions, axis=1)
    dims = (((1,), (1,)), ((), ()))
    scale = 1.0 / math.sqrt(HEAD)
    outs, picked = [], []
    for s in range(slot_count):
        first = s * per_slot

        def part(k):
            low = k * tok_dev
            return jnp.concatenate(
                [got_ref[first + i, low : low + tok_dev, :] for i in range(per_slot)], axis=0
            )

        q_pair, q_last, tree_kv = part(0).astype(f32) * scale, part(1).astype(f32) * scale, part(2)
        q_rows = jnp.concatenate(
            [
                jnp.where(lane_low, q_pair, 0.0),
                jnp.where(lane_low, pltpu.roll(q_pair, HEAD, 1), 0.0),
                jnp.where(lane_low, q_last, 0.0),
            ],
            axis=0,
        ).astype(bf16)
        at = slice(s * page_len, (s + 1) * page_len)
        cache_kv = jnp.concatenate(
            [a for k, part in enumerate(parts) for a in (part[side, at, :], turned_ref[k, at, :])],
            axis=0,
        )
        scores = lax.dot_general(q_rows, cache_kv, dims, preferred_element_type=f32)
        is_valid = positions < number(table_ref, 1 + s)
        scores = jnp.where(is_valid, scores, neg_big)
        reach = reach_ref[s * DRAFT : (s + 1) * DRAFT, s * DRAFT : (s + 1) * DRAFT]
        allowed = jnp.concatenate([reach] * group_size, axis=0) > 0.5
        tree_scores = lax.dot_general(q_rows, tree_kv, dims, preferred_element_type=f32)
        tree_scores = jnp.where(allowed, tree_scores, neg_big)
        top = jnp.maximum(
            jnp.max(scores, axis=1, keepdims=True), jnp.max(tree_scores, axis=1, keepdims=True)
        )
        weights = jnp.where(is_valid, jnp.exp(scores - top), 0.0).astype(bf16)
        tree_weights = jnp.where(allowed, jnp.exp(tree_scores - top), 0.0).astype(bf16)
        total = jnp.sum(weights.astype(f32), axis=1, keepdims=True) + jnp.sum(
            tree_weights.astype(f32), axis=1, keepdims=True
        )
        mixed = jnp.dot(weights, cache_kv, preferred_element_type=f32) + jnp.dot(
            tree_weights, tree_kv, preferred_element_type=f32
        )
        outs.append(mixed / total)
        picked.append(
            jnp.dot(chosen_ref[s], tree_kv, preferred_element_type=f32).astype(bf16)
        )
    pair_rows, last_rows = [], []
    for out in outs:
        head_out = [out[r * DRAFT : (r + 1) * DRAFT] for r in range(group_size)]
        pair_rows.append(
            jnp.where(lane_low, pltpu.roll(head_out[0], HEAD, 1), head_out[1]).astype(bf16)
        )
        last_rows.append(head_out[2])
    last = jnp.where(lane_low, pltpu.roll(last_rows[0], HEAD, 1), last_rows[1]).astype(bf16)
    res_tiles = [res_ref[:, c * WIDE : (c + 1) * WIDE] for c in range(res_ref.shape[1] // WIDE)]
    sent_ref[...] = jnp.concatenate(pair_rows + [last] + res_tiles, axis=0)
    for target in range(sources):
        row = (target % per_slot) * tok_dev
        picked_ref[target] = picked[target // per_slot][row : row + tok_dev]


def fetch_kernel(spans, after_ref, *refs):
    del after_ref
    count = len(spans)
    sems = refs[-1]
    start_all(
        [
            pltpu.make_async_copy(refs[k].at[pl.ds(*spans[k])], refs[count + k], sems.at[k])
            for k in range(count)
        ]
    )


def expert_kernel(
    router_ref, ids_ref, gain_ref, down_ref, picked_ref, *refs
):
    blocks, refs = refs[:KV_HEADS], refs[KV_HEADS:]
    weight_refs, unit_refs, refs = refs[: KV_HEADS // 2 - 1], refs[KV_HEADS // 2 - 1 : -7], refs[-7:]
    far_ref, hid_ref, hidden_ref, attn_ref, x_ref, normed_ref, share_ref = refs
    f32, bf16 = jnp.float32, jnp.bfloat16
    unit_weights = [(ref, k) for ref in unit_refs for k in range(ref.shape[0])]
    units = len(unit_weights)
    tok_dev = hidden_ref.shape[0]
    sources = len(blocks)
    group_rows = sources * tok_dev
    half = group_rows // 2
    model = hidden_ref.shape[1]
    width = sum(ref.shape[0] for ref in weight_refs)
    rank = lax.axis_index("tp")
    lane_low = lax.broadcasted_iota(jnp.int32, (half, WIDE), 1) < HEAD
    head_rows = width // sources
    res_start = group_rows + half
    is_even = lax.rem(rank, 2) == 0
    for k in range(sources // 2):
        pair = lax.bitwise_xor(lax.div(rank, 2), k)
        mine, other = blocks[2 * k][...], blocks[2 * k + 1][...]
        even, odd = jnp.where(is_even, mine, other), jnp.where(is_even, other, mine)
        last_even = even[group_rows:res_start].astype(f32)
        last_odd = odd[group_rows:res_start].astype(f32)
        odd_swapped = pltpu.roll(odd[:group_rows].astype(f32), HEAD, 1)
        middle = jnp.concatenate(
            [
                jnp.where(lane_low, last_even, odd_swapped[:half]),
                jnp.where(lane_low, pltpu.roll(last_even, HEAD, 1), odd_swapped[half:]),
            ],
            axis=0,
        ).astype(bf16)
        end = jnp.concatenate(
            [
                jnp.where(lane_low, odd_swapped[:half], pltpu.roll(last_odd, HEAD, 1)),
                jnp.where(lane_low, odd_swapped[half:], last_odd),
            ],
            axis=0,
        ).astype(bf16)
        base = pl.multiple_of(pair * 2 * head_rows, WIDE)
        x_ref[:, pl.ds(base, 2 * head_rows)] = jnp.concatenate(
            [even[:group_rows], middle, end], axis=1
        )
        for q, block in enumerate((even, odd)):
            row = pl.multiple_of((2 * pair + q) * tok_dev, tok_dev)
            hid_ref[pl.ds(row, tok_dev), :] = jnp.concatenate(
                [
                    block[res_start + c * tok_dev : res_start + (c + 1) * tok_dev]
                    for c in range(model // WIDE)
                ],
                axis=1,
            ).astype(f32)
    own = pl.multiple_of(rank * tok_dev, tok_dev)
    attn_ref[...] = x_ref[pl.ds(own, tok_dev), :]
    hidden, at = hid_ref[...], 0
    for ref in weight_refs:
        hidden += jnp.dot(x_ref[:, at : at + ref.shape[0]], ref[...], preferred_element_type=f32)
        at += ref.shape[0]
    hid_ref[...] = hidden
    gain = jnp.concatenate([gain_ref[c : c + 1, :] for c in range(model // WIDE)], axis=1)
    scale = lax.rsqrt(jnp.mean(hidden * hidden, axis=1, keepdims=True) + norm_eps)
    normed_ref[...] = (hidden * scale * gain).astype(bf16)
    hidden_ref[...] = hid_ref[pl.ds(own, tok_dev), :]
    logits = lax.dot_general(
        normed_ref[...], router_ref[...], (((1,), (1,)), ((), ())), preferred_element_type=f32
    )
    experts = router_ref.shape[0]
    ids = ids_ref[...].astype(f32).T
    expert_range = lax.broadcasted_iota(jnp.int32, (group_rows, experts), 1)
    expert_names = expert_range.astype(f32)
    count = jnp.zeros((group_rows, experts), f32)
    for k in range(ids_ref.shape[0]):
        count = count + jnp.where(ids[:, k : k + 1] == expert_names, 1.0, 0.0)
    expo = jnp.where(count > 0.0, jnp.exp(logits), 0.0) * count
    routing = expo / jnp.sum(expo, axis=1, keepdims=True)
    unit_width = unit_refs[0].shape[2] // 2
    span = FF_E // unit_width
    each = span if units % span == 0 else 1
    for u in range(0, units, each):
        expert = (rank * units + u) // span
        share = jnp.sum(jnp.where(expert_range == expert, routing, 0.0), axis=1, keepdims=True)
        share_ref[u : u + each] = jnp.broadcast_to(share[None], (each, group_rows, unit_width))

    def one_unit(u):
        ref, k = unit_weights[u]
        both = jnp.dot(normed_ref[...], ref[k], preferred_element_type=f32)
        gate, up = both[:, :unit_width], both[:, unit_width:]
        return (gate / (1.0 + jnp.exp(-gate)) * up * share_ref[u]).astype(bf16)

    for i in range(units // STEP):
        act = jnp.concatenate([one_unit(i * STEP + k) for k in range(STEP)], axis=1)
        down = down_ref[i * STEP : (i + 1) * STEP].reshape(STEP * unit_width, model)
        part = jnp.dot(act, down, preferred_element_type=f32)
        hid_ref[...] = part if i == 0 else hid_ref[...] + part
    for k in range(far_ref.shape[0]):
        copy_sums(sources // 4 + k, True, hid_ref, picked_ref, far_ref.at[k])


def copy_sums(k, crossing, hid_ref, picked_ref, ref):
    tok_dev, model = ref.shape[0], hid_ref.shape[1]
    rank = lax.axis_index("tp")
    side = lax.rem(rank, 2)
    pair = lax.bitwise_xor(lax.div(rank, 2), k)
    target = 2 * pair + (1 - side if crossing else side)
    row = pl.multiple_of(target * tok_dev, tok_dev)
    ref[:, :model] = hid_ref[pl.ds(row, tok_dev), :].astype(ref.dtype)
    ref[:, model:] = picked_ref[target].astype(ref.dtype)


def near_kernel(hid_ref, picked_ref, mine_ref, near_ref):
    for k in range(mine_ref.shape[0]):
        copy_sums(k, False, hid_ref, picked_ref, mine_ref.at[k])
    for k in range(near_ref.shape[0]):
        copy_sums(k, True, hid_ref, picked_ref, near_ref.at[k])


def fold_kernel(first, after_ref, mine_ref, got_ref, hidden_ref, *sent_refs):
    del after_ref
    model = hidden_ref.shape[1]
    is_even = lax.rem(lax.axis_index("tp"), 2) == 0
    for k, ref in enumerate(sent_refs, first):
        mine, got = mine_ref[k], got_ref[k - first].astype(jnp.float32)
        total = mine[:, :model] + got[:, :model]
        if k == 0:
            total = total + hidden_ref[...]
        ref[:, :model] = total.astype(ref.dtype)
        low, high = mine[:, model:], got[:, model:]
        even, odd = jnp.where(is_even, low, high), jnp.where(is_even, high, low)
        ref[:, model:] = jnp.concatenate([even, odd], axis=1).astype(ref.dtype)


def finish_kernel(attn_in_ref, *refs):
    parts, (attn_ref, layer_ref, accepted_ref) = refs[:-3], refs[-3:]
    attn_ref[...] = attn_in_ref[...]
    f32, bf16 = jnp.float32, jnp.bfloat16
    tok_dev, model = layer_ref.shape
    kv_width = accepted_ref.shape[1] // 2
    total = parts[0][:, :model]
    for part in parts[1:]:
        total = total + part[:, :model].astype(f32)
    layer_ref[...] = total.astype(bf16)
    low = lax.broadcasted_iota(jnp.int32, (tok_dev, WIDE), 1) < HEAD
    for k, part in enumerate(parts):
        pair = lax.bitwise_xor(lax.div(lax.axis_index("tp"), 2), k)
        even = part[:, model : model + WIDE].astype(f32)
        odd = part[:, model + WIDE :].astype(f32)
        at = pl.multiple_of(pair * WIDE, WIDE)
        accepted_ref[:, pl.ds(at, WIDE)] = jnp.where(low, even, pltpu.roll(odd, HEAD, 1)).astype(bf16)
        accepted_ref[:, pl.ds(kv_width + at, WIDE)] = jnp.where(
            low, pltpu.roll(even, HEAD, 1), odd
        ).astype(bf16)


def in_hbm(*arrays):
    return tuple(pltpu.with_memory_space_constraint(a, pltpu.HBM) for a in arrays)


def spaces(text):
    kinds = {"a": pl.ANY, "v": pltpu.VMEM}
    return [pl.BlockSpec(memory_space=kinds[c]) for c in text]


def params(mebibytes=12):
    return pltpu.CompilerParams(vmem_limit_bytes=mebibytes << 20)


def cost(mebibytes):
    return pl.CostEstimate(flops=0, transcendentals=0, bytes_accessed=mebibytes << 20)


def swap(rows, mask):
    count = lax.axis_size("tp")
    return lax.ppermute(rows, "tp", [(i, i ^ mask) for i in range(count)])


def fetch(name, after, *spans):
    shapes = [(rows,) + array.shape[1:] for array, _, rows in spans]
    return pl.pallas_call(
        functools.partial(fetch_kernel, tuple((first, rows) for _, first, rows in spans)),
        out_shape=tuple(pltpu.VMEM(shape, jnp.bfloat16) for shape in shapes),
        in_specs=spaces("a" * (1 + len(spans))),
        out_specs=tuple(spaces("v" * len(spans))),
        scratch_shapes=[pltpu.SemaphoreType.DMA((len(spans),))],
        compiler_params=params(),
        cost_estimate=cost(sum(2 * math.prod(shape) for shape in shapes) >> 20),
        name="fetch_" + name,
    )(after, *in_hbm(*[array for array, _, _ in spans]))


def per_device_packed(
    queries,
    new_kv,
    residual,
    placement,
    lengths,
    page_table,
    cache_keys,
    cache_values,
    parents,
    accept_leaf,
    out_weight,
    norm_gain,
    router_weight,
    expert_ids,
    gate_up,
    down_weight,
):
    f32, bf16 = jnp.float32, jnp.bfloat16
    tok_dev, model = residual.shape
    tp_count = lax.axis_size("tp")
    slot_count = placement.shape[0]
    page_len, kv_width = cache_keys.shape[1:]
    group_rows = tok_dev * tp_count
    sent = lambda rows: jax.ShapeDtypeStruct((tp_count, rows, WIDE), bf16)
    dma = pltpu.SemaphoreType.DMA
    slots_smem = pltpu.SMEM((slot_count,), jnp.int32)
    pairs = tp_count // 2
    part = jax.ShapeDtypeStruct((2, slot_count * page_len, WIDE), bf16)
    loaded = (
        page_table.reshape(slot_count),
        placement,
        lengths,
        accept_leaf,
        cache_keys,
        cache_values,
        queries,
        new_kv,
        residual,
        parents,
        router_weight.T,
        expert_ids.T,
        norm_gain.reshape(model // WIDE, WIDE),
    )
    *parts, joined, table, parents, router, ids, gain = pl.pallas_call(
        functools.partial(split_kernel, pairs),
        out_shape=(part,) * pairs
        + (
            jax.ShapeDtypeStruct((tok_dev, 2 * (model + kv_width)), bf16),
            pltpu.VMEM((8, WIDE), f32),
        )
        + tuple(pltpu.VMEM(a.shape, a.dtype) for a in loaded[9:]),
        in_specs=spaces("a" * len(loaded)),
        out_specs=tuple(spaces("v" * (pairs + 6))),
        scratch_shapes=[
            slots_smem,
            slots_smem,
            slots_smem,
            slots_smem,
            pltpu.VMEM(cache_keys.shape, bf16),
            pltpu.VMEM(cache_values.shape, bf16),
            pltpu.VMEM((pairs,) + part.shape, bf16),
            dma((len(loaded),)),
        ],
        compiler_params=params(),
        cost_estimate=cost(4),
        name="split",
    )(*in_hbm(*loaded))
    parts = parts[::-1]
    parts = [parts[0]] + [swap(parts[k], 2 * k) for k in range(1, pairs)]
    pulled = lax.all_gather(joined, "req", axis=0)
    nodes = slot_count * DRAFT
    down_weight, reach, chosen = pl.pallas_call(
        tree_kernel,
        out_shape=(
            pltpu.VMEM(down_weight.shape, bf16),
            jax.ShapeDtypeStruct((nodes, nodes), f32),
            jax.ShapeDtypeStruct((slot_count, DRAFT, DRAFT), bf16),
        ),
        in_specs=spaces("aavv"),
        out_specs=tuple(spaces("vvv")),
        scratch_shapes=[dma],
        compiler_params=params(),
        cost_estimate=cost(8),
        name="tree",
    )(pulled, *in_hbm(down_weight), table, parents)
    packed, own_res, turned = pl.pallas_call(
        functools.partial(route_kernel, kv_width),
        out_shape=(
            sent(3 * tok_dev),
            jax.ShapeDtypeStruct(residual.shape, bf16),
            jax.ShapeDtypeStruct((pairs,) + part.shape[1:], bf16),
        ),
        in_specs=spaces("avv" + "v" * pairs),
        out_specs=tuple(spaces("vvv")),
        compiler_params=params(),
        cost_estimate=cost(4),
        name="route",
    )(down_weight, table, pulled, *parts)
    turned = swap(turned, 1)
    packed = lax.all_to_all(packed, "tp", 0, 0, tiled=True)
    gate_up = pltpu.with_memory_space_constraint(gate_up, pltpu.VMEM)
    block, picked = pl.pallas_call(
        attend_kernel,
        out_shape=(
            jax.ShapeDtypeStruct(
                (group_rows + group_rows // 2 + (model // WIDE) * tok_dev, WIDE), bf16
            ),
            sent(tok_dev),
        ),
        in_specs=spaces("v" * (7 + pairs)),
        out_specs=tuple(spaces("vv")),
        compiler_params=params(),
        cost_estimate=cost(8),
        name="attend",
    )(gate_up, table, reach, chosen, packed, own_res, turned, *parts)
    units = gate_up.shape[0]
    reached = [swap(block, 2 * k) for k in range(1, pairs)]
    weights, after = [], block
    rows = out_weight.shape[0] // (pairs - 1)
    for step, k in enumerate(ORDER):
        (weight,) = fetch("dense", after, (out_weight, step * rows, rows))
        reached[k - 1], weight = lax.optimization_barrier((reached[k - 1], weight))
        after = reached[k - 1]
        weights.append(weight)
    blocks = [a for rows in [block] + reached for a in (rows, swap(rows, 1))]
    unit_weights = (gate_up,)
    far, sums, hidden, attn_own = pl.pallas_call(
        expert_kernel,
        out_shape=(
            jax.ShapeDtypeStruct((pairs // 2, tok_dev, model + WIDE), bf16),
            jax.ShapeDtypeStruct((group_rows, model), f32),
            jax.ShapeDtypeStruct((tok_dev, model), f32),
            pltpu.VMEM(queries.shape, bf16),
        ),
        in_specs=spaces("v" * (5 + len(weights) + len(unit_weights) + tp_count)),
        out_specs=tuple(spaces("vvvv")),
        scratch_shapes=[
            pltpu.VMEM((group_rows, HEADS * HEAD), bf16),
            pltpu.VMEM((group_rows, model), bf16),
            pltpu.VMEM((units, group_rows, gate_up.shape[2] // 2), f32),
        ],
        compiler_params=params(),
        name="experts",
    )(
        router,
        ids,
        gain,
        down_weight,
        picked,
        *blocks,
        *weights,
        *unit_weights,
    )
    far = swap(far, 1)
    mine, near = pl.pallas_call(
        near_kernel,
        out_shape=(
            jax.ShapeDtypeStruct((pairs, tok_dev, model + WIDE), f32),
            jax.ShapeDtypeStruct((pairs // 2, tok_dev, model + WIDE), bf16),
        ),
        in_specs=spaces("vv"),
        out_specs=tuple(spaces("vv")),
        compiler_params=params(),
        cost_estimate=cost(4),
        name="near",
    )(sums, picked)
    near = swap(near, 1)
    fold = lambda first, after, got: pl.pallas_call(
        functools.partial(fold_kernel, first),
        out_shape=tuple(
            jax.ShapeDtypeStruct((tok_dev, model + 2 * WIDE), f32 if k == 0 else bf16)
            for k in range(first, first + pairs // 2)
        ),
        in_specs=spaces("avvv"),
        out_specs=tuple(spaces("v" * (pairs // 2))),
        compiler_params=params(),
        cost_estimate=cost(1),
        name="fold",
    )(after, mine, got, hidden)
    sums = fold(pairs // 2, hidden, far)
    folded = sums[0]
    sums = [swap(a, 2 * k) for k, a in enumerate(sums, pairs // 2)]
    close = fold(0, folded, near)
    sums = [close[0]] + [swap(close[k], 2 * k) for k in range(1, pairs // 2)] + sums
    return pl.pallas_call(
        finish_kernel,
        out_shape=(
            jax.ShapeDtypeStruct(queries.shape, bf16),
            jax.ShapeDtypeStruct(residual.shape, bf16),
            jax.ShapeDtypeStruct(new_kv.shape, bf16),
        ),
        in_specs=spaces("v" * (1 + pairs)),
        out_specs=tuple(spaces("vvv")),
        compiler_params=params(),
        name="finish",
    )(attn_own, *sums)


def per_device(queries, new_kv, residual, placement, *rest):
    tok_dev = queries.shape[0]
    one_head_each = lax.axis_size("tp") == KV_HEADS
    whole_tiles = tok_dev % 16 == 0 and placement.shape[0] == 2 and tok_dev * KV_HEADS == 2 * DRAFT
    if one_head_each and whole_tiles and rest[1].shape[1] == 1:
        return per_device_packed(queries, new_kv, residual, placement, *rest)
    return per_device_plain(queries, new_kv, residual, placement, *rest)


def solution(mesh):
    in_specs = (
        P(("req", "tp"), None),
        P(("req", "tp"), None),
        P(("req", "tp"), None),
        P("req"),
        P("req"),
        P("req", None, "tp"),
        P(("req", "tp"), None, None),
        P(("req", "tp"), None, None),
        P("req", None),
        P("req"),
        P(),
        P(),
        P(),
        P("req", None),
        P("tp", None, None),
        P("tp", None, None),
    )
    out_specs = (P(("req", "tp"), None), P(("req", "tp"), None), P(("req", "tp"), None))
    return jax.shard_map(
        per_device, mesh=mesh, in_specs=in_specs, out_specs=out_specs, check_vma=False
    )
```

```python
import functools
import math

import jax
import jax.numpy as jnp
from jax import lax
from jax.experimental import pallas as pl
from jax.experimental.pallas import tpu as pltpu
from jax.sharding import PartitionSpec as P

HEADS = 24
KV_HEADS = 8
HEAD = 64
FF_E = 512
UNIT = 128
DRAFT = 64
WIDE = 128
STEP = 2
ORDER = (1, 3, 2)
FETCHES = ((0, 1), (3,), (2,))


neg_big = -1e30
norm_eps = 1e-06


def joined_2(part, axis, combine):
    gathered = jax.tree.map(lambda a: lax.all_gather(a, axis), part)

    def take(source):
        return jax.tree.map(lambda a: lax.dynamic_index_in_dim(a, source, 0, False), gathered)

    return lax.fori_loop(
        1, lax.axis_size(axis), lambda source, state: combine(state, take(source)), take(0)
    )


def ancestry(parents):
    node_count = parents.shape[-1]
    node_ids = jnp.arange(node_count, dtype=jnp.int32)
    linked = (parents[:, :, None] == node_ids[None, None, :]) & (node_ids[None, :, None] > 0)
    reached = jnp.maximum(linked.astype(jnp.float32), jnp.eye(node_count, dtype=jnp.float32)[None])
    for _ in range(node_count.bit_length()):
        reached = jnp.minimum(
            jnp.einsum("rnm,rmk->rnk", reached, reached, precision=lax.Precision.HIGHEST), 1.0
        )
    return reached


def combine_stats(left_stats, right_stats):
    left_max, left_sum, left_out = left_stats
    right_max, right_sum, right_out = right_stats
    top_score = jnp.maximum(left_max, right_max)
    left_scale = jnp.exp(left_max - top_score)
    right_scale = jnp.exp(right_max - top_score)
    row_count, head_count = left_max.shape
    out_sum = (
        left_out.reshape(row_count, head_count, -1) * left_scale[..., None]
        + right_out.reshape(row_count, head_count, -1) * right_scale[..., None]
    )
    return (
        top_score,
        left_sum * left_scale + right_sum * right_scale,
        out_sum.reshape(row_count, -1),
    )


def finish_rows(stat_sum, stat_out):
    row_count, head_count = stat_sum.shape
    return (
        (stat_out.reshape(row_count, head_count, -1) / stat_sum[..., None])
        .reshape(row_count, -1)
        .astype(jnp.bfloat16)
    )


def project_rows(attn_rows, res_rows, out_weight):
    return res_rows.astype(jnp.float32) + jnp.dot(
        attn_rows, out_weight, preferred_element_type=jnp.float32
    )


def rms_normed(hidden, norm_gain):
    scale_rows = lax.rsqrt(jnp.mean(hidden * hidden, axis=-1, keepdims=True) + norm_eps)
    return (hidden * scale_rows * norm_gain).astype(jnp.bfloat16)


def unit_shares(normed_all, router_weight, expert_ids, tp_rank, units_dev):
    logits = jnp.dot(normed_all, router_weight, preferred_element_type=jnp.float32)
    expert_range = jnp.arange(router_weight.shape[1], dtype=jnp.int32)
    onehot = (expert_ids[:, :, None] == expert_range[None, None, :]).astype(jnp.float32)
    chosen = jnp.sum(logits[:, None, :] * onehot, axis=-1)
    expo_chosen = jnp.exp(chosen)
    expert_probs = expo_chosen / jnp.sum(expo_chosen, axis=-1, keepdims=True)
    routing = jnp.sum(expert_probs[:, :, None] * onehot, axis=1)
    unit_ids = tp_rank * units_dev + jnp.arange(units_dev, dtype=jnp.int32)
    expert_of_unit = unit_ids // (FF_E // UNIT)
    pick = (expert_range[:, None] == expert_of_unit[None, :]).astype(jnp.float32)
    return jnp.dot(routing, pick, precision=lax.Precision.HIGHEST)


def per_device_plain(
    queries,
    new_kv,
    residual,
    placement,
    lengths,
    page_table,
    cache_keys,
    cache_values,
    parents,
    accept_leaf,
    out_weight,
    norm_gain,
    router_weight,
    expert_ids,
    gate_up,
    down_weight,
):
    tok_dev = queries.shape[0]
    tp_count = lax.axis_size("tp")
    tp_rank = lax.axis_index("tp")
    group_rows = tok_dev * tp_count
    slot_count = placement.shape[0]
    kv_width = cache_keys.shape[2]
    page_len = cache_keys.shape[1]
    group_size = HEADS // KV_HEADS
    score_scale = 1.0 / math.sqrt(HEAD)
    row_start = tp_rank * tok_dev
    pulled_q, pulled_kv, pulled_res = (
        lax.all_gather(queries, "req", axis=0, tiled=True),
        lax.all_gather(new_kv, "req", axis=0, tiled=True),
        lax.all_gather(residual, "req", axis=0, tiled=True),
    )
    row_offsets = jnp.arange(tok_dev, dtype=jnp.int32)
    row_pos = row_start + row_offsets
    row_slot = row_pos // DRAFT
    slot_match = row_slot[:, None] == jnp.arange(slot_count, dtype=jnp.int32)[None, :]
    source_group = jnp.sum(jnp.where(slot_match, placement[None, :] // slot_count, 0), axis=1)
    source_rows = source_group * tok_dev + row_offsets
    own_q = jnp.take(pulled_q, source_rows, axis=0)
    own_kv = jnp.take(pulled_kv, source_rows, axis=0)
    own_res = jnp.take(pulled_res, source_rows, axis=0)
    all_q, all_kv = (
        lax.all_gather(own_q, "tp", axis=0, tiled=True),
        lax.all_gather(own_kv, "tp", axis=0, tiled=True),
    )
    local_pages = page_table.shape[1]
    page_ids = page_table[:, :, 0].reshape(-1)
    keys_local = jnp.take(cache_keys, page_ids, axis=0).reshape(
        slot_count, local_pages, page_len, KV_HEADS, HEAD
    )
    values_local = jnp.take(cache_values, page_ids, axis=0).reshape(
        slot_count, local_pages, page_len, KV_HEADS, HEAD
    )
    query_blocks = all_q.reshape(slot_count, DRAFT, KV_HEADS, group_size, HEAD)
    scores = (
        jnp.einsum(
            "sqgrd,sltgd->sqgrlt", query_blocks, keys_local, preferred_element_type=jnp.float32
        )
        * score_scale
    )
    positions = (
        jnp.arange(local_pages, dtype=jnp.int32)[:, None] * tp_count + tp_rank
    ) * page_len + jnp.arange(page_len, dtype=jnp.int32)[None, :]
    is_valid = (positions[None] < lengths[:, None, None])[:, None, None, None]
    scores = jnp.where(is_valid, scores, neg_big)
    block_max = jnp.max(scores, axis=-1)
    weights = jnp.where(is_valid, jnp.exp(scores - block_max[..., None]), 0.0).astype(jnp.bfloat16)
    block_sum = jnp.sum(weights.astype(jnp.float32), axis=-1)
    block_out = jnp.einsum(
        "sqgrlt,sltgd->sqgrld", weights, values_local, preferred_element_type=jnp.float32
    )
    page_top = jnp.max(block_max, axis=-1)
    page_scale = jnp.exp(block_max - page_top[..., None])
    stat_max = page_top.reshape(group_rows, HEADS)
    stat_sum = jnp.sum(block_sum * page_scale, axis=-1).reshape(group_rows, HEADS)
    stat_out = jnp.sum(block_out * page_scale[..., None], axis=-2).reshape(group_rows, HEADS * HEAD)
    reached = ancestry(parents)
    reach_rows = jnp.take(reached.reshape(slot_count * DRAFT, DRAFT), row_pos, axis=0)
    key_slot = jnp.arange(group_rows, dtype=jnp.int32) // DRAFT
    same_slot = key_slot[None, :] == row_slot[:, None]
    allowed = same_slot & (jnp.tile(reach_rows, (1, slot_count)) > 0.5)
    tree_keys = all_kv[:, :kv_width].reshape(group_rows, KV_HEADS, HEAD)
    tree_values = all_kv[:, kv_width:].reshape(group_rows, KV_HEADS, HEAD)
    own_blocks = own_q.reshape(tok_dev, KV_HEADS, group_size, HEAD)
    tree_scores = (
        jnp.einsum("igrd,kgd->igrk", own_blocks, tree_keys, preferred_element_type=jnp.float32)
        * score_scale
    )
    tree_mask = allowed[:, None, None, :]
    tree_scores = jnp.where(tree_mask, tree_scores, neg_big)
    tree_max = jnp.max(tree_scores, axis=-1)
    tree_weights = jnp.where(tree_mask, jnp.exp(tree_scores - tree_max[..., None]), 0.0).astype(
        jnp.bfloat16
    )
    tree_sum = jnp.sum(tree_weights.astype(jnp.float32), axis=-1)
    tree_out = jnp.einsum(
        "igrk,kgd->igrd", tree_weights, tree_values, preferred_element_type=jnp.float32
    )
    own_stats = (
        lax.dynamic_slice_in_dim(stat_max, row_start, tok_dev, 0),
        lax.dynamic_slice_in_dim(stat_sum, row_start, tok_dev, 0),
        lax.dynamic_slice_in_dim(stat_out, row_start, tok_dev, 0),
    )
    tree_stats = (
        tree_max.reshape(tok_dev, HEADS),
        tree_sum.reshape(tok_dev, HEADS),
        tree_out.reshape(tok_dev, HEADS * HEAD),
    )
    joined = combine_stats(own_stats, tree_stats)
    stat_max = lax.dynamic_update_slice_in_dim(stat_max, joined[0], row_start, 0)
    stat_sum = lax.dynamic_update_slice_in_dim(stat_sum, joined[1], row_start, 0)
    stat_out = lax.dynamic_update_slice_in_dim(stat_out, joined[2], row_start, 0)
    normed_all = None
    merged = joined_2((stat_max, stat_sum, stat_out), "tp", combine_stats)
    attn_own = finish_rows(
        lax.dynamic_slice_in_dim(merged[1], row_start, tok_dev, 0),
        lax.dynamic_slice_in_dim(merged[2], row_start, tok_dev, 0),
    )
    hidden_own = project_rows(attn_own, own_res, out_weight)
    normed_own = rms_normed(hidden_own, norm_gain)
    units_dev = gate_up.shape[0]
    unit_width = gate_up.shape[2] // 2
    normed_all = lax.all_gather(normed_own, "tp", axis=0, tiled=True)
    shares = unit_shares(normed_all, router_weight, expert_ids, tp_rank, units_dev)
    gate_both = jnp.einsum("td,udh->tuh", normed_all, gate_up, preferred_element_type=jnp.float32)
    activated = (
        jax.nn.silu(gate_both[..., :unit_width]) * gate_both[..., unit_width:] * shares[:, :, None]
    ).astype(jnp.bfloat16)
    moe_own = lax.psum_scatter(
        jnp.einsum("tuh,uhd->td", activated, down_weight, preferred_element_type=jnp.float32),
        "tp",
        scatter_dimension=0,
        tiled=True,
    )
    layer_out = (hidden_own + moe_own).astype(jnp.bfloat16)
    node_ids = jnp.arange(DRAFT, dtype=jnp.int32)
    leaf_pick = (accept_leaf[:, None] == node_ids[None, :]).astype(jnp.float32)
    path_weight = jnp.einsum("sn,snk->sk", leaf_pick, reached, precision=lax.Precision.HIGHEST)
    path_flags = (path_weight > 0.5).astype(jnp.int32)
    path_rank = jnp.cumsum(path_flags, axis=1) - 1
    chosen_node = (path_flags[:, None, :] > 0) & (path_rank[:, None, :] == node_ids[None, :, None])
    own_choice = jnp.take(chosen_node.reshape(slot_count * DRAFT, DRAFT), row_pos, axis=0)
    spread = same_slot & jnp.tile(own_choice, (1, slot_count))
    accepted = jnp.dot(
        spread.astype(jnp.bfloat16), all_kv, preferred_element_type=jnp.float32
    ).astype(jnp.bfloat16)
    return (attn_own, layer_out, accepted)


def start_all(copies):
    for copy in copies:
        copy.start()
    for copy in copies:
        copy.wait()


def split_kernel(pairs, *refs):
    (
        pages_hbm, placement_hbm, lengths_hbm, leaf_hbm, keys_hbm, values_hbm, queries_hbm,
        new_kv_hbm, residual_hbm, parents_hbm, router_hbm, ids_hbm, gain_hbm,
    ) = refs[:13]
    parts, refs = refs[13 : 13 + pairs], refs[13 + pairs :]
    joined_ref, table_ref, parents_ref, router_ref, ids_ref, gain_ref = refs[:6]
    pages_ref, placement_ref, lengths_ref, leaf_ref, keys_ref, values_ref, split_ref, sems = refs[6:]
    slot_count = pages_ref.shape[0]
    page_len = keys_ref.shape[1]
    tok_dev = joined_ref.shape[0]
    moves = [
        (pages_hbm, pages_ref),
        (keys_hbm, keys_ref),
        (values_hbm, values_ref),
        (placement_hbm, placement_ref),
        (lengths_hbm, lengths_ref),
        (leaf_hbm, leaf_ref),
        (parents_hbm, parents_ref),
        (router_hbm, router_ref),
        (ids_hbm, ids_ref),
        (gain_hbm, gain_ref),
    ]
    column = 0
    for source in (queries_hbm, new_kv_hbm, residual_hbm):
        moves.append((source, joined_ref.at[:, column : column + source.shape[1]]))
        column += source.shape[1]
    start_all(
        [pltpu.make_async_copy(a, b, sems.at[k]) for k, (a, b) in enumerate(moves)]
    )
    slot = lax.div(lax.axis_index("tp") * tok_dev, DRAFT)
    numbers = [lax.div(placement_ref[slot], slot_count)]
    numbers += [lengths_ref[s] for s in range(slot_count)]
    numbers += [leaf_ref[s] for s in range(slot_count)]
    for row, number in enumerate(numbers):
        table_ref[row : row + 1, :] = jnp.full((1, WIDE), number, jnp.int32).astype(jnp.float32)
    for head in range(KV_HEADS):
        low = head * HEAD
        for s in range(slot_count):
            page = pages_ref[s]
            split_ref[head // 2, head % 2, s * page_len : (s + 1) * page_len, :] = jnp.concatenate(
                [keys_ref[page, :, low : low + HEAD], values_ref[page, :, low : low + HEAD]], axis=1
            )
    pair = lax.div(lax.axis_index("tp"), 2)
    for k, part in enumerate(parts):
        part[...] = split_ref[lax.bitwise_xor(pair, pairs - 1 - k)]


def number(table_ref, row):
    return jnp.max(table_ref[row : row + 1, :]).astype(jnp.int32)


def route_kernel(kv_width, after_ref, table_ref, pulled_ref, *refs):
    del after_ref
    parts, (sent_ref, res_ref, turned_ref, kv_ref) = refs[:-4], refs[-4:]
    rank = lax.axis_index("tp")
    other = 1 - lax.rem(rank, 2)
    size = parts[0].shape[1]
    for k, part in enumerate(parts):
        turned_ref[k * size : (k + 1) * size, :] = part[other]
    q_width = HEADS * HEAD
    tok_dev = pulled_ref.shape[1]
    rows = pulled_ref[number(table_ref, 0)]
    res_ref[...] = rows[:, q_width + 2 * kv_width :]
    tiles = [rows[:, q_width + c : q_width + c + WIDE] for c in range(0, 2 * kv_width, WIDE)]
    kv_ref[...] = jnp.concatenate(tiles, axis=0)
    head_rows = (HEADS // KV_HEADS) * HEAD
    tail = jnp.zeros((tok_dev, 2 * WIDE - head_rows), rows.dtype)
    for head in range(KV_HEADS):
        q_low = head * head_rows
        pair = jnp.concatenate([rows[:, q_low : q_low + head_rows], tail], axis=1)
        sent_ref[head, :tok_dev, :] = pair[:, :WIDE]
        sent_ref[head, tok_dev : 2 * tok_dev, :] = pair[:, WIDE:]
        k_low = q_width + head * HEAD
        sent_ref[head, 2 * tok_dev :, :] = jnp.concatenate(
            [rows[:, k_low : k_low + HEAD], rows[:, k_low + kv_width : k_low + kv_width + HEAD]],
            axis=1,
        )


def ancestor_rows(parents_ref):
    slot_count = parents_ref.shape[0]
    total = slot_count * DRAFT
    row = jnp.concatenate(
        [parents_ref[s : s + 1, :] + s * DRAFT for s in range(slot_count)], axis=1
    )
    from_ids = lax.broadcasted_iota(jnp.int32, (total, total), 0)
    to_ids = lax.broadcasted_iota(jnp.int32, (total, total), 1)
    linked = (from_ids == jnp.broadcast_to(row, (total, total))) & (lax.rem(to_ids, DRAFT) > 0)
    reached = jnp.where(linked | (from_ids == to_ids), 1.0, 0.0)
    for _ in range((DRAFT - 1).bit_length()):
        half = reached.astype(jnp.bfloat16)
        reached = jnp.minimum(jnp.dot(half, half, preferred_element_type=jnp.float32), 1.0)
    return reached.T


def tree_kernel(
    after_ref, down_hbm, table_ref, parents_ref, ids_ref, down_ref, reach_ref, chosen_ref,
    count_ref, sem,
):
    del after_ref
    copy = pltpu.make_async_copy(down_hbm, down_ref, sem)
    copy.start()
    slot_count = parents_ref.shape[0]
    reach_ref[...] = ancestor_rows(parents_ref)
    node_from = lax.broadcasted_iota(jnp.int32, (DRAFT, DRAFT), 0)
    node_to = lax.broadcasted_iota(jnp.int32, (DRAFT, DRAFT), 1)
    upto = jnp.where(node_from <= node_to, 1.0, 0.0).astype(jnp.bfloat16)
    for s in range(slot_count):
        leaf = number(table_ref, 1 + slot_count + s)
        path = reach_ref[pl.ds(s * DRAFT + leaf, 1), s * DRAFT : (s + 1) * DRAFT]
        path = jnp.broadcast_to(path, (DRAFT, DRAFT))
        rank = jnp.dot(path.astype(jnp.bfloat16), upto, preferred_element_type=jnp.float32)
        chosen = (path > 0.5) & (rank == (node_from + 1).astype(jnp.float32))
        chosen_ref[s] = jnp.where(chosen, 1.0, 0.0).astype(jnp.bfloat16)
    ids = ids_ref[...].astype(jnp.float32).T
    names = lax.broadcasted_iota(jnp.int32, count_ref.shape, 1).astype(jnp.float32)
    count = jnp.zeros(count_ref.shape, jnp.float32)
    for k in range(ids.shape[1]):
        count = count + jnp.where(ids[:, k : k + 1] == names, 1.0, 0.0)
    count_ref[...] = count
    copy.wait()


def attend_kernel(units_ref, table_ref, reach_ref, got_ref, res_ref, turned_ref, kv_ref, *refs):
    del units_ref
    parts, (sent_ref, near_ref) = refs[:-2], refs[-2:]
    slot_count = reach_ref.shape[0] // DRAFT
    sources = got_ref.shape[0]
    tok_dev = res_ref.shape[0]
    page_len = parts[0].shape[1] // slot_count
    per_slot = DRAFT // tok_dev
    group_size = HEADS // KV_HEADS
    f32, bf16 = jnp.float32, jnp.bfloat16
    lane_low = lax.broadcasted_iota(jnp.int32, (DRAFT, WIDE), 1) < HEAD
    rank = lax.axis_index("tp")
    side = lax.rem(rank, 2)
    within = lax.broadcasted_iota(jnp.int32, (1, page_len), 1)
    positions = []
    for k in range(len(parts)):
        pair = lax.bitwise_xor(lax.div(rank, 2), k)
        for page in (2 * pair + side, 2 * pair + 1 - side):
            positions.append(within + page * page_len)
    positions = jnp.concatenate(positions, axis=1)
    dims = (((1,), (1,)), ((), ()))
    scale = 1.0 / math.sqrt(HEAD)
    outs = []
    for s in range(slot_count):
        first = s * per_slot

        def part(k):
            low = k * tok_dev
            return jnp.concatenate(
                [got_ref[first + i, low : low + tok_dev, :] for i in range(per_slot)], axis=0
            )

        q_pair, q_last, tree_kv = part(0).astype(f32) * scale, part(1).astype(f32) * scale, part(2)
        q_rows = jnp.concatenate(
            [
                jnp.where(lane_low, q_pair, 0.0),
                jnp.where(lane_low, pltpu.roll(q_pair, HEAD, 1), 0.0),
                jnp.where(lane_low, q_last, 0.0),
            ],
            axis=0,
        ).astype(bf16)
        at = slice(s * page_len, (s + 1) * page_len)
        cache_kv = jnp.concatenate(
            [a for k, part in enumerate(parts) for a in (part[side, at, :], turned_ref[k * parts[0].shape[1] + at.start : k * parts[0].shape[1] + at.stop, :])],
            axis=0,
        )
        scores = lax.dot_general(q_rows, cache_kv, dims, preferred_element_type=f32)
        is_valid = positions < number(table_ref, 1 + s)
        scores = jnp.where(is_valid, scores, neg_big)
        reach = reach_ref[s * DRAFT : (s + 1) * DRAFT, s * DRAFT : (s + 1) * DRAFT]
        allowed = jnp.concatenate([reach] * group_size, axis=0) > 0.5
        tree_scores = lax.dot_general(q_rows, tree_kv, dims, preferred_element_type=f32)
        tree_scores = jnp.where(allowed, tree_scores, neg_big)
        top = jnp.maximum(
            jnp.max(scores, axis=1, keepdims=True), jnp.max(tree_scores, axis=1, keepdims=True)
        )
        weights = jnp.where(is_valid, jnp.exp(scores - top), 0.0).astype(bf16)
        tree_weights = jnp.where(allowed, jnp.exp(tree_scores - top), 0.0).astype(bf16)
        total = jnp.sum(weights.astype(f32), axis=1, keepdims=True) + jnp.sum(
            tree_weights.astype(f32), axis=1, keepdims=True
        )
        mixed = jnp.dot(weights, cache_kv, preferred_element_type=f32) + jnp.dot(
            tree_weights, tree_kv, preferred_element_type=f32
        )
        outs.append(mixed / total)
    pair_rows, last_rows = [], []
    for out in outs:
        head_out = [out[r * DRAFT : (r + 1) * DRAFT] for r in range(group_size)]
        pair_rows.append(
            jnp.where(lane_low, pltpu.roll(head_out[0], HEAD, 1), head_out[1]).astype(bf16)
        )
        last_rows.append(head_out[2])
    last = jnp.where(lane_low, pltpu.roll(last_rows[0], HEAD, 1), last_rows[1]).astype(bf16)
    res_tiles = [res_ref[:, c * WIDE : (c + 1) * WIDE] for c in range(res_ref.shape[1] // WIDE)]
    sent_ref[...] = jnp.concatenate(pair_rows + [last] + res_tiles, axis=0)
    rows = sent_ref.shape[0]
    near_ref[:rows, :] = sent_ref[...]
    near_ref[rows:, :] = kv_ref[...]


def accept_kernel(rows, chosen_ref, *refs):
    accepted_ref = refs[-1]
    tok_dev, width = accepted_ref.shape
    rank = lax.axis_index("tp")
    per_slot = DRAFT // tok_dev
    place = lax.rem(rank, per_slot)
    chosen = chosen_ref[lax.div(rank, per_slot), pl.ds(pl.multiple_of(place * tok_dev, tok_dev), tok_dev), :]
    is_even, is_first = lax.rem(place, 2) == 0, place < 2
    for c in range(width // WIDE):
        low = rows + c * tok_dev
        pairs = []
        for mine, other in (refs[:2], refs[2:4]):
            a, b = mine[low : low + tok_dev, :], other[low : low + tok_dev, :]
            pairs.append(
                jnp.concatenate([jnp.where(is_even, a, b), jnp.where(is_even, b, a)], axis=0)
            )
        near, far = pairs
        nodes = jnp.concatenate(
            [jnp.where(is_first, near, far), jnp.where(is_first, far, near)], axis=0
        )
        accepted_ref[:, c * WIDE : (c + 1) * WIDE] = jnp.dot(
            chosen, nodes, preferred_element_type=jnp.float32
        ).astype(jnp.bfloat16)


def fetch_kernel(picks, after_ref, source_ref, target_ref, sems):
    del after_ref
    rows = target_ref.shape[0] // len(picks)
    copies = []
    for place, k in enumerate(picks):
        pair = lax.bitwise_xor(lax.div(lax.axis_index("tp"), 2), k)
        start = pl.multiple_of(pair * rows, WIDE)
        copies.append(
            pltpu.make_async_copy(
                source_ref.at[pl.ds(start, rows)],
                target_ref.at[place * rows : (place + 1) * rows],
                sems.at[place],
            )
        )
    start_all(copies)


def join_heads(k, rows, group_rows, mine_ref, other_ref, residual_ref):
    f32, bf16 = jnp.float32, jnp.bfloat16
    half = group_rows // 2
    tok_dev = group_rows // KV_HEADS
    model = residual_ref.shape[1]
    res_start = group_rows + half
    rank = lax.axis_index("tp")
    is_even = lax.rem(rank, 2) == 0
    pair = lax.bitwise_xor(lax.div(rank, 2), k)
    lane_low = lax.broadcasted_iota(jnp.int32, (half, WIDE), 1) < HEAD
    mine, other = mine_ref[:rows, :], other_ref[:rows, :]
    even, odd = jnp.where(is_even, mine, other), jnp.where(is_even, other, mine)
    last_even = even[group_rows:res_start].astype(f32)
    last_odd = odd[group_rows:res_start].astype(f32)
    odd_swapped = pltpu.roll(odd[:group_rows].astype(f32), HEAD, 1)
    middle = jnp.concatenate(
        [
            jnp.where(lane_low, last_even, odd_swapped[:half]),
            jnp.where(lane_low, pltpu.roll(last_even, HEAD, 1), odd_swapped[half:]),
        ],
        axis=0,
    ).astype(bf16)
    end = jnp.concatenate(
        [
            jnp.where(lane_low, odd_swapped[:half], pltpu.roll(last_odd, HEAD, 1)),
            jnp.where(lane_low, odd_swapped[half:], last_odd),
        ],
        axis=0,
    ).astype(bf16)
    for q, block in enumerate((even, odd)):
        row = pl.multiple_of((2 * pair + q) * tok_dev, tok_dev)
        residual_ref[pl.ds(row, tok_dev), :] = jnp.concatenate(
            [
                block[res_start + c * tok_dev : res_start + (c + 1) * tok_dev]
                for c in range(model // WIDE)
            ],
            axis=1,
        ).astype(f32)
    return jnp.concatenate([even[:group_rows], middle, end], axis=1)


def keep_own(k, heads_ref, at, attn_ref):
    tok_dev = attn_ref.shape[0]
    width = attn_ref.shape[1] * 2 // KV_HEADS
    rank = lax.axis_index("tp")
    pair = lax.bitwise_xor(lax.div(rank, 2), k)
    own = pl.multiple_of(rank * tok_dev, tok_dev)
    attn_ref[:, pl.ds(pl.multiple_of(pair * width, WIDE), width)] = heads_ref[
        pl.ds(own, tok_dev), at : at + width
    ]


def early_kernel(rows, after_ref, weight_ref, *refs):
    del after_ref
    blocks, (hid_ref, attn_ref, residual_ref, x_ref) = refs[:-4], refs[-4:]
    group_rows = hid_ref.shape[0]
    residual_ref[...] = jnp.zeros_like(residual_ref)
    width = x_ref.shape[1] * 2 // len(blocks)
    for k in range(len(blocks) // 2):
        x_ref[:, k * width : (k + 1) * width] = join_heads(
            k, rows, group_rows, blocks[2 * k], blocks[2 * k + 1], residual_ref
        )
    for k in range(len(blocks) // 2):
        keep_own(k, x_ref, k * width, attn_ref)
    hid_ref[...] = residual_ref[...] + jnp.dot(
        x_ref[...], weight_ref[...], preferred_element_type=jnp.float32
    )


def expert_kernel(
    rows, count_ref, router_ref, gain_ref, down_ref, before_ref, part_ref, *refs
):
    refs, late = refs[:-8], refs[-8:]
    far_ref, hid_ref, hidden_ref, attn_ref, x_ref, normed_ref, share_ref, residual_ref = late
    f32, bf16 = jnp.float32, jnp.bfloat16
    pairs = KV_HEADS // 2
    first = pairs // 2
    blocks, refs = refs[: 2 * (pairs - first)], refs[2 * (pairs - first) :]
    weight_refs, unit_refs = refs[: pairs - first], refs[pairs - first :]
    unit_weights = [(ref, k) for ref in unit_refs for k in range(ref.shape[0])]
    units = len(unit_weights)
    tok_dev, model = hidden_ref.shape
    sources = KV_HEADS
    group_rows = sources * tok_dev
    rank = lax.axis_index("tp")
    own = pl.multiple_of(rank * tok_dev, tok_dev)
    attn_ref[...] = part_ref[...]
    residual_ref[...] = jnp.zeros_like(residual_ref)
    hidden, width = before_ref[...], x_ref.shape[1] // (pairs - first)
    for q, k in enumerate(range(first, pairs)):
        heads = join_heads(k, rows, group_rows, blocks[2 * q], blocks[2 * q + 1], residual_ref)
        x_ref[:, q * width : (q + 1) * width] = heads
        keep_own(k, x_ref, q * width, attn_ref)
        hidden += jnp.dot(heads, weight_refs[q][...], preferred_element_type=f32)
    hidden += residual_ref[...]
    hid_ref[...] = hidden
    gain = jnp.concatenate([gain_ref[c : c + 1, :] for c in range(model // WIDE)], axis=1)
    scale = lax.rsqrt(jnp.mean(hidden * hidden, axis=1, keepdims=True) + norm_eps)
    normed_ref[...] = (hidden * scale * gain).astype(bf16)
    hidden_ref[...] = hid_ref[pl.ds(own, tok_dev), :]
    logits = lax.dot_general(
        normed_ref[...], router_ref[...], (((1,), (1,)), ((), ())), preferred_element_type=f32
    )
    experts = router_ref.shape[0]
    expert_range = lax.broadcasted_iota(jnp.int32, (group_rows, experts), 1)
    count = count_ref[...]
    expo = jnp.where(count > 0.0, jnp.exp(logits), 0.0) * count
    routing = expo / jnp.sum(expo, axis=1, keepdims=True)
    unit_width = unit_refs[0].shape[2] // 2
    span = FF_E // unit_width
    each = span if units % span == 0 else 1
    for u in range(0, units, each):
        expert = (rank * units + u) // span
        share = jnp.sum(jnp.where(expert_range == expert, routing, 0.0), axis=1, keepdims=True)
        share_ref[u : u + each] = jnp.broadcast_to(share[None], (each, group_rows, unit_width))

    def one_unit(u):
        ref, k = unit_weights[u]
        both = jnp.dot(normed_ref[...], ref[k], preferred_element_type=f32)
        gate, up = both[:, :unit_width], both[:, unit_width:]
        return (gate / (1.0 + jnp.exp(-gate)) * up * share_ref[u]).astype(bf16)

    for i in range(units // STEP):
        act = jnp.concatenate([one_unit(i * STEP + k) for k in range(STEP)], axis=1)
        down = down_ref[i * STEP : (i + 1) * STEP].reshape(STEP * unit_width, model)
        part = jnp.dot(act, down, preferred_element_type=f32)
        hid_ref[...] = part if i == 0 else hid_ref[...] + part
    for k in range(far_ref.shape[0]):
        copy_sums(sources // 4 + k, True, hid_ref, far_ref.at[k])


def copy_sums(k, crossing, hid_ref, ref):
    tok_dev = ref.shape[0]
    rank = lax.axis_index("tp")
    side = lax.rem(rank, 2)
    pair = lax.bitwise_xor(lax.div(rank, 2), k)
    target = 2 * pair + (1 - side if crossing else side)
    row = pl.multiple_of(target * tok_dev, tok_dev)
    ref[...] = hid_ref[pl.ds(row, tok_dev), :].astype(ref.dtype)


def near_kernel(hid_ref, mine_ref, near_ref):
    for k in range(mine_ref.shape[0]):
        copy_sums(k, False, hid_ref, mine_ref.at[k])
    for k in range(near_ref.shape[0]):
        copy_sums(k, True, hid_ref, near_ref.at[k])


def fold_kernel(first, after_ref, mine_ref, got_ref, hidden_ref, *sent_refs):
    del after_ref
    for k, ref in enumerate(sent_refs, first):
        total = mine_ref[k] + got_ref[k - first].astype(jnp.float32)
        if k == 0:
            total = total + hidden_ref[...]
        ref[...] = total.astype(ref.dtype)


def finish_kernel(attn_in_ref, accepted_in_ref, *refs):
    parts, (attn_ref, layer_ref, accepted_ref) = refs[:-3], refs[-3:]
    attn_ref[...] = attn_in_ref[...]
    accepted_ref[...] = accepted_in_ref[...]
    total = parts[0][...]
    for part in parts[1:]:
        total = total + part[...].astype(jnp.float32)
    layer_ref[...] = total.astype(jnp.bfloat16)


def in_hbm(*arrays):
    return tuple(pltpu.with_memory_space_constraint(a, pltpu.HBM) for a in arrays)


def spaces(text):
    kinds = {"a": pl.ANY, "v": pltpu.VMEM}
    return [pl.BlockSpec(memory_space=kinds[c]) for c in text]


def params(mebibytes=12):
    return pltpu.CompilerParams(vmem_limit_bytes=mebibytes << 20)


def cost(mebibytes):
    return pl.CostEstimate(flops=0, transcendentals=0, bytes_accessed=mebibytes << 20)


def swap(rows, mask):
    count = lax.axis_size("tp")
    return lax.ppermute(rows, "tp", [(i, i ^ mask) for i in range(count)])


def fetch(after, array, rows, picks):
    shape = (rows * len(picks),) + array.shape[1:]
    return pl.pallas_call(
        functools.partial(fetch_kernel, picks),
        out_shape=pltpu.VMEM(shape, array.dtype),
        in_specs=spaces("aa"),
        out_specs=spaces("v")[0],
        scratch_shapes=[pltpu.SemaphoreType.DMA((len(picks),))],
        compiler_params=params(),
        cost_estimate=cost(2 * math.prod(shape) >> 20),
        name="fetch",
    )(after, *in_hbm(array))


def per_device_packed(
    queries,
    new_kv,
    residual,
    placement,
    lengths,
    page_table,
    cache_keys,
    cache_values,
    parents,
    accept_leaf,
    out_weight,
    norm_gain,
    router_weight,
    expert_ids,
    gate_up,
    down_weight,
):
    f32, bf16 = jnp.float32, jnp.bfloat16
    tok_dev, model = residual.shape
    tp_count = lax.axis_size("tp")
    slot_count = placement.shape[0]
    page_len, kv_width = cache_keys.shape[1:]
    group_rows = tok_dev * tp_count
    sent = lambda rows: jax.ShapeDtypeStruct((tp_count, rows, WIDE), bf16)
    dma = pltpu.SemaphoreType.DMA
    slots_smem = pltpu.SMEM((slot_count,), jnp.int32)
    pairs = tp_count // 2
    part = jax.ShapeDtypeStruct((2, slot_count * page_len, WIDE), bf16)
    loaded = (
        page_table.reshape(slot_count),
        placement,
        lengths,
        accept_leaf,
        cache_keys,
        cache_values,
        queries,
        new_kv,
        residual,
        parents,
        router_weight.T,
        expert_ids.T,
        norm_gain.reshape(model // WIDE, WIDE),
    )
    *parts, joined, table, parents, router, ids, gain = pl.pallas_call(
        functools.partial(split_kernel, pairs),
        out_shape=(part,) * pairs
        + (
            jax.ShapeDtypeStruct((tok_dev, 2 * (model + kv_width)), bf16),
            pltpu.VMEM((8, WIDE), f32),
        )
        + tuple(pltpu.VMEM(a.shape, a.dtype) for a in loaded[9:]),
        in_specs=spaces("a" * len(loaded)),
        out_specs=tuple(spaces("v" * (pairs + 6))),
        scratch_shapes=[
            slots_smem,
            slots_smem,
            slots_smem,
            slots_smem,
            pltpu.VMEM(cache_keys.shape, bf16),
            pltpu.VMEM(cache_values.shape, bf16),
            pltpu.VMEM((pairs,) + part.shape, bf16),
            dma((len(loaded),)),
        ],
        compiler_params=params(),
        cost_estimate=cost(4),
        name="split",
    )(*in_hbm(*loaded))
    parts = parts[::-1]
    parts = [parts[0]] + [swap(parts[k], 2 * k) for k in range(1, pairs)]
    pulled = lax.all_gather(joined, "req", axis=0)
    nodes = slot_count * DRAFT
    down_weight, reach, chosen, count = pl.pallas_call(
        tree_kernel,
        out_shape=(
            pltpu.VMEM(down_weight.shape, bf16),
            jax.ShapeDtypeStruct((nodes, nodes), f32),
            jax.ShapeDtypeStruct((slot_count, DRAFT, DRAFT), bf16),
            jax.ShapeDtypeStruct((group_rows, router_weight.shape[1]), f32),
        ),
        in_specs=spaces("aavvv"),
        out_specs=tuple(spaces("vvvv")),
        scratch_shapes=[dma],
        compiler_params=params(),
        cost_estimate=cost(8),
        name="tree",
    )(pulled, *in_hbm(down_weight), table, parents, ids)
    kv_rows = 2 * kv_width // WIDE * tok_dev
    packed, own_res, turned, own_kv = pl.pallas_call(
        functools.partial(route_kernel, kv_width),
        out_shape=(
            sent(3 * tok_dev),
            jax.ShapeDtypeStruct(residual.shape, bf16),
            jax.ShapeDtypeStruct((pairs * part.shape[1], WIDE), bf16),
            jax.ShapeDtypeStruct((kv_rows, WIDE), bf16),
        ),
        in_specs=spaces("avv" + "v" * pairs),
        out_specs=tuple(spaces("vvvv")),
        compiler_params=params(),
        cost_estimate=cost(4),
        name="route",
    )(down_weight, table, pulled, *parts)
    turned = swap(turned, 1)
    packed = lax.all_to_all(packed, "tp", 0, 0, tiled=True)
    gate_up = pltpu.with_memory_space_constraint(gate_up, pltpu.VMEM)
    block_rows = group_rows + group_rows // 2 + (model // WIDE) * tok_dev
    block, near_block = pl.pallas_call(
        attend_kernel,
        out_shape=(
            jax.ShapeDtypeStruct((block_rows, WIDE), bf16),
            jax.ShapeDtypeStruct((block_rows + kv_rows, WIDE), bf16),
        ),
        in_specs=spaces("v" * (7 + pairs)),
        out_specs=tuple(spaces("vv")),
        compiler_params=params(),
        cost_estimate=cost(8),
        name="attend",
    )(gate_up, table, reach, packed, own_res, turned, own_kv, *parts)
    units = gate_up.shape[0]
    reached = [swap(near_block, 2)] + [swap(block, 2 * k) for k in range(2, pairs)]
    weights, after = [], block
    rows = out_weight.shape[0] // pairs
    for k, picks in zip(ORDER, FETCHES):
        weight = fetch(after, out_weight, rows, picks)
        reached[k - 1], weight = lax.optimization_barrier((reached[k - 1], weight))
        after = reached[k - 1]
        weights.append(weight)
    blocks = [block, swap(near_block, 1)]
    blocks += [a for got in reached for a in (got, swap(got, 1))]
    before, attn_part = pl.pallas_call(
        functools.partial(early_kernel, block_rows),
        out_shape=(
            jax.ShapeDtypeStruct((group_rows, model), f32),
            pltpu.VMEM(queries.shape, bf16),
        ),
        in_specs=spaces("av" + "v" * pairs),
        out_specs=tuple(spaces("vv")),
        scratch_shapes=[
            pltpu.VMEM((group_rows, model), f32),
            pltpu.VMEM((group_rows, HEADS * HEAD // 2), bf16),
        ],
        compiler_params=params(),
        cost_estimate=cost(4),
        name="early",
    )(after, weights[0], *blocks[:pairs])
    accepted = pl.pallas_call(
        functools.partial(accept_kernel, block_rows),
        out_shape=pltpu.VMEM(new_kv.shape, bf16),
        in_specs=spaces("vvvvv"),
        out_specs=spaces("v")[0],
        compiler_params=params(),
        cost_estimate=cost(1),
        name="accept",
    )(chosen, near_block, *blocks[1:4])
    unit_weights = (gate_up,)
    far, sums, hidden, attn_own = pl.pallas_call(
        functools.partial(expert_kernel, block_rows),
        out_shape=(
            jax.ShapeDtypeStruct((pairs // 2, tok_dev, model), bf16),
            jax.ShapeDtypeStruct((group_rows, model), f32),
            jax.ShapeDtypeStruct((tok_dev, model), f32),
            pltpu.VMEM(queries.shape, bf16),
        ),
        in_specs=spaces("v" * (6 + pairs + pairs // 2 + len(unit_weights))),
        out_specs=tuple(spaces("vvvv")),
        scratch_shapes=[
            pltpu.VMEM((group_rows, HEADS * HEAD // 2), bf16),
            pltpu.VMEM((group_rows, model), bf16),
            pltpu.VMEM((units, group_rows, gate_up.shape[2] // 2), f32),
            pltpu.VMEM((group_rows, model), f32),
        ],
        compiler_params=params(),
        name="experts",
    )(
        count,
        router,
        gain,
        down_weight,
        before,
        attn_part,
        *blocks[pairs:],
        weights[2],
        weights[1],
        *unit_weights,
    )
    far = swap(far, 1)
    mine, near = pl.pallas_call(
        near_kernel,
        out_shape=(
            jax.ShapeDtypeStruct((pairs, tok_dev, model), f32),
            jax.ShapeDtypeStruct((pairs // 2, tok_dev, model), bf16),
        ),
        in_specs=spaces("v"),
        out_specs=tuple(spaces("vv")),
        compiler_params=params(),
        cost_estimate=cost(4),
        name="near",
    )(sums)
    near = swap(near, 1)
    fold = lambda first, after, got: pl.pallas_call(
        functools.partial(fold_kernel, first),
        out_shape=tuple(
            jax.ShapeDtypeStruct((tok_dev, model), f32 if k == 0 else bf16)
            for k in range(first, first + pairs // 2)
        ),
        in_specs=spaces("avvv"),
        out_specs=tuple(spaces("v" * (pairs // 2))),
        compiler_params=params(),
        cost_estimate=cost(1),
        name="fold",
    )(after, mine, got, hidden)
    sums = fold(pairs // 2, hidden, far)
    folded = sums[0]
    sums = [swap(a, 2 * k) for k, a in enumerate(sums, pairs // 2)]
    close = fold(0, folded, near)
    sums = [close[0]] + [swap(close[k], 2 * k) for k in range(1, pairs // 2)] + sums
    return pl.pallas_call(
        finish_kernel,
        out_shape=(
            jax.ShapeDtypeStruct(queries.shape, bf16),
            jax.ShapeDtypeStruct(residual.shape, bf16),
            jax.ShapeDtypeStruct(new_kv.shape, bf16),
        ),
        in_specs=spaces("v" * (2 + pairs)),
        out_specs=tuple(spaces("vvv")),
        compiler_params=params(),
        name="finish",
    )(attn_own, accepted, *sums)


def per_device(queries, new_kv, residual, placement, *rest):
    tok_dev = queries.shape[0]
    one_head_each = lax.axis_size("tp") == KV_HEADS
    whole_tiles = tok_dev % 16 == 0 and placement.shape[0] == 2 and tok_dev * KV_HEADS == 2 * DRAFT
    if one_head_each and whole_tiles and rest[1].shape[1] == 1:
        return per_device_packed(queries, new_kv, residual, placement, *rest)
    return per_device_plain(queries, new_kv, residual, placement, *rest)


def solution(mesh):
    in_specs = (
        P(("req", "tp"), None),
        P(("req", "tp"), None),
        P(("req", "tp"), None),
        P("req"),
        P("req"),
        P("req", None, "tp"),
        P(("req", "tp"), None, None),
        P(("req", "tp"), None, None),
        P("req", None),
        P("req"),
        P(),
        P(),
        P(),
        P("req", None),
        P("tp", None, None),
        P("tp", None, None),
    )
    out_specs = (P(("req", "tp"), None), P(("req", "tp"), None), P(("req", "tp"), None))
    return jax.shard_map(
        per_device, mesh=mesh, in_specs=in_specs, out_specs=out_specs, check_vma=False
    )
```

```python
import functools
import math

import jax
import jax.numpy as jnp
from jax import lax
from jax.experimental import pallas as pl
from jax.experimental.pallas import tpu as pltpu
from jax.sharding import PartitionSpec as P

HEADS = 24
KV_HEADS = 8
HEAD = 64
FF_E = 512
UNIT = 128
DRAFT = 64
WIDE = 128
STEP = 2
READY = 12
ORDER = (1, 3, 2)
FETCHES = ((0, 1), (3,), (2,))


neg_big = -1e30
norm_eps = 1e-06


def joined_2(part, axis, combine):
    gathered = jax.tree.map(lambda a: lax.all_gather(a, axis), part)

    def take(source):
        return jax.tree.map(lambda a: lax.dynamic_index_in_dim(a, source, 0, False), gathered)

    return lax.fori_loop(
        1, lax.axis_size(axis), lambda source, state: combine(state, take(source)), take(0)
    )


def ancestry(parents):
    node_count = parents.shape[-1]
    node_ids = jnp.arange(node_count, dtype=jnp.int32)
    linked = (parents[:, :, None] == node_ids[None, None, :]) & (node_ids[None, :, None] > 0)
    reached = jnp.maximum(linked.astype(jnp.float32), jnp.eye(node_count, dtype=jnp.float32)[None])
    for _ in range(node_count.bit_length()):
        reached = jnp.minimum(
            jnp.einsum("rnm,rmk->rnk", reached, reached, precision=lax.Precision.HIGHEST), 1.0
        )
    return reached


def combine_stats(left_stats, right_stats):
    left_max, left_sum, left_out = left_stats
    right_max, right_sum, right_out = right_stats
    top_score = jnp.maximum(left_max, right_max)
    left_scale = jnp.exp(left_max - top_score)
    right_scale = jnp.exp(right_max - top_score)
    row_count, head_count = left_max.shape
    out_sum = (
        left_out.reshape(row_count, head_count, -1) * left_scale[..., None]
        + right_out.reshape(row_count, head_count, -1) * right_scale[..., None]
    )
    return (
        top_score,
        left_sum * left_scale + right_sum * right_scale,
        out_sum.reshape(row_count, -1),
    )


def finish_rows(stat_sum, stat_out):
    row_count, head_count = stat_sum.shape
    return (
        (stat_out.reshape(row_count, head_count, -1) / stat_sum[..., None])
        .reshape(row_count, -1)
        .astype(jnp.bfloat16)
    )


def project_rows(attn_rows, res_rows, out_weight):
    return res_rows.astype(jnp.float32) + jnp.dot(
        attn_rows, out_weight, preferred_element_type=jnp.float32
    )


def rms_normed(hidden, norm_gain):
    scale_rows = lax.rsqrt(jnp.mean(hidden * hidden, axis=-1, keepdims=True) + norm_eps)
    return (hidden * scale_rows * norm_gain).astype(jnp.bfloat16)


def unit_shares(normed_all, router_weight, expert_ids, tp_rank, units_dev):
    logits = jnp.dot(normed_all, router_weight, preferred_element_type=jnp.float32)
    expert_range = jnp.arange(router_weight.shape[1], dtype=jnp.int32)
    onehot = (expert_ids[:, :, None] == expert_range[None, None, :]).astype(jnp.float32)
    chosen = jnp.sum(logits[:, None, :] * onehot, axis=-1)
    expo_chosen = jnp.exp(chosen)
    expert_probs = expo_chosen / jnp.sum(expo_chosen, axis=-1, keepdims=True)
    routing = jnp.sum(expert_probs[:, :, None] * onehot, axis=1)
    unit_ids = tp_rank * units_dev + jnp.arange(units_dev, dtype=jnp.int32)
    expert_of_unit = unit_ids // (FF_E // UNIT)
    pick = (expert_range[:, None] == expert_of_unit[None, :]).astype(jnp.float32)
    return jnp.dot(routing, pick, precision=lax.Precision.HIGHEST)


def per_device_plain(
    queries,
    new_kv,
    residual,
    placement,
    lengths,
    page_table,
    cache_keys,
    cache_values,
    parents,
    accept_leaf,
    out_weight,
    norm_gain,
    router_weight,
    expert_ids,
    gate_up,
    down_weight,
):
    tok_dev = queries.shape[0]
    tp_count = lax.axis_size("tp")
    tp_rank = lax.axis_index("tp")
    group_rows = tok_dev * tp_count
    slot_count = placement.shape[0]
    kv_width = cache_keys.shape[2]
    page_len = cache_keys.shape[1]
    group_size = HEADS // KV_HEADS
    score_scale = 1.0 / math.sqrt(HEAD)
    row_start = tp_rank * tok_dev
    pulled_q, pulled_kv, pulled_res = (
        lax.all_gather(queries, "req", axis=0, tiled=True),
        lax.all_gather(new_kv, "req", axis=0, tiled=True),
        lax.all_gather(residual, "req", axis=0, tiled=True),
    )
    row_offsets = jnp.arange(tok_dev, dtype=jnp.int32)
    row_pos = row_start + row_offsets
    row_slot = row_pos // DRAFT
    slot_match = row_slot[:, None] == jnp.arange(slot_count, dtype=jnp.int32)[None, :]
    source_group = jnp.sum(jnp.where(slot_match, placement[None, :] // slot_count, 0), axis=1)
    source_rows = source_group * tok_dev + row_offsets
    own_q = jnp.take(pulled_q, source_rows, axis=0)
    own_kv = jnp.take(pulled_kv, source_rows, axis=0)
    own_res = jnp.take(pulled_res, source_rows, axis=0)
    all_q, all_kv = (
        lax.all_gather(own_q, "tp", axis=0, tiled=True),
        lax.all_gather(own_kv, "tp", axis=0, tiled=True),
    )
    local_pages = page_table.shape[1]
    page_ids = page_table[:, :, 0].reshape(-1)
    keys_local = jnp.take(cache_keys, page_ids, axis=0).reshape(
        slot_count, local_pages, page_len, KV_HEADS, HEAD
    )
    values_local = jnp.take(cache_values, page_ids, axis=0).reshape(
        slot_count, local_pages, page_len, KV_HEADS, HEAD
    )
    query_blocks = all_q.reshape(slot_count, DRAFT, KV_HEADS, group_size, HEAD)
    scores = (
        jnp.einsum(
            "sqgrd,sltgd->sqgrlt", query_blocks, keys_local, preferred_element_type=jnp.float32
        )
        * score_scale
    )
    positions = (
        jnp.arange(local_pages, dtype=jnp.int32)[:, None] * tp_count + tp_rank
    ) * page_len + jnp.arange(page_len, dtype=jnp.int32)[None, :]
    is_valid = (positions[None] < lengths[:, None, None])[:, None, None, None]
    scores = jnp.where(is_valid, scores, neg_big)
    block_max = jnp.max(scores, axis=-1)
    weights = jnp.where(is_valid, jnp.exp(scores - block_max[..., None]), 0.0).astype(jnp.bfloat16)
    block_sum = jnp.sum(weights.astype(jnp.float32), axis=-1)
    block_out = jnp.einsum(
        "sqgrlt,sltgd->sqgrld", weights, values_local, preferred_element_type=jnp.float32
    )
    page_top = jnp.max(block_max, axis=-1)
    page_scale = jnp.exp(block_max - page_top[..., None])
    stat_max = page_top.reshape(group_rows, HEADS)
    stat_sum = jnp.sum(block_sum * page_scale, axis=-1).reshape(group_rows, HEADS)
    stat_out = jnp.sum(block_out * page_scale[..., None], axis=-2).reshape(group_rows, HEADS * HEAD)
    reached = ancestry(parents)
    reach_rows = jnp.take(reached.reshape(slot_count * DRAFT, DRAFT), row_pos, axis=0)
    key_slot = jnp.arange(group_rows, dtype=jnp.int32) // DRAFT
    same_slot = key_slot[None, :] == row_slot[:, None]
    allowed = same_slot & (jnp.tile(reach_rows, (1, slot_count)) > 0.5)
    tree_keys = all_kv[:, :kv_width].reshape(group_rows, KV_HEADS, HEAD)
    tree_values = all_kv[:, kv_width:].reshape(group_rows, KV_HEADS, HEAD)
    own_blocks = own_q.reshape(tok_dev, KV_HEADS, group_size, HEAD)
    tree_scores = (
        jnp.einsum("igrd,kgd->igrk", own_blocks, tree_keys, preferred_element_type=jnp.float32)
        * score_scale
    )
    tree_mask = allowed[:, None, None, :]
    tree_scores = jnp.where(tree_mask, tree_scores, neg_big)
    tree_max = jnp.max(tree_scores, axis=-1)
    tree_weights = jnp.where(tree_mask, jnp.exp(tree_scores - tree_max[..., None]), 0.0).astype(
        jnp.bfloat16
    )
    tree_sum = jnp.sum(tree_weights.astype(jnp.float32), axis=-1)
    tree_out = jnp.einsum(
        "igrk,kgd->igrd", tree_weights, tree_values, preferred_element_type=jnp.float32
    )
    own_stats = (
        lax.dynamic_slice_in_dim(stat_max, row_start, tok_dev, 0),
        lax.dynamic_slice_in_dim(stat_sum, row_start, tok_dev, 0),
        lax.dynamic_slice_in_dim(stat_out, row_start, tok_dev, 0),
    )
    tree_stats = (
        tree_max.reshape(tok_dev, HEADS),
        tree_sum.reshape(tok_dev, HEADS),
        tree_out.reshape(tok_dev, HEADS * HEAD),
    )
    joined = combine_stats(own_stats, tree_stats)
    stat_max = lax.dynamic_update_slice_in_dim(stat_max, joined[0], row_start, 0)
    stat_sum = lax.dynamic_update_slice_in_dim(stat_sum, joined[1], row_start, 0)
    stat_out = lax.dynamic_update_slice_in_dim(stat_out, joined[2], row_start, 0)
    normed_all = None
    merged = joined_2((stat_max, stat_sum, stat_out), "tp", combine_stats)
    attn_own = finish_rows(
        lax.dynamic_slice_in_dim(merged[1], row_start, tok_dev, 0),
        lax.dynamic_slice_in_dim(merged[2], row_start, tok_dev, 0),
    )
    hidden_own = project_rows(attn_own, own_res, out_weight)
    normed_own = rms_normed(hidden_own, norm_gain)
    units_dev = gate_up.shape[0]
    unit_width = gate_up.shape[2] // 2
    normed_all = lax.all_gather(normed_own, "tp", axis=0, tiled=True)
    shares = unit_shares(normed_all, router_weight, expert_ids, tp_rank, units_dev)
    gate_both = jnp.einsum("td,udh->tuh", normed_all, gate_up, preferred_element_type=jnp.float32)
    activated = (
        jax.nn.silu(gate_both[..., :unit_width]) * gate_both[..., unit_width:] * shares[:, :, None]
    ).astype(jnp.bfloat16)
    moe_own = lax.psum_scatter(
        jnp.einsum("tuh,uhd->td", activated, down_weight, preferred_element_type=jnp.float32),
        "tp",
        scatter_dimension=0,
        tiled=True,
    )
    layer_out = (hidden_own + moe_own).astype(jnp.bfloat16)
    node_ids = jnp.arange(DRAFT, dtype=jnp.int32)
    leaf_pick = (accept_leaf[:, None] == node_ids[None, :]).astype(jnp.float32)
    path_weight = jnp.einsum("sn,snk->sk", leaf_pick, reached, precision=lax.Precision.HIGHEST)
    path_flags = (path_weight > 0.5).astype(jnp.int32)
    path_rank = jnp.cumsum(path_flags, axis=1) - 1
    chosen_node = (path_flags[:, None, :] > 0) & (path_rank[:, None, :] == node_ids[None, :, None])
    own_choice = jnp.take(chosen_node.reshape(slot_count * DRAFT, DRAFT), row_pos, axis=0)
    spread = same_slot & jnp.tile(own_choice, (1, slot_count))
    accepted = jnp.dot(
        spread.astype(jnp.bfloat16), all_kv, preferred_element_type=jnp.float32
    ).astype(jnp.bfloat16)
    return (attn_own, layer_out, accepted)


def start_all(copies):
    for copy in copies:
        copy.start()
    for copy in copies:
        copy.wait()


def split_kernel(pairs, *refs):
    (
        pages_hbm, placement_hbm, lengths_hbm, leaf_hbm, keys_hbm, values_hbm, queries_hbm,
        new_kv_hbm, residual_hbm, parents_hbm, router_hbm, ids_hbm, gain_hbm,
    ) = refs[:13]
    parts, refs = refs[13 : 13 + pairs], refs[13 + pairs :]
    joined_ref, table_ref, parents_ref, router_ref, ids_ref, gain_ref = refs[:6]
    pages_ref, placement_ref, lengths_ref, leaf_ref, keys_ref, values_ref, split_ref, sems = refs[6:]
    slot_count = pages_ref.shape[0]
    page_len = keys_ref.shape[1]
    tok_dev = joined_ref.shape[0]
    moves = [
        (pages_hbm, pages_ref),
        (keys_hbm, keys_ref),
        (values_hbm, values_ref),
        (placement_hbm, placement_ref),
        (lengths_hbm, lengths_ref),
        (leaf_hbm, leaf_ref),
        (parents_hbm, parents_ref),
        (router_hbm, router_ref),
        (ids_hbm, ids_ref),
        (gain_hbm, gain_ref),
    ]
    column = 0
    for source in (queries_hbm, new_kv_hbm, residual_hbm):
        moves.append((source, joined_ref.at[:, column : column + source.shape[1]]))
        column += source.shape[1]
    start_all(
        [pltpu.make_async_copy(a, b, sems.at[k]) for k, (a, b) in enumerate(moves)]
    )
    slot = lax.div(lax.axis_index("tp") * tok_dev, DRAFT)
    numbers = [lax.div(placement_ref[slot], slot_count)]
    numbers += [lengths_ref[s] for s in range(slot_count)]
    numbers += [leaf_ref[s] for s in range(slot_count)]
    for row, number in enumerate(numbers):
        table_ref[row : row + 1, :] = jnp.full((1, WIDE), number, jnp.int32).astype(jnp.float32)
    for head in range(KV_HEADS):
        low = head * HEAD
        for s in range(slot_count):
            page = pages_ref[s]
            split_ref[head // 2, head % 2, s * page_len : (s + 1) * page_len, :] = jnp.concatenate(
                [keys_ref[page, :, low : low + HEAD], values_ref[page, :, low : low + HEAD]], axis=1
            )
    pair = lax.div(lax.axis_index("tp"), 2)
    for k, part in enumerate(parts):
        part[...] = split_ref[lax.bitwise_xor(pair, pairs - 1 - k)]


def number(table_ref, row):
    return jnp.max(table_ref[row : row + 1, :]).astype(jnp.int32)


def route_kernel(kv_width, after_ref, table_ref, pulled_ref, *refs):
    del after_ref
    parts, (sent_ref, res_ref, turned_ref, kv_ref) = refs[:-4][::-1], refs[-4:]
    rank = lax.axis_index("tp")
    other = 1 - lax.rem(rank, 2)
    size = parts[0].shape[1]
    for k, part in enumerate(parts):
        turned_ref[k * size : (k + 1) * size, :] = part[other]
    q_width = HEADS * HEAD
    tok_dev = pulled_ref.shape[1]
    rows = pulled_ref[number(table_ref, 0)]
    res_ref[...] = rows[:, q_width + 2 * kv_width :]
    tiles = [rows[:, q_width + c : q_width + c + WIDE] for c in range(0, 2 * kv_width, WIDE)]
    kv_ref[...] = jnp.concatenate(tiles, axis=0)
    head_rows = (HEADS // KV_HEADS) * HEAD
    tail = jnp.zeros((tok_dev, 2 * WIDE - head_rows), rows.dtype)
    for head in range(KV_HEADS):
        q_low = head * head_rows
        pair = jnp.concatenate([rows[:, q_low : q_low + head_rows], tail], axis=1)
        sent_ref[head, :tok_dev, :] = pair[:, :WIDE]
        sent_ref[head, tok_dev : 2 * tok_dev, :] = pair[:, WIDE:]
        k_low = q_width + head * HEAD
        sent_ref[head, 2 * tok_dev :, :] = jnp.concatenate(
            [rows[:, k_low : k_low + HEAD], rows[:, k_low + kv_width : k_low + kv_width + HEAD]],
            axis=1,
        )


def ancestor_rows(parents_ref):
    slot_count = parents_ref.shape[0]
    total = slot_count * DRAFT
    row = jnp.concatenate(
        [parents_ref[s : s + 1, :] + s * DRAFT for s in range(slot_count)], axis=1
    )
    from_ids = lax.broadcasted_iota(jnp.int32, (total, total), 0)
    to_ids = lax.broadcasted_iota(jnp.int32, (total, total), 1)
    linked = (from_ids == jnp.broadcast_to(row, (total, total))) & (lax.rem(to_ids, DRAFT) > 0)
    reached = jnp.where(linked | (from_ids == to_ids), 1.0, 0.0)
    for _ in range((DRAFT - 1).bit_length()):
        half = reached.astype(jnp.bfloat16)
        reached = jnp.minimum(jnp.dot(half, half, preferred_element_type=jnp.float32), 1.0)
    return reached.T


def tree_kernel(
    after_ref, down_hbm, table_ref, parents_ref, ids_ref, down_ref, reach_ref, chosen_ref,
    count_ref, sem,
):
    del after_ref
    copy = pltpu.make_async_copy(down_hbm.at[: down_ref.shape[0]], down_ref, sem)
    copy.start()
    slot_count = parents_ref.shape[0]
    reach_ref[...] = ancestor_rows(parents_ref)
    node_from = lax.broadcasted_iota(jnp.int32, (DRAFT, DRAFT), 0)
    node_to = lax.broadcasted_iota(jnp.int32, (DRAFT, DRAFT), 1)
    upto = jnp.where(node_from <= node_to, 1.0, 0.0).astype(jnp.bfloat16)
    for s in range(slot_count):
        leaf = number(table_ref, 1 + slot_count + s)
        path = reach_ref[pl.ds(s * DRAFT + leaf, 1), s * DRAFT : (s + 1) * DRAFT]
        path = jnp.broadcast_to(path, (DRAFT, DRAFT))
        rank = jnp.dot(path.astype(jnp.bfloat16), upto, preferred_element_type=jnp.float32)
        chosen = (path > 0.5) & (rank == (node_from + 1).astype(jnp.float32))
        chosen_ref[s] = jnp.where(chosen, 1.0, 0.0).astype(jnp.bfloat16)
    ids = ids_ref[...].astype(jnp.float32).T
    names = lax.broadcasted_iota(jnp.int32, count_ref.shape, 1).astype(jnp.float32)
    count = jnp.zeros(count_ref.shape, jnp.float32)
    for k in range(ids.shape[1]):
        count = count + jnp.where(ids[:, k : k + 1] == names, 1.0, 0.0)
    count_ref[...] = count
    copy.wait()


def attend_kernel(units_ref, table_ref, reach_ref, got_ref, res_ref, turned_ref, kv_ref, *refs):
    del units_ref
    parts, (sent_ref, near_ref) = refs[:-2][::-1], refs[-2:]
    slot_count = reach_ref.shape[0] // DRAFT
    sources = got_ref.shape[0]
    tok_dev = res_ref.shape[0]
    page_len = parts[0].shape[1] // slot_count
    per_slot = DRAFT // tok_dev
    group_size = HEADS // KV_HEADS
    f32, bf16 = jnp.float32, jnp.bfloat16
    lane_low = lax.broadcasted_iota(jnp.int32, (DRAFT, WIDE), 1) < HEAD
    rank = lax.axis_index("tp")
    side = lax.rem(rank, 2)
    within = lax.broadcasted_iota(jnp.int32, (1, page_len), 1)
    positions = []
    for k in range(len(parts)):
        pair = lax.bitwise_xor(lax.div(rank, 2), k)
        for page in (2 * pair + side, 2 * pair + 1 - side):
            positions.append(within + page * page_len)
    positions = jnp.concatenate(positions, axis=1)
    dims = (((1,), (1,)), ((), ()))
    scale = 1.0 / math.sqrt(HEAD)
    outs = []
    for s in range(slot_count):
        first = s * per_slot

        def part(k):
            low = k * tok_dev
            return jnp.concatenate(
                [got_ref[first + i, low : low + tok_dev, :] for i in range(per_slot)], axis=0
            )

        q_pair, q_last, tree_kv = part(0).astype(f32) * scale, part(1).astype(f32) * scale, part(2)
        q_rows = jnp.concatenate(
            [
                jnp.where(lane_low, q_pair, 0.0),
                jnp.where(lane_low, pltpu.roll(q_pair, HEAD, 1), 0.0),
                jnp.where(lane_low, q_last, 0.0),
            ],
            axis=0,
        ).astype(bf16)
        at = slice(s * page_len, (s + 1) * page_len)
        cache_kv = jnp.concatenate(
            [a for k, part in enumerate(parts) for a in (part[side, at, :], turned_ref[k * parts[0].shape[1] + at.start : k * parts[0].shape[1] + at.stop, :])],
            axis=0,
        )
        scores = lax.dot_general(q_rows, cache_kv, dims, preferred_element_type=f32)
        is_valid = positions < number(table_ref, 1 + s)
        scores = jnp.where(is_valid, scores, neg_big)
        reach = reach_ref[s * DRAFT : (s + 1) * DRAFT, s * DRAFT : (s + 1) * DRAFT]
        allowed = jnp.concatenate([reach] * group_size, axis=0) > 0.5
        tree_scores = lax.dot_general(q_rows, tree_kv, dims, preferred_element_type=f32)
        tree_scores = jnp.where(allowed, tree_scores, neg_big)
        top = jnp.maximum(
            jnp.max(scores, axis=1, keepdims=True), jnp.max(tree_scores, axis=1, keepdims=True)
        )
        weights = jnp.where(is_valid, jnp.exp(scores - top), 0.0).astype(bf16)
        tree_weights = jnp.where(allowed, jnp.exp(tree_scores - top), 0.0).astype(bf16)
        total = jnp.sum(weights.astype(f32), axis=1, keepdims=True) + jnp.sum(
            tree_weights.astype(f32), axis=1, keepdims=True
        )
        mixed = jnp.dot(weights, cache_kv, preferred_element_type=f32) + jnp.dot(
            tree_weights, tree_kv, preferred_element_type=f32
        )
        outs.append(mixed / total)
    pair_rows, last_rows = [], []
    for out in outs:
        head_out = [out[r * DRAFT : (r + 1) * DRAFT] for r in range(group_size)]
        pair_rows.append(
            jnp.where(lane_low, pltpu.roll(head_out[0], HEAD, 1), head_out[1]).astype(bf16)
        )
        last_rows.append(head_out[2])
    last = jnp.where(lane_low, pltpu.roll(last_rows[0], HEAD, 1), last_rows[1]).astype(bf16)
    res_tiles = [res_ref[:, c * WIDE : (c + 1) * WIDE] for c in range(res_ref.shape[1] // WIDE)]
    sent_ref[...] = jnp.concatenate(pair_rows + [last] + res_tiles, axis=0)
    rows = sent_ref.shape[0]
    near_ref[:rows, :] = sent_ref[...]
    near_ref[rows:, :] = kv_ref[...]


def accept_kernel(rows, chosen_ref, *refs):
    accepted_ref = refs[-1]
    tok_dev, width = accepted_ref.shape
    rank = lax.axis_index("tp")
    per_slot = DRAFT // tok_dev
    place = lax.rem(rank, per_slot)
    chosen = chosen_ref[lax.div(rank, per_slot), pl.ds(pl.multiple_of(place * tok_dev, tok_dev), tok_dev), :]
    is_even, is_first = lax.rem(place, 2) == 0, place < 2
    for c in range(width // WIDE):
        low = rows + c * tok_dev
        pairs = []
        for mine, other in (refs[:2], refs[2:4]):
            a, b = mine[low : low + tok_dev, :], other[low : low + tok_dev, :]
            pairs.append(
                jnp.concatenate([jnp.where(is_even, a, b), jnp.where(is_even, b, a)], axis=0)
            )
        near, far = pairs
        nodes = jnp.concatenate(
            [jnp.where(is_first, near, far), jnp.where(is_first, far, near)], axis=0
        )
        accepted_ref[:, c * WIDE : (c + 1) * WIDE] = jnp.dot(
            chosen, nodes, preferred_element_type=jnp.float32
        ).astype(jnp.bfloat16)


def fetch_kernel(picks, after_ref, source_ref, target_ref, sems):
    del after_ref
    rows = target_ref.shape[0] // len(picks)
    copies = []
    for place, k in enumerate(picks):
        pair = lax.bitwise_xor(lax.div(lax.axis_index("tp"), 2), k)
        start = pl.multiple_of(pair * rows, WIDE)
        copies.append(
            pltpu.make_async_copy(
                source_ref.at[pl.ds(start, rows)],
                target_ref.at[place * rows : (place + 1) * rows],
                sems.at[place],
            )
        )
    start_all(copies)


def join_heads(k, rows, group_rows, mine_ref, other_ref, residual_ref):
    f32, bf16 = jnp.float32, jnp.bfloat16
    half = group_rows // 2
    tok_dev = group_rows // KV_HEADS
    model = residual_ref.shape[1]
    res_start = group_rows + half
    rank = lax.axis_index("tp")
    is_even = lax.rem(rank, 2) == 0
    pair = lax.bitwise_xor(lax.div(rank, 2), k)
    lane_low = lax.broadcasted_iota(jnp.int32, (half, WIDE), 1) < HEAD
    mine, other = mine_ref[:rows, :], other_ref[:rows, :]
    even, odd = jnp.where(is_even, mine, other), jnp.where(is_even, other, mine)
    last_even = even[group_rows:res_start].astype(f32)
    last_odd = odd[group_rows:res_start].astype(f32)
    odd_swapped = pltpu.roll(odd[:group_rows].astype(f32), HEAD, 1)
    middle = jnp.concatenate(
        [
            jnp.where(lane_low, last_even, odd_swapped[:half]),
            jnp.where(lane_low, pltpu.roll(last_even, HEAD, 1), odd_swapped[half:]),
        ],
        axis=0,
    ).astype(bf16)
    end = jnp.concatenate(
        [
            jnp.where(lane_low, odd_swapped[:half], pltpu.roll(last_odd, HEAD, 1)),
            jnp.where(lane_low, odd_swapped[half:], last_odd),
        ],
        axis=0,
    ).astype(bf16)
    for q, block in enumerate((even, odd)):
        row = pl.multiple_of((2 * pair + q) * tok_dev, tok_dev)
        residual_ref[pl.ds(row, tok_dev), :] = jnp.concatenate(
            [
                block[res_start + c * tok_dev : res_start + (c + 1) * tok_dev]
                for c in range(model // WIDE)
            ],
            axis=1,
        ).astype(f32)
    return jnp.concatenate([even[:group_rows], middle, end], axis=1)


def keep_own(k, heads_ref, at, attn_ref):
    tok_dev = attn_ref.shape[0]
    width = attn_ref.shape[1] * 2 // KV_HEADS
    rank = lax.axis_index("tp")
    pair = lax.bitwise_xor(lax.div(rank, 2), k)
    own = pl.multiple_of(rank * tok_dev, tok_dev)
    attn_ref[:, pl.ds(pl.multiple_of(pair * width, WIDE), width)] = heads_ref[
        pl.ds(own, tok_dev), at : at + width
    ]


def early_kernel(rows, after_ref, down_hbm, weight_ref, *refs):
    del after_ref
    blocks, refs = refs[:-6], refs[-6:]
    hid_ref, attn_ref, down_ref, residual_ref, x_ref, sem = refs
    start = down_hbm.shape[0] - down_ref.shape[0]
    copy = pltpu.make_async_copy(down_hbm.at[start:], down_ref, sem)
    copy.start()
    group_rows = hid_ref.shape[0]
    residual_ref[...] = jnp.zeros_like(residual_ref)
    width = x_ref.shape[1] * 2 // len(blocks)
    for k in range(len(blocks) // 2):
        x_ref[:, k * width : (k + 1) * width] = join_heads(
            k, rows, group_rows, blocks[2 * k], blocks[2 * k + 1], residual_ref
        )
    for k in range(len(blocks) // 2):
        keep_own(k, x_ref, k * width, attn_ref)
    hid_ref[...] = residual_ref[...] + jnp.dot(
        x_ref[...], weight_ref[...], preferred_element_type=jnp.float32
    )
    copy.wait()


def expert_kernel(
    rows, count_ref, router_ref, gain_ref, down_ref, rest_ref, before_ref, part_ref, *refs
):
    refs, late = refs[:-8], refs[-8:]
    far_ref, hid_ref, hidden_ref, attn_ref, x_ref, normed_ref, share_ref, residual_ref = late
    f32, bf16 = jnp.float32, jnp.bfloat16
    pairs = KV_HEADS // 2
    first = pairs // 2
    blocks, refs = refs[: 2 * (pairs - first)], refs[2 * (pairs - first) :]
    weight_refs, unit_refs = refs[: pairs - first], refs[pairs - first :]
    unit_weights = [(ref, k) for ref in unit_refs for k in range(ref.shape[0])]
    units = len(unit_weights)
    tok_dev, model = hidden_ref.shape
    sources = KV_HEADS
    group_rows = sources * tok_dev
    rank = lax.axis_index("tp")
    own = pl.multiple_of(rank * tok_dev, tok_dev)
    attn_ref[...] = part_ref[...]
    residual_ref[...] = jnp.zeros_like(residual_ref)
    hidden, width = before_ref[...], x_ref.shape[1] // (pairs - first)
    for q, k in enumerate(reversed(range(first, pairs))):
        heads = join_heads(k, rows, group_rows, blocks[2 * q], blocks[2 * q + 1], residual_ref)
        x_ref[:, q * width : (q + 1) * width] = heads
        keep_own(k, x_ref, q * width, attn_ref)
        hidden += jnp.dot(heads, weight_refs[q][...], preferred_element_type=f32)
    hidden += residual_ref[...]
    hid_ref[...] = hidden
    gain = jnp.concatenate([gain_ref[c : c + 1, :] for c in range(model // WIDE)], axis=1)
    scale = lax.rsqrt(jnp.mean(hidden * hidden, axis=1, keepdims=True) + norm_eps)
    normed_ref[...] = (hidden * scale * gain).astype(bf16)
    hidden_ref[...] = hid_ref[pl.ds(own, tok_dev), :]
    logits = lax.dot_general(
        normed_ref[...], router_ref[...], (((1,), (1,)), ((), ())), preferred_element_type=f32
    )
    experts = router_ref.shape[0]
    expert_range = lax.broadcasted_iota(jnp.int32, (group_rows, experts), 1)
    count = count_ref[...]
    expo = jnp.where(count > 0.0, jnp.exp(logits), 0.0) * count
    routing = expo / jnp.sum(expo, axis=1, keepdims=True)
    unit_width = unit_refs[0].shape[2] // 2
    span = FF_E // unit_width
    each = span if units % span == 0 else 1
    for u in range(0, units, each):
        expert = (rank * units + u) // span
        share = jnp.sum(jnp.where(expert_range == expert, routing, 0.0), axis=1, keepdims=True)
        share_ref[u : u + each] = jnp.broadcast_to(share[None], (each, group_rows, unit_width))

    def one_unit(u):
        ref, k = unit_weights[u]
        both = jnp.dot(normed_ref[...], ref[k], preferred_element_type=f32)
        gate, up = both[:, :unit_width], both[:, unit_width:]
        return (gate / (1.0 + jnp.exp(-gate)) * up * share_ref[u]).astype(bf16)

    ready = down_ref.shape[0] // STEP
    for i in range(units // STEP):
        act = jnp.concatenate([one_unit(i * STEP + k) for k in range(STEP)], axis=1)
        ref, at = (down_ref, i) if i < ready else (rest_ref, i - ready)
        down = ref[at * STEP : (at + 1) * STEP].reshape(STEP * unit_width, model)
        part = jnp.dot(act, down, preferred_element_type=f32)
        hid_ref[...] = part if i == 0 else hid_ref[...] + part
    for k in range(far_ref.shape[0]):
        copy_sums(sources // 4 + k, True, hid_ref, far_ref.at[k])


def copy_sums(k, crossing, hid_ref, ref):
    tok_dev = ref.shape[0]
    rank = lax.axis_index("tp")
    side = lax.rem(rank, 2)
    pair = lax.bitwise_xor(lax.div(rank, 2), k)
    target = 2 * pair + (1 - side if crossing else side)
    row = pl.multiple_of(target * tok_dev, tok_dev)
    ref[...] = hid_ref[pl.ds(row, tok_dev), :].astype(ref.dtype)


def near_kernel(hid_ref, mine_ref, near_ref):
    for k in range(mine_ref.shape[0]):
        copy_sums(k, False, hid_ref, mine_ref.at[k])
    for k in range(near_ref.shape[0]):
        copy_sums(k, True, hid_ref, near_ref.at[k])


def fold_kernel(first, after_ref, mine_ref, got_ref, hidden_ref, *sent_refs):
    del after_ref
    for k, ref in enumerate(sent_refs, first):
        total = mine_ref[k] + got_ref[k - first].astype(jnp.float32)
        if k == 0:
            total = total + hidden_ref[...]
        ref[...] = total.astype(ref.dtype)


def finish_kernel(attn_in_ref, accepted_in_ref, *refs):
    parts, (attn_ref, layer_ref, accepted_ref) = refs[:-3], refs[-3:]
    attn_ref[...] = attn_in_ref[...]
    accepted_ref[...] = accepted_in_ref[...]
    total = parts[0][...]
    for part in parts[1:]:
        total = total + part[...].astype(jnp.float32)
    layer_ref[...] = total.astype(jnp.bfloat16)


def in_hbm(*arrays):
    return tuple(pltpu.with_memory_space_constraint(a, pltpu.HBM) for a in arrays)


def spaces(text):
    kinds = {"a": pl.ANY, "v": pltpu.VMEM}
    return [pl.BlockSpec(memory_space=kinds[c]) for c in text]


def params(mebibytes=12):
    return pltpu.CompilerParams(vmem_limit_bytes=mebibytes << 20)


def cost(mebibytes):
    return pl.CostEstimate(flops=0, transcendentals=0, bytes_accessed=mebibytes << 20)


def swap(rows, mask):
    count = lax.axis_size("tp")
    return lax.ppermute(rows, "tp", [(i, i ^ mask) for i in range(count)])


def fetch(after, array, rows, picks):
    shape = (rows * len(picks),) + array.shape[1:]
    return pl.pallas_call(
        functools.partial(fetch_kernel, picks),
        out_shape=pltpu.VMEM(shape, array.dtype),
        in_specs=spaces("aa"),
        out_specs=spaces("v")[0],
        scratch_shapes=[pltpu.SemaphoreType.DMA((len(picks),))],
        compiler_params=params(),
        cost_estimate=cost(2 * math.prod(shape) >> 20),
        name="fetch",
    )(after, *in_hbm(array))


def per_device_packed(
    queries,
    new_kv,
    residual,
    placement,
    lengths,
    page_table,
    cache_keys,
    cache_values,
    parents,
    accept_leaf,
    out_weight,
    norm_gain,
    router_weight,
    expert_ids,
    gate_up,
    down_weight,
):
    f32, bf16 = jnp.float32, jnp.bfloat16
    tok_dev, model = residual.shape
    tp_count = lax.axis_size("tp")
    slot_count = placement.shape[0]
    page_len, kv_width = cache_keys.shape[1:]
    group_rows = tok_dev * tp_count
    sent = lambda rows: jax.ShapeDtypeStruct((tp_count, rows, WIDE), bf16)
    dma = pltpu.SemaphoreType.DMA
    slots_smem = pltpu.SMEM((slot_count,), jnp.int32)
    pairs = tp_count // 2
    part = jax.ShapeDtypeStruct((2, slot_count * page_len, WIDE), bf16)
    loaded = (
        page_table.reshape(slot_count),
        placement,
        lengths,
        accept_leaf,
        cache_keys,
        cache_values,
        queries,
        new_kv,
        residual,
        parents,
        router_weight.T,
        expert_ids.T,
        norm_gain.reshape(model // WIDE, WIDE),
    )
    *parts, joined, table, parents, router, ids, gain = pl.pallas_call(
        functools.partial(split_kernel, pairs),
        out_shape=(part,) * pairs
        + (
            jax.ShapeDtypeStruct((tok_dev, 2 * (model + kv_width)), bf16),
            pltpu.VMEM((8, WIDE), f32),
        )
        + tuple(pltpu.VMEM(a.shape, a.dtype) for a in loaded[9:]),
        in_specs=spaces("a" * len(loaded)),
        out_specs=tuple(spaces("v" * (pairs + 6))),
        scratch_shapes=[
            slots_smem,
            slots_smem,
            slots_smem,
            slots_smem,
            pltpu.VMEM(cache_keys.shape, bf16),
            pltpu.VMEM(cache_values.shape, bf16),
            pltpu.VMEM((pairs,) + part.shape, bf16),
            dma((len(loaded),)),
        ],
        compiler_params=params(),
        cost_estimate=cost(4),
        name="split",
    )(*in_hbm(*loaded))
    parts = parts[::-1]
    parts = [parts[0]] + [swap(parts[k], 2 * k) for k in range(1, pairs)]
    pulled = lax.all_gather(joined, "req", axis=0)
    nodes = slot_count * DRAFT
    units = gate_up.shape[0]
    ready = READY * units // 20 // STEP * STEP
    down_ready, reach, chosen, count = pl.pallas_call(
        tree_kernel,
        out_shape=(
            pltpu.VMEM((ready,) + down_weight.shape[1:], bf16),
            jax.ShapeDtypeStruct((nodes, nodes), f32),
            jax.ShapeDtypeStruct((slot_count, DRAFT, DRAFT), bf16),
            jax.ShapeDtypeStruct((group_rows, router_weight.shape[1]), f32),
        ),
        in_specs=spaces("aavvv"),
        out_specs=tuple(spaces("vvvv")),
        scratch_shapes=[dma],
        compiler_params=params(),
        cost_estimate=cost(8),
        name="tree",
    )(pulled, *in_hbm(down_weight), table, parents, ids)
    kv_rows = 2 * kv_width // WIDE * tok_dev
    packed, own_res, turned, own_kv = pl.pallas_call(
        functools.partial(route_kernel, kv_width),
        out_shape=(
            sent(3 * tok_dev),
            jax.ShapeDtypeStruct(residual.shape, bf16),
            jax.ShapeDtypeStruct((pairs * part.shape[1], WIDE), bf16),
            jax.ShapeDtypeStruct((kv_rows, WIDE), bf16),
        ),
        in_specs=spaces("avv" + "v" * pairs),
        out_specs=tuple(spaces("vvvv")),
        compiler_params=params(),
        cost_estimate=cost(4),
        name="route",
    )(down_ready, table, pulled, *parts[::-1])
    turned = swap(turned, 1)
    packed = lax.all_to_all(packed, "tp", 0, 0, tiled=True)
    gate_up = pltpu.with_memory_space_constraint(gate_up, pltpu.VMEM)
    block_rows = group_rows + group_rows // 2 + (model // WIDE) * tok_dev
    block, near_block = pl.pallas_call(
        attend_kernel,
        out_shape=(
            jax.ShapeDtypeStruct((block_rows, WIDE), bf16),
            jax.ShapeDtypeStruct((block_rows + kv_rows, WIDE), bf16),
        ),
        in_specs=spaces("v" * (7 + pairs)),
        out_specs=tuple(spaces("vv")),
        compiler_params=params(),
        cost_estimate=cost(8),
        name="attend",
    )(gate_up, table, reach, packed, own_res, turned, own_kv, *parts[::-1])
    reached = [swap(near_block, 2)] + [swap(block, 2 * k) for k in range(2, pairs)]
    weights, after = [], block
    rows = out_weight.shape[0] // pairs
    for k, picks in zip(ORDER, FETCHES):
        weight = fetch(after, out_weight, rows, picks)
        reached[k - 1], weight = lax.optimization_barrier((reached[k - 1], weight))
        after = reached[k - 1]
        weights.append(weight)
    blocks = [block, swap(near_block, 1)]
    blocks += [a for got in reached for a in (got, swap(got, 1))]
    before, attn_part, down_rest = pl.pallas_call(
        functools.partial(early_kernel, block_rows),
        out_shape=(
            jax.ShapeDtypeStruct((group_rows, model), f32),
            pltpu.VMEM(queries.shape, bf16),
            pltpu.VMEM((units - ready,) + down_weight.shape[1:], bf16),
        ),
        in_specs=spaces("aav" + "v" * pairs),
        out_specs=tuple(spaces("vvv")),
        scratch_shapes=[
            pltpu.VMEM((group_rows, model), f32),
            pltpu.VMEM((group_rows, HEADS * HEAD // 2), bf16),
            dma,
        ],
        compiler_params=params(),
        cost_estimate=cost(4),
        name="early",
    )(after, *in_hbm(down_weight), weights[0], *blocks[:pairs])
    accepted = pl.pallas_call(
        functools.partial(accept_kernel, block_rows),
        out_shape=pltpu.VMEM(new_kv.shape, bf16),
        in_specs=spaces("vvvvv"),
        out_specs=spaces("v")[0],
        compiler_params=params(),
        cost_estimate=cost(1),
        name="accept",
    )(chosen, near_block, *blocks[1:4])
    unit_weights = (gate_up,)
    far, sums, hidden, attn_own = pl.pallas_call(
        functools.partial(expert_kernel, block_rows),
        out_shape=(
            jax.ShapeDtypeStruct((pairs // 2, tok_dev, model), bf16),
            jax.ShapeDtypeStruct((group_rows, model), f32),
            jax.ShapeDtypeStruct((tok_dev, model), f32),
            pltpu.VMEM(queries.shape, bf16),
        ),
        in_specs=spaces("v" * (7 + pairs + pairs // 2 + len(unit_weights))),
        out_specs=tuple(spaces("vvvv")),
        scratch_shapes=[
            pltpu.VMEM((group_rows, HEADS * HEAD // 2), bf16),
            pltpu.VMEM((group_rows, model), bf16),
            pltpu.VMEM((units, group_rows, gate_up.shape[2] // 2), f32),
            pltpu.VMEM((group_rows, model), f32),
        ],
        compiler_params=params(),
        name="experts",
    )(
        count,
        router,
        gain,
        down_ready,
        down_rest,
        before,
        attn_part,
        *[a for k in reversed(range(pairs // 2, pairs)) for a in blocks[2 * k : 2 * k + 2]],
        weights[1],
        weights[2],
        *unit_weights,
    )
    far = swap(far, 1)
    mine, near = pl.pallas_call(
        near_kernel,
        out_shape=(
            jax.ShapeDtypeStruct((pairs, tok_dev, model), f32),
            jax.ShapeDtypeStruct((pairs // 2, tok_dev, model), bf16),
        ),
        in_specs=spaces("v"),
        out_specs=tuple(spaces("vv")),
        compiler_params=params(),
        cost_estimate=cost(4),
        name="near",
    )(sums)
    near = swap(near, 1)
    fold = lambda first, after, got: pl.pallas_call(
        functools.partial(fold_kernel, first),
        out_shape=tuple(
            jax.ShapeDtypeStruct((tok_dev, model), f32 if k == 0 else bf16)
            for k in range(first, first + pairs // 2)
        ),
        in_specs=spaces("avvv"),
        out_specs=tuple(spaces("v" * (pairs // 2))),
        compiler_params=params(),
        cost_estimate=cost(1),
        name="fold",
    )(after, mine, got, hidden)
    sums = fold(pairs // 2, hidden, far)
    folded = sums[0]
    sums = [swap(a, 2 * k) for k, a in enumerate(sums, pairs // 2)]
    close = fold(0, folded, near)
    sums = [close[0]] + [swap(close[k], 2 * k) for k in range(1, pairs // 2)] + sums
    return pl.pallas_call(
        finish_kernel,
        out_shape=(
            jax.ShapeDtypeStruct(queries.shape, bf16),
            jax.ShapeDtypeStruct(residual.shape, bf16),
            jax.ShapeDtypeStruct(new_kv.shape, bf16),
        ),
        in_specs=spaces("v" * (2 + pairs)),
        out_specs=tuple(spaces("vvv")),
        compiler_params=params(),
        name="finish",
    )(attn_own, accepted, sums[0], *sums[:0:-1])


def per_device(queries, new_kv, residual, placement, *rest):
    tok_dev = queries.shape[0]
    one_head_each = lax.axis_size("tp") == KV_HEADS
    whole_tiles = tok_dev % 16 == 0 and placement.shape[0] == 2 and tok_dev * KV_HEADS == 2 * DRAFT
    if one_head_each and whole_tiles and rest[1].shape[1] == 1:
        return per_device_packed(queries, new_kv, residual, placement, *rest)
    return per_device_plain(queries, new_kv, residual, placement, *rest)


def solution(mesh):
    in_specs = (
        P(("req", "tp"), None),
        P(("req", "tp"), None),
        P(("req", "tp"), None),
        P("req"),
        P("req"),
        P("req", None, "tp"),
        P(("req", "tp"), None, None),
        P(("req", "tp"), None, None),
        P("req", None),
        P("req"),
        P(),
        P(),
        P(),
        P("req", None),
        P("tp", None, None),
        P("tp", None, None),
    )
    out_specs = (P(("req", "tp"), None), P(("req", "tp"), None), P(("req", "tp"), None))
    return jax.shard_map(
        per_device, mesh=mesh, in_specs=in_specs, out_specs=out_specs, check_vma=False
    )
```

```python
import functools
import math

import jax
import jax.numpy as jnp
from jax import lax
from jax.experimental import pallas as pl
from jax.experimental.pallas import tpu as pltpu
from jax.sharding import PartitionSpec as P

HEADS = 24
KV_HEADS = 8
HEAD = 64
FF_E = 512
UNIT = 128
DRAFT = 64
WIDE = 128
STEP = 2
CUTS = (6, 8, 10, 12)
ORDER = (1, 3, 2)
FETCHES = ((0, 1), (3,), (2,))


neg_big = -1e30
norm_eps = 1e-06


def joined_2(part, axis, combine):
    gathered = jax.tree.map(lambda a: lax.all_gather(a, axis), part)

    def take(source):
        return jax.tree.map(lambda a: lax.dynamic_index_in_dim(a, source, 0, False), gathered)

    return lax.fori_loop(
        1, lax.axis_size(axis), lambda source, state: combine(state, take(source)), take(0)
    )


def ancestry(parents):
    node_count = parents.shape[-1]
    node_ids = jnp.arange(node_count, dtype=jnp.int32)
    linked = (parents[:, :, None] == node_ids[None, None, :]) & (node_ids[None, :, None] > 0)
    reached = jnp.maximum(linked.astype(jnp.float32), jnp.eye(node_count, dtype=jnp.float32)[None])
    for _ in range(node_count.bit_length()):
        reached = jnp.minimum(
            jnp.einsum("rnm,rmk->rnk", reached, reached, precision=lax.Precision.HIGHEST), 1.0
        )
    return reached


def combine_stats(left_stats, right_stats):
    left_max, left_sum, left_out = left_stats
    right_max, right_sum, right_out = right_stats
    top_score = jnp.maximum(left_max, right_max)
    left_scale = jnp.exp(left_max - top_score)
    right_scale = jnp.exp(right_max - top_score)
    row_count, head_count = left_max.shape
    out_sum = (
        left_out.reshape(row_count, head_count, -1) * left_scale[..., None]
        + right_out.reshape(row_count, head_count, -1) * right_scale[..., None]
    )
    return (
        top_score,
        left_sum * left_scale + right_sum * right_scale,
        out_sum.reshape(row_count, -1),
    )


def finish_rows(stat_sum, stat_out):
    row_count, head_count = stat_sum.shape
    return (
        (stat_out.reshape(row_count, head_count, -1) / stat_sum[..., None])
        .reshape(row_count, -1)
        .astype(jnp.bfloat16)
    )


def project_rows(attn_rows, res_rows, out_weight):
    return res_rows.astype(jnp.float32) + jnp.dot(
        attn_rows, out_weight, preferred_element_type=jnp.float32
    )


def rms_normed(hidden, norm_gain):
    scale_rows = lax.rsqrt(jnp.mean(hidden * hidden, axis=-1, keepdims=True) + norm_eps)
    return (hidden * scale_rows * norm_gain).astype(jnp.bfloat16)


def unit_shares(normed_all, router_weight, expert_ids, tp_rank, units_dev):
    logits = jnp.dot(normed_all, router_weight, preferred_element_type=jnp.float32)
    expert_range = jnp.arange(router_weight.shape[1], dtype=jnp.int32)
    onehot = (expert_ids[:, :, None] == expert_range[None, None, :]).astype(jnp.float32)
    chosen = jnp.sum(logits[:, None, :] * onehot, axis=-1)
    expo_chosen = jnp.exp(chosen)
    expert_probs = expo_chosen / jnp.sum(expo_chosen, axis=-1, keepdims=True)
    routing = jnp.sum(expert_probs[:, :, None] * onehot, axis=1)
    unit_ids = tp_rank * units_dev + jnp.arange(units_dev, dtype=jnp.int32)
    expert_of_unit = unit_ids // (FF_E // UNIT)
    pick = (expert_range[:, None] == expert_of_unit[None, :]).astype(jnp.float32)
    return jnp.dot(routing, pick, precision=lax.Precision.HIGHEST)


def per_device_plain(
    queries,
    new_kv,
    residual,
    placement,
    lengths,
    page_table,
    cache_keys,
    cache_values,
    parents,
    accept_leaf,
    out_weight,
    norm_gain,
    router_weight,
    expert_ids,
    gate_up,
    down_weight,
):
    tok_dev = queries.shape[0]
    tp_count = lax.axis_size("tp")
    tp_rank = lax.axis_index("tp")
    group_rows = tok_dev * tp_count
    slot_count = placement.shape[0]
    kv_width = cache_keys.shape[2]
    page_len = cache_keys.shape[1]
    group_size = HEADS // KV_HEADS
    score_scale = 1.0 / math.sqrt(HEAD)
    row_start = tp_rank * tok_dev
    pulled_q, pulled_kv, pulled_res = (
        lax.all_gather(queries, "req", axis=0, tiled=True),
        lax.all_gather(new_kv, "req", axis=0, tiled=True),
        lax.all_gather(residual, "req", axis=0, tiled=True),
    )
    row_offsets = jnp.arange(tok_dev, dtype=jnp.int32)
    row_pos = row_start + row_offsets
    row_slot = row_pos // DRAFT
    slot_match = row_slot[:, None] == jnp.arange(slot_count, dtype=jnp.int32)[None, :]
    source_group = jnp.sum(jnp.where(slot_match, placement[None, :] // slot_count, 0), axis=1)
    source_rows = source_group * tok_dev + row_offsets
    own_q = jnp.take(pulled_q, source_rows, axis=0)
    own_kv = jnp.take(pulled_kv, source_rows, axis=0)
    own_res = jnp.take(pulled_res, source_rows, axis=0)
    all_q, all_kv = (
        lax.all_gather(own_q, "tp", axis=0, tiled=True),
        lax.all_gather(own_kv, "tp", axis=0, tiled=True),
    )
    local_pages = page_table.shape[1]
    page_ids = page_table[:, :, 0].reshape(-1)
    keys_local = jnp.take(cache_keys, page_ids, axis=0).reshape(
        slot_count, local_pages, page_len, KV_HEADS, HEAD
    )
    values_local = jnp.take(cache_values, page_ids, axis=0).reshape(
        slot_count, local_pages, page_len, KV_HEADS, HEAD
    )
    query_blocks = all_q.reshape(slot_count, DRAFT, KV_HEADS, group_size, HEAD)
    scores = (
        jnp.einsum(
            "sqgrd,sltgd->sqgrlt", query_blocks, keys_local, preferred_element_type=jnp.float32
        )
        * score_scale
    )
    positions = (
        jnp.arange(local_pages, dtype=jnp.int32)[:, None] * tp_count + tp_rank
    ) * page_len + jnp.arange(page_len, dtype=jnp.int32)[None, :]
    is_valid = (positions[None] < lengths[:, None, None])[:, None, None, None]
    scores = jnp.where(is_valid, scores, neg_big)
    block_max = jnp.max(scores, axis=-1)
    weights = jnp.where(is_valid, jnp.exp(scores - block_max[..., None]), 0.0).astype(jnp.bfloat16)
    block_sum = jnp.sum(weights.astype(jnp.float32), axis=-1)
    block_out = jnp.einsum(
        "sqgrlt,sltgd->sqgrld", weights, values_local, preferred_element_type=jnp.float32
    )
    page_top = jnp.max(block_max, axis=-1)
    page_scale = jnp.exp(block_max - page_top[..., None])
    stat_max = page_top.reshape(group_rows, HEADS)
    stat_sum = jnp.sum(block_sum * page_scale, axis=-1).reshape(group_rows, HEADS)
    stat_out = jnp.sum(block_out * page_scale[..., None], axis=-2).reshape(group_rows, HEADS * HEAD)
    reached = ancestry(parents)
    reach_rows = jnp.take(reached.reshape(slot_count * DRAFT, DRAFT), row_pos, axis=0)
    key_slot = jnp.arange(group_rows, dtype=jnp.int32) // DRAFT
    same_slot = key_slot[None, :] == row_slot[:, None]
    allowed = same_slot & (jnp.tile(reach_rows, (1, slot_count)) > 0.5)
    tree_keys = all_kv[:, :kv_width].reshape(group_rows, KV_HEADS, HEAD)
    tree_values = all_kv[:, kv_width:].reshape(group_rows, KV_HEADS, HEAD)
    own_blocks = own_q.reshape(tok_dev, KV_HEADS, group_size, HEAD)
    tree_scores = (
        jnp.einsum("igrd,kgd->igrk", own_blocks, tree_keys, preferred_element_type=jnp.float32)
        * score_scale
    )
    tree_mask = allowed[:, None, None, :]
    tree_scores = jnp.where(tree_mask, tree_scores, neg_big)
    tree_max = jnp.max(tree_scores, axis=-1)
    tree_weights = jnp.where(tree_mask, jnp.exp(tree_scores - tree_max[..., None]), 0.0).astype(
        jnp.bfloat16
    )
    tree_sum = jnp.sum(tree_weights.astype(jnp.float32), axis=-1)
    tree_out = jnp.einsum(
        "igrk,kgd->igrd", tree_weights, tree_values, preferred_element_type=jnp.float32
    )
    own_stats = (
        lax.dynamic_slice_in_dim(stat_max, row_start, tok_dev, 0),
        lax.dynamic_slice_in_dim(stat_sum, row_start, tok_dev, 0),
        lax.dynamic_slice_in_dim(stat_out, row_start, tok_dev, 0),
    )
    tree_stats = (
        tree_max.reshape(tok_dev, HEADS),
        tree_sum.reshape(tok_dev, HEADS),
        tree_out.reshape(tok_dev, HEADS * HEAD),
    )
    joined = combine_stats(own_stats, tree_stats)
    stat_max = lax.dynamic_update_slice_in_dim(stat_max, joined[0], row_start, 0)
    stat_sum = lax.dynamic_update_slice_in_dim(stat_sum, joined[1], row_start, 0)
    stat_out = lax.dynamic_update_slice_in_dim(stat_out, joined[2], row_start, 0)
    normed_all = None
    merged = joined_2((stat_max, stat_sum, stat_out), "tp", combine_stats)
    attn_own = finish_rows(
        lax.dynamic_slice_in_dim(merged[1], row_start, tok_dev, 0),
        lax.dynamic_slice_in_dim(merged[2], row_start, tok_dev, 0),
    )
    hidden_own = project_rows(attn_own, own_res, out_weight)
    normed_own = rms_normed(hidden_own, norm_gain)
    units_dev = gate_up.shape[0]
    unit_width = gate_up.shape[2] // 2
    normed_all = lax.all_gather(normed_own, "tp", axis=0, tiled=True)
    shares = unit_shares(normed_all, router_weight, expert_ids, tp_rank, units_dev)
    gate_both = jnp.einsum("td,udh->tuh", normed_all, gate_up, preferred_element_type=jnp.float32)
    activated = (
        jax.nn.silu(gate_both[..., :unit_width]) * gate_both[..., unit_width:] * shares[:, :, None]
    ).astype(jnp.bfloat16)
    moe_own = lax.psum_scatter(
        jnp.einsum("tuh,uhd->td", activated, down_weight, preferred_element_type=jnp.float32),
        "tp",
        scatter_dimension=0,
        tiled=True,
    )
    layer_out = (hidden_own + moe_own).astype(jnp.bfloat16)
    node_ids = jnp.arange(DRAFT, dtype=jnp.int32)
    leaf_pick = (accept_leaf[:, None] == node_ids[None, :]).astype(jnp.float32)
    path_weight = jnp.einsum("sn,snk->sk", leaf_pick, reached, precision=lax.Precision.HIGHEST)
    path_flags = (path_weight > 0.5).astype(jnp.int32)
    path_rank = jnp.cumsum(path_flags, axis=1) - 1
    chosen_node = (path_flags[:, None, :] > 0) & (path_rank[:, None, :] == node_ids[None, :, None])
    own_choice = jnp.take(chosen_node.reshape(slot_count * DRAFT, DRAFT), row_pos, axis=0)
    spread = same_slot & jnp.tile(own_choice, (1, slot_count))
    accepted = jnp.dot(
        spread.astype(jnp.bfloat16), all_kv, preferred_element_type=jnp.float32
    ).astype(jnp.bfloat16)
    return (attn_own, layer_out, accepted)


def start_all(copies):
    for copy in copies:
        copy.start()
    for copy in copies:
        copy.wait()


def split_kernel(pairs, *refs):
    (
        pages_hbm, placement_hbm, lengths_hbm, leaf_hbm, keys_hbm, values_hbm, queries_hbm,
        new_kv_hbm, residual_hbm, parents_hbm, router_hbm, ids_hbm, gain_hbm,
    ) = refs[:13]
    parts, refs = refs[13 : 13 + pairs], refs[13 + pairs :]
    joined_ref, table_ref, parents_ref, router_ref, ids_ref, gain_ref = refs[:6]
    pages_ref, placement_ref, lengths_ref, leaf_ref, keys_ref, values_ref, split_ref, sems = refs[6:]
    slot_count = pages_ref.shape[0]
    page_len = keys_ref.shape[1]
    tok_dev = joined_ref.shape[0]
    moves = [
        (pages_hbm, pages_ref),
        (keys_hbm, keys_ref),
        (values_hbm, values_ref),
        (placement_hbm, placement_ref),
        (lengths_hbm, lengths_ref),
        (leaf_hbm, leaf_ref),
        (parents_hbm, parents_ref),
        (router_hbm, router_ref),
        (ids_hbm, ids_ref),
        (gain_hbm, gain_ref),
    ]
    column = 0
    for source in (queries_hbm, new_kv_hbm, residual_hbm):
        moves.append((source, joined_ref.at[:, column : column + source.shape[1]]))
        column += source.shape[1]
    start_all(
        [pltpu.make_async_copy(a, b, sems.at[k]) for k, (a, b) in enumerate(moves)]
    )
    slot = lax.div(lax.axis_index("tp") * tok_dev, DRAFT)
    numbers = [lax.div(placement_ref[slot], slot_count)]
    numbers += [lengths_ref[s] for s in range(slot_count)]
    numbers += [leaf_ref[s] for s in range(slot_count)]
    for row, number in enumerate(numbers):
        table_ref[row : row + 1, :] = jnp.full((1, WIDE), number, jnp.int32).astype(jnp.float32)
    for head in range(KV_HEADS):
        low = head * HEAD
        for s in range(slot_count):
            page = pages_ref[s]
            split_ref[head // 2, head % 2, s * page_len : (s + 1) * page_len, :] = jnp.concatenate(
                [keys_ref[page, :, low : low + HEAD], values_ref[page, :, low : low + HEAD]], axis=1
            )
    pair = lax.div(lax.axis_index("tp"), 2)
    for k, part in enumerate(parts):
        part[...] = split_ref[lax.bitwise_xor(pair, pairs - 1 - k)]


def number(table_ref, row):
    return jnp.max(table_ref[row : row + 1, :]).astype(jnp.int32)


def route_kernel(kv_width, after_ref, weight_hbm, table_ref, pulled_ref, *refs):
    del after_ref, weight_hbm
    parts, (sent_ref, res_ref, turned_ref, kv_ref) = refs[:-4][::-1], refs[-4:]
    rank = lax.axis_index("tp")
    other = 1 - lax.rem(rank, 2)
    size = parts[0].shape[1]
    for k, part in enumerate(parts):
        turned_ref[k * size : (k + 1) * size, :] = part[other]
    q_width = HEADS * HEAD
    tok_dev = pulled_ref.shape[1]
    rows = pulled_ref[number(table_ref, 0)]
    res_ref[...] = rows[:, q_width + 2 * kv_width :]
    tiles = [rows[:, q_width + c : q_width + c + WIDE] for c in range(0, 2 * kv_width, WIDE)]
    kv_ref[...] = jnp.concatenate(tiles, axis=0)
    head_rows = (HEADS // KV_HEADS) * HEAD
    tail = jnp.zeros((tok_dev, 2 * WIDE - head_rows), rows.dtype)
    for head in range(KV_HEADS):
        q_low = head * head_rows
        pair = jnp.concatenate([rows[:, q_low : q_low + head_rows], tail], axis=1)
        sent_ref[head, :tok_dev, :] = pair[:, :WIDE]
        sent_ref[head, tok_dev : 2 * tok_dev, :] = pair[:, WIDE:]
        k_low = q_width + head * HEAD
        sent_ref[head, 2 * tok_dev :, :] = jnp.concatenate(
            [rows[:, k_low : k_low + HEAD], rows[:, k_low + kv_width : k_low + kv_width + HEAD]],
            axis=1,
        )


def ancestor_rows(parents_ref):
    slot_count = parents_ref.shape[0]
    total = slot_count * DRAFT
    row = jnp.concatenate(
        [parents_ref[s : s + 1, :] + s * DRAFT for s in range(slot_count)], axis=1
    )
    from_ids = lax.broadcasted_iota(jnp.int32, (total, total), 0)
    to_ids = lax.broadcasted_iota(jnp.int32, (total, total), 1)
    linked = (from_ids == jnp.broadcast_to(row, (total, total))) & (lax.rem(to_ids, DRAFT) > 0)
    reached = jnp.where(linked | (from_ids == to_ids), 1.0, 0.0)
    for _ in range((DRAFT - 1).bit_length()):
        half = reached.astype(jnp.bfloat16)
        reached = jnp.minimum(jnp.dot(half, half, preferred_element_type=jnp.float32), 1.0)
    return reached.T


def tree_kernel(
    after_ref, down_hbm, table_ref, parents_ref, ids_ref, down_ref, reach_ref, chosen_ref,
    count_ref, sem,
):
    del after_ref
    copy = pltpu.make_async_copy(down_hbm.at[: down_ref.shape[0]], down_ref, sem)
    copy.start()
    slot_count = parents_ref.shape[0]
    reach_ref[...] = ancestor_rows(parents_ref)
    node_from = lax.broadcasted_iota(jnp.int32, (DRAFT, DRAFT), 0)
    node_to = lax.broadcasted_iota(jnp.int32, (DRAFT, DRAFT), 1)
    upto = jnp.where(node_from <= node_to, 1.0, 0.0).astype(jnp.bfloat16)
    for s in range(slot_count):
        leaf = number(table_ref, 1 + slot_count + s)
        path = reach_ref[pl.ds(s * DRAFT + leaf, 1), s * DRAFT : (s + 1) * DRAFT]
        path = jnp.broadcast_to(path, (DRAFT, DRAFT))
        rank = jnp.dot(path.astype(jnp.bfloat16), upto, preferred_element_type=jnp.float32)
        chosen = (path > 0.5) & (rank == (node_from + 1).astype(jnp.float32))
        chosen_ref[s] = jnp.where(chosen, 1.0, 0.0).astype(jnp.bfloat16)
    ids = ids_ref[...].astype(jnp.float32).T
    names = lax.broadcasted_iota(jnp.int32, count_ref.shape, 1).astype(jnp.float32)
    count = jnp.zeros(count_ref.shape, jnp.float32)
    for k in range(ids.shape[1]):
        count = count + jnp.where(ids[:, k : k + 1] == names, 1.0, 0.0)
    count_ref[...] = count
    copy.wait()


def attend_kernel(units_ref, table_ref, reach_ref, got_ref, res_ref, turned_ref, kv_ref, *refs):
    del units_ref
    parts, (sent_ref, near_ref) = refs[:-2][::-1], refs[-2:]
    slot_count = reach_ref.shape[0] // DRAFT
    sources = got_ref.shape[0]
    tok_dev = res_ref.shape[0]
    page_len = parts[0].shape[1] // slot_count
    per_slot = DRAFT // tok_dev
    group_size = HEADS // KV_HEADS
    f32, bf16 = jnp.float32, jnp.bfloat16
    lane_low = lax.broadcasted_iota(jnp.int32, (DRAFT, WIDE), 1) < HEAD
    rank = lax.axis_index("tp")
    side = lax.rem(rank, 2)
    within = lax.broadcasted_iota(jnp.int32, (1, page_len), 1)
    positions = []
    for k in range(len(parts)):
        pair = lax.bitwise_xor(lax.div(rank, 2), k)
        for page in (2 * pair + side, 2 * pair + 1 - side):
            positions.append(within + page * page_len)
    positions = jnp.concatenate(positions, axis=1)
    dims = (((1,), (1,)), ((), ()))
    scale = 1.0 / math.sqrt(HEAD)
    outs = []
    for s in range(slot_count):
        first = s * per_slot

        def part(k):
            low = k * tok_dev
            return jnp.concatenate(
                [got_ref[first + i, low : low + tok_dev, :] for i in range(per_slot)], axis=0
            )

        q_pair, q_last, tree_kv = part(0).astype(f32) * scale, part(1).astype(f32) * scale, part(2)
        q_rows = jnp.concatenate(
            [
                jnp.where(lane_low, q_pair, 0.0),
                jnp.where(lane_low, pltpu.roll(q_pair, HEAD, 1), 0.0),
                jnp.where(lane_low, q_last, 0.0),
            ],
            axis=0,
        ).astype(bf16)
        at = slice(s * page_len, (s + 1) * page_len)
        cache_kv = jnp.concatenate(
            [a for k, part in enumerate(parts) for a in (part[side, at, :], turned_ref[k * parts[0].shape[1] + at.start : k * parts[0].shape[1] + at.stop, :])],
            axis=0,
        )
        scores = lax.dot_general(q_rows, cache_kv, dims, preferred_element_type=f32)
        is_valid = positions < number(table_ref, 1 + s)
        scores = jnp.where(is_valid, scores, neg_big)
        reach = reach_ref[s * DRAFT : (s + 1) * DRAFT, s * DRAFT : (s + 1) * DRAFT]
        allowed = jnp.concatenate([reach] * group_size, axis=0) > 0.5
        tree_scores = lax.dot_general(q_rows, tree_kv, dims, preferred_element_type=f32)
        tree_scores = jnp.where(allowed, tree_scores, neg_big)
        top = jnp.maximum(
            jnp.max(scores, axis=1, keepdims=True), jnp.max(tree_scores, axis=1, keepdims=True)
        )
        weights = jnp.where(is_valid, jnp.exp(scores - top), 0.0).astype(bf16)
        tree_weights = jnp.where(allowed, jnp.exp(tree_scores - top), 0.0).astype(bf16)
        total = jnp.sum(weights.astype(f32), axis=1, keepdims=True) + jnp.sum(
            tree_weights.astype(f32), axis=1, keepdims=True
        )
        mixed = jnp.dot(weights, cache_kv, preferred_element_type=f32) + jnp.dot(
            tree_weights, tree_kv, preferred_element_type=f32
        )
        outs.append(mixed / total)
    pair_rows, last_rows = [], []
    for out in outs:
        head_out = [out[r * DRAFT : (r + 1) * DRAFT] for r in range(group_size)]
        pair_rows.append(
            jnp.where(lane_low, pltpu.roll(head_out[0], HEAD, 1), head_out[1]).astype(bf16)
        )
        last_rows.append(head_out[2])
    last = jnp.where(lane_low, pltpu.roll(last_rows[0], HEAD, 1), last_rows[1]).astype(bf16)
    res_tiles = [res_ref[:, c * WIDE : (c + 1) * WIDE] for c in range(res_ref.shape[1] // WIDE)]
    sent_ref[...] = jnp.concatenate(pair_rows + [last] + res_tiles, axis=0)
    rows = sent_ref.shape[0]
    near_ref[:rows, :] = sent_ref[...]
    near_ref[rows:, :] = kv_ref[...]


def accept_kernel(rows, chosen_ref, *refs):
    accepted_ref = refs[-1]
    tok_dev, width = accepted_ref.shape
    rank = lax.axis_index("tp")
    per_slot = DRAFT // tok_dev
    place = lax.rem(rank, per_slot)
    chosen = chosen_ref[lax.div(rank, per_slot), pl.ds(pl.multiple_of(place * tok_dev, tok_dev), tok_dev), :]
    is_even, is_first = lax.rem(place, 2) == 0, place < 2
    for c in range(width // WIDE):
        low = rows + c * tok_dev
        pairs = []
        for mine, other in (refs[:2], refs[2:4]):
            a, b = mine[low : low + tok_dev, :], other[low : low + tok_dev, :]
            pairs.append(
                jnp.concatenate([jnp.where(is_even, a, b), jnp.where(is_even, b, a)], axis=0)
            )
        near, far = pairs
        nodes = jnp.concatenate(
            [jnp.where(is_first, near, far), jnp.where(is_first, far, near)], axis=0
        )
        accepted_ref[:, c * WIDE : (c + 1) * WIDE] = jnp.dot(
            chosen, nodes, preferred_element_type=jnp.float32
        ).astype(jnp.bfloat16)


def fetch_kernel(picks, first, after_ref, source_ref, down_hbm, target_ref, down_ref, sems):
    del after_ref
    rows = target_ref.shape[0] // len(picks)
    span = pl.ds(first, down_ref.shape[0])
    copies = [pltpu.make_async_copy(down_hbm.at[span], down_ref, sems.at[len(picks)])]
    for place, k in enumerate(picks):
        pair = lax.bitwise_xor(lax.div(lax.axis_index("tp"), 2), k)
        start = pl.multiple_of(pair * rows, WIDE)
        copies.append(
            pltpu.make_async_copy(
                source_ref.at[pl.ds(start, rows)],
                target_ref.at[place * rows : (place + 1) * rows],
                sems.at[place],
            )
        )
    start_all(copies)


def join_heads(k, rows, group_rows, mine_ref, other_ref, residual_ref):
    f32, bf16 = jnp.float32, jnp.bfloat16
    half = group_rows // 2
    tok_dev = group_rows // KV_HEADS
    model = residual_ref.shape[1]
    res_start = group_rows + half
    rank = lax.axis_index("tp")
    is_even = lax.rem(rank, 2) == 0
    pair = lax.bitwise_xor(lax.div(rank, 2), k)
    lane_low = lax.broadcasted_iota(jnp.int32, (half, WIDE), 1) < HEAD
    mine, other = mine_ref[:rows, :], other_ref[:rows, :]
    even, odd = jnp.where(is_even, mine, other), jnp.where(is_even, other, mine)
    last_even = even[group_rows:res_start].astype(f32)
    last_odd = odd[group_rows:res_start].astype(f32)
    odd_swapped = pltpu.roll(odd[:group_rows].astype(f32), HEAD, 1)
    middle = jnp.concatenate(
        [
            jnp.where(lane_low, last_even, odd_swapped[:half]),
            jnp.where(lane_low, pltpu.roll(last_even, HEAD, 1), odd_swapped[half:]),
        ],
        axis=0,
    ).astype(bf16)
    end = jnp.concatenate(
        [
            jnp.where(lane_low, odd_swapped[:half], pltpu.roll(last_odd, HEAD, 1)),
            jnp.where(lane_low, odd_swapped[half:], last_odd),
        ],
        axis=0,
    ).astype(bf16)
    for q, block in enumerate((even, odd)):
        row = pl.multiple_of((2 * pair + q) * tok_dev, tok_dev)
        residual_ref[pl.ds(row, tok_dev), :] = jnp.concatenate(
            [
                block[res_start + c * tok_dev : res_start + (c + 1) * tok_dev]
                for c in range(model // WIDE)
            ],
            axis=1,
        ).astype(f32)
    return jnp.concatenate([even[:group_rows], middle, end], axis=1)


def keep_own(k, heads_ref, at, attn_ref):
    tok_dev = attn_ref.shape[0]
    width = attn_ref.shape[1] * 2 // KV_HEADS
    rank = lax.axis_index("tp")
    pair = lax.bitwise_xor(lax.div(rank, 2), k)
    own = pl.multiple_of(rank * tok_dev, tok_dev)
    attn_ref[:, pl.ds(pl.multiple_of(pair * width, WIDE), width)] = heads_ref[
        pl.ds(own, tok_dev), at : at + width
    ]


def early_kernel(rows, after_ref, down_hbm, weight_ref, *refs):
    del after_ref
    blocks, refs = refs[:-6], refs[-6:]
    hid_ref, attn_ref, down_ref, residual_ref, x_ref, sem = refs
    start = down_hbm.shape[0] - down_ref.shape[0]
    copy = pltpu.make_async_copy(down_hbm.at[start:], down_ref, sem)
    copy.start()
    group_rows = hid_ref.shape[0]
    residual_ref[...] = jnp.zeros_like(residual_ref)
    width = x_ref.shape[1] * 2 // len(blocks)
    for k in range(len(blocks) // 2):
        x_ref[:, k * width : (k + 1) * width] = join_heads(
            k, rows, group_rows, blocks[2 * k], blocks[2 * k + 1], residual_ref
        )
    for k in range(len(blocks) // 2):
        keep_own(k, x_ref, k * width, attn_ref)
    hid_ref[...] = residual_ref[...] + jnp.dot(
        x_ref[...], weight_ref[...], preferred_element_type=jnp.float32
    )
    copy.wait()


def expert_kernel(
    rows, count_ref, router_ref, gain_ref, before_ref, part_ref, *refs
):
    refs, late = refs[:-8], refs[-8:]
    far_ref, hid_ref, hidden_ref, attn_ref, x_ref, normed_ref, share_ref, residual_ref = late
    f32, bf16 = jnp.float32, jnp.bfloat16
    pairs = KV_HEADS // 2
    first = pairs // 2
    down_refs, refs = refs[: pairs + 1], refs[pairs + 1 :]
    blocks, refs = refs[: 2 * (pairs - first)], refs[2 * (pairs - first) :]
    weight_refs, unit_refs = refs[: pairs - first], refs[pairs - first :]
    unit_weights = [(ref, k) for ref in unit_refs for k in range(ref.shape[0])]
    units = len(unit_weights)
    tok_dev, model = hidden_ref.shape
    sources = KV_HEADS
    group_rows = sources * tok_dev
    rank = lax.axis_index("tp")
    own = pl.multiple_of(rank * tok_dev, tok_dev)
    attn_ref[...] = part_ref[...]
    residual_ref[...] = jnp.zeros_like(residual_ref)
    hidden, width = before_ref[...], x_ref.shape[1] // (pairs - first)
    for q, k in enumerate(reversed(range(first, pairs))):
        heads = join_heads(k, rows, group_rows, blocks[2 * q], blocks[2 * q + 1], residual_ref)
        x_ref[:, q * width : (q + 1) * width] = heads
        keep_own(k, x_ref, q * width, attn_ref)
        hidden += jnp.dot(heads, weight_refs[q][...], preferred_element_type=f32)
    hidden += residual_ref[...]
    hid_ref[...] = hidden
    gain = jnp.concatenate([gain_ref[c : c + 1, :] for c in range(model // WIDE)], axis=1)
    scale = lax.rsqrt(jnp.mean(hidden * hidden, axis=1, keepdims=True) + norm_eps)
    normed_ref[...] = (hidden * scale * gain).astype(bf16)
    hidden_ref[...] = hid_ref[pl.ds(own, tok_dev), :]
    logits = lax.dot_general(
        normed_ref[...], router_ref[...], (((1,), (1,)), ((), ())), preferred_element_type=f32
    )
    experts = router_ref.shape[0]
    expert_range = lax.broadcasted_iota(jnp.int32, (group_rows, experts), 1)
    count = count_ref[...]
    expo = jnp.where(count > 0.0, jnp.exp(logits), 0.0) * count
    routing = expo / jnp.sum(expo, axis=1, keepdims=True)
    unit_width = unit_refs[0].shape[2] // 2
    span = FF_E // unit_width
    each = span if units % span == 0 else 1
    for u in range(0, units, each):
        expert = (rank * units + u) // span
        share = jnp.sum(jnp.where(expert_range == expert, routing, 0.0), axis=1, keepdims=True)
        share_ref[u : u + each] = jnp.broadcast_to(share[None], (each, group_rows, unit_width))

    def one_unit(u):
        ref, k = unit_weights[u]
        both = jnp.dot(normed_ref[...], ref[k], preferred_element_type=f32)
        gate, up = both[:, :unit_width], both[:, unit_width:]
        return (gate / (1.0 + jnp.exp(-gate)) * up * share_ref[u]).astype(bf16)

    down_steps = [(ref, at) for ref in down_refs for at in range(ref.shape[0] // STEP)]
    for i in range(units // STEP):
        act = jnp.concatenate([one_unit(i * STEP + k) for k in range(STEP)], axis=1)
        ref, at = down_steps[i]
        down = ref[at * STEP : (at + 1) * STEP].reshape(STEP * unit_width, model)
        part = jnp.dot(act, down, preferred_element_type=f32)
        hid_ref[...] = part if i == 0 else hid_ref[...] + part
    for k in range(far_ref.shape[0]):
        copy_sums(sources // 4 + k, True, hid_ref, far_ref.at[k])


def copy_sums(k, crossing, hid_ref, ref):
    tok_dev = ref.shape[0]
    rank = lax.axis_index("tp")
    side = lax.rem(rank, 2)
    pair = lax.bitwise_xor(lax.div(rank, 2), k)
    target = 2 * pair + (1 - side if crossing else side)
    row = pl.multiple_of(target * tok_dev, tok_dev)
    ref[...] = hid_ref[pl.ds(row, tok_dev), :].astype(ref.dtype)


def near_kernel(hid_ref, mine_ref, near_ref):
    for k in range(mine_ref.shape[0]):
        copy_sums(k, False, hid_ref, mine_ref.at[k])
    for k in range(near_ref.shape[0]):
        copy_sums(k, True, hid_ref, near_ref.at[k])


def fold_kernel(first, after_ref, mine_ref, got_ref, hidden_ref, *sent_refs):
    del after_ref
    for k, ref in enumerate(sent_refs, first):
        total = mine_ref[k] + got_ref[k - first].astype(jnp.float32)
        if k == 0:
            total = total + hidden_ref[...]
        ref[...] = total.astype(ref.dtype)


def finish_kernel(attn_in_ref, accepted_in_ref, *refs):
    parts, (attn_ref, layer_ref, accepted_ref) = refs[:-3], refs[-3:]
    attn_ref[...] = attn_in_ref[...]
    accepted_ref[...] = accepted_in_ref[...]
    total = parts[0][...]
    for part in parts[1:]:
        total = total + part[...].astype(jnp.float32)
    layer_ref[...] = total.astype(jnp.bfloat16)


def in_hbm(*arrays):
    return tuple(pltpu.with_memory_space_constraint(a, pltpu.HBM) for a in arrays)


def spaces(text):
    kinds = {"a": pl.ANY, "v": pltpu.VMEM}
    return [pl.BlockSpec(memory_space=kinds[c]) for c in text]


def params(mebibytes=12):
    return pltpu.CompilerParams(vmem_limit_bytes=mebibytes << 20)


def cost(mebibytes):
    return pl.CostEstimate(flops=0, transcendentals=0, bytes_accessed=mebibytes << 20)


def swap(rows, mask):
    count = lax.axis_size("tp")
    return lax.ppermute(rows, "tp", [(i, i ^ mask) for i in range(count)])


def fetch(after, array, rows, picks, down_weight, first, units):
    shape = (rows * len(picks),) + array.shape[1:]
    down_shape = (units,) + down_weight.shape[1:]
    return pl.pallas_call(
        functools.partial(fetch_kernel, picks, first),
        out_shape=(pltpu.VMEM(shape, array.dtype), pltpu.VMEM(down_shape, array.dtype)),
        in_specs=spaces("aaa"),
        out_specs=tuple(spaces("vv")),
        scratch_shapes=[pltpu.SemaphoreType.DMA((len(picks) + 1,))],
        compiler_params=params(),
        cost_estimate=cost(2 * (math.prod(shape) + math.prod(down_shape)) >> 20),
        name="fetch",
    )(after, *in_hbm(array, down_weight))


def per_device_packed(
    queries,
    new_kv,
    residual,
    placement,
    lengths,
    page_table,
    cache_keys,
    cache_values,
    parents,
    accept_leaf,
    out_weight,
    norm_gain,
    router_weight,
    expert_ids,
    gate_up,
    down_weight,
):
    f32, bf16 = jnp.float32, jnp.bfloat16
    tok_dev, model = residual.shape
    tp_count = lax.axis_size("tp")
    slot_count = placement.shape[0]
    page_len, kv_width = cache_keys.shape[1:]
    group_rows = tok_dev * tp_count
    sent = lambda rows: jax.ShapeDtypeStruct((tp_count, rows, WIDE), bf16)
    dma = pltpu.SemaphoreType.DMA
    slots_smem = pltpu.SMEM((slot_count,), jnp.int32)
    pairs = tp_count // 2
    part = jax.ShapeDtypeStruct((2, slot_count * page_len, WIDE), bf16)
    loaded = (
        page_table.reshape(slot_count),
        placement,
        lengths,
        accept_leaf,
        cache_keys,
        cache_values,
        queries,
        new_kv,
        residual,
        parents,
        router_weight.T,
        expert_ids.T,
        norm_gain.reshape(model // WIDE, WIDE),
    )
    *parts, joined, table, parents, router, ids, gain = pl.pallas_call(
        functools.partial(split_kernel, pairs),
        out_shape=(part,) * pairs
        + (
            jax.ShapeDtypeStruct((tok_dev, 2 * (model + kv_width)), bf16),
            pltpu.VMEM((8, WIDE), f32),
        )
        + tuple(pltpu.VMEM(a.shape, a.dtype) for a in loaded[9:]),
        in_specs=spaces("a" * len(loaded)),
        out_specs=tuple(spaces("v" * (pairs + 6))),
        scratch_shapes=[
            slots_smem,
            slots_smem,
            slots_smem,
            slots_smem,
            pltpu.VMEM(cache_keys.shape, bf16),
            pltpu.VMEM(cache_values.shape, bf16),
            pltpu.VMEM((pairs,) + part.shape, bf16),
            dma((len(loaded),)),
        ],
        compiler_params=params(),
        cost_estimate=cost(4),
        name="split",
    )(*in_hbm(*loaded))
    parts = parts[::-1]
    parts = [parts[0]] + [swap(parts[k], 2 * k) for k in range(1, pairs)]
    pulled = lax.all_gather(joined, "req", axis=0)
    nodes = slot_count * DRAFT
    units = gate_up.shape[0]
    cuts = [units * c // 20 // STEP * STEP for c in CUTS]
    ready = cuts[0]
    down_ready, reach, chosen, count = pl.pallas_call(
        tree_kernel,
        out_shape=(
            pltpu.VMEM((ready,) + down_weight.shape[1:], bf16),
            jax.ShapeDtypeStruct((nodes, nodes), f32),
            jax.ShapeDtypeStruct((slot_count, DRAFT, DRAFT), bf16),
            jax.ShapeDtypeStruct((group_rows, router_weight.shape[1]), f32),
        ),
        in_specs=spaces("aavvv"),
        out_specs=tuple(spaces("vvvv")),
        scratch_shapes=[dma],
        compiler_params=params(),
        cost_estimate=cost(8),
        name="tree",
    )(pulled, *in_hbm(down_weight), table, parents, ids)
    kv_rows = 2 * kv_width // WIDE * tok_dev
    packed, own_res, turned, own_kv = pl.pallas_call(
        functools.partial(route_kernel, kv_width),
        out_shape=(
            sent(3 * tok_dev),
            jax.ShapeDtypeStruct(residual.shape, bf16),
            jax.ShapeDtypeStruct((pairs * part.shape[1], WIDE), bf16),
            jax.ShapeDtypeStruct((kv_rows, WIDE), bf16),
        ),
        in_specs=spaces("aavv" + "v" * pairs),
        out_specs=tuple(spaces("vvvv")),
        compiler_params=params(),
        cost_estimate=cost(4),
        name="route",
    )(down_ready, *in_hbm(down_weight), table, pulled, *parts[::-1])
    turned = swap(turned, 1)
    packed = lax.all_to_all(packed, "tp", 0, 0, tiled=True)
    gate_up = pltpu.with_memory_space_constraint(gate_up, pltpu.VMEM)
    block_rows = group_rows + group_rows // 2 + (model // WIDE) * tok_dev
    block, near_block = pl.pallas_call(
        attend_kernel,
        out_shape=(
            jax.ShapeDtypeStruct((block_rows, WIDE), bf16),
            jax.ShapeDtypeStruct((block_rows + kv_rows, WIDE), bf16),
        ),
        in_specs=spaces("v" * (7 + pairs)),
        out_specs=tuple(spaces("vv")),
        compiler_params=params(),
        cost_estimate=cost(8),
        name="attend",
    )(gate_up, table, reach, packed, own_res, turned, own_kv, *parts[::-1])
    reached = [swap(near_block, 2)] + [swap(block, 2 * k) for k in range(2, pairs)]
    weights, downs, after = [], [down_ready], block
    rows = out_weight.shape[0] // pairs
    for k, picks in zip(ORDER, FETCHES):
        start, size = cuts[len(weights)], cuts[len(weights) + 1] - cuts[len(weights)]
        weight, down = fetch(after, out_weight, rows, picks, down_weight, start, size)
        fetched = (reached[k - 1], weight, down)
        reached[k - 1], weight, down = lax.optimization_barrier(fetched)
        downs.append(down)
        after = reached[k - 1]
        weights.append(weight)
    blocks = [block, swap(near_block, 1)]
    blocks += [a for got in reached for a in (got, swap(got, 1))]
    before, attn_part, down_rest = pl.pallas_call(
        functools.partial(early_kernel, block_rows),
        out_shape=(
            jax.ShapeDtypeStruct((group_rows, model), f32),
            pltpu.VMEM(queries.shape, bf16),
            pltpu.VMEM((units - cuts[-1],) + down_weight.shape[1:], bf16),
        ),
        in_specs=spaces("aav" + "v" * pairs),
        out_specs=tuple(spaces("vvv")),
        scratch_shapes=[
            pltpu.VMEM((group_rows, model), f32),
            pltpu.VMEM((group_rows, HEADS * HEAD // 2), bf16),
            dma,
        ],
        compiler_params=params(),
        cost_estimate=cost(4),
        name="early",
    )(after, *in_hbm(down_weight), weights[0], *blocks[:pairs])
    accepted = pl.pallas_call(
        functools.partial(accept_kernel, block_rows),
        out_shape=pltpu.VMEM(new_kv.shape, bf16),
        in_specs=spaces("vvvvv"),
        out_specs=spaces("v")[0],
        compiler_params=params(),
        cost_estimate=cost(1),
        name="accept",
    )(chosen, near_block, *blocks[1:4])
    unit_weights = (gate_up,)
    far, sums, hidden, attn_own = pl.pallas_call(
        functools.partial(expert_kernel, block_rows),
        out_shape=(
            jax.ShapeDtypeStruct((pairs // 2, tok_dev, model), bf16),
            jax.ShapeDtypeStruct((group_rows, model), f32),
            jax.ShapeDtypeStruct((tok_dev, model), f32),
            pltpu.VMEM(queries.shape, bf16),
        ),
        in_specs=spaces("v" * (6 + len(downs) + pairs + pairs // 2 + len(unit_weights))),
        out_specs=tuple(spaces("vvvv")),
        scratch_shapes=[
            pltpu.VMEM((group_rows, HEADS * HEAD // 2), bf16),
            pltpu.VMEM((group_rows, model), bf16),
            pltpu.VMEM((units, group_rows, gate_up.shape[2] // 2), f32),
            pltpu.VMEM((group_rows, model), f32),
        ],
        compiler_params=params(),
        name="experts",
    )(
        count,
        router,
        gain,
        before,
        attn_part,
        *downs,
        down_rest,
        *[a for k in reversed(range(pairs // 2, pairs)) for a in blocks[2 * k : 2 * k + 2]],
        weights[1],
        weights[2],
        *unit_weights,
    )
    far = swap(far, 1)
    mine, near = pl.pallas_call(
        near_kernel,
        out_shape=(
            jax.ShapeDtypeStruct((pairs, tok_dev, model), f32),
            jax.ShapeDtypeStruct((pairs // 2, tok_dev, model), bf16),
        ),
        in_specs=spaces("v"),
        out_specs=tuple(spaces("vv")),
        compiler_params=params(),
        cost_estimate=cost(4),
        name="near",
    )(sums)
    near = swap(near, 1)
    fold = lambda first, after, got: pl.pallas_call(
        functools.partial(fold_kernel, first),
        out_shape=tuple(
            jax.ShapeDtypeStruct((tok_dev, model), f32 if k == 0 else bf16)
            for k in range(first, first + pairs // 2)
        ),
        in_specs=spaces("avvv"),
        out_specs=tuple(spaces("v" * (pairs // 2))),
        compiler_params=params(),
        cost_estimate=cost(1),
        name="fold",
    )(after, mine, got, hidden)
    sums = fold(pairs // 2, hidden, far)
    folded = sums[0]
    sums = [swap(a, 2 * k) for k, a in enumerate(sums, pairs // 2)]
    close = fold(0, folded, near)
    sums = [close[0]] + [swap(close[k], 2 * k) for k in range(1, pairs // 2)] + sums
    return pl.pallas_call(
        finish_kernel,
        out_shape=(
            jax.ShapeDtypeStruct(queries.shape, bf16),
            jax.ShapeDtypeStruct(residual.shape, bf16),
            jax.ShapeDtypeStruct(new_kv.shape, bf16),
        ),
        in_specs=spaces("v" * (2 + pairs)),
        out_specs=tuple(spaces("vvv")),
        compiler_params=params(),
        name="finish",
    )(attn_own, accepted, sums[0], *sums[:0:-1])


def per_device(queries, new_kv, residual, placement, *rest):
    tok_dev = queries.shape[0]
    one_head_each = lax.axis_size("tp") == KV_HEADS
    whole_tiles = tok_dev % 16 == 0 and placement.shape[0] == 2 and tok_dev * KV_HEADS == 2 * DRAFT
    if one_head_each and whole_tiles and rest[1].shape[1] == 1:
        return per_device_packed(queries, new_kv, residual, placement, *rest)
    return per_device_plain(queries, new_kv, residual, placement, *rest)


def solution(mesh):
    in_specs = (
        P(("req", "tp"), None),
        P(("req", "tp"), None),
        P(("req", "tp"), None),
        P("req"),
        P("req"),
        P("req", None, "tp"),
        P(("req", "tp"), None, None),
        P(("req", "tp"), None, None),
        P("req", None),
        P("req"),
        P(),
        P(),
        P(),
        P("req", None),
        P("tp", None, None),
        P("tp", None, None),
    )
    out_specs = (P(("req", "tp"), None), P(("req", "tp"), None), P(("req", "tp"), None))
    return jax.shard_map(
        per_device, mesh=mesh, in_specs=in_specs, out_specs=out_specs, check_vma=False
    )
```

```python
import functools
import math

import jax
import jax.numpy as jnp
from jax import lax
from jax.experimental import pallas as pl
from jax.experimental.pallas import tpu as pltpu
from jax.sharding import PartitionSpec as P

HEADS = 24
KV_HEADS = 8
HEAD = 64
FF_E = 512
UNIT = 128
DRAFT = 64
WIDE = 128
STEP = 2
CUTS = (6, 8, 10, 12)
ORDER = (1, 3, 2)
FETCHES = ((0, 1), (3,), (2,))


neg_big = -1e30
norm_eps = 1e-06


def joined_2(part, axis, combine):
    gathered = jax.tree.map(lambda a: lax.all_gather(a, axis), part)

    def take(source):
        return jax.tree.map(lambda a: lax.dynamic_index_in_dim(a, source, 0, False), gathered)

    return lax.fori_loop(
        1, lax.axis_size(axis), lambda source, state: combine(state, take(source)), take(0)
    )


def ancestry(parents):
    node_count = parents.shape[-1]
    node_ids = jnp.arange(node_count, dtype=jnp.int32)
    linked = (parents[:, :, None] == node_ids[None, None, :]) & (node_ids[None, :, None] > 0)
    reached = jnp.maximum(linked.astype(jnp.float32), jnp.eye(node_count, dtype=jnp.float32)[None])
    for _ in range(node_count.bit_length()):
        reached = jnp.minimum(
            jnp.einsum("rnm,rmk->rnk", reached, reached, precision=lax.Precision.HIGHEST), 1.0
        )
    return reached


def combine_stats(left_stats, right_stats):
    left_max, left_sum, left_out = left_stats
    right_max, right_sum, right_out = right_stats
    top_score = jnp.maximum(left_max, right_max)
    left_scale = jnp.exp(left_max - top_score)
    right_scale = jnp.exp(right_max - top_score)
    row_count, head_count = left_max.shape
    out_sum = (
        left_out.reshape(row_count, head_count, -1) * left_scale[..., None]
        + right_out.reshape(row_count, head_count, -1) * right_scale[..., None]
    )
    return (
        top_score,
        left_sum * left_scale + right_sum * right_scale,
        out_sum.reshape(row_count, -1),
    )


def finish_rows(stat_sum, stat_out):
    row_count, head_count = stat_sum.shape
    return (
        (stat_out.reshape(row_count, head_count, -1) / stat_sum[..., None])
        .reshape(row_count, -1)
        .astype(jnp.bfloat16)
    )


def project_rows(attn_rows, res_rows, out_weight):
    return res_rows.astype(jnp.float32) + jnp.dot(
        attn_rows, out_weight, preferred_element_type=jnp.float32
    )


def rms_normed(hidden, norm_gain):
    scale_rows = lax.rsqrt(jnp.mean(hidden * hidden, axis=-1, keepdims=True) + norm_eps)
    return (hidden * scale_rows * norm_gain).astype(jnp.bfloat16)


def unit_shares(normed_all, router_weight, expert_ids, tp_rank, units_dev):
    logits = jnp.dot(normed_all, router_weight, preferred_element_type=jnp.float32)
    expert_range = jnp.arange(router_weight.shape[1], dtype=jnp.int32)
    onehot = (expert_ids[:, :, None] == expert_range[None, None, :]).astype(jnp.float32)
    chosen = jnp.sum(logits[:, None, :] * onehot, axis=-1)
    expo_chosen = jnp.exp(chosen)
    expert_probs = expo_chosen / jnp.sum(expo_chosen, axis=-1, keepdims=True)
    routing = jnp.sum(expert_probs[:, :, None] * onehot, axis=1)
    unit_ids = tp_rank * units_dev + jnp.arange(units_dev, dtype=jnp.int32)
    expert_of_unit = unit_ids // (FF_E // UNIT)
    pick = (expert_range[:, None] == expert_of_unit[None, :]).astype(jnp.float32)
    return jnp.dot(routing, pick, precision=lax.Precision.HIGHEST)


def per_device_plain(
    queries,
    new_kv,
    residual,
    placement,
    lengths,
    page_table,
    cache_keys,
    cache_values,
    parents,
    accept_leaf,
    out_weight,
    norm_gain,
    router_weight,
    expert_ids,
    gate_up,
    down_weight,
):
    tok_dev = queries.shape[0]
    tp_count = lax.axis_size("tp")
    tp_rank = lax.axis_index("tp")
    group_rows = tok_dev * tp_count
    slot_count = placement.shape[0]
    kv_width = cache_keys.shape[2]
    page_len = cache_keys.shape[1]
    group_size = HEADS // KV_HEADS
    score_scale = 1.0 / math.sqrt(HEAD)
    row_start = tp_rank * tok_dev
    pulled_q, pulled_kv, pulled_res = (
        lax.all_gather(queries, "req", axis=0, tiled=True),
        lax.all_gather(new_kv, "req", axis=0, tiled=True),
        lax.all_gather(residual, "req", axis=0, tiled=True),
    )
    row_offsets = jnp.arange(tok_dev, dtype=jnp.int32)
    row_pos = row_start + row_offsets
    row_slot = row_pos // DRAFT
    slot_match = row_slot[:, None] == jnp.arange(slot_count, dtype=jnp.int32)[None, :]
    source_group = jnp.sum(jnp.where(slot_match, placement[None, :] // slot_count, 0), axis=1)
    source_rows = source_group * tok_dev + row_offsets
    own_q = jnp.take(pulled_q, source_rows, axis=0)
    own_kv = jnp.take(pulled_kv, source_rows, axis=0)
    own_res = jnp.take(pulled_res, source_rows, axis=0)
    all_q, all_kv = (
        lax.all_gather(own_q, "tp", axis=0, tiled=True),
        lax.all_gather(own_kv, "tp", axis=0, tiled=True),
    )
    local_pages = page_table.shape[1]
    page_ids = page_table[:, :, 0].reshape(-1)
    keys_local = jnp.take(cache_keys, page_ids, axis=0).reshape(
        slot_count, local_pages, page_len, KV_HEADS, HEAD
    )
    values_local = jnp.take(cache_values, page_ids, axis=0).reshape(
        slot_count, local_pages, page_len, KV_HEADS, HEAD
    )
    query_blocks = all_q.reshape(slot_count, DRAFT, KV_HEADS, group_size, HEAD)
    scores = (
        jnp.einsum(
            "sqgrd,sltgd->sqgrlt", query_blocks, keys_local, preferred_element_type=jnp.float32
        )
        * score_scale
    )
    positions = (
        jnp.arange(local_pages, dtype=jnp.int32)[:, None] * tp_count + tp_rank
    ) * page_len + jnp.arange(page_len, dtype=jnp.int32)[None, :]
    is_valid = (positions[None] < lengths[:, None, None])[:, None, None, None]
    scores = jnp.where(is_valid, scores, neg_big)
    block_max = jnp.max(scores, axis=-1)
    weights = jnp.where(is_valid, jnp.exp(scores - block_max[..., None]), 0.0).astype(jnp.bfloat16)
    block_sum = jnp.sum(weights.astype(jnp.float32), axis=-1)
    block_out = jnp.einsum(
        "sqgrlt,sltgd->sqgrld", weights, values_local, preferred_element_type=jnp.float32
    )
    page_top = jnp.max(block_max, axis=-1)
    page_scale = jnp.exp(block_max - page_top[..., None])
    stat_max = page_top.reshape(group_rows, HEADS)
    stat_sum = jnp.sum(block_sum * page_scale, axis=-1).reshape(group_rows, HEADS)
    stat_out = jnp.sum(block_out * page_scale[..., None], axis=-2).reshape(group_rows, HEADS * HEAD)
    reached = ancestry(parents)
    reach_rows = jnp.take(reached.reshape(slot_count * DRAFT, DRAFT), row_pos, axis=0)
    key_slot = jnp.arange(group_rows, dtype=jnp.int32) // DRAFT
    same_slot = key_slot[None, :] == row_slot[:, None]
    allowed = same_slot & (jnp.tile(reach_rows, (1, slot_count)) > 0.5)
    tree_keys = all_kv[:, :kv_width].reshape(group_rows, KV_HEADS, HEAD)
    tree_values = all_kv[:, kv_width:].reshape(group_rows, KV_HEADS, HEAD)
    own_blocks = own_q.reshape(tok_dev, KV_HEADS, group_size, HEAD)
    tree_scores = (
        jnp.einsum("igrd,kgd->igrk", own_blocks, tree_keys, preferred_element_type=jnp.float32)
        * score_scale
    )
    tree_mask = allowed[:, None, None, :]
    tree_scores = jnp.where(tree_mask, tree_scores, neg_big)
    tree_max = jnp.max(tree_scores, axis=-1)
    tree_weights = jnp.where(tree_mask, jnp.exp(tree_scores - tree_max[..., None]), 0.0).astype(
        jnp.bfloat16
    )
    tree_sum = jnp.sum(tree_weights.astype(jnp.float32), axis=-1)
    tree_out = jnp.einsum(
        "igrk,kgd->igrd", tree_weights, tree_values, preferred_element_type=jnp.float32
    )
    own_stats = (
        lax.dynamic_slice_in_dim(stat_max, row_start, tok_dev, 0),
        lax.dynamic_slice_in_dim(stat_sum, row_start, tok_dev, 0),
        lax.dynamic_slice_in_dim(stat_out, row_start, tok_dev, 0),
    )
    tree_stats = (
        tree_max.reshape(tok_dev, HEADS),
        tree_sum.reshape(tok_dev, HEADS),
        tree_out.reshape(tok_dev, HEADS * HEAD),
    )
    joined = combine_stats(own_stats, tree_stats)
    stat_max = lax.dynamic_update_slice_in_dim(stat_max, joined[0], row_start, 0)
    stat_sum = lax.dynamic_update_slice_in_dim(stat_sum, joined[1], row_start, 0)
    stat_out = lax.dynamic_update_slice_in_dim(stat_out, joined[2], row_start, 0)
    normed_all = None
    merged = joined_2((stat_max, stat_sum, stat_out), "tp", combine_stats)
    attn_own = finish_rows(
        lax.dynamic_slice_in_dim(merged[1], row_start, tok_dev, 0),
        lax.dynamic_slice_in_dim(merged[2], row_start, tok_dev, 0),
    )
    hidden_own = project_rows(attn_own, own_res, out_weight)
    normed_own = rms_normed(hidden_own, norm_gain)
    units_dev = gate_up.shape[0]
    unit_width = gate_up.shape[2] // 2
    normed_all = lax.all_gather(normed_own, "tp", axis=0, tiled=True)
    shares = unit_shares(normed_all, router_weight, expert_ids, tp_rank, units_dev)
    gate_both = jnp.einsum("td,udh->tuh", normed_all, gate_up, preferred_element_type=jnp.float32)
    activated = (
        jax.nn.silu(gate_both[..., :unit_width]) * gate_both[..., unit_width:] * shares[:, :, None]
    ).astype(jnp.bfloat16)
    moe_own = lax.psum_scatter(
        jnp.einsum("tuh,uhd->td", activated, down_weight, preferred_element_type=jnp.float32),
        "tp",
        scatter_dimension=0,
        tiled=True,
    )
    layer_out = (hidden_own + moe_own).astype(jnp.bfloat16)
    node_ids = jnp.arange(DRAFT, dtype=jnp.int32)
    leaf_pick = (accept_leaf[:, None] == node_ids[None, :]).astype(jnp.float32)
    path_weight = jnp.einsum("sn,snk->sk", leaf_pick, reached, precision=lax.Precision.HIGHEST)
    path_flags = (path_weight > 0.5).astype(jnp.int32)
    path_rank = jnp.cumsum(path_flags, axis=1) - 1
    chosen_node = (path_flags[:, None, :] > 0) & (path_rank[:, None, :] == node_ids[None, :, None])
    own_choice = jnp.take(chosen_node.reshape(slot_count * DRAFT, DRAFT), row_pos, axis=0)
    spread = same_slot & jnp.tile(own_choice, (1, slot_count))
    accepted = jnp.dot(
        spread.astype(jnp.bfloat16), all_kv, preferred_element_type=jnp.float32
    ).astype(jnp.bfloat16)
    return (attn_own, layer_out, accepted)


def start_all(copies):
    for copy in copies:
        copy.start()
    for copy in copies:
        copy.wait()


def split_kernel(pairs, *refs):
    (
        pages_hbm, placement_hbm, lengths_hbm, leaf_hbm, keys_hbm, values_hbm, queries_hbm,
        new_kv_hbm, residual_hbm, parents_hbm, ids_hbm, gain_hbm,
    ) = refs[:12]
    parts, refs = refs[12 : 12 + pairs], refs[12 + pairs :]
    joined_ref, table_ref, parents_ref, ids_ref, gain_ref = refs[:5]
    pages_ref, placement_ref, lengths_ref, leaf_ref, keys_ref, values_ref, split_ref, sems = refs[5:]
    slot_count = pages_ref.shape[0]
    page_len = keys_ref.shape[1]
    tok_dev = joined_ref.shape[0]
    moves = [
        (pages_hbm, pages_ref),
        (keys_hbm, keys_ref),
        (values_hbm, values_ref),
        (placement_hbm, placement_ref),
        (lengths_hbm, lengths_ref),
        (leaf_hbm, leaf_ref),
        (parents_hbm, parents_ref),
        (ids_hbm, ids_ref),
        (gain_hbm, gain_ref),
    ]
    column = 0
    for source in (queries_hbm, new_kv_hbm, residual_hbm):
        moves.append((source, joined_ref.at[:, column : column + source.shape[1]]))
        column += source.shape[1]
    start_all(
        [pltpu.make_async_copy(a, b, sems.at[k]) for k, (a, b) in enumerate(moves)]
    )
    slot = lax.div(lax.axis_index("tp") * tok_dev, DRAFT)
    numbers = [lax.div(placement_ref[slot], slot_count)]
    numbers += [lengths_ref[s] for s in range(slot_count)]
    numbers += [leaf_ref[s] for s in range(slot_count)]
    for row, number in enumerate(numbers):
        table_ref[row : row + 1, :] = jnp.full((1, WIDE), number, jnp.int32).astype(jnp.float32)
    for head in range(KV_HEADS):
        low = head * HEAD
        for s in range(slot_count):
            page = pages_ref[s]
            split_ref[head // 2, head % 2, s * page_len : (s + 1) * page_len, :] = jnp.concatenate(
                [keys_ref[page, :, low : low + HEAD], values_ref[page, :, low : low + HEAD]], axis=1
            )
    pair = lax.div(lax.axis_index("tp"), 2)
    for k, part in enumerate(parts):
        part[...] = split_ref[lax.bitwise_xor(pair, pairs - 1 - k)]


def number(table_ref, row):
    return jnp.max(table_ref[row : row + 1, :]).astype(jnp.int32)


def route_kernel(kv_width, after_ref, weight_hbm, table_ref, pulled_ref, *refs):
    del after_ref, weight_hbm
    parts, (sent_ref, res_ref, turned_ref, kv_ref) = refs[:-4][::-1], refs[-4:]
    rank = lax.axis_index("tp")
    other = 1 - lax.rem(rank, 2)
    size = parts[0].shape[1]
    for k, part in enumerate(parts):
        turned_ref[k * size : (k + 1) * size, :] = part[other]
    q_width = HEADS * HEAD
    tok_dev = pulled_ref.shape[1]
    rows = pulled_ref[number(table_ref, 0)]
    res_ref[...] = rows[:, q_width + 2 * kv_width :]
    tiles = [rows[:, q_width + c : q_width + c + WIDE] for c in range(0, 2 * kv_width, WIDE)]
    kv_ref[...] = jnp.concatenate(tiles, axis=0)
    head_rows = (HEADS // KV_HEADS) * HEAD
    tail = jnp.zeros((tok_dev, 2 * WIDE - head_rows), rows.dtype)
    for head in range(KV_HEADS):
        q_low = head * head_rows
        pair = jnp.concatenate([rows[:, q_low : q_low + head_rows], tail], axis=1)
        sent_ref[head, :tok_dev, :] = pair[:, :WIDE]
        sent_ref[head, tok_dev : 2 * tok_dev, :] = pair[:, WIDE:]
        k_low = q_width + head * HEAD
        sent_ref[head, 2 * tok_dev :, :] = jnp.concatenate(
            [rows[:, k_low : k_low + HEAD], rows[:, k_low + kv_width : k_low + kv_width + HEAD]],
            axis=1,
        )


def ancestor_rows(parents_ref):
    slot_count = parents_ref.shape[0]
    total = slot_count * DRAFT
    row = jnp.concatenate(
        [parents_ref[s : s + 1, :] + s * DRAFT for s in range(slot_count)], axis=1
    )
    from_ids = lax.broadcasted_iota(jnp.int32, (total, total), 0)
    to_ids = lax.broadcasted_iota(jnp.int32, (total, total), 1)
    linked = (from_ids == jnp.broadcast_to(row, (total, total))) & (lax.rem(to_ids, DRAFT) > 0)
    reached = jnp.where(linked | (from_ids == to_ids), 1.0, 0.0)
    for _ in range((DRAFT - 1).bit_length()):
        half = reached.astype(jnp.bfloat16)
        reached = jnp.minimum(jnp.dot(half, half, preferred_element_type=jnp.float32), 1.0)
    return reached.T


def tree_kernel(
    after_ref, down_hbm, table_ref, parents_ref, ids_ref, down_ref, reach_ref, chosen_ref,
    count_ref, sem,
):
    del after_ref
    copy = pltpu.make_async_copy(down_hbm.at[: down_ref.shape[0]], down_ref, sem)
    copy.start()
    slot_count = parents_ref.shape[0]
    reach_ref[...] = ancestor_rows(parents_ref)
    node_from = lax.broadcasted_iota(jnp.int32, (DRAFT, DRAFT), 0)
    node_to = lax.broadcasted_iota(jnp.int32, (DRAFT, DRAFT), 1)
    upto = jnp.where(node_from <= node_to, 1.0, 0.0).astype(jnp.bfloat16)
    for s in range(slot_count):
        leaf = number(table_ref, 1 + slot_count + s)
        path = reach_ref[pl.ds(s * DRAFT + leaf, 1), s * DRAFT : (s + 1) * DRAFT]
        path = jnp.broadcast_to(path, (DRAFT, DRAFT))
        rank = jnp.dot(path.astype(jnp.bfloat16), upto, preferred_element_type=jnp.float32)
        chosen = (path > 0.5) & (rank == (node_from + 1).astype(jnp.float32))
        chosen_ref[s] = jnp.where(chosen, 1.0, 0.0).astype(jnp.bfloat16)
    ids = ids_ref[...].astype(jnp.float32).T
    names = lax.broadcasted_iota(jnp.int32, count_ref.shape, 1).astype(jnp.float32)
    count = jnp.zeros(count_ref.shape, jnp.float32)
    for k in range(ids.shape[1]):
        count = count + jnp.where(ids[:, k : k + 1] == names, 1.0, 0.0)
    count_ref[...] = count
    copy.wait()


def attend_kernel(units_ref, table_ref, reach_ref, got_ref, res_ref, turned_ref, kv_ref, *refs):
    del units_ref
    parts, (sent_ref, near_ref) = refs[:-2][::-1], refs[-2:]
    slot_count = reach_ref.shape[0] // DRAFT
    sources = got_ref.shape[0]
    tok_dev = res_ref.shape[0]
    page_len = parts[0].shape[1] // slot_count
    per_slot = DRAFT // tok_dev
    group_size = HEADS // KV_HEADS
    f32, bf16 = jnp.float32, jnp.bfloat16
    lane_low = lax.broadcasted_iota(jnp.int32, (DRAFT, WIDE), 1) < HEAD
    rank = lax.axis_index("tp")
    side = lax.rem(rank, 2)
    within = lax.broadcasted_iota(jnp.int32, (1, page_len), 1)
    positions = []
    for k in range(len(parts)):
        pair = lax.bitwise_xor(lax.div(rank, 2), k)
        for page in (2 * pair + side, 2 * pair + 1 - side):
            positions.append(within + page * page_len)
    positions = jnp.concatenate(positions, axis=1)
    dims = (((1,), (1,)), ((), ()))
    scale = 1.0 / math.sqrt(HEAD)
    outs = []
    for s in range(slot_count):
        first = s * per_slot

        def part(k):
            low = k * tok_dev
            return jnp.concatenate(
                [got_ref[first + i, low : low + tok_dev, :] for i in range(per_slot)], axis=0
            )

        q_pair, q_last, tree_kv = part(0).astype(f32) * scale, part(1).astype(f32) * scale, part(2)
        q_rows = jnp.concatenate(
            [
                jnp.where(lane_low, q_pair, 0.0),
                jnp.where(lane_low, pltpu.roll(q_pair, HEAD, 1), 0.0),
                jnp.where(lane_low, q_last, 0.0),
            ],
            axis=0,
        ).astype(bf16)
        at = slice(s * page_len, (s + 1) * page_len)
        cache_kv = jnp.concatenate(
            [a for k, part in enumerate(parts) for a in (part[side, at, :], turned_ref[k * parts[0].shape[1] + at.start : k * parts[0].shape[1] + at.stop, :])],
            axis=0,
        )
        scores = lax.dot_general(q_rows, cache_kv, dims, preferred_element_type=f32)
        is_valid = positions < number(table_ref, 1 + s)
        scores = jnp.where(is_valid, scores, neg_big)
        reach = reach_ref[s * DRAFT : (s + 1) * DRAFT, s * DRAFT : (s + 1) * DRAFT]
        allowed = jnp.concatenate([reach] * group_size, axis=0) > 0.5
        tree_scores = lax.dot_general(q_rows, tree_kv, dims, preferred_element_type=f32)
        tree_scores = jnp.where(allowed, tree_scores, neg_big)
        top = jnp.maximum(
            jnp.max(scores, axis=1, keepdims=True), jnp.max(tree_scores, axis=1, keepdims=True)
        )
        weights = jnp.where(is_valid, jnp.exp(scores - top), 0.0).astype(bf16)
        tree_weights = jnp.where(allowed, jnp.exp(tree_scores - top), 0.0).astype(bf16)
        total = jnp.sum(weights.astype(f32), axis=1, keepdims=True) + jnp.sum(
            tree_weights.astype(f32), axis=1, keepdims=True
        )
        mixed = jnp.dot(weights, cache_kv, preferred_element_type=f32) + jnp.dot(
            tree_weights, tree_kv, preferred_element_type=f32
        )
        outs.append(mixed / total)
    pair_rows, last_rows = [], []
    for out in outs:
        head_out = [out[r * DRAFT : (r + 1) * DRAFT] for r in range(group_size)]
        pair_rows.append(
            jnp.where(lane_low, pltpu.roll(head_out[0], HEAD, 1), head_out[1]).astype(bf16)
        )
        last_rows.append(head_out[2])
    last = jnp.where(lane_low, pltpu.roll(last_rows[0], HEAD, 1), last_rows[1]).astype(bf16)
    res_tiles = [res_ref[:, c * WIDE : (c + 1) * WIDE] for c in range(res_ref.shape[1] // WIDE)]
    sent_ref[...] = jnp.concatenate(pair_rows + [last] + res_tiles, axis=0)
    rows = sent_ref.shape[0]
    near_ref[:rows, :] = sent_ref[...]
    near_ref[rows:, :] = kv_ref[...]


def accept_kernel(rows, chosen_ref, *refs):
    accepted_ref = refs[-1]
    tok_dev, width = accepted_ref.shape
    rank = lax.axis_index("tp")
    per_slot = DRAFT // tok_dev
    place = lax.rem(rank, per_slot)
    chosen = chosen_ref[lax.div(rank, per_slot), pl.ds(pl.multiple_of(place * tok_dev, tok_dev), tok_dev), :]
    is_even, is_first = lax.rem(place, 2) == 0, place < 2
    for c in range(width // WIDE):
        low = rows + c * tok_dev
        pairs = []
        for mine, other in (refs[:2], refs[2:4]):
            a, b = mine[low : low + tok_dev, :], other[low : low + tok_dev, :]
            pairs.append(
                jnp.concatenate([jnp.where(is_even, a, b), jnp.where(is_even, b, a)], axis=0)
            )
        near, far = pairs
        nodes = jnp.concatenate(
            [jnp.where(is_first, near, far), jnp.where(is_first, far, near)], axis=0
        )
        accepted_ref[:, c * WIDE : (c + 1) * WIDE] = jnp.dot(
            chosen, nodes, preferred_element_type=jnp.float32
        ).astype(jnp.bfloat16)


def fetch_kernel(picks, first, after_ref, source_ref, down_hbm, target_ref, down_ref, sems):
    del after_ref
    rows = target_ref.shape[0] // len(picks)
    span = pl.ds(first, down_ref.shape[0])
    copies = [pltpu.make_async_copy(down_hbm.at[span], down_ref, sems.at[len(picks)])]
    for place, k in enumerate(picks):
        pair = lax.bitwise_xor(lax.div(lax.axis_index("tp"), 2), k)
        start = pl.multiple_of(pair * rows, WIDE)
        copies.append(
            pltpu.make_async_copy(
                source_ref.at[pl.ds(start, rows)],
                target_ref.at[place * rows : (place + 1) * rows],
                sems.at[place],
            )
        )
    start_all(copies)


def join_heads(k, rows, group_rows, mine_ref, other_ref, residual_ref):
    f32, bf16 = jnp.float32, jnp.bfloat16
    half = group_rows // 2
    tok_dev = group_rows // KV_HEADS
    model = residual_ref.shape[1]
    res_start = group_rows + half
    rank = lax.axis_index("tp")
    is_even = lax.rem(rank, 2) == 0
    pair = lax.bitwise_xor(lax.div(rank, 2), k)
    lane_low = lax.broadcasted_iota(jnp.int32, (half, WIDE), 1) < HEAD
    mine, other = mine_ref[:rows, :], other_ref[:rows, :]
    even, odd = jnp.where(is_even, mine, other), jnp.where(is_even, other, mine)
    last_even = even[group_rows:res_start].astype(f32)
    last_odd = odd[group_rows:res_start].astype(f32)
    odd_swapped = pltpu.roll(odd[:group_rows].astype(f32), HEAD, 1)
    middle = jnp.concatenate(
        [
            jnp.where(lane_low, last_even, odd_swapped[:half]),
            jnp.where(lane_low, pltpu.roll(last_even, HEAD, 1), odd_swapped[half:]),
        ],
        axis=0,
    ).astype(bf16)
    end = jnp.concatenate(
        [
            jnp.where(lane_low, odd_swapped[:half], pltpu.roll(last_odd, HEAD, 1)),
            jnp.where(lane_low, odd_swapped[half:], last_odd),
        ],
        axis=0,
    ).astype(bf16)
    for q, block in enumerate((even, odd)):
        row = pl.multiple_of((2 * pair + q) * tok_dev, tok_dev)
        residual_ref[pl.ds(row, tok_dev), :] = jnp.concatenate(
            [
                block[res_start + c * tok_dev : res_start + (c + 1) * tok_dev]
                for c in range(model // WIDE)
            ],
            axis=1,
        ).astype(f32)
    return jnp.concatenate([even[:group_rows], middle, end], axis=1)


def keep_own(k, heads_ref, at, attn_ref):
    tok_dev = attn_ref.shape[0]
    width = attn_ref.shape[1] * 2 // KV_HEADS
    rank = lax.axis_index("tp")
    pair = lax.bitwise_xor(lax.div(rank, 2), k)
    own = pl.multiple_of(rank * tok_dev, tok_dev)
    attn_ref[:, pl.ds(pl.multiple_of(pair * width, WIDE), width)] = heads_ref[
        pl.ds(own, tok_dev), at : at + width
    ]


def early_kernel(rows, after_ref, down_hbm, weight_ref, *refs):
    del after_ref
    blocks, refs = refs[:-6], refs[-6:]
    hid_ref, attn_ref, down_ref, residual_ref, x_ref, sem = refs
    start = down_hbm.shape[0] - down_ref.shape[0]
    copy = pltpu.make_async_copy(down_hbm.at[start:], down_ref, sem)
    copy.start()
    group_rows = hid_ref.shape[0]
    residual_ref[...] = jnp.zeros_like(residual_ref)
    width = x_ref.shape[1] * 2 // len(blocks)
    for k in range(len(blocks) // 2):
        x_ref[:, k * width : (k + 1) * width] = join_heads(
            k, rows, group_rows, blocks[2 * k], blocks[2 * k + 1], residual_ref
        )
    for k in range(len(blocks) // 2):
        keep_own(k, x_ref, k * width, attn_ref)
    hid_ref[...] = residual_ref[...] + jnp.dot(
        x_ref[...], weight_ref[...], preferred_element_type=jnp.float32
    )
    copy.wait()


def expert_kernel(
    rows, count_ref, router_ref, gain_ref, before_ref, part_ref, *refs
):
    refs, late = refs[:-8], refs[-8:]
    far_ref, hid_ref, hidden_ref, attn_ref, x_ref, normed_ref, share_ref, residual_ref = late
    f32, bf16 = jnp.float32, jnp.bfloat16
    pairs = KV_HEADS // 2
    first = pairs // 2
    down_refs, refs = refs[: pairs + 1], refs[pairs + 1 :]
    blocks, refs = refs[: 2 * (pairs - first)], refs[2 * (pairs - first) :]
    weight_refs, unit_refs = refs[: pairs - first], refs[pairs - first :]
    unit_weights = [(ref, k) for ref in unit_refs for k in range(ref.shape[0])]
    units = len(unit_weights)
    tok_dev, model = hidden_ref.shape
    sources = KV_HEADS
    group_rows = sources * tok_dev
    rank = lax.axis_index("tp")
    own = pl.multiple_of(rank * tok_dev, tok_dev)
    attn_ref[...] = part_ref[...]
    residual_ref[...] = jnp.zeros_like(residual_ref)
    hidden, width = before_ref[...], x_ref.shape[1] // (pairs - first)
    for q, k in enumerate(reversed(range(first, pairs))):
        heads = join_heads(k, rows, group_rows, blocks[2 * q], blocks[2 * q + 1], residual_ref)
        x_ref[:, q * width : (q + 1) * width] = heads
        keep_own(k, x_ref, q * width, attn_ref)
        hidden += jnp.dot(heads, weight_refs[q][...], preferred_element_type=f32)
    hidden += residual_ref[...]
    hid_ref[...] = hidden
    gain = jnp.concatenate([gain_ref[c : c + 1, :] for c in range(model // WIDE)], axis=1)
    scale = lax.rsqrt(jnp.mean(hidden * hidden, axis=1, keepdims=True) + norm_eps)
    normed_ref[...] = (hidden * scale * gain).astype(bf16)
    hidden_ref[...] = hid_ref[pl.ds(own, tok_dev), :]
    logits = lax.dot_general(
        normed_ref[...], router_ref[...], (((1,), (1,)), ((), ())), preferred_element_type=f32
    )
    experts = router_ref.shape[0]
    expert_range = lax.broadcasted_iota(jnp.int32, (group_rows, experts), 1)
    count = count_ref[...]
    expo = jnp.where(count > 0.0, jnp.exp(logits), 0.0) * count
    routing = expo / jnp.sum(expo, axis=1, keepdims=True)
    unit_width = unit_refs[0].shape[2] // 2
    span = FF_E // unit_width
    each = span if units % span == 0 else 1
    for u in range(0, units, each):
        expert = (rank * units + u) // span
        share = jnp.sum(jnp.where(expert_range == expert, routing, 0.0), axis=1, keepdims=True)
        share_ref[u : u + each] = jnp.broadcast_to(share[None], (each, group_rows, unit_width))

    def one_unit(u):
        ref, k = unit_weights[u]
        both = jnp.dot(normed_ref[...], ref[k], preferred_element_type=f32)
        gate, up = both[:, :unit_width], both[:, unit_width:]
        return (gate / (1.0 + jnp.exp(-gate)) * up * share_ref[u]).astype(bf16)

    down_steps = [(ref, at) for ref in down_refs for at in range(ref.shape[0] // STEP)]
    for i in range(units // STEP):
        act = jnp.concatenate([one_unit(i * STEP + k) for k in range(STEP)], axis=1)
        ref, at = down_steps[i]
        down = ref[at * STEP : (at + 1) * STEP].reshape(STEP * unit_width, model)
        part = jnp.dot(act, down, preferred_element_type=f32)
        hid_ref[...] = part if i == 0 else hid_ref[...] + part
    for k in range(far_ref.shape[0]):
        copy_sums(sources // 4 + k, True, hid_ref, far_ref.at[k])


def copy_sums(k, crossing, hid_ref, ref):
    tok_dev = ref.shape[0]
    rank = lax.axis_index("tp")
    side = lax.rem(rank, 2)
    pair = lax.bitwise_xor(lax.div(rank, 2), k)
    target = 2 * pair + (1 - side if crossing else side)
    row = pl.multiple_of(target * tok_dev, tok_dev)
    ref[...] = hid_ref[pl.ds(row, tok_dev), :].astype(ref.dtype)


def near_kernel(hid_ref, mine_ref, near_ref):
    for k in range(mine_ref.shape[0]):
        copy_sums(k, False, hid_ref, mine_ref.at[k])
    for k in range(near_ref.shape[0]):
        copy_sums(k, True, hid_ref, near_ref.at[k])


def fold_kernel(first, after_ref, mine_ref, got_ref, hidden_ref, *sent_refs):
    del after_ref
    for k, ref in enumerate(sent_refs, first):
        total = mine_ref[k] + got_ref[k - first].astype(jnp.float32)
        if k == 0:
            total = total + hidden_ref[...]
        ref[...] = total.astype(ref.dtype)


def finish_kernel(attn_in_ref, accepted_in_ref, *refs):
    parts, (attn_ref, layer_ref, accepted_ref) = refs[:-3], refs[-3:]
    attn_ref[...] = attn_in_ref[...]
    accepted_ref[...] = accepted_in_ref[...]
    total = parts[0][...]
    for part in parts[1:]:
        total = total + part[...].astype(jnp.float32)
    layer_ref[...] = total.astype(jnp.bfloat16)


def in_hbm(*arrays):
    return tuple(pltpu.with_memory_space_constraint(a, pltpu.HBM) for a in arrays)


def spaces(text):
    kinds = {"a": pl.ANY, "v": pltpu.VMEM}
    return [pl.BlockSpec(memory_space=kinds[c]) for c in text]


def params(mebibytes=12):
    return pltpu.CompilerParams(vmem_limit_bytes=mebibytes << 20)


def cost(mebibytes):
    return pl.CostEstimate(flops=0, transcendentals=0, bytes_accessed=mebibytes << 20)


def swap(rows, mask):
    count = lax.axis_size("tp")
    return lax.ppermute(rows, "tp", [(i, i ^ mask) for i in range(count)])


def fetch(after, array, rows, picks, down_weight, first, units):
    shape = (rows * len(picks),) + array.shape[1:]
    down_shape = (units,) + down_weight.shape[1:]
    return pl.pallas_call(
        functools.partial(fetch_kernel, picks, first),
        out_shape=(pltpu.VMEM(shape, array.dtype), pltpu.VMEM(down_shape, array.dtype)),
        in_specs=spaces("aaa"),
        out_specs=tuple(spaces("vv")),
        scratch_shapes=[pltpu.SemaphoreType.DMA((len(picks) + 1,))],
        compiler_params=params(),
        cost_estimate=cost(2 * (math.prod(shape) + math.prod(down_shape)) >> 20),
        name="fetch",
    )(after, *in_hbm(array, down_weight))


def per_device_packed(
    queries,
    new_kv,
    residual,
    placement,
    lengths,
    page_table,
    cache_keys,
    cache_values,
    parents,
    accept_leaf,
    out_weight,
    norm_gain,
    router_weight,
    expert_ids,
    gate_up,
    down_weight,
):
    f32, bf16 = jnp.float32, jnp.bfloat16
    tok_dev, model = residual.shape
    tp_count = lax.axis_size("tp")
    slot_count = placement.shape[0]
    page_len, kv_width = cache_keys.shape[1:]
    group_rows = tok_dev * tp_count
    sent = lambda rows: jax.ShapeDtypeStruct((tp_count, rows, WIDE), bf16)
    dma = pltpu.SemaphoreType.DMA
    slots_smem = pltpu.SMEM((slot_count,), jnp.int32)
    pairs = tp_count // 2
    part = jax.ShapeDtypeStruct((2, slot_count * page_len, WIDE), bf16)
    loaded = (
        page_table.reshape(slot_count),
        placement,
        lengths,
        accept_leaf,
        cache_keys,
        cache_values,
        queries,
        new_kv,
        residual,
        parents,
        expert_ids.T,
        norm_gain.reshape(model // WIDE, WIDE),
    )
    *parts, joined, table, parents, ids, gain = pl.pallas_call(
        functools.partial(split_kernel, pairs),
        out_shape=(part,) * pairs
        + (
            jax.ShapeDtypeStruct((tok_dev, 2 * (model + kv_width)), bf16),
            pltpu.VMEM((8, WIDE), f32),
        )
        + tuple(pltpu.VMEM(a.shape, a.dtype) for a in loaded[9:]),
        in_specs=spaces("a" * len(loaded)),
        out_specs=tuple(spaces("v" * (pairs + 5))),
        scratch_shapes=[
            slots_smem,
            slots_smem,
            slots_smem,
            slots_smem,
            pltpu.VMEM(cache_keys.shape, bf16),
            pltpu.VMEM(cache_values.shape, bf16),
            pltpu.VMEM((pairs,) + part.shape, bf16),
            dma((len(loaded),)),
        ],
        compiler_params=params(),
        cost_estimate=cost(4),
        name="split",
    )(*in_hbm(*loaded))
    parts = parts[::-1]
    parts = [parts[0]] + [swap(parts[k], 2 * k) for k in range(1, pairs)]
    pulled = lax.all_gather(joined, "req", axis=0)
    nodes = slot_count * DRAFT
    units = gate_up.shape[0]
    cuts = [units * c // 20 // STEP * STEP for c in CUTS]
    ready = cuts[0]
    down_ready, reach, chosen, count = pl.pallas_call(
        tree_kernel,
        out_shape=(
            pltpu.VMEM((ready,) + down_weight.shape[1:], bf16),
            jax.ShapeDtypeStruct((nodes, nodes), f32),
            jax.ShapeDtypeStruct((slot_count, DRAFT, DRAFT), bf16),
            jax.ShapeDtypeStruct((group_rows, router_weight.shape[1]), f32),
        ),
        in_specs=spaces("aavvv"),
        out_specs=tuple(spaces("vvvv")),
        scratch_shapes=[dma],
        compiler_params=params(),
        cost_estimate=cost(8),
        name="tree",
    )(pulled, *in_hbm(down_weight), table, parents, ids)
    kv_rows = 2 * kv_width // WIDE * tok_dev
    packed, own_res, turned, own_kv = pl.pallas_call(
        functools.partial(route_kernel, kv_width),
        out_shape=(
            sent(3 * tok_dev),
            jax.ShapeDtypeStruct(residual.shape, bf16),
            jax.ShapeDtypeStruct((pairs * part.shape[1], WIDE), bf16),
            jax.ShapeDtypeStruct((kv_rows, WIDE), bf16),
        ),
        in_specs=spaces("aavv" + "v" * pairs),
        out_specs=tuple(spaces("vvvv")),
        compiler_params=params(),
        cost_estimate=cost(4),
        name="route",
    )(down_ready, *in_hbm(down_weight), table, pulled, *parts[::-1])
    turned = swap(turned, 1)
    packed = lax.all_to_all(packed, "tp", 0, 0, tiled=True)
    gate_up = pltpu.with_memory_space_constraint(gate_up, pltpu.VMEM)
    block_rows = group_rows + group_rows // 2 + (model // WIDE) * tok_dev
    block, near_block = pl.pallas_call(
        attend_kernel,
        out_shape=(
            jax.ShapeDtypeStruct((block_rows, WIDE), bf16),
            jax.ShapeDtypeStruct((block_rows + kv_rows, WIDE), bf16),
        ),
        in_specs=spaces("v" * (7 + pairs)),
        out_specs=tuple(spaces("vv")),
        compiler_params=params(),
        cost_estimate=cost(8),
        name="attend",
    )(gate_up, table, reach, packed, own_res, turned, own_kv, *parts[::-1])
    reached = [swap(near_block, 2)] + [swap(block, 2 * k) for k in range(2, pairs)]
    weights, downs, after = [], [down_ready], block
    rows = out_weight.shape[0] // pairs
    for k, picks in zip(ORDER, FETCHES):
        start, size = cuts[len(weights)], cuts[len(weights) + 1] - cuts[len(weights)]
        weight, down = fetch(after, out_weight, rows, picks, down_weight, start, size)
        fetched = (reached[k - 1], weight, down)
        reached[k - 1], weight, down = lax.optimization_barrier(fetched)
        downs.append(down)
        after = reached[k - 1]
        weights.append(weight)
    blocks = [block, swap(near_block, 1)]
    blocks += [a for got in reached for a in (got, swap(got, 1))]
    before, attn_part, down_rest = pl.pallas_call(
        functools.partial(early_kernel, block_rows),
        out_shape=(
            jax.ShapeDtypeStruct((group_rows, model), f32),
            pltpu.VMEM(queries.shape, bf16),
            pltpu.VMEM((units - cuts[-1],) + down_weight.shape[1:], bf16),
        ),
        in_specs=spaces("aav" + "v" * pairs),
        out_specs=tuple(spaces("vvv")),
        scratch_shapes=[
            pltpu.VMEM((group_rows, model), f32),
            pltpu.VMEM((group_rows, HEADS * HEAD // 2), bf16),
            dma,
        ],
        compiler_params=params(),
        cost_estimate=cost(4),
        name="early",
    )(after, *in_hbm(down_weight), weights[0], *blocks[:pairs])
    accepted = pl.pallas_call(
        functools.partial(accept_kernel, block_rows),
        out_shape=pltpu.VMEM(new_kv.shape, bf16),
        in_specs=spaces("vvvvv"),
        out_specs=spaces("v")[0],
        compiler_params=params(),
        cost_estimate=cost(1),
        name="accept",
    )(chosen, near_block, *blocks[1:4])
    unit_weights = (gate_up,)
    far, sums, hidden, attn_own = pl.pallas_call(
        functools.partial(expert_kernel, block_rows),
        out_shape=(
            jax.ShapeDtypeStruct((pairs // 2, tok_dev, model), bf16),
            jax.ShapeDtypeStruct((group_rows, model), f32),
            jax.ShapeDtypeStruct((tok_dev, model), f32),
            pltpu.VMEM(queries.shape, bf16),
        ),
        in_specs=spaces("v" * (6 + len(downs) + pairs + pairs // 2 + len(unit_weights))),
        out_specs=tuple(spaces("vvvv")),
        scratch_shapes=[
            pltpu.VMEM((group_rows, HEADS * HEAD // 2), bf16),
            pltpu.VMEM((group_rows, model), bf16),
            pltpu.VMEM((units, group_rows, gate_up.shape[2] // 2), f32),
            pltpu.VMEM((group_rows, model), f32),
        ],
        compiler_params=params(),
        name="experts",
    )(
        count,
        pltpu.with_memory_space_constraint(router_weight.T, pltpu.VMEM),
        gain,
        before,
        attn_part,
        *downs,
        down_rest,
        *[a for k in reversed(range(pairs // 2, pairs)) for a in blocks[2 * k : 2 * k + 2]],
        weights[1],
        weights[2],
        *unit_weights,
    )
    far = swap(far, 1)
    mine, near = pl.pallas_call(
        near_kernel,
        out_shape=(
            jax.ShapeDtypeStruct((pairs, tok_dev, model), f32),
            jax.ShapeDtypeStruct((pairs // 2, tok_dev, model), bf16),
        ),
        in_specs=spaces("v"),
        out_specs=tuple(spaces("vv")),
        compiler_params=params(),
        cost_estimate=cost(4),
        name="near",
    )(sums)
    near = swap(near, 1)
    fold = lambda first, after, got: pl.pallas_call(
        functools.partial(fold_kernel, first),
        out_shape=tuple(
            jax.ShapeDtypeStruct((tok_dev, model), f32 if k == 0 else bf16)
            for k in range(first, first + pairs // 2)
        ),
        in_specs=spaces("avvv"),
        out_specs=tuple(spaces("v" * (pairs // 2))),
        compiler_params=params(),
        cost_estimate=cost(1),
        name="fold",
    )(after, mine, got, hidden)
    sums = fold(pairs // 2, hidden, far)
    folded = sums[0]
    sums = [swap(a, 2 * k) for k, a in enumerate(sums, pairs // 2)]
    close = fold(0, folded, near)
    sums = [close[0]] + [swap(close[k], 2 * k) for k in range(1, pairs // 2)] + sums
    return pl.pallas_call(
        finish_kernel,
        out_shape=(
            jax.ShapeDtypeStruct(queries.shape, bf16),
            jax.ShapeDtypeStruct(residual.shape, bf16),
            jax.ShapeDtypeStruct(new_kv.shape, bf16),
        ),
        in_specs=spaces("v" * (2 + pairs)),
        out_specs=tuple(spaces("vvv")),
        compiler_params=params(),
        name="finish",
    )(attn_own, accepted, sums[0], *sums[:0:-1])


def per_device(queries, new_kv, residual, placement, *rest):
    tok_dev = queries.shape[0]
    one_head_each = lax.axis_size("tp") == KV_HEADS
    whole_tiles = tok_dev % 16 == 0 and placement.shape[0] == 2 and tok_dev * KV_HEADS == 2 * DRAFT
    if one_head_each and whole_tiles and rest[1].shape[1] == 1:
        return per_device_packed(queries, new_kv, residual, placement, *rest)
    return per_device_plain(queries, new_kv, residual, placement, *rest)


def solution(mesh):
    in_specs = (
        P(("req", "tp"), None),
        P(("req", "tp"), None),
        P(("req", "tp"), None),
        P("req"),
        P("req"),
        P("req", None, "tp"),
        P(("req", "tp"), None, None),
        P(("req", "tp"), None, None),
        P("req", None),
        P("req"),
        P(),
        P(),
        P(),
        P("req", None),
        P("tp", None, None),
        P("tp", None, None),
    )
    out_specs = (P(("req", "tp"), None), P(("req", "tp"), None), P(("req", "tp"), None))
    return jax.shard_map(
        per_device, mesh=mesh, in_specs=in_specs, out_specs=out_specs, check_vma=False
    )
```

```python
import functools
import math

import jax
import jax.numpy as jnp
from jax import lax
from jax.experimental import pallas as pl
from jax.experimental.pallas import tpu as pltpu
from jax.sharding import PartitionSpec as P

HEADS = 24
KV_HEADS = 8
HEAD = 64
FF_E = 512
UNIT = 128
DRAFT = 64
WIDE = 128
STEP = 2
READY = 6
ORDER = (1, 3, 2)
FETCHES = ((0, 1), (3,), (2,))


neg_big = -1e30
norm_eps = 1e-06


def joined_2(part, axis, combine):
    gathered = jax.tree.map(lambda a: lax.all_gather(a, axis), part)

    def take(source):
        return jax.tree.map(lambda a: lax.dynamic_index_in_dim(a, source, 0, False), gathered)

    return lax.fori_loop(
        1, lax.axis_size(axis), lambda source, state: combine(state, take(source)), take(0)
    )


def ancestry(parents):
    node_count = parents.shape[-1]
    node_ids = jnp.arange(node_count, dtype=jnp.int32)
    linked = (parents[:, :, None] == node_ids[None, None, :]) & (node_ids[None, :, None] > 0)
    reached = jnp.maximum(linked.astype(jnp.float32), jnp.eye(node_count, dtype=jnp.float32)[None])
    for _ in range(node_count.bit_length()):
        reached = jnp.minimum(
            jnp.einsum("rnm,rmk->rnk", reached, reached, precision=lax.Precision.HIGHEST), 1.0
        )
    return reached


def combine_stats(left_stats, right_stats):
    left_max, left_sum, left_out = left_stats
    right_max, right_sum, right_out = right_stats
    top_score = jnp.maximum(left_max, right_max)
    left_scale = jnp.exp(left_max - top_score)
    right_scale = jnp.exp(right_max - top_score)
    row_count, head_count = left_max.shape
    out_sum = (
        left_out.reshape(row_count, head_count, -1) * left_scale[..., None]
        + right_out.reshape(row_count, head_count, -1) * right_scale[..., None]
    )
    return (
        top_score,
        left_sum * left_scale + right_sum * right_scale,
        out_sum.reshape(row_count, -1),
    )


def finish_rows(stat_sum, stat_out):
    row_count, head_count = stat_sum.shape
    return (
        (stat_out.reshape(row_count, head_count, -1) / stat_sum[..., None])
        .reshape(row_count, -1)
        .astype(jnp.bfloat16)
    )


def project_rows(attn_rows, res_rows, out_weight):
    return res_rows.astype(jnp.float32) + jnp.dot(
        attn_rows, out_weight, preferred_element_type=jnp.float32
    )


def rms_normed(hidden, norm_gain):
    scale_rows = lax.rsqrt(jnp.mean(hidden * hidden, axis=-1, keepdims=True) + norm_eps)
    return (hidden * scale_rows * norm_gain).astype(jnp.bfloat16)


def unit_shares(normed_all, router_weight, expert_ids, tp_rank, units_dev):
    logits = jnp.dot(normed_all, router_weight, preferred_element_type=jnp.float32)
    expert_range = jnp.arange(router_weight.shape[1], dtype=jnp.int32)
    onehot = (expert_ids[:, :, None] == expert_range[None, None, :]).astype(jnp.float32)
    chosen = jnp.sum(logits[:, None, :] * onehot, axis=-1)
    expo_chosen = jnp.exp(chosen)
    expert_probs = expo_chosen / jnp.sum(expo_chosen, axis=-1, keepdims=True)
    routing = jnp.sum(expert_probs[:, :, None] * onehot, axis=1)
    unit_ids = tp_rank * units_dev + jnp.arange(units_dev, dtype=jnp.int32)
    expert_of_unit = unit_ids // (FF_E // UNIT)
    pick = (expert_range[:, None] == expert_of_unit[None, :]).astype(jnp.float32)
    return jnp.dot(routing, pick, precision=lax.Precision.HIGHEST)


def per_device_plain(
    queries,
    new_kv,
    residual,
    placement,
    lengths,
    page_table,
    cache_keys,
    cache_values,
    parents,
    accept_leaf,
    out_weight,
    norm_gain,
    router_weight,
    expert_ids,
    gate_up,
    down_weight,
):
    tok_dev = queries.shape[0]
    tp_count = lax.axis_size("tp")
    tp_rank = lax.axis_index("tp")
    group_rows = tok_dev * tp_count
    slot_count = placement.shape[0]
    kv_width = cache_keys.shape[2]
    page_len = cache_keys.shape[1]
    group_size = HEADS // KV_HEADS
    score_scale = 1.0 / math.sqrt(HEAD)
    row_start = tp_rank * tok_dev
    pulled_q, pulled_kv, pulled_res = (
        lax.all_gather(queries, "req", axis=0, tiled=True),
        lax.all_gather(new_kv, "req", axis=0, tiled=True),
        lax.all_gather(residual, "req", axis=0, tiled=True),
    )
    row_offsets = jnp.arange(tok_dev, dtype=jnp.int32)
    row_pos = row_start + row_offsets
    row_slot = row_pos // DRAFT
    slot_match = row_slot[:, None] == jnp.arange(slot_count, dtype=jnp.int32)[None, :]
    source_group = jnp.sum(jnp.where(slot_match, placement[None, :] // slot_count, 0), axis=1)
    source_rows = source_group * tok_dev + row_offsets
    own_q = jnp.take(pulled_q, source_rows, axis=0)
    own_kv = jnp.take(pulled_kv, source_rows, axis=0)
    own_res = jnp.take(pulled_res, source_rows, axis=0)
    all_q, all_kv = (
        lax.all_gather(own_q, "tp", axis=0, tiled=True),
        lax.all_gather(own_kv, "tp", axis=0, tiled=True),
    )
    local_pages = page_table.shape[1]
    page_ids = page_table[:, :, 0].reshape(-1)
    keys_local = jnp.take(cache_keys, page_ids, axis=0).reshape(
        slot_count, local_pages, page_len, KV_HEADS, HEAD
    )
    values_local = jnp.take(cache_values, page_ids, axis=0).reshape(
        slot_count, local_pages, page_len, KV_HEADS, HEAD
    )
    query_blocks = all_q.reshape(slot_count, DRAFT, KV_HEADS, group_size, HEAD)
    scores = (
        jnp.einsum(
            "sqgrd,sltgd->sqgrlt", query_blocks, keys_local, preferred_element_type=jnp.float32
        )
        * score_scale
    )
    positions = (
        jnp.arange(local_pages, dtype=jnp.int32)[:, None] * tp_count + tp_rank
    ) * page_len + jnp.arange(page_len, dtype=jnp.int32)[None, :]
    is_valid = (positions[None] < lengths[:, None, None])[:, None, None, None]
    scores = jnp.where(is_valid, scores, neg_big)
    block_max = jnp.max(scores, axis=-1)
    weights = jnp.where(is_valid, jnp.exp(scores - block_max[..., None]), 0.0).astype(jnp.bfloat16)
    block_sum = jnp.sum(weights.astype(jnp.float32), axis=-1)
    block_out = jnp.einsum(
        "sqgrlt,sltgd->sqgrld", weights, values_local, preferred_element_type=jnp.float32
    )
    page_top = jnp.max(block_max, axis=-1)
    page_scale = jnp.exp(block_max - page_top[..., None])
    stat_max = page_top.reshape(group_rows, HEADS)
    stat_sum = jnp.sum(block_sum * page_scale, axis=-1).reshape(group_rows, HEADS)
    stat_out = jnp.sum(block_out * page_scale[..., None], axis=-2).reshape(group_rows, HEADS * HEAD)
    reached = ancestry(parents)
    reach_rows = jnp.take(reached.reshape(slot_count * DRAFT, DRAFT), row_pos, axis=0)
    key_slot = jnp.arange(group_rows, dtype=jnp.int32) // DRAFT
    same_slot = key_slot[None, :] == row_slot[:, None]
    allowed = same_slot & (jnp.tile(reach_rows, (1, slot_count)) > 0.5)
    tree_keys = all_kv[:, :kv_width].reshape(group_rows, KV_HEADS, HEAD)
    tree_values = all_kv[:, kv_width:].reshape(group_rows, KV_HEADS, HEAD)
    own_blocks = own_q.reshape(tok_dev, KV_HEADS, group_size, HEAD)
    tree_scores = (
        jnp.einsum("igrd,kgd->igrk", own_blocks, tree_keys, preferred_element_type=jnp.float32)
        * score_scale
    )
    tree_mask = allowed[:, None, None, :]
    tree_scores = jnp.where(tree_mask, tree_scores, neg_big)
    tree_max = jnp.max(tree_scores, axis=-1)
    tree_weights = jnp.where(tree_mask, jnp.exp(tree_scores - tree_max[..., None]), 0.0).astype(
        jnp.bfloat16
    )
    tree_sum = jnp.sum(tree_weights.astype(jnp.float32), axis=-1)
    tree_out = jnp.einsum(
        "igrk,kgd->igrd", tree_weights, tree_values, preferred_element_type=jnp.float32
    )
    own_stats = (
        lax.dynamic_slice_in_dim(stat_max, row_start, tok_dev, 0),
        lax.dynamic_slice_in_dim(stat_sum, row_start, tok_dev, 0),
        lax.dynamic_slice_in_dim(stat_out, row_start, tok_dev, 0),
    )
    tree_stats = (
        tree_max.reshape(tok_dev, HEADS),
        tree_sum.reshape(tok_dev, HEADS),
        tree_out.reshape(tok_dev, HEADS * HEAD),
    )
    joined = combine_stats(own_stats, tree_stats)
    stat_max = lax.dynamic_update_slice_in_dim(stat_max, joined[0], row_start, 0)
    stat_sum = lax.dynamic_update_slice_in_dim(stat_sum, joined[1], row_start, 0)
    stat_out = lax.dynamic_update_slice_in_dim(stat_out, joined[2], row_start, 0)
    normed_all = None
    merged = joined_2((stat_max, stat_sum, stat_out), "tp", combine_stats)
    attn_own = finish_rows(
        lax.dynamic_slice_in_dim(merged[1], row_start, tok_dev, 0),
        lax.dynamic_slice_in_dim(merged[2], row_start, tok_dev, 0),
    )
    hidden_own = project_rows(attn_own, own_res, out_weight)
    normed_own = rms_normed(hidden_own, norm_gain)
    units_dev = gate_up.shape[0]
    unit_width = gate_up.shape[2] // 2
    normed_all = lax.all_gather(normed_own, "tp", axis=0, tiled=True)
    shares = unit_shares(normed_all, router_weight, expert_ids, tp_rank, units_dev)
    gate_both = jnp.einsum("td,udh->tuh", normed_all, gate_up, preferred_element_type=jnp.float32)
    activated = (
        jax.nn.silu(gate_both[..., :unit_width]) * gate_both[..., unit_width:] * shares[:, :, None]
    ).astype(jnp.bfloat16)
    moe_own = lax.psum_scatter(
        jnp.einsum("tuh,uhd->td", activated, down_weight, preferred_element_type=jnp.float32),
        "tp",
        scatter_dimension=0,
        tiled=True,
    )
    layer_out = (hidden_own + moe_own).astype(jnp.bfloat16)
    node_ids = jnp.arange(DRAFT, dtype=jnp.int32)
    leaf_pick = (accept_leaf[:, None] == node_ids[None, :]).astype(jnp.float32)
    path_weight = jnp.einsum("sn,snk->sk", leaf_pick, reached, precision=lax.Precision.HIGHEST)
    path_flags = (path_weight > 0.5).astype(jnp.int32)
    path_rank = jnp.cumsum(path_flags, axis=1) - 1
    chosen_node = (path_flags[:, None, :] > 0) & (path_rank[:, None, :] == node_ids[None, :, None])
    own_choice = jnp.take(chosen_node.reshape(slot_count * DRAFT, DRAFT), row_pos, axis=0)
    spread = same_slot & jnp.tile(own_choice, (1, slot_count))
    accepted = jnp.dot(
        spread.astype(jnp.bfloat16), all_kv, preferred_element_type=jnp.float32
    ).astype(jnp.bfloat16)
    return (attn_own, layer_out, accepted)


def start_all(copies):
    for copy in copies:
        copy.start()
    for copy in copies:
        copy.wait()


def split_kernel(pairs, *refs):
    (
        pages_hbm, placement_hbm, lengths_hbm, leaf_hbm, keys_hbm, values_hbm, queries_hbm,
        new_kv_hbm, residual_hbm, parents_hbm, ids_hbm, gain_hbm,
    ) = refs[:12]
    parts, refs = refs[12 : 12 + pairs], refs[12 + pairs :]
    joined_ref, table_ref, parents_ref, ids_ref, gain_ref = refs[:5]
    pages_ref, placement_ref, lengths_ref, leaf_ref, keys_ref, values_ref, split_ref, sems = refs[5:]
    slot_count = pages_ref.shape[0]
    page_len = keys_ref.shape[1]
    tok_dev = joined_ref.shape[0]
    moves = [
        (pages_hbm, pages_ref),
        (keys_hbm, keys_ref),
        (values_hbm, values_ref),
        (placement_hbm, placement_ref),
        (lengths_hbm, lengths_ref),
        (leaf_hbm, leaf_ref),
        (parents_hbm, parents_ref),
        (ids_hbm, ids_ref),
        (gain_hbm, gain_ref),
    ]
    column = 0
    for source in (queries_hbm, new_kv_hbm, residual_hbm):
        moves.append((source, joined_ref.at[:, column : column + source.shape[1]]))
        column += source.shape[1]
    start_all(
        [pltpu.make_async_copy(a, b, sems.at[k]) for k, (a, b) in enumerate(moves)]
    )
    slot = lax.div(lax.axis_index("tp") * tok_dev, DRAFT)
    numbers = [lax.div(placement_ref[slot], slot_count)]
    numbers += [lengths_ref[s] for s in range(slot_count)]
    numbers += [leaf_ref[s] for s in range(slot_count)]
    for row, number in enumerate(numbers):
        table_ref[row : row + 1, :] = jnp.full((1, WIDE), number, jnp.int32).astype(jnp.float32)
    for head in range(KV_HEADS):
        low = head * HEAD
        for s in range(slot_count):
            page = pages_ref[s]
            split_ref[head // 2, head % 2, s * page_len : (s + 1) * page_len, :] = jnp.concatenate(
                [keys_ref[page, :, low : low + HEAD], values_ref[page, :, low : low + HEAD]], axis=1
            )
    pair = lax.div(lax.axis_index("tp"), 2)
    for k, part in enumerate(parts):
        part[...] = split_ref[lax.bitwise_xor(pair, pairs - 1 - k)]


def number(table_ref, row):
    return jnp.max(table_ref[row : row + 1, :]).astype(jnp.int32)


def route_kernel(kv_width, after_ref, weight_hbm, table_ref, pulled_ref, *refs):
    del after_ref, weight_hbm
    parts, (sent_ref, res_ref, turned_ref, kv_ref) = refs[:-4][::-1], refs[-4:]
    rank = lax.axis_index("tp")
    other = 1 - lax.rem(rank, 2)
    size = parts[0].shape[1]
    for k, part in enumerate(parts):
        turned_ref[k * size : (k + 1) * size, :] = part[other]
    q_width = HEADS * HEAD
    tok_dev = pulled_ref.shape[1]
    rows = pulled_ref[number(table_ref, 0)]
    res_ref[...] = rows[:, q_width + 2 * kv_width :]
    tiles = [rows[:, q_width + c : q_width + c + WIDE] for c in range(0, 2 * kv_width, WIDE)]
    kv_ref[...] = jnp.concatenate(tiles, axis=0)
    head_rows = (HEADS // KV_HEADS) * HEAD
    tail = jnp.zeros((tok_dev, 2 * WIDE - head_rows), rows.dtype)
    for head in range(KV_HEADS):
        q_low = head * head_rows
        pair = jnp.concatenate([rows[:, q_low : q_low + head_rows], tail], axis=1)
        sent_ref[head, :tok_dev, :] = pair[:, :WIDE]
        sent_ref[head, tok_dev : 2 * tok_dev, :] = pair[:, WIDE:]
        k_low = q_width + head * HEAD
        sent_ref[head, 2 * tok_dev :, :] = jnp.concatenate(
            [rows[:, k_low : k_low + HEAD], rows[:, k_low + kv_width : k_low + kv_width + HEAD]],
            axis=1,
        )


def ancestor_rows(parents_ref):
    slot_count = parents_ref.shape[0]
    total = slot_count * DRAFT
    row = jnp.concatenate(
        [parents_ref[s : s + 1, :] + s * DRAFT for s in range(slot_count)], axis=1
    )
    from_ids = lax.broadcasted_iota(jnp.int32, (total, total), 0)
    to_ids = lax.broadcasted_iota(jnp.int32, (total, total), 1)
    linked = (from_ids == jnp.broadcast_to(row, (total, total))) & (lax.rem(to_ids, DRAFT) > 0)
    reached = jnp.where(linked | (from_ids == to_ids), 1.0, 0.0)
    for _ in range((DRAFT - 1).bit_length()):
        half = reached.astype(jnp.bfloat16)
        reached = jnp.minimum(jnp.dot(half, half, preferred_element_type=jnp.float32), 1.0)
    return reached.T


def tree_kernel(
    after_ref, down_hbm, table_ref, parents_ref, ids_ref, down_ref, reach_ref, chosen_ref,
    count_ref, sem,
):
    del after_ref
    copy = pltpu.make_async_copy(down_hbm.at[: down_ref.shape[0]], down_ref, sem)
    copy.start()
    slot_count = parents_ref.shape[0]
    reach_ref[...] = ancestor_rows(parents_ref)
    node_from = lax.broadcasted_iota(jnp.int32, (DRAFT, DRAFT), 0)
    node_to = lax.broadcasted_iota(jnp.int32, (DRAFT, DRAFT), 1)
    upto = jnp.where(node_from <= node_to, 1.0, 0.0).astype(jnp.bfloat16)
    for s in range(slot_count):
        leaf = number(table_ref, 1 + slot_count + s)
        path = reach_ref[pl.ds(s * DRAFT + leaf, 1), s * DRAFT : (s + 1) * DRAFT]
        path = jnp.broadcast_to(path, (DRAFT, DRAFT))
        rank = jnp.dot(path.astype(jnp.bfloat16), upto, preferred_element_type=jnp.float32)
        chosen = (path > 0.5) & (rank == (node_from + 1).astype(jnp.float32))
        chosen_ref[s] = jnp.where(chosen, 1.0, 0.0).astype(jnp.bfloat16)
    ids = ids_ref[...].astype(jnp.float32).T
    names = lax.broadcasted_iota(jnp.int32, count_ref.shape, 1).astype(jnp.float32)
    count = jnp.zeros(count_ref.shape, jnp.float32)
    for k in range(ids.shape[1]):
        count = count + jnp.where(ids[:, k : k + 1] == names, 1.0, 0.0)
    count_ref[...] = count
    copy.wait()


def attend_kernel(units_ref, table_ref, reach_ref, got_ref, res_ref, turned_ref, kv_ref, *refs):
    del units_ref
    parts, (sent_ref, near_ref) = refs[:-2][::-1], refs[-2:]
    slot_count = reach_ref.shape[0] // DRAFT
    sources = got_ref.shape[0]
    tok_dev = res_ref.shape[0]
    page_len = parts[0].shape[1] // slot_count
    per_slot = DRAFT // tok_dev
    group_size = HEADS // KV_HEADS
    f32, bf16 = jnp.float32, jnp.bfloat16
    lane_low = lax.broadcasted_iota(jnp.int32, (DRAFT, WIDE), 1) < HEAD
    rank = lax.axis_index("tp")
    side = lax.rem(rank, 2)
    within = lax.broadcasted_iota(jnp.int32, (1, page_len), 1)
    positions = []
    for k in range(len(parts)):
        pair = lax.bitwise_xor(lax.div(rank, 2), k)
        for page in (2 * pair + side, 2 * pair + 1 - side):
            positions.append(within + page * page_len)
    positions = jnp.concatenate(positions, axis=1)
    dims = (((1,), (1,)), ((), ()))
    scale = 1.0 / math.sqrt(HEAD)
    outs = []
    for s in range(slot_count):
        first = s * per_slot

        def part(k):
            low = k * tok_dev
            return jnp.concatenate(
                [got_ref[first + i, low : low + tok_dev, :] for i in range(per_slot)], axis=0
            )

        q_pair, q_last, tree_kv = part(0).astype(f32) * scale, part(1).astype(f32) * scale, part(2)
        q_rows = jnp.concatenate(
            [
                jnp.where(lane_low, q_pair, 0.0),
                jnp.where(lane_low, pltpu.roll(q_pair, HEAD, 1), 0.0),
                jnp.where(lane_low, q_last, 0.0),
            ],
            axis=0,
        ).astype(bf16)
        at = slice(s * page_len, (s + 1) * page_len)
        cache_kv = jnp.concatenate(
            [a for k, part in enumerate(parts) for a in (part[side, at, :], turned_ref[k * parts[0].shape[1] + at.start : k * parts[0].shape[1] + at.stop, :])],
            axis=0,
        )
        scores = lax.dot_general(q_rows, cache_kv, dims, preferred_element_type=f32)
        is_valid = positions < number(table_ref, 1 + s)
        scores = jnp.where(is_valid, scores, neg_big)
        reach = reach_ref[s * DRAFT : (s + 1) * DRAFT, s * DRAFT : (s + 1) * DRAFT]
        allowed = jnp.concatenate([reach] * group_size, axis=0) > 0.5
        tree_scores = lax.dot_general(q_rows, tree_kv, dims, preferred_element_type=f32)
        tree_scores = jnp.where(allowed, tree_scores, neg_big)
        top = jnp.maximum(
            jnp.max(scores, axis=1, keepdims=True), jnp.max(tree_scores, axis=1, keepdims=True)
        )
        weights = jnp.where(is_valid, jnp.exp(scores - top), 0.0).astype(bf16)
        tree_weights = jnp.where(allowed, jnp.exp(tree_scores - top), 0.0).astype(bf16)
        total = jnp.sum(weights.astype(f32), axis=1, keepdims=True) + jnp.sum(
            tree_weights.astype(f32), axis=1, keepdims=True
        )
        mixed = jnp.dot(weights, cache_kv, preferred_element_type=f32) + jnp.dot(
            tree_weights, tree_kv, preferred_element_type=f32
        )
        outs.append(mixed / total)
    pair_rows, last_rows = [], []
    for out in outs:
        head_out = [out[r * DRAFT : (r + 1) * DRAFT] for r in range(group_size)]
        pair_rows.append(
            jnp.where(lane_low, pltpu.roll(head_out[0], HEAD, 1), head_out[1]).astype(bf16)
        )
        last_rows.append(head_out[2])
    last = jnp.where(lane_low, pltpu.roll(last_rows[0], HEAD, 1), last_rows[1]).astype(bf16)
    res_tiles = [res_ref[:, c * WIDE : (c + 1) * WIDE] for c in range(res_ref.shape[1] // WIDE)]
    sent_ref[...] = jnp.concatenate(pair_rows + [last] + res_tiles, axis=0)
    rows = sent_ref.shape[0]
    near_ref[:rows, :] = sent_ref[...]
    near_ref[rows:, :] = kv_ref[...]


def accept_kernel(rows, chosen_ref, *refs):
    accepted_ref = refs[-1]
    tok_dev, width = accepted_ref.shape
    rank = lax.axis_index("tp")
    per_slot = DRAFT // tok_dev
    place = lax.rem(rank, per_slot)
    chosen = chosen_ref[lax.div(rank, per_slot), pl.ds(pl.multiple_of(place * tok_dev, tok_dev), tok_dev), :]
    is_even, is_first = lax.rem(place, 2) == 0, place < 2
    for c in range(width // WIDE):
        low = rows + c * tok_dev
        pairs = []
        for mine, other in (refs[:2], refs[2:4]):
            a, b = mine[low : low + tok_dev, :], other[low : low + tok_dev, :]
            pairs.append(
                jnp.concatenate([jnp.where(is_even, a, b), jnp.where(is_even, b, a)], axis=0)
            )
        near, far = pairs
        nodes = jnp.concatenate(
            [jnp.where(is_first, near, far), jnp.where(is_first, far, near)], axis=0
        )
        accepted_ref[:, c * WIDE : (c + 1) * WIDE] = jnp.dot(
            chosen, nodes, preferred_element_type=jnp.float32
        ).astype(jnp.bfloat16)


def fetch_kernel(picks, after_ref, source_ref, target_ref, sems):
    del after_ref
    rows = target_ref.shape[0] // len(picks)
    copies = []
    for place, k in enumerate(picks):
        pair = lax.bitwise_xor(lax.div(lax.axis_index("tp"), 2), k)
        start = pl.multiple_of(pair * rows, WIDE)
        copies.append(
            pltpu.make_async_copy(
                source_ref.at[pl.ds(start, rows)],
                target_ref.at[place * rows : (place + 1) * rows],
                sems.at[place],
            )
        )
    start_all(copies)


def join_heads(k, rows, group_rows, mine_ref, other_ref, residual_ref):
    f32, bf16 = jnp.float32, jnp.bfloat16
    half = group_rows // 2
    tok_dev = group_rows // KV_HEADS
    model = residual_ref.shape[1]
    res_start = group_rows + half
    rank = lax.axis_index("tp")
    is_even = lax.rem(rank, 2) == 0
    pair = lax.bitwise_xor(lax.div(rank, 2), k)
    lane_low = lax.broadcasted_iota(jnp.int32, (half, WIDE), 1) < HEAD
    mine, other = mine_ref[:rows, :], other_ref[:rows, :]
    even, odd = jnp.where(is_even, mine, other), jnp.where(is_even, other, mine)
    last_even = even[group_rows:res_start].astype(f32)
    last_odd = odd[group_rows:res_start].astype(f32)
    odd_swapped = pltpu.roll(odd[:group_rows].astype(f32), HEAD, 1)
    middle = jnp.concatenate(
        [
            jnp.where(lane_low, last_even, odd_swapped[:half]),
            jnp.where(lane_low, pltpu.roll(last_even, HEAD, 1), odd_swapped[half:]),
        ],
        axis=0,
    ).astype(bf16)
    end = jnp.concatenate(
        [
            jnp.where(lane_low, odd_swapped[:half], pltpu.roll(last_odd, HEAD, 1)),
            jnp.where(lane_low, odd_swapped[half:], last_odd),
        ],
        axis=0,
    ).astype(bf16)
    for q, block in enumerate((even, odd)):
        row = pl.multiple_of((2 * pair + q) * tok_dev, tok_dev)
        residual_ref[pl.ds(row, tok_dev), :] = jnp.concatenate(
            [
                block[res_start + c * tok_dev : res_start + (c + 1) * tok_dev]
                for c in range(model // WIDE)
            ],
            axis=1,
        ).astype(f32)
    return jnp.concatenate([even[:group_rows], middle, end], axis=1)


def keep_own(k, heads_ref, at, attn_ref):
    tok_dev = attn_ref.shape[0]
    width = attn_ref.shape[1] * 2 // KV_HEADS
    rank = lax.axis_index("tp")
    pair = lax.bitwise_xor(lax.div(rank, 2), k)
    own = pl.multiple_of(rank * tok_dev, tok_dev)
    attn_ref[:, pl.ds(pl.multiple_of(pair * width, WIDE), width)] = heads_ref[
        pl.ds(own, tok_dev), at : at + width
    ]


def early_kernel(rows, after_ref, down_hbm, weight_ref, *refs):
    del after_ref
    blocks, refs = refs[:-6], refs[-6:]
    hid_ref, attn_ref, down_ref, residual_ref, x_ref, sem = refs
    start = down_hbm.shape[0] - down_ref.shape[0]
    copy = pltpu.make_async_copy(down_hbm.at[start:], down_ref, sem)
    copy.start()
    group_rows = hid_ref.shape[0]
    residual_ref[...] = jnp.zeros_like(residual_ref)
    width = x_ref.shape[1] * 2 // len(blocks)
    for k in range(len(blocks) // 2):
        x_ref[:, k * width : (k + 1) * width] = join_heads(
            k, rows, group_rows, blocks[2 * k], blocks[2 * k + 1], residual_ref
        )
    for k in range(len(blocks) // 2):
        keep_own(k, x_ref, k * width, attn_ref)
    hid_ref[...] = residual_ref[...] + jnp.dot(
        x_ref[...], weight_ref[...], preferred_element_type=jnp.float32
    )
    copy.wait()


def expert_kernel(
    rows, count_ref, router_ref, gain_ref, before_ref, part_ref, *refs
):
    refs, late = refs[:-8], refs[-8:]
    far_ref, hid_ref, hidden_ref, attn_ref, x_ref, normed_ref, share_ref, residual_ref = late
    f32, bf16 = jnp.float32, jnp.bfloat16
    pairs = KV_HEADS // 2
    first = pairs // 2
    down_refs, refs = refs[:2], refs[2:]
    blocks, refs = refs[: 2 * (pairs - first)], refs[2 * (pairs - first) :]
    weight_refs, unit_refs = refs[: pairs - first], refs[pairs - first :]
    unit_weights = [(ref, k) for ref in unit_refs for k in range(ref.shape[0])]
    units = len(unit_weights)
    tok_dev, model = hidden_ref.shape
    sources = KV_HEADS
    group_rows = sources * tok_dev
    rank = lax.axis_index("tp")
    own = pl.multiple_of(rank * tok_dev, tok_dev)
    attn_ref[...] = part_ref[...]
    residual_ref[...] = jnp.zeros_like(residual_ref)
    hidden, width = before_ref[...], x_ref.shape[1] // (pairs - first)
    for q, k in enumerate(reversed(range(first, pairs))):
        heads = join_heads(k, rows, group_rows, blocks[2 * q], blocks[2 * q + 1], residual_ref)
        x_ref[:, q * width : (q + 1) * width] = heads
        keep_own(k, x_ref, q * width, attn_ref)
        hidden += jnp.dot(heads, weight_refs[q][...], preferred_element_type=f32)
    hidden += residual_ref[...]
    hid_ref[...] = hidden
    gain = jnp.concatenate([gain_ref[c : c + 1, :] for c in range(model // WIDE)], axis=1)
    scale = lax.rsqrt(jnp.mean(hidden * hidden, axis=1, keepdims=True) + norm_eps)
    normed_ref[...] = (hidden * scale * gain).astype(bf16)
    hidden_ref[...] = hid_ref[pl.ds(own, tok_dev), :]
    logits = lax.dot_general(
        normed_ref[...], router_ref[...], (((1,), (1,)), ((), ())), preferred_element_type=f32
    )
    experts = router_ref.shape[0]
    expert_range = lax.broadcasted_iota(jnp.int32, (group_rows, experts), 1)
    count = count_ref[...]
    expo = jnp.where(count > 0.0, jnp.exp(logits), 0.0) * count
    routing = expo / jnp.sum(expo, axis=1, keepdims=True)
    unit_width = unit_refs[0].shape[2] // 2
    span = FF_E // unit_width
    each = span if units % span == 0 else 1
    for u in range(0, units, each):
        expert = (rank * units + u) // span
        share = jnp.sum(jnp.where(expert_range == expert, routing, 0.0), axis=1, keepdims=True)
        share_ref[u : u + each] = jnp.broadcast_to(share[None], (each, group_rows, unit_width))

    def one_unit(u):
        ref, k = unit_weights[u]
        both = jnp.dot(normed_ref[...], ref[k], preferred_element_type=f32)
        gate, up = both[:, :unit_width], both[:, unit_width:]
        return (gate / (1.0 + jnp.exp(-gate)) * up * share_ref[u]).astype(bf16)

    down_steps = [(ref, at) for ref in down_refs for at in range(ref.shape[0] // STEP)]
    for i in range(units // STEP):
        act = jnp.concatenate([one_unit(i * STEP + k) for k in range(STEP)], axis=1)
        ref, at = down_steps[i]
        down = ref[at * STEP : (at + 1) * STEP].reshape(STEP * unit_width, model)
        part = jnp.dot(act, down, preferred_element_type=f32)
        hid_ref[...] = part if i == 0 else hid_ref[...] + part
    for k in range(far_ref.shape[0]):
        copy_sums(sources // 4 + k, True, hid_ref, far_ref.at[k])


def copy_sums(k, crossing, hid_ref, ref):
    tok_dev = ref.shape[0]
    rank = lax.axis_index("tp")
    side = lax.rem(rank, 2)
    pair = lax.bitwise_xor(lax.div(rank, 2), k)
    target = 2 * pair + (1 - side if crossing else side)
    row = pl.multiple_of(target * tok_dev, tok_dev)
    ref[...] = hid_ref[pl.ds(row, tok_dev), :].astype(ref.dtype)


def near_kernel(hid_ref, mine_ref, near_ref):
    for k in range(mine_ref.shape[0]):
        copy_sums(k, False, hid_ref, mine_ref.at[k])
    for k in range(near_ref.shape[0]):
        copy_sums(k, True, hid_ref, near_ref.at[k])


def fold_kernel(first, after_ref, mine_ref, got_ref, hidden_ref, *sent_refs):
    del after_ref
    for k, ref in enumerate(sent_refs, first):
        total = mine_ref[k] + got_ref[k - first].astype(jnp.float32)
        if k == 0:
            total = total + hidden_ref[...]
        ref[...] = total.astype(ref.dtype)


def finish_kernel(attn_in_ref, accepted_in_ref, *refs):
    parts, (attn_ref, layer_ref, accepted_ref) = refs[:-3], refs[-3:]
    attn_ref[...] = attn_in_ref[...]
    accepted_ref[...] = accepted_in_ref[...]
    total = parts[0][...]
    for part in parts[1:]:
        total = total + part[...].astype(jnp.float32)
    layer_ref[...] = total.astype(jnp.bfloat16)


def in_hbm(*arrays):
    return tuple(pltpu.with_memory_space_constraint(a, pltpu.HBM) for a in arrays)


def spaces(text):
    kinds = {"a": pl.ANY, "v": pltpu.VMEM}
    return [pl.BlockSpec(memory_space=kinds[c]) for c in text]


def params(mebibytes=12):
    return pltpu.CompilerParams(vmem_limit_bytes=mebibytes << 20)


def cost(mebibytes):
    return pl.CostEstimate(flops=0, transcendentals=0, bytes_accessed=mebibytes << 20)


def swap(rows, mask):
    count = lax.axis_size("tp")
    return lax.ppermute(rows, "tp", [(i, i ^ mask) for i in range(count)])


def fetch(after, array, rows, picks):
    shape = (rows * len(picks),) + array.shape[1:]
    return pl.pallas_call(
        functools.partial(fetch_kernel, picks),
        out_shape=pltpu.VMEM(shape, array.dtype),
        in_specs=spaces("aa"),
        out_specs=spaces("v")[0],
        scratch_shapes=[pltpu.SemaphoreType.DMA((len(picks),))],
        compiler_params=params(),
        cost_estimate=cost(2 * math.prod(shape) >> 20),
        name="fetch",
    )(after, *in_hbm(array))


def per_device_packed(
    queries,
    new_kv,
    residual,
    placement,
    lengths,
    page_table,
    cache_keys,
    cache_values,
    parents,
    accept_leaf,
    out_weight,
    norm_gain,
    router_weight,
    expert_ids,
    gate_up,
    down_weight,
):
    f32, bf16 = jnp.float32, jnp.bfloat16
    tok_dev, model = residual.shape
    tp_count = lax.axis_size("tp")
    slot_count = placement.shape[0]
    page_len, kv_width = cache_keys.shape[1:]
    group_rows = tok_dev * tp_count
    sent = lambda rows: jax.ShapeDtypeStruct((tp_count, rows, WIDE), bf16)
    dma = pltpu.SemaphoreType.DMA
    slots_smem = pltpu.SMEM((slot_count,), jnp.int32)
    pairs = tp_count // 2
    part = jax.ShapeDtypeStruct((2, slot_count * page_len, WIDE), bf16)
    loaded = (
        page_table.reshape(slot_count),
        placement,
        lengths,
        accept_leaf,
        cache_keys,
        cache_values,
        queries,
        new_kv,
        residual,
        parents,
        expert_ids.T,
        norm_gain.reshape(model // WIDE, WIDE),
    )
    *parts, joined, table, parents, ids, gain = pl.pallas_call(
        functools.partial(split_kernel, pairs),
        out_shape=(part,) * pairs
        + (
            jax.ShapeDtypeStruct((tok_dev, 2 * (model + kv_width)), bf16),
            pltpu.VMEM((8, WIDE), f32),
        )
        + tuple(pltpu.VMEM(a.shape, a.dtype) for a in loaded[9:]),
        in_specs=spaces("a" * len(loaded)),
        out_specs=tuple(spaces("v" * (pairs + 5))),
        scratch_shapes=[
            slots_smem,
            slots_smem,
            slots_smem,
            slots_smem,
            pltpu.VMEM(cache_keys.shape, bf16),
            pltpu.VMEM(cache_values.shape, bf16),
            pltpu.VMEM((pairs,) + part.shape, bf16),
            dma((len(loaded),)),
        ],
        compiler_params=params(),
        cost_estimate=cost(4),
        name="split",
    )(*in_hbm(*loaded))
    parts = parts[::-1]
    parts = [parts[0]] + [swap(parts[k], 2 * k) for k in range(1, pairs)]
    pulled = lax.all_gather(joined, "req", axis=0)
    nodes = slot_count * DRAFT
    units = gate_up.shape[0]
    ready = READY * units // 20 // STEP * STEP
    down_ready, reach, chosen, count = pl.pallas_call(
        tree_kernel,
        out_shape=(
            pltpu.VMEM((ready,) + down_weight.shape[1:], bf16),
            jax.ShapeDtypeStruct((nodes, nodes), f32),
            jax.ShapeDtypeStruct((slot_count, DRAFT, DRAFT), bf16),
            jax.ShapeDtypeStruct((group_rows, router_weight.shape[1]), f32),
        ),
        in_specs=spaces("aavvv"),
        out_specs=tuple(spaces("vvvv")),
        scratch_shapes=[dma],
        compiler_params=params(),
        cost_estimate=cost(8),
        name="tree",
    )(pulled, *in_hbm(down_weight), table, parents, ids)
    kv_rows = 2 * kv_width // WIDE * tok_dev
    packed, own_res, turned, own_kv = pl.pallas_call(
        functools.partial(route_kernel, kv_width),
        out_shape=(
            sent(3 * tok_dev),
            jax.ShapeDtypeStruct(residual.shape, bf16),
            jax.ShapeDtypeStruct((pairs * part.shape[1], WIDE), bf16),
            jax.ShapeDtypeStruct((kv_rows, WIDE), bf16),
        ),
        in_specs=spaces("aavv" + "v" * pairs),
        out_specs=tuple(spaces("vvvv")),
        compiler_params=params(),
        cost_estimate=cost(4),
        name="route",
    )(down_ready, *in_hbm(down_weight), table, pulled, *parts[::-1])
    turned = swap(turned, 1)
    packed = lax.all_to_all(packed, "tp", 0, 0, tiled=True)
    gate_up = pltpu.with_memory_space_constraint(gate_up, pltpu.VMEM)
    block_rows = group_rows + group_rows // 2 + (model // WIDE) * tok_dev
    block, near_block = pl.pallas_call(
        attend_kernel,
        out_shape=(
            jax.ShapeDtypeStruct((block_rows, WIDE), bf16),
            jax.ShapeDtypeStruct((block_rows + kv_rows, WIDE), bf16),
        ),
        in_specs=spaces("v" * (7 + pairs)),
        out_specs=tuple(spaces("vv")),
        compiler_params=params(),
        cost_estimate=cost(8),
        name="attend",
    )(gate_up, table, reach, packed, own_res, turned, own_kv, *parts[::-1])
    reached = [swap(near_block, 2)] + [swap(block, 2 * k) for k in range(2, pairs)]
    weights, after = [], block
    rows = out_weight.shape[0] // pairs
    for k, picks in zip(ORDER, FETCHES):
        weight = fetch(after, out_weight, rows, picks)
        reached[k - 1], weight = lax.optimization_barrier((reached[k - 1], weight))
        after = reached[k - 1]
        weights.append(weight)
    blocks = [block, swap(near_block, 1)]
    blocks += [a for got in reached for a in (got, swap(got, 1))]
    before, attn_part, down_rest = pl.pallas_call(
        functools.partial(early_kernel, block_rows),
        out_shape=(
            jax.ShapeDtypeStruct((group_rows, model), f32),
            pltpu.VMEM(queries.shape, bf16),
            pltpu.VMEM((units - ready,) + down_weight.shape[1:], bf16),
        ),
        in_specs=spaces("aav" + "v" * pairs),
        out_specs=tuple(spaces("vvv")),
        scratch_shapes=[
            pltpu.VMEM((group_rows, model), f32),
            pltpu.VMEM((group_rows, HEADS * HEAD // 2), bf16),
            dma,
        ],
        compiler_params=params(),
        cost_estimate=cost(4),
        name="early",
    )(after, *in_hbm(down_weight), weights[0], *blocks[:pairs])
    accepted = pl.pallas_call(
        functools.partial(accept_kernel, block_rows),
        out_shape=pltpu.VMEM(new_kv.shape, bf16),
        in_specs=spaces("vvvvv"),
        out_specs=spaces("v")[0],
        compiler_params=params(),
        cost_estimate=cost(1),
        name="accept",
    )(chosen, near_block, *blocks[1:4])
    unit_weights = (gate_up,)
    far, sums, hidden, attn_own = pl.pallas_call(
        functools.partial(expert_kernel, block_rows),
        out_shape=(
            jax.ShapeDtypeStruct((pairs // 2, tok_dev, model), bf16),
            jax.ShapeDtypeStruct((group_rows, model), f32),
            jax.ShapeDtypeStruct((tok_dev, model), f32),
            pltpu.VMEM(queries.shape, bf16),
        ),
        in_specs=spaces("v" * (7 + pairs + pairs // 2 + len(unit_weights))),
        out_specs=tuple(spaces("vvvv")),
        scratch_shapes=[
            pltpu.VMEM((group_rows, HEADS * HEAD // 2), bf16),
            pltpu.VMEM((group_rows, model), bf16),
            pltpu.VMEM((units, group_rows, gate_up.shape[2] // 2), f32),
            pltpu.VMEM((group_rows, model), f32),
        ],
        compiler_params=params(),
        name="experts",
    )(
        count,
        pltpu.with_memory_space_constraint(router_weight.T, pltpu.VMEM),
        gain,
        before,
        attn_part,
        down_ready,
        down_rest,
        *[a for k in reversed(range(pairs // 2, pairs)) for a in blocks[2 * k : 2 * k + 2]],
        weights[1],
        weights[2],
        *unit_weights,
    )
    far = swap(far, 1)
    mine, near = pl.pallas_call(
        near_kernel,
        out_shape=(
            jax.ShapeDtypeStruct((pairs, tok_dev, model), f32),
            jax.ShapeDtypeStruct((pairs // 2, tok_dev, model), bf16),
        ),
        in_specs=spaces("v"),
        out_specs=tuple(spaces("vv")),
        compiler_params=params(),
        cost_estimate=cost(4),
        name="near",
    )(sums)
    near = swap(near, 1)
    fold = lambda first, after, got: pl.pallas_call(
        functools.partial(fold_kernel, first),
        out_shape=tuple(
            jax.ShapeDtypeStruct((tok_dev, model), f32 if k == 0 else bf16)
            for k in range(first, first + pairs // 2)
        ),
        in_specs=spaces("avvv"),
        out_specs=tuple(spaces("v" * (pairs // 2))),
        compiler_params=params(),
        cost_estimate=cost(1),
        name="fold",
    )(after, mine, got, hidden)
    sums = fold(pairs // 2, hidden, far)
    folded = sums[0]
    sums = [swap(a, 2 * k) for k, a in enumerate(sums, pairs // 2)]
    close = fold(0, folded, near)
    sums = [close[0]] + [swap(close[k], 2 * k) for k in range(1, pairs // 2)] + sums
    return pl.pallas_call(
        finish_kernel,
        out_shape=(
            jax.ShapeDtypeStruct(queries.shape, bf16),
            jax.ShapeDtypeStruct(residual.shape, bf16),
            jax.ShapeDtypeStruct(new_kv.shape, bf16),
        ),
        in_specs=spaces("v" * (2 + pairs)),
        out_specs=tuple(spaces("vvv")),
        compiler_params=params(),
        name="finish",
    )(attn_own, accepted, sums[0], *sums[:0:-1])


def per_device(queries, new_kv, residual, placement, *rest):
    tok_dev = queries.shape[0]
    one_head_each = lax.axis_size("tp") == KV_HEADS
    whole_tiles = tok_dev % 16 == 0 and placement.shape[0] == 2 and tok_dev * KV_HEADS == 2 * DRAFT
    if one_head_each and whole_tiles and rest[1].shape[1] == 1:
        return per_device_packed(queries, new_kv, residual, placement, *rest)
    return per_device_plain(queries, new_kv, residual, placement, *rest)


def solution(mesh):
    in_specs = (
        P(("req", "tp"), None),
        P(("req", "tp"), None),
        P(("req", "tp"), None),
        P("req"),
        P("req"),
        P("req", None, "tp"),
        P(("req", "tp"), None, None),
        P(("req", "tp"), None, None),
        P("req", None),
        P("req"),
        P(),
        P(),
        P(),
        P("req", None),
        P("tp", None, None),
        P("tp", None, None),
    )
    out_specs = (P(("req", "tp"), None), P(("req", "tp"), None), P(("req", "tp"), None))
    return jax.shard_map(
        per_device, mesh=mesh, in_specs=in_specs, out_specs=out_specs, check_vma=False
    )
```

```python
import functools
import math

import jax
import jax.numpy as jnp
from jax import lax
from jax.experimental import pallas as pl
from jax.experimental.pallas import tpu as pltpu
from jax.sharding import PartitionSpec as P

HEADS = 24
KV_HEADS = 8
HEAD = 64
FF_E = 512
UNIT = 128
DRAFT = 64
WIDE = 128
STEP = 2
CUTS = (6, 8, 10, 12)
ORDER = (1, 3, 2)
FETCHES = ((0, 1), (3,), (2,))


neg_big = -1e30
norm_eps = 1e-06


def joined_2(part, axis, combine):
    gathered = jax.tree.map(lambda a: lax.all_gather(a, axis), part)

    def take(source):
        return jax.tree.map(lambda a: lax.dynamic_index_in_dim(a, source, 0, False), gathered)

    return lax.fori_loop(
        1, lax.axis_size(axis), lambda source, state: combine(state, take(source)), take(0)
    )


def ancestry(parents):
    node_count = parents.shape[-1]
    node_ids = jnp.arange(node_count, dtype=jnp.int32)
    linked = (parents[:, :, None] == node_ids[None, None, :]) & (node_ids[None, :, None] > 0)
    reached = jnp.maximum(linked.astype(jnp.float32), jnp.eye(node_count, dtype=jnp.float32)[None])
    for _ in range(node_count.bit_length()):
        reached = jnp.minimum(
            jnp.einsum("rnm,rmk->rnk", reached, reached, precision=lax.Precision.HIGHEST), 1.0
        )
    return reached


def combine_stats(left_stats, right_stats):
    left_max, left_sum, left_out = left_stats
    right_max, right_sum, right_out = right_stats
    top_score = jnp.maximum(left_max, right_max)
    left_scale = jnp.exp(left_max - top_score)
    right_scale = jnp.exp(right_max - top_score)
    row_count, head_count = left_max.shape
    out_sum = (
        left_out.reshape(row_count, head_count, -1) * left_scale[..., None]
        + right_out.reshape(row_count, head_count, -1) * right_scale[..., None]
    )
    return (
        top_score,
        left_sum * left_scale + right_sum * right_scale,
        out_sum.reshape(row_count, -1),
    )


def finish_rows(stat_sum, stat_out):
    row_count, head_count = stat_sum.shape
    return (
        (stat_out.reshape(row_count, head_count, -1) / stat_sum[..., None])
        .reshape(row_count, -1)
        .astype(jnp.bfloat16)
    )


def project_rows(attn_rows, res_rows, out_weight):
    return res_rows.astype(jnp.float32) + jnp.dot(
        attn_rows, out_weight, preferred_element_type=jnp.float32
    )


def rms_normed(hidden, norm_gain):
    scale_rows = lax.rsqrt(jnp.mean(hidden * hidden, axis=-1, keepdims=True) + norm_eps)
    return (hidden * scale_rows * norm_gain).astype(jnp.bfloat16)


def unit_shares(normed_all, router_weight, expert_ids, tp_rank, units_dev):
    logits = jnp.dot(normed_all, router_weight, preferred_element_type=jnp.float32)
    expert_range = jnp.arange(router_weight.shape[1], dtype=jnp.int32)
    onehot = (expert_ids[:, :, None] == expert_range[None, None, :]).astype(jnp.float32)
    chosen = jnp.sum(logits[:, None, :] * onehot, axis=-1)
    expo_chosen = jnp.exp(chosen)
    expert_probs = expo_chosen / jnp.sum(expo_chosen, axis=-1, keepdims=True)
    routing = jnp.sum(expert_probs[:, :, None] * onehot, axis=1)
    unit_ids = tp_rank * units_dev + jnp.arange(units_dev, dtype=jnp.int32)
    expert_of_unit = unit_ids // (FF_E // UNIT)
    pick = (expert_range[:, None] == expert_of_unit[None, :]).astype(jnp.float32)
    return jnp.dot(routing, pick, precision=lax.Precision.HIGHEST)


def per_device_plain(
    queries,
    new_kv,
    residual,
    placement,
    lengths,
    page_table,
    cache_keys,
    cache_values,
    parents,
    accept_leaf,
    out_weight,
    norm_gain,
    router_weight,
    expert_ids,
    gate_up,
    down_weight,
):
    tok_dev = queries.shape[0]
    tp_count = lax.axis_size("tp")
    tp_rank = lax.axis_index("tp")
    group_rows = tok_dev * tp_count
    slot_count = placement.shape[0]
    kv_width = cache_keys.shape[2]
    page_len = cache_keys.shape[1]
    group_size = HEADS // KV_HEADS
    score_scale = 1.0 / math.sqrt(HEAD)
    row_start = tp_rank * tok_dev
    pulled_q, pulled_kv, pulled_res = (
        lax.all_gather(queries, "req", axis=0, tiled=True),
        lax.all_gather(new_kv, "req", axis=0, tiled=True),
        lax.all_gather(residual, "req", axis=0, tiled=True),
    )
    row_offsets = jnp.arange(tok_dev, dtype=jnp.int32)
    row_pos = row_start + row_offsets
    row_slot = row_pos // DRAFT
    slot_match = row_slot[:, None] == jnp.arange(slot_count, dtype=jnp.int32)[None, :]
    source_group = jnp.sum(jnp.where(slot_match, placement[None, :] // slot_count, 0), axis=1)
    source_rows = source_group * tok_dev + row_offsets
    own_q = jnp.take(pulled_q, source_rows, axis=0)
    own_kv = jnp.take(pulled_kv, source_rows, axis=0)
    own_res = jnp.take(pulled_res, source_rows, axis=0)
    all_q, all_kv = (
        lax.all_gather(own_q, "tp", axis=0, tiled=True),
        lax.all_gather(own_kv, "tp", axis=0, tiled=True),
    )
    local_pages = page_table.shape[1]
    page_ids = page_table[:, :, 0].reshape(-1)
    keys_local = jnp.take(cache_keys, page_ids, axis=0).reshape(
        slot_count, local_pages, page_len, KV_HEADS, HEAD
    )
    values_local = jnp.take(cache_values, page_ids, axis=0).reshape(
        slot_count, local_pages, page_len, KV_HEADS, HEAD
    )
    query_blocks = all_q.reshape(slot_count, DRAFT, KV_HEADS, group_size, HEAD)
    scores = (
        jnp.einsum(
            "sqgrd,sltgd->sqgrlt", query_blocks, keys_local, preferred_element_type=jnp.float32
        )
        * score_scale
    )
    positions = (
        jnp.arange(local_pages, dtype=jnp.int32)[:, None] * tp_count + tp_rank
    ) * page_len + jnp.arange(page_len, dtype=jnp.int32)[None, :]
    is_valid = (positions[None] < lengths[:, None, None])[:, None, None, None]
    scores = jnp.where(is_valid, scores, neg_big)
    block_max = jnp.max(scores, axis=-1)
    weights = jnp.where(is_valid, jnp.exp(scores - block_max[..., None]), 0.0).astype(jnp.bfloat16)
    block_sum = jnp.sum(weights.astype(jnp.float32), axis=-1)
    block_out = jnp.einsum(
        "sqgrlt,sltgd->sqgrld", weights, values_local, preferred_element_type=jnp.float32
    )
    page_top = jnp.max(block_max, axis=-1)
    page_scale = jnp.exp(block_max - page_top[..., None])
    stat_max = page_top.reshape(group_rows, HEADS)
    stat_sum = jnp.sum(block_sum * page_scale, axis=-1).reshape(group_rows, HEADS)
    stat_out = jnp.sum(block_out * page_scale[..., None], axis=-2).reshape(group_rows, HEADS * HEAD)
    reached = ancestry(parents)
    reach_rows = jnp.take(reached.reshape(slot_count * DRAFT, DRAFT), row_pos, axis=0)
    key_slot = jnp.arange(group_rows, dtype=jnp.int32) // DRAFT
    same_slot = key_slot[None, :] == row_slot[:, None]
    allowed = same_slot & (jnp.tile(reach_rows, (1, slot_count)) > 0.5)
    tree_keys = all_kv[:, :kv_width].reshape(group_rows, KV_HEADS, HEAD)
    tree_values = all_kv[:, kv_width:].reshape(group_rows, KV_HEADS, HEAD)
    own_blocks = own_q.reshape(tok_dev, KV_HEADS, group_size, HEAD)
    tree_scores = (
        jnp.einsum("igrd,kgd->igrk", own_blocks, tree_keys, preferred_element_type=jnp.float32)
        * score_scale
    )
    tree_mask = allowed[:, None, None, :]
    tree_scores = jnp.where(tree_mask, tree_scores, neg_big)
    tree_max = jnp.max(tree_scores, axis=-1)
    tree_weights = jnp.where(tree_mask, jnp.exp(tree_scores - tree_max[..., None]), 0.0).astype(
        jnp.bfloat16
    )
    tree_sum = jnp.sum(tree_weights.astype(jnp.float32), axis=-1)
    tree_out = jnp.einsum(
        "igrk,kgd->igrd", tree_weights, tree_values, preferred_element_type=jnp.float32
    )
    own_stats = (
        lax.dynamic_slice_in_dim(stat_max, row_start, tok_dev, 0),
        lax.dynamic_slice_in_dim(stat_sum, row_start, tok_dev, 0),
        lax.dynamic_slice_in_dim(stat_out, row_start, tok_dev, 0),
    )
    tree_stats = (
        tree_max.reshape(tok_dev, HEADS),
        tree_sum.reshape(tok_dev, HEADS),
        tree_out.reshape(tok_dev, HEADS * HEAD),
    )
    joined = combine_stats(own_stats, tree_stats)
    stat_max = lax.dynamic_update_slice_in_dim(stat_max, joined[0], row_start, 0)
    stat_sum = lax.dynamic_update_slice_in_dim(stat_sum, joined[1], row_start, 0)
    stat_out = lax.dynamic_update_slice_in_dim(stat_out, joined[2], row_start, 0)
    normed_all = None
    merged = joined_2((stat_max, stat_sum, stat_out), "tp", combine_stats)
    attn_own = finish_rows(
        lax.dynamic_slice_in_dim(merged[1], row_start, tok_dev, 0),
        lax.dynamic_slice_in_dim(merged[2], row_start, tok_dev, 0),
    )
    hidden_own = project_rows(attn_own, own_res, out_weight)
    normed_own = rms_normed(hidden_own, norm_gain)
    units_dev = gate_up.shape[0]
    unit_width = gate_up.shape[2] // 2
    normed_all = lax.all_gather(normed_own, "tp", axis=0, tiled=True)
    shares = unit_shares(normed_all, router_weight, expert_ids, tp_rank, units_dev)
    gate_both = jnp.einsum("td,udh->tuh", normed_all, gate_up, preferred_element_type=jnp.float32)
    activated = (
        jax.nn.silu(gate_both[..., :unit_width]) * gate_both[..., unit_width:] * shares[:, :, None]
    ).astype(jnp.bfloat16)
    moe_own = lax.psum_scatter(
        jnp.einsum("tuh,uhd->td", activated, down_weight, preferred_element_type=jnp.float32),
        "tp",
        scatter_dimension=0,
        tiled=True,
    )
    layer_out = (hidden_own + moe_own).astype(jnp.bfloat16)
    node_ids = jnp.arange(DRAFT, dtype=jnp.int32)
    leaf_pick = (accept_leaf[:, None] == node_ids[None, :]).astype(jnp.float32)
    path_weight = jnp.einsum("sn,snk->sk", leaf_pick, reached, precision=lax.Precision.HIGHEST)
    path_flags = (path_weight > 0.5).astype(jnp.int32)
    path_rank = jnp.cumsum(path_flags, axis=1) - 1
    chosen_node = (path_flags[:, None, :] > 0) & (path_rank[:, None, :] == node_ids[None, :, None])
    own_choice = jnp.take(chosen_node.reshape(slot_count * DRAFT, DRAFT), row_pos, axis=0)
    spread = same_slot & jnp.tile(own_choice, (1, slot_count))
    accepted = jnp.dot(
        spread.astype(jnp.bfloat16), all_kv, preferred_element_type=jnp.float32
    ).astype(jnp.bfloat16)
    return (attn_own, layer_out, accepted)


def start_all(copies):
    for copy in copies:
        copy.start()
    for copy in copies:
        copy.wait()


def split_kernel(pairs, *refs):
    (
        pages_hbm, placement_hbm, lengths_hbm, leaf_hbm, keys_hbm, values_hbm, queries_hbm,
        new_kv_hbm, residual_hbm, parents_hbm, ids_hbm, gain_hbm,
    ) = refs[:12]
    parts, refs = refs[12 : 12 + pairs], refs[12 + pairs :]
    joined_ref, table_ref, parents_ref, ids_ref, gain_ref = refs[:5]
    pages_ref, placement_ref, lengths_ref, leaf_ref, keys_ref, values_ref, split_ref, sems = refs[5:]
    slot_count = pages_ref.shape[0]
    page_len = keys_ref.shape[1]
    tok_dev = joined_ref.shape[0]
    moves = [
        (pages_hbm, pages_ref),
        (keys_hbm, keys_ref),
        (values_hbm, values_ref),
        (placement_hbm, placement_ref),
        (lengths_hbm, lengths_ref),
        (leaf_hbm, leaf_ref),
        (parents_hbm, parents_ref),
        (ids_hbm, ids_ref),
        (gain_hbm, gain_ref),
    ]
    column = 0
    for source in (queries_hbm, new_kv_hbm, residual_hbm):
        moves.append((source, joined_ref.at[:, column : column + source.shape[1]]))
        column += source.shape[1]
    start_all(
        [pltpu.make_async_copy(a, b, sems.at[k]) for k, (a, b) in enumerate(moves)]
    )
    slot = lax.div(lax.axis_index("tp") * tok_dev, DRAFT)
    numbers = [lax.div(placement_ref[slot], slot_count)]
    numbers += [lengths_ref[s] for s in range(slot_count)]
    numbers += [leaf_ref[s] for s in range(slot_count)]
    for row, number in enumerate(numbers):
        table_ref[row : row + 1, :] = jnp.full((1, WIDE), number, jnp.int32).astype(jnp.float32)
    for head in range(KV_HEADS):
        low = head * HEAD
        for s in range(slot_count):
            page = pages_ref[s]
            split_ref[head // 2, head % 2, s * page_len : (s + 1) * page_len, :] = jnp.concatenate(
                [keys_ref[page, :, low : low + HEAD], values_ref[page, :, low : low + HEAD]], axis=1
            )
    pair = lax.div(lax.axis_index("tp"), 2)
    for k, part in enumerate(parts):
        part[...] = split_ref[lax.bitwise_xor(pair, pairs - 1 - k)]


def number(table_ref, row):
    return jnp.max(table_ref[row : row + 1, :]).astype(jnp.int32)


def route_kernel(kv_width, after_ref, weight_hbm, table_ref, pulled_ref, *refs):
    del after_ref, weight_hbm
    parts, (sent_ref, res_ref, turned_ref, kv_ref) = refs[:-4][::-1], refs[-4:]
    rank = lax.axis_index("tp")
    other = 1 - lax.rem(rank, 2)
    size = parts[0].shape[1]
    for k, part in enumerate(parts):
        turned_ref[k * size : (k + 1) * size, :] = part[other]
    q_width = HEADS * HEAD
    tok_dev = pulled_ref.shape[1]
    rows = pulled_ref[number(table_ref, 0)]
    res_ref[...] = rows[:, q_width + 2 * kv_width :]
    tiles = [rows[:, q_width + c : q_width + c + WIDE] for c in range(0, 2 * kv_width, WIDE)]
    kv_ref[...] = jnp.concatenate(tiles, axis=0)
    head_rows = (HEADS // KV_HEADS) * HEAD
    tail = jnp.zeros((tok_dev, 2 * WIDE - head_rows), rows.dtype)
    for head in range(KV_HEADS):
        q_low = head * head_rows
        pair = jnp.concatenate([rows[:, q_low : q_low + head_rows], tail], axis=1)
        sent_ref[head, :tok_dev, :] = pair[:, :WIDE]
        sent_ref[head, tok_dev : 2 * tok_dev, :] = pair[:, WIDE:]
        k_low = q_width + head * HEAD
        sent_ref[head, 2 * tok_dev :, :] = jnp.concatenate(
            [rows[:, k_low : k_low + HEAD], rows[:, k_low + kv_width : k_low + kv_width + HEAD]],
            axis=1,
        )


def ancestor_rows(parents_ref):
    slot_count = parents_ref.shape[0]
    total = slot_count * DRAFT
    row = jnp.concatenate(
        [parents_ref[s : s + 1, :] + s * DRAFT for s in range(slot_count)], axis=1
    )
    from_ids = lax.broadcasted_iota(jnp.int32, (total, total), 0)
    to_ids = lax.broadcasted_iota(jnp.int32, (total, total), 1)
    linked = (from_ids == jnp.broadcast_to(row, (total, total))) & (lax.rem(to_ids, DRAFT) > 0)
    reached = jnp.where(linked | (from_ids == to_ids), 1.0, 0.0)
    for _ in range((DRAFT - 1).bit_length()):
        half = reached.astype(jnp.bfloat16)
        reached = jnp.minimum(jnp.dot(half, half, preferred_element_type=jnp.float32), 1.0)
    return reached.T


def tree_kernel(
    after_ref, down_hbm, table_ref, parents_ref, ids_ref, down_ref, reach_ref, chosen_ref,
    count_ref, sem,
):
    del after_ref
    copy = pltpu.make_async_copy(down_hbm.at[: down_ref.shape[0]], down_ref, sem)
    copy.start()
    slot_count = parents_ref.shape[0]
    reach_ref[...] = ancestor_rows(parents_ref)
    node_from = lax.broadcasted_iota(jnp.int32, (DRAFT, DRAFT), 0)
    node_to = lax.broadcasted_iota(jnp.int32, (DRAFT, DRAFT), 1)
    upto = jnp.where(node_from <= node_to, 1.0, 0.0).astype(jnp.bfloat16)
    for s in range(slot_count):
        leaf = number(table_ref, 1 + slot_count + s)
        path = reach_ref[pl.ds(s * DRAFT + leaf, 1), s * DRAFT : (s + 1) * DRAFT]
        path = jnp.broadcast_to(path, (DRAFT, DRAFT))
        rank = jnp.dot(path.astype(jnp.bfloat16), upto, preferred_element_type=jnp.float32)
        chosen = (path > 0.5) & (rank == (node_from + 1).astype(jnp.float32))
        chosen_ref[s] = jnp.where(chosen, 1.0, 0.0).astype(jnp.bfloat16)
    ids = ids_ref[...].astype(jnp.float32).T
    names = lax.broadcasted_iota(jnp.int32, count_ref.shape, 1).astype(jnp.float32)
    count = jnp.zeros(count_ref.shape, jnp.float32)
    for k in range(ids.shape[1]):
        count = count + jnp.where(ids[:, k : k + 1] == names, 1.0, 0.0)
    count_ref[...] = count
    copy.wait()


def attend_kernel(units_ref, table_ref, reach_ref, got_ref, res_ref, turned_ref, kv_ref, *refs):
    del units_ref
    parts, (sent_ref, near_ref) = refs[:-2][::-1], refs[-2:]
    slot_count = reach_ref.shape[0] // DRAFT
    sources = got_ref.shape[0]
    tok_dev = res_ref.shape[0]
    page_len = parts[0].shape[1] // slot_count
    per_slot = DRAFT // tok_dev
    group_size = HEADS // KV_HEADS
    f32, bf16 = jnp.float32, jnp.bfloat16
    lane_low = lax.broadcasted_iota(jnp.int32, (DRAFT, WIDE), 1) < HEAD
    rank = lax.axis_index("tp")
    side = lax.rem(rank, 2)
    within = lax.broadcasted_iota(jnp.int32, (1, page_len), 1)
    positions = []
    for k in range(len(parts)):
        pair = lax.bitwise_xor(lax.div(rank, 2), k)
        for page in (2 * pair + side, 2 * pair + 1 - side):
            positions.append(within + page * page_len)
    positions = jnp.concatenate(positions, axis=1)
    dims = (((1,), (1,)), ((), ()))
    scale = 1.0 / math.sqrt(HEAD)
    outs = []
    for s in range(slot_count):
        first = s * per_slot

        def part(k):
            low = k * tok_dev
            return jnp.concatenate(
                [got_ref[first + i, low : low + tok_dev, :] for i in range(per_slot)], axis=0
            )

        q_pair, q_last, tree_kv = part(0).astype(f32) * scale, part(1).astype(f32) * scale, part(2)
        q_rows = jnp.concatenate(
            [
                jnp.where(lane_low, q_pair, 0.0),
                jnp.where(lane_low, pltpu.roll(q_pair, HEAD, 1), 0.0),
                jnp.where(lane_low, q_last, 0.0),
            ],
            axis=0,
        ).astype(bf16)
        at = slice(s * page_len, (s + 1) * page_len)
        cache_kv = jnp.concatenate(
            [a for k, part in enumerate(parts) for a in (part[side, at, :], turned_ref[k * parts[0].shape[1] + at.start : k * parts[0].shape[1] + at.stop, :])],
            axis=0,
        )
        scores = lax.dot_general(q_rows, cache_kv, dims, preferred_element_type=f32)
        is_valid = positions < number(table_ref, 1 + s)
        scores = jnp.where(is_valid, scores, neg_big)
        reach = reach_ref[s * DRAFT : (s + 1) * DRAFT, s * DRAFT : (s + 1) * DRAFT]
        allowed = jnp.concatenate([reach] * group_size, axis=0) > 0.5
        tree_scores = lax.dot_general(q_rows, tree_kv, dims, preferred_element_type=f32)
        tree_scores = jnp.where(allowed, tree_scores, neg_big)
        top = jnp.maximum(
            jnp.max(scores, axis=1, keepdims=True), jnp.max(tree_scores, axis=1, keepdims=True)
        )
        weights = jnp.where(is_valid, jnp.exp(scores - top), 0.0).astype(bf16)
        tree_weights = jnp.where(allowed, jnp.exp(tree_scores - top), 0.0).astype(bf16)
        total = jnp.sum(weights.astype(f32), axis=1, keepdims=True) + jnp.sum(
            tree_weights.astype(f32), axis=1, keepdims=True
        )
        mixed = jnp.dot(weights, cache_kv, preferred_element_type=f32) + jnp.dot(
            tree_weights, tree_kv, preferred_element_type=f32
        )
        outs.append(mixed / total)
    pair_rows, last_rows = [], []
    for out in outs:
        head_out = [out[r * DRAFT : (r + 1) * DRAFT] for r in range(group_size)]
        pair_rows.append(
            jnp.where(lane_low, pltpu.roll(head_out[0], HEAD, 1), head_out[1]).astype(bf16)
        )
        last_rows.append(head_out[2])
    last = jnp.where(lane_low, pltpu.roll(last_rows[0], HEAD, 1), last_rows[1]).astype(bf16)
    res_tiles = [res_ref[:, c * WIDE : (c + 1) * WIDE] for c in range(res_ref.shape[1] // WIDE)]
    sent_ref[...] = jnp.concatenate(pair_rows + [last] + res_tiles, axis=0)
    rows = sent_ref.shape[0]
    near_ref[:rows, :] = sent_ref[...]
    near_ref[rows:, :] = kv_ref[...]


def accept_kernel(rows, chosen_ref, *refs):
    accepted_ref = refs[-1]
    tok_dev, width = accepted_ref.shape
    rank = lax.axis_index("tp")
    per_slot = DRAFT // tok_dev
    place = lax.rem(rank, per_slot)
    chosen = chosen_ref[lax.div(rank, per_slot), pl.ds(pl.multiple_of(place * tok_dev, tok_dev), tok_dev), :]
    is_even, is_first = lax.rem(place, 2) == 0, place < 2
    for c in range(width // WIDE):
        low = rows + c * tok_dev
        pairs = []
        for mine, other in (refs[:2], refs[2:4]):
            a, b = mine[low : low + tok_dev, :], other[low : low + tok_dev, :]
            pairs.append(
                jnp.concatenate([jnp.where(is_even, a, b), jnp.where(is_even, b, a)], axis=0)
            )
        near, far = pairs
        nodes = jnp.concatenate(
            [jnp.where(is_first, near, far), jnp.where(is_first, far, near)], axis=0
        )
        accepted_ref[:, c * WIDE : (c + 1) * WIDE] = jnp.dot(
            chosen, nodes, preferred_element_type=jnp.float32
        ).astype(jnp.bfloat16)


def fetch_kernel(picks, first, after_ref, source_ref, down_hbm, target_ref, down_ref, sems):
    del after_ref
    rows = target_ref.shape[0] // len(picks)
    span = pl.ds(first, down_ref.shape[0])
    copies = [pltpu.make_async_copy(down_hbm.at[span], down_ref, sems.at[len(picks)])]
    for place, k in enumerate(picks):
        pair = lax.bitwise_xor(lax.div(lax.axis_index("tp"), 2), k)
        start = pl.multiple_of(pair * rows, WIDE)
        copies.append(
            pltpu.make_async_copy(
                source_ref.at[pl.ds(start, rows)],
                target_ref.at[place * rows : (place + 1) * rows],
                sems.at[place],
            )
        )
    start_all(copies)


def join_heads(k, rows, group_rows, mine_ref, other_ref, residual_ref):
    f32, bf16 = jnp.float32, jnp.bfloat16
    half = group_rows // 2
    tok_dev = group_rows // KV_HEADS
    model = residual_ref.shape[1]
    res_start = group_rows + half
    rank = lax.axis_index("tp")
    is_even = lax.rem(rank, 2) == 0
    pair = lax.bitwise_xor(lax.div(rank, 2), k)
    lane_low = lax.broadcasted_iota(jnp.int32, (half, WIDE), 1) < HEAD
    mine, other = mine_ref[:rows, :], other_ref[:rows, :]
    even, odd = jnp.where(is_even, mine, other), jnp.where(is_even, other, mine)
    last_even = even[group_rows:res_start].astype(f32)
    last_odd = odd[group_rows:res_start].astype(f32)
    odd_swapped = pltpu.roll(odd[:group_rows].astype(f32), HEAD, 1)
    middle = jnp.concatenate(
        [
            jnp.where(lane_low, last_even, odd_swapped[:half]),
            jnp.where(lane_low, pltpu.roll(last_even, HEAD, 1), odd_swapped[half:]),
        ],
        axis=0,
    ).astype(bf16)
    end = jnp.concatenate(
        [
            jnp.where(lane_low, odd_swapped[:half], pltpu.roll(last_odd, HEAD, 1)),
            jnp.where(lane_low, odd_swapped[half:], last_odd),
        ],
        axis=0,
    ).astype(bf16)
    for q, block in enumerate((even, odd)):
        row = pl.multiple_of((2 * pair + q) * tok_dev, tok_dev)
        residual_ref[pl.ds(row, tok_dev), :] = jnp.concatenate(
            [
                block[res_start + c * tok_dev : res_start + (c + 1) * tok_dev]
                for c in range(model // WIDE)
            ],
            axis=1,
        ).astype(f32)
    return jnp.concatenate([even[:group_rows], middle, end], axis=1)


def keep_own(k, heads_ref, at, attn_ref):
    tok_dev = attn_ref.shape[0]
    width = attn_ref.shape[1] * 2 // KV_HEADS
    rank = lax.axis_index("tp")
    pair = lax.bitwise_xor(lax.div(rank, 2), k)
    own = pl.multiple_of(rank * tok_dev, tok_dev)
    attn_ref[:, pl.ds(pl.multiple_of(pair * width, WIDE), width)] = heads_ref[
        pl.ds(own, tok_dev), at : at + width
    ]


def early_kernel(rows, after_ref, down_hbm, weight_ref, *refs):
    del after_ref
    blocks, refs = refs[:-6], refs[-6:]
    hid_ref, attn_ref, down_ref, residual_ref, x_ref, sem = refs
    start = down_hbm.shape[0] - down_ref.shape[0]
    copy = pltpu.make_async_copy(down_hbm.at[start:], down_ref, sem)
    copy.start()
    group_rows = hid_ref.shape[0]
    residual_ref[...] = jnp.zeros_like(residual_ref)
    width = x_ref.shape[1] * 2 // len(blocks)
    for k in range(len(blocks) // 2):
        x_ref[:, k * width : (k + 1) * width] = join_heads(
            k, rows, group_rows, blocks[2 * k], blocks[2 * k + 1], residual_ref
        )
    for k in range(len(blocks) // 2):
        keep_own(k, x_ref, k * width, attn_ref)
    hid_ref[...] = residual_ref[...] + jnp.dot(
        x_ref[...], weight_ref[...], preferred_element_type=jnp.float32
    )
    copy.wait()


def middle_kernel(k, rows, before_ref, part_ref, weight_ref, mine_ref, other_ref, *refs):
    hid_ref, attn_ref, residual_ref, x_ref = refs
    residual_ref[...] = jnp.zeros_like(residual_ref)
    x_ref[...] = join_heads(k, rows, hid_ref.shape[0], mine_ref, other_ref, residual_ref)
    attn_ref[...] = part_ref[...]
    keep_own(k, x_ref, 0, attn_ref)
    projected = jnp.dot(x_ref[...], weight_ref[...], preferred_element_type=jnp.float32)
    hid_ref[...] = before_ref[...] + residual_ref[...] + projected


def expert_kernel(
    rows, count_ref, router_ref, gain_ref, before_ref, part_ref, *refs
):
    refs, late = refs[:-8], refs[-8:]
    far_ref, hid_ref, hidden_ref, attn_ref, x_ref, normed_ref, share_ref, residual_ref = late
    f32, bf16 = jnp.float32, jnp.bfloat16
    pairs = KV_HEADS // 2
    first, pairs = pairs // 2, pairs // 2 + 1
    down_refs, refs = refs[: KV_HEADS // 2 + 1], refs[KV_HEADS // 2 + 1 :]
    blocks, refs = refs[: 2 * (pairs - first)], refs[2 * (pairs - first) :]
    weight_refs, unit_refs = refs[: pairs - first], refs[pairs - first :]
    unit_weights = [(ref, k) for ref in unit_refs for k in range(ref.shape[0])]
    units = len(unit_weights)
    tok_dev, model = hidden_ref.shape
    sources = KV_HEADS
    group_rows = sources * tok_dev
    rank = lax.axis_index("tp")
    own = pl.multiple_of(rank * tok_dev, tok_dev)
    attn_ref[...] = part_ref[...]
    residual_ref[...] = jnp.zeros_like(residual_ref)
    hidden, width = before_ref[...], x_ref.shape[1] // (pairs - first)
    for q, k in enumerate(reversed(range(first, pairs))):
        heads = join_heads(k, rows, group_rows, blocks[2 * q], blocks[2 * q + 1], residual_ref)
        x_ref[:, q * width : (q + 1) * width] = heads
        keep_own(k, x_ref, q * width, attn_ref)
        hidden += jnp.dot(heads, weight_refs[q][...], preferred_element_type=f32)
    hidden += residual_ref[...]
    hid_ref[...] = hidden
    gain = jnp.concatenate([gain_ref[c : c + 1, :] for c in range(model // WIDE)], axis=1)
    scale = lax.rsqrt(jnp.mean(hidden * hidden, axis=1, keepdims=True) + norm_eps)
    normed_ref[...] = (hidden * scale * gain).astype(bf16)
    hidden_ref[...] = hid_ref[pl.ds(own, tok_dev), :]
    logits = lax.dot_general(
        normed_ref[...], router_ref[...], (((1,), (1,)), ((), ())), preferred_element_type=f32
    )
    experts = router_ref.shape[0]
    expert_range = lax.broadcasted_iota(jnp.int32, (group_rows, experts), 1)
    count = count_ref[...]
    expo = jnp.where(count > 0.0, jnp.exp(logits), 0.0) * count
    routing = expo / jnp.sum(expo, axis=1, keepdims=True)
    unit_width = unit_refs[0].shape[2] // 2
    span = FF_E // unit_width
    each = span if units % span == 0 else 1
    for u in range(0, units, each):
        expert = (rank * units + u) // span
        share = jnp.sum(jnp.where(expert_range == expert, routing, 0.0), axis=1, keepdims=True)
        share_ref[u : u + each] = jnp.broadcast_to(share[None], (each, group_rows, unit_width))

    def one_unit(u):
        ref, k = unit_weights[u]
        both = jnp.dot(normed_ref[...], ref[k], preferred_element_type=f32)
        gate, up = both[:, :unit_width], both[:, unit_width:]
        return (gate / (1.0 + jnp.exp(-gate)) * up * share_ref[u]).astype(bf16)

    down_steps = [(ref, at) for ref in down_refs for at in range(ref.shape[0] // STEP)]
    for i in range(units // STEP):
        act = jnp.concatenate([one_unit(i * STEP + k) for k in range(STEP)], axis=1)
        ref, at = down_steps[i]
        down = ref[at * STEP : (at + 1) * STEP].reshape(STEP * unit_width, model)
        part = jnp.dot(act, down, preferred_element_type=f32)
        hid_ref[...] = part if i == 0 else hid_ref[...] + part
    for k in range(far_ref.shape[0]):
        copy_sums(sources // 4 + k, True, hid_ref, far_ref.at[k])


def copy_sums(k, crossing, hid_ref, ref):
    tok_dev = ref.shape[0]
    rank = lax.axis_index("tp")
    side = lax.rem(rank, 2)
    pair = lax.bitwise_xor(lax.div(rank, 2), k)
    target = 2 * pair + (1 - side if crossing else side)
    row = pl.multiple_of(target * tok_dev, tok_dev)
    ref[...] = hid_ref[pl.ds(row, tok_dev), :].astype(ref.dtype)


def near_kernel(hid_ref, mine_ref, near_ref):
    for k in range(mine_ref.shape[0]):
        copy_sums(k, False, hid_ref, mine_ref.at[k])
    for k in range(near_ref.shape[0]):
        copy_sums(k, True, hid_ref, near_ref.at[k])


def fold_kernel(first, after_ref, mine_ref, got_ref, hidden_ref, *sent_refs):
    del after_ref
    for k, ref in enumerate(sent_refs, first):
        total = mine_ref[k] + got_ref[k - first].astype(jnp.float32)
        if k == 0:
            total = total + hidden_ref[...]
        ref[...] = total.astype(ref.dtype)


def finish_kernel(attn_in_ref, accepted_in_ref, *refs):
    parts, (attn_ref, layer_ref, accepted_ref) = refs[:-3], refs[-3:]
    attn_ref[...] = attn_in_ref[...]
    accepted_ref[...] = accepted_in_ref[...]
    total = parts[0][...]
    for part in parts[1:]:
        total = total + part[...].astype(jnp.float32)
    layer_ref[...] = total.astype(jnp.bfloat16)


def in_hbm(*arrays):
    return tuple(pltpu.with_memory_space_constraint(a, pltpu.HBM) for a in arrays)


def spaces(text):
    kinds = {"a": pl.ANY, "v": pltpu.VMEM}
    return [pl.BlockSpec(memory_space=kinds[c]) for c in text]


def params(mebibytes=12):
    return pltpu.CompilerParams(vmem_limit_bytes=mebibytes << 20)


def cost(mebibytes):
    return pl.CostEstimate(flops=0, transcendentals=0, bytes_accessed=mebibytes << 20)


def swap(rows, mask):
    count = lax.axis_size("tp")
    return lax.ppermute(rows, "tp", [(i, i ^ mask) for i in range(count)])


def fetch(after, array, rows, picks, down_weight, first, units):
    shape = (rows * len(picks),) + array.shape[1:]
    down_shape = (units,) + down_weight.shape[1:]
    return pl.pallas_call(
        functools.partial(fetch_kernel, picks, first),
        out_shape=(pltpu.VMEM(shape, array.dtype), pltpu.VMEM(down_shape, array.dtype)),
        in_specs=spaces("aaa"),
        out_specs=tuple(spaces("vv")),
        scratch_shapes=[pltpu.SemaphoreType.DMA((len(picks) + 1,))],
        compiler_params=params(),
        cost_estimate=cost(2 * (math.prod(shape) + math.prod(down_shape)) >> 20),
        name="fetch",
    )(after, *in_hbm(array, down_weight))


def per_device_packed(
    queries,
    new_kv,
    residual,
    placement,
    lengths,
    page_table,
    cache_keys,
    cache_values,
    parents,
    accept_leaf,
    out_weight,
    norm_gain,
    router_weight,
    expert_ids,
    gate_up,
    down_weight,
):
    f32, bf16 = jnp.float32, jnp.bfloat16
    tok_dev, model = residual.shape
    tp_count = lax.axis_size("tp")
    slot_count = placement.shape[0]
    page_len, kv_width = cache_keys.shape[1:]
    group_rows = tok_dev * tp_count
    sent = lambda rows: jax.ShapeDtypeStruct((tp_count, rows, WIDE), bf16)
    dma = pltpu.SemaphoreType.DMA
    slots_smem = pltpu.SMEM((slot_count,), jnp.int32)
    pairs = tp_count // 2
    part = jax.ShapeDtypeStruct((2, slot_count * page_len, WIDE), bf16)
    loaded = (
        page_table.reshape(slot_count),
        placement,
        lengths,
        accept_leaf,
        cache_keys,
        cache_values,
        queries,
        new_kv,
        residual,
        parents,
        expert_ids.T,
        norm_gain.reshape(model // WIDE, WIDE),
    )
    *parts, joined, table, parents, ids, gain = pl.pallas_call(
        functools.partial(split_kernel, pairs),
        out_shape=(part,) * pairs
        + (
            jax.ShapeDtypeStruct((tok_dev, 2 * (model + kv_width)), bf16),
            pltpu.VMEM((8, WIDE), f32),
        )
        + tuple(pltpu.VMEM(a.shape, a.dtype) for a in loaded[9:]),
        in_specs=spaces("a" * len(loaded)),
        out_specs=tuple(spaces("v" * (pairs + 5))),
        scratch_shapes=[
            slots_smem,
            slots_smem,
            slots_smem,
            slots_smem,
            pltpu.VMEM(cache_keys.shape, bf16),
            pltpu.VMEM(cache_values.shape, bf16),
            pltpu.VMEM((pairs,) + part.shape, bf16),
            dma((len(loaded),)),
        ],
        compiler_params=params(),
        cost_estimate=cost(4),
        name="split",
    )(*in_hbm(*loaded))
    parts = parts[::-1]
    parts = [parts[0]] + [swap(parts[k], 2 * k) for k in range(1, pairs)]
    pulled = lax.all_gather(joined, "req", axis=0)
    nodes = slot_count * DRAFT
    units = gate_up.shape[0]
    cuts = [units * c // 20 // STEP * STEP for c in CUTS]
    ready = cuts[0]
    down_ready, reach, chosen, count = pl.pallas_call(
        tree_kernel,
        out_shape=(
            pltpu.VMEM((ready,) + down_weight.shape[1:], bf16),
            jax.ShapeDtypeStruct((nodes, nodes), f32),
            jax.ShapeDtypeStruct((slot_count, DRAFT, DRAFT), bf16),
            jax.ShapeDtypeStruct((group_rows, router_weight.shape[1]), f32),
        ),
        in_specs=spaces("aavvv"),
        out_specs=tuple(spaces("vvvv")),
        scratch_shapes=[dma],
        compiler_params=params(),
        cost_estimate=cost(8),
        name="tree",
    )(pulled, *in_hbm(down_weight), table, parents, ids)
    kv_rows = 2 * kv_width // WIDE * tok_dev
    packed, own_res, turned, own_kv = pl.pallas_call(
        functools.partial(route_kernel, kv_width),
        out_shape=(
            sent(3 * tok_dev),
            jax.ShapeDtypeStruct(residual.shape, bf16),
            jax.ShapeDtypeStruct((pairs * part.shape[1], WIDE), bf16),
            jax.ShapeDtypeStruct((kv_rows, WIDE), bf16),
        ),
        in_specs=spaces("aavv" + "v" * pairs),
        out_specs=tuple(spaces("vvvv")),
        compiler_params=params(),
        cost_estimate=cost(4),
        name="route",
    )(down_ready, *in_hbm(down_weight), table, pulled, *parts[::-1])
    turned = swap(turned, 1)
    packed = lax.all_to_all(packed, "tp", 0, 0, tiled=True)
    gate_up = pltpu.with_memory_space_constraint(gate_up, pltpu.VMEM)
    block_rows = group_rows + group_rows // 2 + (model // WIDE) * tok_dev
    block, near_block = pl.pallas_call(
        attend_kernel,
        out_shape=(
            jax.ShapeDtypeStruct((block_rows, WIDE), bf16),
            jax.ShapeDtypeStruct((block_rows + kv_rows, WIDE), bf16),
        ),
        in_specs=spaces("v" * (7 + pairs)),
        out_specs=tuple(spaces("vv")),
        compiler_params=params(),
        cost_estimate=cost(8),
        name="attend",
    )(gate_up, table, reach, packed, own_res, turned, own_kv, *parts[::-1])
    reached = [swap(near_block, 2)] + [swap(block, 2 * k) for k in range(2, pairs)]
    weights, downs, after = [], [down_ready], block
    rows = out_weight.shape[0] // pairs
    for k, picks in zip(ORDER, FETCHES):
        start, size = cuts[len(weights)], cuts[len(weights) + 1] - cuts[len(weights)]
        weight, down = fetch(after, out_weight, rows, picks, down_weight, start, size)
        fetched = (reached[k - 1], weight, down)
        reached[k - 1], weight, down = lax.optimization_barrier(fetched)
        downs.append(down)
        after = reached[k - 1]
        weights.append(weight)
    blocks = [block, swap(near_block, 1)]
    blocks += [a for got in reached for a in (got, swap(got, 1))]
    before, attn_part, down_rest = pl.pallas_call(
        functools.partial(early_kernel, block_rows),
        out_shape=(
            jax.ShapeDtypeStruct((group_rows, model), f32),
            pltpu.VMEM(queries.shape, bf16),
            pltpu.VMEM((units - cuts[-1],) + down_weight.shape[1:], bf16),
        ),
        in_specs=spaces("aav" + "v" * pairs),
        out_specs=tuple(spaces("vvv")),
        scratch_shapes=[
            pltpu.VMEM((group_rows, model), f32),
            pltpu.VMEM((group_rows, HEADS * HEAD // 2), bf16),
            dma,
        ],
        compiler_params=params(),
        cost_estimate=cost(4),
        name="early",
    )(after, *in_hbm(down_weight), weights[0], *blocks[:pairs])
    accepted = pl.pallas_call(
        functools.partial(accept_kernel, block_rows),
        out_shape=pltpu.VMEM(new_kv.shape, bf16),
        in_specs=spaces("vvvvv"),
        out_specs=spaces("v")[0],
        compiler_params=params(),
        cost_estimate=cost(1),
        name="accept",
    )(chosen, near_block, *blocks[1:4])
    unit_weights = (gate_up,)
    before, attn_part = pl.pallas_call(
        functools.partial(middle_kernel, pairs - 1, block_rows),
        out_shape=(
            jax.ShapeDtypeStruct((group_rows, model), f32),
            pltpu.VMEM(queries.shape, bf16),
        ),
        in_specs=spaces("v" * 5),
        out_specs=tuple(spaces("vv")),
        scratch_shapes=[
            pltpu.VMEM((group_rows, model), f32),
            pltpu.VMEM((group_rows, HEADS * HEAD // pairs), bf16),
        ],
        compiler_params=params(),
        cost_estimate=cost(1),
        name="middle",
    )(before, attn_part, weights[1], *blocks[-2:])
    far, sums, hidden, attn_own = pl.pallas_call(
        functools.partial(expert_kernel, block_rows),
        out_shape=(
            jax.ShapeDtypeStruct((pairs // 2, tok_dev, model), bf16),
            jax.ShapeDtypeStruct((group_rows, model), f32),
            jax.ShapeDtypeStruct((tok_dev, model), f32),
            pltpu.VMEM(queries.shape, bf16),
        ),
        in_specs=spaces("v" * (6 + len(downs) + 3 + len(unit_weights))),
        out_specs=tuple(spaces("vvvv")),
        scratch_shapes=[
            pltpu.VMEM((group_rows, HEADS * HEAD // pairs), bf16),
            pltpu.VMEM((group_rows, model), bf16),
            pltpu.VMEM((units, group_rows, gate_up.shape[2] // 2), f32),
            pltpu.VMEM((group_rows, model), f32),
        ],
        compiler_params=params(),
        name="experts",
    )(
        count,
        pltpu.with_memory_space_constraint(router_weight.T, pltpu.VMEM),
        gain,
        before,
        attn_part,
        *downs,
        down_rest,
        *blocks[pairs : pairs + 2],
        weights[2],
        *unit_weights,
    )
    far = swap(far, 1)
    mine, near = pl.pallas_call(
        near_kernel,
        out_shape=(
            jax.ShapeDtypeStruct((pairs, tok_dev, model), f32),
            jax.ShapeDtypeStruct((pairs // 2, tok_dev, model), bf16),
        ),
        in_specs=spaces("v"),
        out_specs=tuple(spaces("vv")),
        compiler_params=params(),
        cost_estimate=cost(4),
        name="near",
    )(sums)
    near = swap(near, 1)
    fold = lambda first, after, got: pl.pallas_call(
        functools.partial(fold_kernel, first),
        out_shape=tuple(
            jax.ShapeDtypeStruct((tok_dev, model), f32 if k == 0 else bf16)
            for k in range(first, first + pairs // 2)
        ),
        in_specs=spaces("avvv"),
        out_specs=tuple(spaces("v" * (pairs // 2))),
        compiler_params=params(),
        cost_estimate=cost(1),
        name="fold",
    )(after, mine, got, hidden)
    sums = fold(pairs // 2, hidden, far)
    folded = sums[0]
    sums = [swap(a, 2 * k) for k, a in enumerate(sums, pairs // 2)]
    close = fold(0, folded, near)
    sums = [close[0]] + [swap(close[k], 2 * k) for k in range(1, pairs // 2)] + sums
    return pl.pallas_call(
        finish_kernel,
        out_shape=(
            jax.ShapeDtypeStruct(queries.shape, bf16),
            jax.ShapeDtypeStruct(residual.shape, bf16),
            jax.ShapeDtypeStruct(new_kv.shape, bf16),
        ),
        in_specs=spaces("v" * (2 + pairs)),
        out_specs=tuple(spaces("vvv")),
        compiler_params=params(),
        name="finish",
    )(attn_own, accepted, sums[0], *sums[:0:-1])


def per_device(queries, new_kv, residual, placement, *rest):
    tok_dev = queries.shape[0]
    one_head_each = lax.axis_size("tp") == KV_HEADS
    whole_tiles = tok_dev % 16 == 0 and placement.shape[0] == 2 and tok_dev * KV_HEADS == 2 * DRAFT
    if one_head_each and whole_tiles and rest[1].shape[1] == 1:
        return per_device_packed(queries, new_kv, residual, placement, *rest)
    return per_device_plain(queries, new_kv, residual, placement, *rest)


def solution(mesh):
    in_specs = (
        P(("req", "tp"), None),
        P(("req", "tp"), None),
        P(("req", "tp"), None),
        P("req"),
        P("req"),
        P("req", None, "tp"),
        P(("req", "tp"), None, None),
        P(("req", "tp"), None, None),
        P("req", None),
        P("req"),
        P(),
        P(),
        P(),
        P("req", None),
        P("tp", None, None),
        P("tp", None, None),
    )
    out_specs = (P(("req", "tp"), None), P(("req", "tp"), None), P(("req", "tp"), None))
    return jax.shard_map(
        per_device, mesh=mesh, in_specs=in_specs, out_specs=out_specs, check_vma=False
    )
```
